32 devices in a mesh: groups: 2 (over y), span: 4 (over z), mp: 2 (over x), seq: 2 (over core).
Axes of the slice: x: 2, y: 2, z: 4, core: 2. Of those that a mesh axis runs over, the one named last changes fastest.
Arguments:
- query: bfloat16 [4, 8, 144, 3072], P(None, ('groups', 'span'), None, ('mp', 'seq')), parts along dimension 1, may hold values from -600 to 600
- noisy_kv: bfloat16 [4, 2, 8, 144, 3072], P(None, None, ('groups', 'span'), None, ('mp', 'seq')), parts along dimension 2, may hold values from -11 to 11
- clean_kv: bfloat16 [2, 8, 144, 3072], P(None, ('groups', 'span'), None, ('mp', 'seq')), parts along dimension 1, may hold values from -11 to 11
- causal_mask: int32 [8, 4], P('groups'), parts along dimension 0, may hold values from 0 to 1, as said below
- step_index: int32 [8, 4], P('groups'), parts along dimension 0, may hold values from 0 to 63, as said below
- finished: bfloat16 [8, 144, 3072], P(('groups', 'span'), None, ('mp', 'seq')), parts along dimension 0, may hold values from -6 to 6
- w_in: bfloat16 [3072, 512], P(('mp', 'seq')), may hold values from -0.109375 to 0.109375
- conv_w: bfloat16 [3, 512, 512], replicated, may hold values from -0.15625 to 0.15625
- fade_count: int32 [8], P(('groups', 'span')), parts along dimension 0, may hold values from 0 to 2, as said below
Outputs:
- attended: bfloat16 [4, 8, 144, 3072], P(None, ('groups', 'span'), None, ('mp', 'seq')), parts along dimension 1
- decoded: bfloat16 [8, 144, 512], P(('groups', 'span'), ('mp', 'seq')), parts along dimension 0
The draws below stay inside these ranges and needn't reach their ends.
There are 2 independent parts, one for each index of `groups`. The reference program is written for one: setup_inputs(seed, part) draws one part's arguments, and reference() takes and returns one part's arrays. A program takes and returns all parts, laid end to end along the dimension named above; an argument that names none is the same for every part. Nothing has to cross between parts.
Inputs may be any that keep to these rules, and one draw needn't show every extreme that they name: `causal_mask`: zero on and above the diagonal. `step_index`: each row counts up by one from its first entry; some row starts at 0 and some at 60. `fade_count`: some segment other than the first has 2.
All inputs are finite; a program needn't handle non-finite values.
Results may differ from the reference program's by a relative error of at most 0.015.
Values may be sent and summed in bfloat16 or wider, within the bound.
No kernel may reach another device: no remote copies, remote signals or barrier semaphores. Data moves between devices by JAX's collectives and lax.ppermute only.
A program may use at most 64 MiB of HBM per device.

```python
import math
import jax
import jax.numpy as jnp
from jax import lax

FR = 6
SP = 24
CT = 144
HEADS = 24
HD = 128
DC = 512
KT = 3
FADE = 2
NSTEPS = 64
STEPS = 4
NSEG = 4


def head_gains():
    exponent = jnp.arange(HEADS).astype(jnp.float32) / (HEADS - 1) - 0.5
    gains = 3.0 ** exponent
    return jnp.repeat(gains, HD)


def attention_inputs(key):
    folded = jax.random.fold_in(key, 7)
    key_query, key_keys, key_values = jax.random.split(folded, 3)
    columns = HEADS * HD
    shape = (STEPS, NSEG, CT, columns)
    queries = jnp.clip(jax.random.normal(key_query, shape, jnp.float32), -6.0, 6.0)
    all_keys = jnp.clip(jax.random.normal(key_keys, shape, jnp.float32), -6.0, 6.0)
    values = jnp.clip(jax.random.normal(key_values, shape, jnp.float32), -6.0, 6.0)
    values = values * head_gains()
    return (queries, jnp.stack([all_keys, values], 1))


def draw_query(key, part):
    return attention_inputs(key)[0].astype(jnp.bfloat16)


def draw_noisy_kv(key, part):
    return attention_inputs(key)[1].astype(jnp.bfloat16)


def draw_clean_kv(key, part):
    folded = jax.random.fold_in(key, 13)
    key_keys, key_values = jax.random.split(folded, 2)
    shape = (NSEG, CT, HEADS * HD)
    all_keys = jnp.clip(jax.random.normal(key_keys, shape, jnp.float32), -6.0, 6.0)
    values = jnp.clip(jax.random.normal(key_values, shape, jnp.float32), -6.0, 6.0)
    values = values * head_gains()
    return jnp.stack([all_keys, values], 0).astype(jnp.bfloat16)


def draw_causal_mask(key, part):
    folded = jax.random.fold_in(key, 21)
    key_bits, key_row, key_col = jax.random.split(folded, 3)
    chosen = jax.random.randint(key_bits, (NSEG, NSEG), 0, 2)
    row_ids = jnp.arange(NSEG)[:, None]
    col_ids = jnp.arange(NSEG)[None, :]
    result = jnp.where((chosen > 0) & (row_ids > col_ids), 1, 0).astype(jnp.int32)
    forced_row = jax.random.randint(key_row, (), 1, NSEG)
    forced_col = jax.random.randint(key_col, (), 0, NSEG - 1)
    result = result.at[forced_row, 0].set(1)
    result = result.at[NSEG - 1, forced_col].set(1)
    return result.astype(jnp.int32)


def draw_step_index(key, part):
    folded = jax.random.fold_in(key, 31)
    key_first, key_spot = jax.random.split(folded, 2)
    first_index = jax.random.randint(key_first, (NSEG,), 0, NSTEPS - STEPS + 1)
    low_spot = jax.random.randint(key_spot, (), 0, NSEG)
    first_index = first_index.at[low_spot].set(0)
    first_index = first_index.at[(low_spot + 1) % NSEG].set(NSTEPS - STEPS)
    offsets = jnp.arange(STEPS).astype(jnp.int32)
    return (first_index[:, None] + offsets[None, :]).astype(jnp.int32)


def draw_fade_count(key, part):
    folded = jax.random.fold_in(key, 41)
    key_counts, key_spot = jax.random.split(folded, 2)
    counts = jax.random.randint(key_counts, (NSEG,), 0, FADE + 1)
    full_spot = jax.random.randint(key_spot, (), 1, NSEG)
    return counts.at[full_spot].set(FADE).astype(jnp.int32)


def block_scale(own_key, shape, cuts, low, high):
    def one(dim, blocks):
        steps = jax.random.uniform(jax.random.fold_in(jax.random.fold_in(own_key, 6), dim), (blocks,), jnp.float32, low / len(cuts), high / len(cuts))
        return jnp.repeat(jnp.exp(steps), shape[dim] // blocks).reshape((-1,) + (1,) * (len(shape) - dim - 1))

    gain = one(*cuts[0])
    for cut in cuts[1:]:
        gain = gain * one(*cut)
    return gain


def noise(own_key, dims, spread, limit, pieces=(), held_as=jnp.bfloat16):
    drawn = spread * jax.random.normal(own_key, dims, jnp.float32)
    if pieces:
        drawn = drawn * block_scale(own_key, dims, pieces, -0.22, 0.18)
    return jnp.clip(drawn, -limit, limit).astype(held_as)


def setup_inputs(seed: int = 0, part: int = 0) -> dict:
    key_list = jax.random.split(jax.random.key(seed), 10)
    part_splits = jax.random.split(jax.random.fold_in(key_list[9], part), 10)
    query = draw_query(jax.random.fold_in(jax.random.fold_in(key_list[9], part), 71), part)
    noisy_kv = draw_noisy_kv(jax.random.fold_in(jax.random.fold_in(key_list[9], part), 71), part)
    clean_kv = draw_clean_kv(jax.random.fold_in(jax.random.fold_in(key_list[9], part), 71), part)
    causal_mask = draw_causal_mask(jax.random.fold_in(jax.random.fold_in(key_list[9], part), 71), part)
    step_index = draw_step_index(jax.random.fold_in(jax.random.fold_in(key_list[9], part), 71), part)
    finished = noise(part_splits[5], (NSEG, CT, HEADS * HD), 1.0, 6.0, ((0, 4), (2, 4)))
    w_in = noise(key_list[6], (HEADS * HD, DC), (HEADS * HD) ** -0.5, 0.109375, ((0, 4),))
    conv_w = noise(key_list[7], (KT, DC, DC), (KT * DC) ** -0.5, 0.15625)
    fade_count = draw_fade_count(jax.random.fold_in(jax.random.fold_in(key_list[9], part), 71), part)
    return {"query": query, "noisy_kv": noisy_kv, "clean_kv": clean_kv, "causal_mask": causal_mask, "step_index": step_index, "finished": finished, "w_in": w_in, "conv_w": conv_w, "fade_count": fade_count}


def noise_level(indices):
    fraction = 1.0 - indices.astype(jnp.float32) / NSTEPS
    return 3.0 * fraction / (1.0 + 2.0 * fraction)

def rounded_copy(values):
    return lax.optimization_barrier(values.astype(jnp.bfloat16)).astype(jnp.float32)

def reference(query, noisy_kv, clean_kv, causal_mask, step_index, finished, w_in, conv_w, fade_count):
    scales = (0.5 + noise_level(step_index)) / math.sqrt(HD)
    clean_keys = clean_kv[0].reshape(NSEG * CT, HEADS, HD).astype(jnp.float32)
    clean_values = clean_kv[1].reshape(NSEG * CT, HEADS, HD).astype(jnp.float32)

    def one_segment(segment_id):
        queries = query[:, segment_id].reshape(STEPS, CT, HEADS, HD).astype(jnp.float32)
        own_keys = noisy_kv[:, 0, segment_id].reshape(STEPS, CT, HEADS, HD).astype(jnp.float32)
        own_values = noisy_kv[:, 1, segment_id].reshape(STEPS, CT, HEADS, HD).astype(jnp.float32)
        segment_scale = scales[segment_id][:, None, None, None]
        visible = jnp.repeat(causal_mask[segment_id], CT) > 0
        bias = jnp.where(visible, 0.0, -1e+30).astype(jnp.float32)
        own_scores = jnp.einsum('srhd,skhd->shrk', queries, own_keys) * segment_scale
        far_scores = jnp.einsum('srhd,khd->shrk', queries, clean_keys) * segment_scale + bias
        highest = jnp.maximum(own_scores.max(-1), far_scores.max(-1))[..., None]
        own_weights = jnp.exp(own_scores - highest)
        far_weights = jnp.exp(far_scores - highest)
        totals = own_weights.sum(-1) + far_weights.sum(-1)
        numer = jnp.einsum('shrk,skhd->shrd', rounded_copy(own_weights), own_values)
        numer = numer + jnp.einsum('shrk,khd->shrd', rounded_copy(far_weights), clean_values)
        averaged = numer / totals[..., None]
        normed = averaged * lax.rsqrt(lax.optimization_barrier(jnp.mean(averaged * averaged, axis=(1, 3), keepdims=True)) + 1e-06)
        return normed.transpose(0, 2, 1, 3).reshape(STEPS, CT, HEADS * HD).astype(jnp.bfloat16)
    per_segment = lax.map(one_segment, jnp.arange(NSEG))
    attended = jnp.transpose(per_segment, (1, 0, 2, 3))
    hidden = jnp.dot(finished.reshape(NSEG * CT, HEADS * HD), w_in, preferred_element_type=jnp.float32)
    hidden = hidden.astype(jnp.bfloat16).reshape(NSEG, SP, FR, DC)
    cache = jnp.concatenate([jnp.zeros((1, SP, KT - 1, DC), jnp.bfloat16), hidden[:-1, :, FR - KT + 1:]], 0)
    extended = jnp.concatenate([cache, hidden], 2)
    conv_total = jnp.zeros((NSEG * SP * FR, DC), jnp.float32)
    for tap_index in range(KT):
        window = extended[:, :, KT - 1 - tap_index:KT - 1 - tap_index + FR].reshape(NSEG * SP * FR, DC)
        conv_total = conv_total + jnp.dot(window, conv_w[tap_index], preferred_element_type=jnp.float32)
    frames = jax.nn.silu(conv_total).astype(jnp.bfloat16).reshape(NSEG, SP, FR, DC)
    tails = frames[:, :, FR - FADE:]
    prev_tails = jnp.concatenate([jnp.zeros((1, SP, FADE, DC), jnp.bfloat16), tails[:-1]], 0)
    padded = jnp.concatenate([prev_tails, jnp.zeros((NSEG, SP, FADE, DC), jnp.bfloat16)], 2)

    def align(pad_one, fade_one):
        return lax.dynamic_slice_in_dim(pad_one, (FADE - fade_one).astype(jnp.int32), FADE, 1)
    aligned = jax.vmap(align)(padded, fade_count)
    frame_pos = jnp.arange(FADE).astype(jnp.float32)
    fade_float = fade_count.astype(jnp.float32)[:, None]
    active = (frame_pos[None, :] < fade_float) & (jnp.arange(NSEG)[:, None] > 0)
    weights = jnp.where(active, (frame_pos[None, :] + 1.0) / (fade_float + 1.0), 1.0)
    head_frames = weights[:, None, :, None] * frames[:, :, :FADE].astype(jnp.float32)
    head_frames = head_frames + (1.0 - weights)[:, None, :, None] * aligned.astype(jnp.float32)
    blended = jnp.concatenate([head_frames, frames[:, :, FADE:].astype(jnp.float32)], 2)
    decoded = blended.astype(jnp.bfloat16).reshape(NSEG, CT, DC)
    return (attended, decoded)
```

```python
import functools
import math

import jax
import jax.numpy as jnp
from jax import lax
from jax.experimental import pallas as pl
from jax.experimental.pallas import tpu as pltpu
from jax.sharding import PartitionSpec as P

FR = 6
HD = 128
KT = 3
FADE = 2
NSTEPS = 64
LOG2E = 1.4426950408889634
VMEM_LIMIT = 24 * 1024 * 1024

SMEM_SPEC = pl.BlockSpec(memory_space=pltpu.SMEM)
VMEM_SPEC = pl.BlockSpec(memory_space=pltpu.VMEM)


def params():
    return pltpu.CompilerParams(vmem_limit_bytes=VMEM_LIMIT)


def cost(flops, nbytes):
    return pl.CostEstimate(flops=flops, bytes_accessed=nbytes, transcendentals=0)


def hop(value, axis, steps):
    count = lax.axis_size(axis)
    return lax.ppermute(value, axis, [(source, source + steps) for source in range(count - steps)])


def swap(value, axes, offset):
    count = lax.axis_size(axes)
    if count & (count - 1) == 0:
        pairs = [(source, source ^ offset) for source in range(count)]
    else:
        pairs = [(source, (source + offset) % count) for source in range(count)]
    return lax.ppermute(value, axes, pairs)


def target_of(axes, offset):
    count = lax.axis_size(axes)
    mine = lax.axis_index(axes)
    if count & (count - 1) == 0:
        return mine ^ offset
    return lax.rem(mine + offset, count)


def nt_dot(left, right):
    return lax.dot_general(left, right, (((1,), (1,)), ((), ())), preferred_element_type=jnp.float32)


def nn_dot(left, right):
    return jnp.dot(left, right, preferred_element_type=jnp.float32)


def step_factor(step_ref, position, step, width):
    index = jnp.full((1, width), step_ref[position, step], jnp.int32).astype(jnp.float32)
    fraction = 1.0 - index / NSTEPS
    level = 3.0 * fraction / (1.0 + 2.0 * fraction)
    return (0.5 + level) * (LOG2E / math.sqrt(HD))


def scaled_scores(step_ref, position, q_ref, keys, rows):
    steps = q_ref.shape[0]
    queries = q_ref[:, 0].reshape(steps * rows, HD)
    scores = nt_dot(queries, keys)
    parts = [
        scores[step * rows : (step + 1) * rows]
        * step_factor(step_ref, position, step, keys.shape[0])
        for step in range(steps)
    ]
    return jnp.concatenate(parts, 0)


def put_lane(ref, lane, column):
    lanes = lax.broadcasted_iota(jnp.int32, ref.shape, 1)
    ref[...] = jnp.where(lanes == lane, column, ref[...])


def get_lane(ref, lane):
    lanes = lax.broadcasted_iota(jnp.int32, ref.shape, 1)
    return jnp.sum(jnp.where(lanes == lane, ref[...], 0.0), axis=1, keepdims=True)


def own_kernel(step_ref, q_ref, kv_ref, acc_ref, top_ref, total_ref):
    head = pl.program_id(0)
    position = lax.axis_index("span")
    steps, _, rows, _ = q_ref.shape

    @pl.when(head == 0)
    def _():
        top_ref[...] = jnp.zeros_like(top_ref)
        total_ref[...] = jnp.zeros_like(total_ref)

    tops, totals = [], []
    for step in range(steps):
        scores = nt_dot(q_ref[step, 0], kv_ref[step, 0, 0])
        scores = scores * step_factor(step_ref, position, step, rows)
        top = jnp.max(scores, axis=1, keepdims=True)
        weights = jnp.exp2(scores - top)
        acc_ref[step] = nn_dot(weights.astype(jnp.bfloat16), kv_ref[step, 1, 0])
        tops.append(top)
        totals.append(jnp.sum(weights, axis=1, keepdims=True))
    put_lane(top_ref, head, jnp.concatenate(tops, 0))
    put_lane(total_ref, head, jnp.concatenate(totals, 0))


def visible(mask_ref, position, back):
    return (position >= back) & (mask_ref[position, jnp.maximum(position - back, 0)] > 0)


def mid_kernel(backs, step_ref, mask_ref, q_ref, *refs):
    count = len(backs)
    key_refs, value_refs = refs[:count], refs[count : 2 * count]
    acc_in, top_in, total_in, acc_ref, top_ref, total_ref = refs[2 * count :]
    head = pl.program_id(0)
    position = lax.axis_index("span")
    steps, _, rows, _ = q_ref.shape

    @pl.when(head == 0)
    def _():
        top_ref[...] = top_in[...]
        total_ref[...] = total_in[...]

    acc_ref[...] = acc_in[...]
    for back, key_ref, value_ref in zip(backs, key_refs, value_refs):

        @pl.when(visible(mask_ref, position, back))
        def _(key_ref=key_ref, value_ref=value_ref):
            scores = scaled_scores(step_ref, position, q_ref, key_ref[0], rows)
            old = get_lane(top_ref, head)
            top = jnp.maximum(old, jnp.max(scores, axis=1, keepdims=True))
            factor = jnp.exp2(old - top)
            weights = jnp.exp2(scores - top)
            total = get_lane(total_ref, head) * factor + jnp.sum(weights, axis=1, keepdims=True)
            acc = acc_ref[...].reshape(steps * rows, HD) * factor
            acc = acc + nn_dot(weights.astype(jnp.bfloat16), value_ref[0])
            acc_ref[...] = acc.reshape(steps, rows, HD)
            put_lane(top_ref, head, top)
            put_lane(total_ref, head, total)


def last_kernel(back, step_ref, mask_ref, q_ref, key_ref, acc_in, top_in, total_in, acc_ref, w_ref):
    head = pl.program_id(0)
    position = lax.axis_index("span")
    steps, _, rows, _ = q_ref.shape
    seen = visible(mask_ref, position, back)

    @pl.when(seen)
    def _():
        scores = scaled_scores(step_ref, position, q_ref, key_ref[0], rows)
        old = get_lane(top_in, head)
        top = jnp.maximum(old, jnp.max(scores, axis=1, keepdims=True))
        factor = jnp.exp2(old - top)
        weights = jnp.exp2(scores - top)
        total = get_lane(total_in, head) * factor + jnp.sum(weights, axis=1, keepdims=True)
        inverse = 1.0 / total
        w_ref[0] = (weights * inverse).astype(jnp.bfloat16)
        acc = acc_in[...].reshape(steps * rows, HD) * (factor * inverse)
        acc_ref[...] = acc.reshape(steps, rows, HD)

    @pl.when(jnp.logical_not(seen))
    def _():
        w_ref[...] = jnp.zeros_like(w_ref)
        acc = acc_in[...].reshape(steps * rows, HD) * (1.0 / get_lane(total_in, head))
        acc_ref[...] = acc.reshape(steps, rows, HD)


def average_kernel(acc_in, w_ref, value_ref, out_ref, square_ref):
    steps, rows, columns = acc_in.shape
    squares = jnp.zeros((steps * rows, HD), jnp.float32)
    for head in range(columns // HD):
        lanes = slice(head * HD, (head + 1) * HD)
        average = acc_in[:, :, lanes].reshape(steps * rows, HD)
        average = average + nn_dot(w_ref[head], value_ref[0, :, lanes])
        out_ref[:, :, lanes] = average.reshape(steps, rows, HD)
        squares = squares + average * average
    square_ref[...] = jnp.sum(squares.T, axis=0, keepdims=True)


def scale_kernel(width, *refs):
    average_ref, out_ref = refs[0], refs[-1]
    total = refs[1][...]
    for ref in refs[2:-1]:
        total = total + ref[...]
    inverse = lax.rsqrt(total / width + 1e-06)
    steps, rows, columns = average_ref.shape
    spread = jnp.broadcast_to(inverse, (HD, steps * rows)).T
    for head in range(columns // HD):
        lanes = slice(head * HD, (head + 1) * HD)
        average = average_ref[:, :, lanes].reshape(steps * rows, HD)
        out_ref[:, 0, :, lanes] = (average * spread).astype(jnp.bfloat16).reshape(steps, rows, HD)


def attention(query, noisy_kv, clean_kv, causal_mask, step_index):
    steps, _, rows, columns = query.shape
    heads = columns // HD
    row_count = steps * rows
    span = lax.axis_size("span")
    keys, values = [clean_kv[0]], [clean_kv[1]]
    for _ in range(span - 1):
        keys.append(hop(keys[-1], "span", 1))
        values.append(hop(values[-1], "span", 1))

    q_spec = pl.BlockSpec((steps, 1, rows, HD), lambda head: (0, 0, 0, head))
    block_spec = pl.BlockSpec((1, rows, HD), lambda head: (0, 0, head))
    acc_spec = pl.BlockSpec((steps, rows, HD), lambda head: (0, 0, head))
    stat_spec = pl.BlockSpec((row_count, HD), lambda head: (0, 0))
    acc_shape = jax.ShapeDtypeStruct((steps, rows, columns), jnp.float32)
    stat_shape = jax.ShapeDtypeStruct((row_count, HD), jnp.float32)
    pair_flops = 4 * row_count * rows * columns
    carry = pl.pallas_call(
        own_kernel,
        grid=(heads,),
        in_specs=[
            SMEM_SPEC,
            q_spec,
            pl.BlockSpec((steps, 2, 1, rows, HD), lambda head: (0, 0, 0, 0, head)),
        ],
        out_specs=[acc_spec, stat_spec, stat_spec],
        out_shape=[acc_shape, stat_shape, stat_shape],
        compiler_params=params(),
        cost_estimate=cost(pair_flops, 8 * row_count * columns),
        name="own",
    )(step_index, query, noisy_kv)
    for first in range(1, span - 1, 2):
        backs = list(range(first, min(first + 2, span - 1)))
        carry = pl.pallas_call(
            functools.partial(mid_kernel, backs),
            grid=(heads,),
            in_specs=[SMEM_SPEC, SMEM_SPEC, q_spec]
            + [block_spec] * (2 * len(backs))
            + [acc_spec, stat_spec, stat_spec],
            out_specs=[acc_spec, stat_spec, stat_spec],
            out_shape=[acc_shape, stat_shape, stat_shape],
            compiler_params=params(),
            cost_estimate=cost(len(backs) * pair_flops, 12 * row_count * columns),
            name="middle",
        )(step_index, causal_mask, query, *[keys[b] for b in backs], *[values[b] for b in backs], *carry)
    acc, weights = pl.pallas_call(
        functools.partial(last_kernel, span - 1),
        grid=(heads,),
        in_specs=[SMEM_SPEC, SMEM_SPEC, q_spec, block_spec, acc_spec, stat_spec, stat_spec],
        out_specs=[acc_spec, pl.BlockSpec((1, row_count, rows), lambda head: (head, 0, 0))],
        out_shape=[acc_shape, jax.ShapeDtypeStruct((heads, row_count, rows), jnp.bfloat16)],
        compiler_params=params(),
        cost_estimate=cost(pair_flops // 2, 12 * row_count * columns),
        name="last",
    )(step_index, causal_mask, query, keys[-1], *carry)
    averaged, squares = pl.pallas_call(
        average_kernel,
        in_specs=[VMEM_SPEC] * 3,
        out_specs=[VMEM_SPEC] * 2,
        out_shape=[acc_shape, jax.ShapeDtypeStruct((1, row_count), jnp.float32)],
        compiler_params=params(),
        cost_estimate=cost(pair_flops // 2, 12 * row_count * columns),
        name="average",
    )(acc, weights, values[-1])
    axes = ("mp", "seq")
    others = [swap(squares, axes, offset) for offset in range(1, lax.axis_size(axes))]
    return pl.pallas_call(
        functools.partial(scale_kernel, columns * lax.axis_size(axes)),
        in_specs=[VMEM_SPEC] * (2 + len(others)),
        out_specs=VMEM_SPEC,
        out_shape=jax.ShapeDtypeStruct(query.shape, jnp.bfloat16),
        compiler_params=params(),
        cost_estimate=cost(row_count * columns, 6 * row_count * columns),
        name="scale",
    )(averaged, squares, *others)


def picker(shape, wanted):
    row = lax.broadcasted_iota(jnp.int32, shape, 0)
    column = lax.broadcasted_iota(jnp.int32, shape, 1)
    return jnp.where(column == wanted(row), 1.0, 0.0).astype(jnp.bfloat16)


def project_kernel(axes, x_ref, w_ref, *out_refs):
    rows = x_ref.shape[1]
    share = out_refs[0].shape[0]
    projected = nn_dot(x_ref[0], w_ref[...]).astype(jnp.bfloat16)
    for offset, out_ref in enumerate(out_refs):
        first = target_of(axes, offset) * share
        chosen = picker((share, rows), lambda row: row + first)
        out_ref[...] = nn_dot(chosen, projected).astype(jnp.bfloat16)


def gather_kernel(*refs):
    hidden_ref, tail_ref = refs[-2:]
    total = refs[0][...].astype(jnp.float32)
    for ref in refs[1:-2]:
        total = total + ref[...].astype(jnp.float32)
    hidden = total.astype(jnp.bfloat16)
    hidden_ref[...] = hidden
    kept = KT - 1 + FADE
    shape = (tail_ref.shape[0], hidden.shape[0])
    chosen = picker(shape, lambda row: row // kept * FR + FR - kept + row % kept)
    tail_ref[...] = nn_dot(chosen, hidden).astype(jnp.bfloat16)


def decode_kernel(fade_ref, hidden_ref, tail_ref, conv_ref, out_ref):
    position = lax.axis_index("span")
    share = hidden_ref.shape[0]
    spatial = share // FR
    kept = KT - 1 + FADE
    wide = FADE + FR
    hidden, tail = hidden_ref[...], tail_ref[...]
    mixed = jnp.zeros((spatial * wide, out_ref.shape[2]), jnp.float32)
    for tap in range(KT):
        def from_tail(row):
            place = row % wide + KT - 1 - tap
            return jnp.where(place < kept, row // wide * kept + place, -1)

        def from_hidden(row):
            place = row % wide + KT - 1 - tap
            return jnp.where(place >= kept, row // wide * FR + place - kept, -1)

        window = nn_dot(picker((spatial * wide, tail.shape[0]), from_tail), tail)
        window = window + nn_dot(picker((spatial * wide, share), from_hidden), hidden)
        mixed = mixed + nn_dot(window.astype(jnp.bfloat16), conv_ref[tap])
    frames = (mixed * jax.nn.sigmoid(mixed)).astype(jnp.bfloat16)
    fade = fade_ref[0]
    shape = (share, spatial * wide)
    current = nn_dot(picker(shape, lambda row: row // FR * wide + FADE + row % FR), frames)

    def faded(row):
        return jnp.where(row % FR < fade, row // FR * wide + FADE - fade + row % FR, -1)

    previous = nn_dot(picker(shape, faded), frames)
    frame = lax.broadcasted_iota(jnp.int32, (share, out_ref.shape[2]), 0) % FR
    fade_float = jnp.full(frame.shape, fade, jnp.int32).astype(jnp.float32)
    weight = (frame.astype(jnp.float32) + 1.0) / (fade_float + 1.0)
    weight = jnp.where((frame < fade) & (position > 0), weight, 1.0)
    out_ref[0] = (weight * current + (1.0 - weight) * previous).astype(jnp.bfloat16)


def decoder(finished, w_in, conv_w, fade_count):
    axes = ("mp", "seq")
    parts = lax.axis_size(axes)
    rows = finished.shape[1]
    channels = w_in.shape[1]
    share = rows // parts
    spatial = share // FR
    piece = jax.ShapeDtypeStruct((share, channels), jnp.bfloat16)
    pieces = pl.pallas_call(
        functools.partial(project_kernel, axes),
        in_specs=[VMEM_SPEC] * 2,
        out_specs=[VMEM_SPEC] * parts,
        out_shape=[piece] * parts,
        compiler_params=params(),
        cost_estimate=cost(2 * rows * finished.shape[2] * channels, 2 * finished.shape[2] * channels),
        name="project",
    )(finished, w_in)
    received = [swap(pieces[offset], axes, offset) for offset in range(1, parts)]
    hidden, tail = pl.pallas_call(
        gather_kernel,
        in_specs=[VMEM_SPEC] * parts,
        out_specs=[VMEM_SPEC] * 2,
        out_shape=[piece, jax.ShapeDtypeStruct((spatial * (KT - 1 + FADE), channels), jnp.bfloat16)],
        compiler_params=params(),
        cost_estimate=cost(rows * channels, 2 * rows * channels),
        name="gather",
    )(pieces[0], *received)
    tail = hop(tail, "span", 1)
    return pl.pallas_call(
        decode_kernel,
        in_specs=[SMEM_SPEC] + [VMEM_SPEC] * 3,
        out_specs=VMEM_SPEC,
        out_shape=jax.ShapeDtypeStruct((1, share, channels), jnp.bfloat16),
        compiler_params=params(),
        cost_estimate=cost(2 * share * KT * channels * channels, 2 * KT * channels * channels),
        name="decode",
    )(fade_count, hidden, tail, conv_w)


def per_device(
    query, noisy_kv, clean_kv, causal_mask, step_index, finished, w_in, conv_w, fade_count
):
    attended = attention(query, noisy_kv, clean_kv, causal_mask, step_index)
    decoded = decoder(finished, w_in, conv_w, fade_count)
    return (attended, decoded)


def solution(mesh):
    placed = (
        P(None, ("groups", "span"), None, ("mp", "seq")),
        P(None, None, ("groups", "span"), None, ("mp", "seq")),
        P(None, ("groups", "span"), None, ("mp", "seq")),
        P("groups", None),
        P("groups", None),
        P(("groups", "span"), None, ("mp", "seq")),
        P(("mp", "seq"), None),
        P(),
        P(("groups", "span")),
    )
    return jax.shard_map(
        per_device,
        mesh=mesh,
        in_specs=placed,
        out_specs=(
            P(None, ("groups", "span"), None, ("mp", "seq")),
            P(("groups", "span"), ("mp", "seq"), None),
        ),
        check_vma=False,
    )
```

```python
import functools
import math

import jax
import jax.numpy as jnp
from jax import lax
from jax.experimental import pallas as pl
from jax.experimental.pallas import tpu as pltpu
from jax.sharding import PartitionSpec as P

FR = 6
HD = 128
KT = 3
FADE = 2
NSTEPS = 64
LOG2E = 1.4426950408889634
VMEM_LIMIT = 24 * 1024 * 1024

SMEM_SPEC = pl.BlockSpec(memory_space=pltpu.SMEM)
VMEM_SPEC = pl.BlockSpec(memory_space=pltpu.VMEM)


def params():
    return pltpu.CompilerParams(vmem_limit_bytes=VMEM_LIMIT)


def cost(flops, nbytes):
    return pl.CostEstimate(flops=flops, bytes_accessed=nbytes, transcendentals=0)


def hop(value, axis, steps):
    count = lax.axis_size(axis)
    return lax.ppermute(value, axis, [(source, source + steps) for source in range(count - steps)])


def swap(value, axes, offset):
    count = lax.axis_size(axes)
    if count & (count - 1) == 0:
        pairs = [(source, source ^ offset) for source in range(count)]
    else:
        pairs = [(source, (source + offset) % count) for source in range(count)]
    return lax.ppermute(value, axes, pairs)


def target_of(axes, offset):
    count = lax.axis_size(axes)
    mine = lax.axis_index(axes)
    if count & (count - 1) == 0:
        return mine ^ offset
    return lax.rem(mine + offset, count)


def after(value, *earlier):
    return lax.optimization_barrier((value, *earlier))[0]


def nt_dot(left, right):
    return lax.dot_general(left, right, (((1,), (1,)), ((), ())), preferred_element_type=jnp.float32)


def tn_dot(left, right):
    return lax.dot_general(left, right, (((0,), (0,)), ((), ())), preferred_element_type=jnp.float32)


def nn_dot(left, right):
    return jnp.dot(left, right, preferred_element_type=jnp.float32)


def row_factors(step_ref, position, steps, rows):
    lane = lax.broadcasted_iota(jnp.int32, (1, steps * rows), 1)
    index = jnp.full(lane.shape, step_ref[position, 0], jnp.int32)
    for step in range(1, steps):
        index = jnp.where(lane >= step * rows, step_ref[position, step], index)
    fraction = 1.0 - index.astype(jnp.float32) / NSTEPS
    level = 3.0 * fraction / (1.0 + 2.0 * fraction)
    return (0.5 + level) * (LOG2E / math.sqrt(HD))


def lane_windows(steps, rows):
    total = steps * rows
    return [
        (step * rows // HD * HD, min(total, -(-(step + 1) * rows // HD) * HD))
        for step in range(steps)
    ]


def join_steps(pieces, windows, rows):
    total = windows[-1][1]
    tiles = []
    for first in range(0, total, HD):
        stop = min(first + HD, total)
        tile = None
        for step, (begin, end) in enumerate(windows):
            if begin <= first and stop <= end and step * rows < stop and first < (step + 1) * rows:
                part = pieces[step][:, first - begin : stop - begin]
                if tile is None:
                    tile = part
                else:
                    lane = lax.broadcasted_iota(jnp.int32, part.shape, 1) + first
                    tile = jnp.where(lane >= step * rows, part, tile)
        tiles.append(tile)
    return jnp.concatenate(tiles, 1)


def own_kernel(step_ref, q_ref, kv_ref, acc_ref, top_ref, total_ref):
    position = lax.axis_index("span")
    steps, _, rows, columns = q_ref.shape
    factors = row_factors(step_ref, position, steps, rows)
    windows = lane_windows(steps, rows)
    for head in range(columns // HD):
        cut = slice(head * HD, (head + 1) * HD)
        queries = q_ref[:, 0, :, cut].reshape(steps * rows, HD)
        scores = join_steps(
            [nt_dot(kv_ref[s, 0, 0, :, cut], queries[a:b]) for s, (a, b) in enumerate(windows)],
            windows,
            rows,
        )
        scores = scores * factors
        top = jnp.max(scores, axis=0, keepdims=True)
        weights = jnp.exp2(scores - top)
        rounded = weights.astype(jnp.bfloat16)
        acc_ref[head] = join_steps(
            [tn_dot(kv_ref[s, 1, 0, :, cut], rounded[:, a:b]) for s, (a, b) in enumerate(windows)],
            windows,
            rows,
        )
        top_ref[head : head + 1] = top
        total_ref[head : head + 1] = jnp.sum(weights, axis=0, keepdims=True)


def absorb(queries, keys, values, factors, acc, top, total):
    scores = nt_dot(keys, queries) * factors
    newest = jnp.maximum(top, jnp.max(scores, axis=0, keepdims=True))
    weights = jnp.exp2(scores - newest)
    shrink = jnp.exp2(top - newest)
    total = total * shrink + jnp.sum(weights, axis=0, keepdims=True)
    acc = acc * shrink + tn_dot(values, weights.astype(jnp.bfloat16))
    return acc, newest, total


def visible(mask_ref, position, blocks):
    seen = False
    for place, block in blocks.items():
        seen = seen | ((position == place) & (mask_ref[place, block] > 0))
    return seen


def mid_kernel(plans, step_ref, mask_ref, q_ref, *refs):
    block_refs = refs[: len(plans)]
    acc_in, top_in, total_in, acc_ref, top_ref, total_ref = refs[len(plans) :]
    position = lax.axis_index("span")
    steps, _, rows, columns = q_ref.shape
    acc_ref[...] = acc_in[...]
    top_ref[...] = top_in[...]
    total_ref[...] = total_in[...]
    for blocks, block_ref in zip(plans, block_refs):

        @pl.when(visible(mask_ref, position, blocks))
        def _(block_ref=block_ref):
            factors = row_factors(step_ref, position, steps, rows)
            for head in range(columns // HD):
                cut = slice(head * HD, (head + 1) * HD)
                queries = q_ref[:, 0, :, cut].reshape(steps * rows, HD)
                acc, top, total = absorb(
                    queries,
                    block_ref[0, 0, :, cut],
                    block_ref[1, 0, :, cut],
                    factors,
                    acc_ref[head],
                    top_ref[head : head + 1],
                    total_ref[head : head + 1],
                )
                acc_ref[head] = acc
                top_ref[head : head + 1] = top
                total_ref[head : head + 1] = total


def last_kernel(plans, step_ref, mask_ref, q_ref, *refs):
    block_refs = refs[: len(plans)]
    acc_in, top_in, total_in, average_ref, square_ref = refs[len(plans) :]
    position = lax.axis_index("span")
    steps, _, rows, columns = q_ref.shape

    def finish(block_ref):
        factors = row_factors(step_ref, position, steps, rows)
        squares = jnp.zeros((1, steps * rows), jnp.float32)
        for head in range(columns // HD):
            cut = slice(head * HD, (head + 1) * HD)
            acc, top, total = acc_in[head], top_in[head : head + 1], total_in[head : head + 1]
            if block_ref is not None:
                queries = q_ref[:, 0, :, cut].reshape(steps * rows, HD)
                acc, top, total = absorb(
                    queries,
                    block_ref[0, 0, :, cut],
                    block_ref[1, 0, :, cut],
                    factors,
                    acc,
                    top,
                    total,
                )
            average = acc * (1.0 / total)
            average_ref[head] = average
            squares = squares + jnp.sum(average * average, axis=0, keepdims=True)
        square_ref[...] = squares

    rest = True
    for blocks, block_ref in zip(plans, block_refs):
        seen = visible(mask_ref, position, blocks)
        rest = jnp.logical_and(rest, jnp.logical_not(seen))
        pl.when(seen)(functools.partial(finish, block_ref))
    pl.when(rest)(functools.partial(finish, None))


def turn_kernel(in_ref, out_ref):
    heads = in_ref.shape[0]
    steps, rows, _ = out_ref.shape
    for head in range(heads):
        out_ref[:, :, head * HD : (head + 1) * HD] = in_ref[head].T.reshape(steps, rows, HD)


def scale_kernel(width, *refs):
    average_ref, out_ref = refs[0], refs[-1]
    total = refs[1][...]
    for ref in refs[2:-1]:
        total = total + ref[...]
    inverse = lax.rsqrt(total / width + 1e-06)
    steps, rows, columns = average_ref.shape
    spread = jnp.broadcast_to(inverse, (HD, steps * rows)).T
    for head in range(columns // HD):
        lanes = slice(head * HD, (head + 1) * HD)
        average = average_ref[:, :, lanes].reshape(steps * rows, HD)
        out_ref[:, 0, :, lanes] = (average * spread).astype(jnp.bfloat16).reshape(steps, rows, HD)


def send(value, pairs):
    return lax.ppermute(value, "span", pairs)


def delivered(span, back):
    return {place: place - back for place in range(back, span)}


def plain_call(kernel, name, out_shape, flops, operands, scalars=0):
    nbytes = sum(math.prod(o.shape) * o.dtype.itemsize for o in operands)
    many = isinstance(out_shape, (list, tuple))
    return pl.pallas_call(
        kernel,
        in_specs=[SMEM_SPEC] * scalars + [VMEM_SPEC] * (len(operands) - scalars),
        out_specs=[VMEM_SPEC] * len(out_shape) if many else VMEM_SPEC,
        out_shape=out_shape,
        compiler_params=params(),
        cost_estimate=cost(flops, nbytes),
        name=name,
    )(*operands)


def picker(shape, wanted):
    row = lax.broadcasted_iota(jnp.int32, shape, 0)
    column = lax.broadcasted_iota(jnp.int32, shape, 1)
    return jnp.where(column == wanted(row), 1.0, 0.0).astype(jnp.bfloat16)


def project_kernel(axes, x_ref, w_ref, *out_refs):
    rows = x_ref.shape[1]
    share = out_refs[0].shape[0]
    projected = nn_dot(x_ref[0], w_ref[...]).astype(jnp.bfloat16)
    for offset, out_ref in enumerate(out_refs):
        first = target_of(axes, offset) * share
        chosen = picker((share, rows), lambda row: row + first)
        out_ref[...] = nn_dot(chosen, projected).astype(jnp.bfloat16)


def gather_kernel(*refs):
    hidden_ref, tail_ref = refs[-2:]
    total = refs[0][...].astype(jnp.float32)
    for ref in refs[1:-2]:
        total = total + ref[...].astype(jnp.float32)
    hidden = total.astype(jnp.bfloat16)
    hidden_ref[...] = hidden
    kept = KT - 1 + FADE
    shape = (tail_ref.shape[0], hidden.shape[0])
    chosen = picker(shape, lambda row: row // kept * FR + FR - kept + row % kept)
    tail_ref[...] = nn_dot(chosen, hidden).astype(jnp.bfloat16)


def decode_kernel(fade_ref, hidden_ref, tail_ref, conv_ref, out_ref):
    position = lax.axis_index("span")
    share = hidden_ref.shape[0]
    spatial = share // FR
    kept = KT - 1 + FADE
    wide = FADE + FR
    hidden, tail = hidden_ref[...], tail_ref[...]
    mixed = jnp.zeros((spatial * wide, out_ref.shape[2]), jnp.float32)
    for tap in range(KT):
        def from_tail(row):
            place = row % wide + KT - 1 - tap
            return jnp.where(place < kept, row // wide * kept + place, -1)

        def from_hidden(row):
            place = row % wide + KT - 1 - tap
            return jnp.where(place >= kept, row // wide * FR + place - kept, -1)

        window = nn_dot(picker((spatial * wide, tail.shape[0]), from_tail), tail)
        window = window + nn_dot(picker((spatial * wide, share), from_hidden), hidden)
        mixed = mixed + nn_dot(window.astype(jnp.bfloat16), conv_ref[tap])
    frames = (mixed * jax.nn.sigmoid(mixed)).astype(jnp.bfloat16)
    fade = fade_ref[0]
    shape = (share, spatial * wide)
    current = nn_dot(picker(shape, lambda row: row // FR * wide + FADE + row % FR), frames)

    def faded(row):
        return jnp.where(row % FR < fade, row // FR * wide + FADE - fade + row % FR, -1)

    previous = nn_dot(picker(shape, faded), frames)
    frame = lax.broadcasted_iota(jnp.int32, (share, out_ref.shape[2]), 0) % FR
    fade_float = jnp.full(frame.shape, fade, jnp.int32).astype(jnp.float32)
    weight = (frame.astype(jnp.float32) + 1.0) / (fade_float + 1.0)
    weight = jnp.where((frame < fade) & (position > 0), weight, 1.0)
    out_ref[0] = (weight * current + (1.0 - weight) * previous).astype(jnp.bfloat16)


def project(finished, w_in):
    axes = ("mp", "seq")
    parts = lax.axis_size(axes)
    rows, channels = finished.shape[1], w_in.shape[1]
    return plain_call(
        functools.partial(project_kernel, axes),
        "project",
        [jax.ShapeDtypeStruct((rows // parts, channels), jnp.bfloat16)] * parts,
        2 * rows * finished.shape[2] * channels,
        (finished, w_in),
    )


def gather(parts, rows):
    share, channels = parts[0].shape
    tail_rows = share // FR * (KT - 1 + FADE)
    return plain_call(
        gather_kernel,
        "gather",
        [jax.ShapeDtypeStruct((count, channels), jnp.bfloat16) for count in (share, tail_rows)],
        rows * channels,
        parts,
    )


def decode(hidden, tail, conv_w, fade_count):
    share, channels = hidden.shape
    return plain_call(
        decode_kernel,
        "decode",
        jax.ShapeDtypeStruct((1, share, channels), jnp.bfloat16),
        2 * share * KT * channels * channels,
        (fade_count, hidden, tail, conv_w),
        1,
    )


def per_device(
    query, noisy_kv, clean_kv, causal_mask, step_index, finished, w_in, conv_w, fade_count
):
    steps, _, rows, columns = query.shape
    heads = columns // HD
    row_count = steps * rows
    span = lax.axis_size("span")
    axes = ("mp", "seq")
    acc_shape = jax.ShapeDtypeStruct((heads, HD, row_count), jnp.float32)
    stat_shape = jax.ShapeDtypeStruct((heads, row_count), jnp.float32)
    pair_flops = 4 * row_count * rows * columns

    near = hop(clean_kv, "span", 1)
    if span == 4:
        direct = send(clean_kv, [(0, 3)])
    pieces = project(finished, w_in)
    parts = [pieces[0]] + [swap(p, axes, offset + 1) for offset, p in enumerate(pieces[1:])]
    carry = plain_call(
        own_kernel,
        "own",
        [acc_shape, stat_shape, stat_shape],
        pair_flops,
        (step_index, query, noisy_kv),
        1,
    )
    hidden, tail = gather(parts, rows)
    if span == 4:
        early = [(near, delivered(span, 1)), (direct, {3: 0})]
        late = [(send(after(clean_kv, tail), [(0, 2)]), {2: 0})]
        near = after(near, carry[0], tail)
        late.append((send(near, [(2, 3)]), {3: 1}))
    else:
        ring = [near]
        for _ in range(2, span):
            ring.append(hop(ring[-1], "span", 1))
        blocks = [(block, delivered(span, back + 1)) for back, block in enumerate(ring)]
        early, late = blocks[:-1], blocks[-1:]
    tail = hop(tail, "span", 1)
    decoded = decode(hidden, tail, conv_w, fade_count)
    for first in range(0, len(early), 2):
        group = early[first : first + 2]
        carry = plain_call(
            functools.partial(mid_kernel, [plan for _, plan in group]),
            "middle",
            [acc_shape, stat_shape, stat_shape],
            len(group) * pair_flops,
            (step_index, causal_mask, query, *[block for block, _ in group], *carry),
            2,
        )
    averaged, squares = plain_call(
        functools.partial(last_kernel, [plan for _, plan in late]),
        "last",
        [acc_shape, jax.ShapeDtypeStruct((1, row_count), jnp.float32)],
        pair_flops,
        (step_index, causal_mask, query, *[block for block, _ in late], *carry),
        2,
    )
    others = [swap(squares, axes, offset) for offset in range(1, lax.axis_size(axes))]
    turned = plain_call(
        turn_kernel,
        "turn",
        jax.ShapeDtypeStruct((steps, rows, columns), jnp.float32),
        row_count * columns,
        (averaged,),
    )
    attended = plain_call(
        functools.partial(scale_kernel, columns * lax.axis_size(axes)),
        "scale",
        jax.ShapeDtypeStruct(query.shape, jnp.bfloat16),
        row_count * columns,
        (turned, squares, *others),
    )
    return (attended, decoded)


def solution(mesh):
    placed = (
        P(None, ("groups", "span"), None, ("mp", "seq")),
        P(None, None, ("groups", "span"), None, ("mp", "seq")),
        P(None, ("groups", "span"), None, ("mp", "seq")),
        P("groups", None),
        P("groups", None),
        P(("groups", "span"), None, ("mp", "seq")),
        P(("mp", "seq"), None),
        P(),
        P(("groups", "span")),
    )
    return jax.shard_map(
        per_device,
        mesh=mesh,
        in_specs=placed,
        out_specs=(
            P(None, ("groups", "span"), None, ("mp", "seq")),
            P(("groups", "span"), ("mp", "seq"), None),
        ),
        check_vma=False,
    )
```

```python
import functools
import math

import jax
import jax.numpy as jnp
from jax import lax
from jax.experimental import pallas as pl
from jax.experimental.pallas import tpu as pltpu
from jax.sharding import PartitionSpec as P

FR = 6
HD = 128
KT = 3
FADE = 2
NSTEPS = 64
LOG2E = 1.4426950408889634
VMEM_LIMIT = 24 * 1024 * 1024
VMEM_ALL = 60 * 1024 * 1024

SMEM_SPEC = pl.BlockSpec(memory_space=pltpu.SMEM)
VMEM_SPEC = pl.BlockSpec(memory_space=pltpu.VMEM)
HBM_SPEC = pl.BlockSpec(memory_space=pltpu.HBM)


def cost(flops, nbytes):
    return pl.CostEstimate(flops=flops, bytes_accessed=nbytes, transcendentals=0)


def hop(value, axis, steps):
    count = lax.axis_size(axis)
    return lax.ppermute(value, axis, [(source, source + steps) for source in range(count - steps)])


def swap(value, axes, offset):
    count = lax.axis_size(axes)
    if count & (count - 1) == 0:
        pairs = [(source, source ^ offset) for source in range(count)]
    else:
        pairs = [(source, (source + offset) % count) for source in range(count)]
    return lax.ppermute(value, axes, pairs)


def target_of(axes, offset):
    count = lax.axis_size(axes)
    mine = lax.axis_index(axes)
    if count & (count - 1) == 0:
        return mine ^ offset
    return lax.rem(mine + offset, count)


def after(value, *earlier):
    return lax.optimization_barrier((value, *earlier))[0]


def nt_dot(left, right):
    return lax.dot_general(left, right, (((1,), (1,)), ((), ())), preferred_element_type=jnp.float32)


def tn_dot(left, right):
    return lax.dot_general(left, right, (((0,), (0,)), ((), ())), preferred_element_type=jnp.float32)


def nn_dot(left, right):
    return jnp.dot(left, right, preferred_element_type=jnp.float32)


def row_factors(step_ref, position, steps, rows):
    lane = lax.broadcasted_iota(jnp.int32, (1, steps * rows), 1)
    index = jnp.full(lane.shape, step_ref[position, 0], jnp.int32)
    for step in range(1, steps):
        index = jnp.where(lane >= step * rows, step_ref[position, step], index)
    fraction = 1.0 - index.astype(jnp.float32) / NSTEPS
    level = 3.0 * fraction / (1.0 + 2.0 * fraction)
    return (0.5 + level) * (LOG2E / math.sqrt(HD))


def lane_windows(steps, rows):
    total = steps * rows
    return [
        (step * rows // HD * HD, min(total, -(-(step + 1) * rows // HD) * HD))
        for step in range(steps)
    ]


def join_steps(pieces, windows, rows):
    total = windows[-1][1]
    tiles = []
    for first in range(0, total, HD):
        stop = min(first + HD, total)
        tile = None
        for step, (begin, end) in enumerate(windows):
            if begin <= first and stop <= end and step * rows < stop and first < (step + 1) * rows:
                part = pieces[step][:, first - begin : stop - begin]
                if tile is None:
                    tile = part
                else:
                    lane = lax.broadcasted_iota(jnp.int32, part.shape, 1) + first
                    tile = jnp.where(lane >= step * rows, part, tile)
        tiles.append(tile)
    return jnp.concatenate(tiles, 1)


def own_kernel(step_ref, q_hbm, kv_hbm, acc_ref, top_ref, total_ref, q_ref, kv_ref, q_sem, kv_sem):
    position = lax.axis_index("span")
    steps, rows, columns = q_ref.shape
    heads = columns // HD
    cuts = [slice(head * HD, (head + 1) * HD) for head in range(heads)]
    copies = []
    for head, cut in enumerate(cuts):
        copies.append(
            (
                pltpu.make_async_copy(q_hbm.at[:, 0, :, cut], q_ref.at[:, :, cut], q_sem.at[head]),
                pltpu.make_async_copy(
                    kv_hbm.at[:, :, 0, :, cut], kv_ref.at[:, :, :, cut], kv_sem.at[head]
                ),
            )
        )
        for copy in copies[-1]:
            copy.start()
    factors = row_factors(step_ref, position, steps, rows)
    windows = lane_windows(steps, rows)
    for head, cut in enumerate(cuts):
        for copy in copies[head]:
            copy.wait()
        queries = q_ref[:, :, cut].reshape(steps * rows, HD)
        scores = join_steps(
            [nt_dot(kv_ref[s, 0, :, cut], queries[a:b]) for s, (a, b) in enumerate(windows)],
            windows,
            rows,
        )
        scores = scores * factors
        top = jnp.max(scores, axis=0, keepdims=True)
        weights = jnp.exp2(scores - top)
        rounded = weights.astype(jnp.bfloat16)
        acc_ref[head] = join_steps(
            [tn_dot(kv_ref[s, 1, :, cut], rounded[:, a:b]) for s, (a, b) in enumerate(windows)],
            windows,
            rows,
        )
        top_ref[head : head + 1] = top
        total_ref[head : head + 1] = jnp.sum(weights, axis=0, keepdims=True)


def absorb(queries, keys, values, factors, acc, top, total):
    scores = nt_dot(keys, queries) * factors
    newest = jnp.maximum(top, jnp.max(scores, axis=0, keepdims=True))
    weights = jnp.exp2(scores - newest)
    shrink = jnp.exp2(top - newest)
    total = total * shrink + jnp.sum(weights, axis=0, keepdims=True)
    acc = acc * shrink + tn_dot(values, weights.astype(jnp.bfloat16))
    return acc, newest, total


def visible(mask_ref, position, blocks):
    seen = False
    for place, block in blocks.items():
        seen = seen | ((position == place) & (mask_ref[place, block] > 0))
    return seen


def mid_kernel(plans, step_ref, mask_ref, q_ref, *refs):
    block_refs = refs[: len(plans)]
    acc_in, top_in, total_in, acc_ref, top_ref, total_ref = refs[len(plans) :]
    position = lax.axis_index("span")
    steps, _, rows, columns = q_ref.shape
    acc_ref[...] = acc_in[...]
    top_ref[...] = top_in[...]
    total_ref[...] = total_in[...]
    for blocks, block_ref in zip(plans, block_refs):

        @pl.when(visible(mask_ref, position, blocks))
        def _(block_ref=block_ref):
            factors = row_factors(step_ref, position, steps, rows)
            for head in range(columns // HD):
                cut = slice(head * HD, (head + 1) * HD)
                queries = q_ref[:, 0, :, cut].reshape(steps * rows, HD)
                acc, top, total = absorb(
                    queries,
                    block_ref[0, 0, :, cut],
                    block_ref[1, 0, :, cut],
                    factors,
                    acc_ref[head],
                    top_ref[head : head + 1],
                    total_ref[head : head + 1],
                )
                acc_ref[head] = acc
                top_ref[head : head + 1] = top
                total_ref[head : head + 1] = total


def score_kernel(plan, step_ref, mask_ref, q_ref, key_ref, acc_in, top_in, total_in, acc_ref, w_ref):
    position = lax.axis_index("span")
    steps, _, rows, columns = q_ref.shape
    seen = visible(mask_ref, position, plan)

    @pl.when(seen)
    def _():
        factors = row_factors(step_ref, position, steps, rows)
        for head in range(columns // HD):
            cut = slice(head * HD, (head + 1) * HD)
            queries = q_ref[:, 0, :, cut].reshape(steps * rows, HD)
            scores = nt_dot(key_ref[0, :, cut], queries) * factors
            top = top_in[head : head + 1]
            newest = jnp.maximum(top, jnp.max(scores, axis=0, keepdims=True))
            weights = jnp.exp2(scores - newest)
            shrink = jnp.exp2(top - newest)
            total = total_in[head : head + 1] * shrink + jnp.sum(weights, axis=0, keepdims=True)
            inverse = 1.0 / total
            w_ref[head] = (weights * inverse).astype(jnp.bfloat16)
            acc_ref[head] = acc_in[head] * (shrink * inverse)

    @pl.when(jnp.logical_not(seen))
    def _():
        w_ref[...] = jnp.zeros_like(w_ref)
        for head in range(columns // HD):
            acc_ref[head] = acc_in[head] * (1.0 / total_in[head : head + 1])


def average_kernel(acc_ref, w_ref, value_ref, average_ref, square_ref):
    squares = jnp.zeros(square_ref.shape, jnp.float32)
    for head in range(acc_ref.shape[0]):
        values = value_ref[0, :, head * HD : (head + 1) * HD]
        average = acc_ref[head] + tn_dot(values, w_ref[head])
        average_ref[head] = average
        squares = squares + jnp.sum(average * average, axis=0, keepdims=True)
    square_ref[...] = squares


def turn_kernel(in_ref, out_ref):
    heads = in_ref.shape[0]
    steps, rows, _ = out_ref.shape
    for head in range(heads):
        out_ref[:, :, head * HD : (head + 1) * HD] = in_ref[head].T.reshape(steps, rows, HD)


def scale_kernel(width, average_ref, *refs):
    part_refs, (out_hbm, out_ref, sem) = refs[:-3], refs[-3:]
    total = part_refs[0][...]
    for ref in part_refs[1:]:
        total = total + ref[...]
    inverse = lax.rsqrt(total / width + 1e-06)
    steps, rows, columns = average_ref.shape
    spread = jnp.broadcast_to(inverse, (HD, steps * rows)).T
    copies = []
    for step in range(steps):
        factor = spread[step * rows : (step + 1) * rows]
        for first in range(0, columns, HD):
            cut = slice(first, first + HD)
            out_ref[step, :, cut] = (average_ref[step, :, cut] * factor).astype(jnp.bfloat16)
        copies.append(pltpu.make_async_copy(out_ref.at[step], out_hbm.at[step, 0], sem.at[step]))
        copies[-1].start()
    for copy in copies:
        copy.wait()


def send(value, pairs):
    return lax.ppermute(value, "span", pairs)


def delivered(span, back):
    return {place: place - back for place in range(back, span)}


def plain_call(kernel, name, out_shape, flops, operands, in_specs=(), out_specs=None, scratch=(), limit=VMEM_LIMIT):
    nbytes = sum(math.prod(o.shape) * o.dtype.itemsize for o in operands)
    if out_specs is None:
        out_specs = [VMEM_SPEC] * len(out_shape)
    return pl.pallas_call(
        kernel,
        in_specs=list(in_specs) + [VMEM_SPEC] * (len(operands) - len(in_specs)),
        out_specs=out_specs,
        out_shape=out_shape,
        scratch_shapes=list(scratch),
        compiler_params=pltpu.CompilerParams(vmem_limit_bytes=limit),
        cost_estimate=cost(flops, nbytes),
        name=name,
    )(*operands)


def picker(shape, wanted):
    row = lax.broadcasted_iota(jnp.int32, shape, 0)
    column = lax.broadcasted_iota(jnp.int32, shape, 1)
    return jnp.where(column == wanted(row), 1.0, 0.0).astype(jnp.bfloat16)


def project_kernel(axes, x_hbm, w_hbm, *refs):
    out_refs, (x_ref, w_ref, x_sem, w_sem) = refs[:-4], refs[-4:]
    rows, depth = x_ref.shape
    share = out_refs[0].shape[0]
    copies = []
    for place, first in enumerate(range(0, depth, 2 * HD)):
        cut = slice(first, min(first + 2 * HD, depth))
        copies.append(
            (
                cut,
                pltpu.make_async_copy(x_hbm.at[0, :, cut], x_ref.at[:, cut], x_sem.at[place]),
                pltpu.make_async_copy(w_hbm.at[cut], w_ref.at[cut], w_sem.at[place]),
            )
        )
        copies[-1][1].start()
        copies[-1][2].start()
    total = jnp.zeros((rows, w_ref.shape[1]), jnp.float32)
    for cut, x_copy, w_copy in copies:
        x_copy.wait()
        w_copy.wait()
        total = total + nn_dot(x_ref[:, cut], w_ref[cut])
    projected = total.astype(jnp.bfloat16)
    for offset, out_ref in enumerate(out_refs):
        first = target_of(axes, offset) * share
        chosen = picker((share, rows), lambda row: row + first)
        out_ref[...] = nn_dot(chosen, projected).astype(jnp.bfloat16)


def gather_kernel(*refs):
    hidden_ref, tail_ref = refs[-2:]
    total = refs[0][...].astype(jnp.float32)
    for ref in refs[1:-2]:
        total = total + ref[...].astype(jnp.float32)
    hidden = total.astype(jnp.bfloat16)
    hidden_ref[...] = hidden
    kept = KT - 1 + FADE
    shape = (tail_ref.shape[0], hidden.shape[0])
    chosen = picker(shape, lambda row: row // kept * FR + FR - kept + row % kept)
    tail_ref[...] = nn_dot(chosen, hidden).astype(jnp.bfloat16)


def decode_kernel(fade_ref, hidden_ref, tail_ref, conv_ref, out_ref):
    position = lax.axis_index("span")
    share = hidden_ref.shape[0]
    spatial = share // FR
    kept = KT - 1 + FADE
    wide = FADE + FR
    hidden, tail = hidden_ref[...], tail_ref[...]
    mixed = jnp.zeros((spatial * wide, out_ref.shape[2]), jnp.float32)
    for tap in range(KT):
        def from_tail(row):
            place = row % wide + KT - 1 - tap
            return jnp.where(place < kept, row // wide * kept + place, -1)

        def from_hidden(row):
            place = row % wide + KT - 1 - tap
            return jnp.where(place >= kept, row // wide * FR + place - kept, -1)

        window = nn_dot(picker((spatial * wide, tail.shape[0]), from_tail), tail)
        window = window + nn_dot(picker((spatial * wide, share), from_hidden), hidden)
        mixed = mixed + nn_dot(window.astype(jnp.bfloat16), conv_ref[tap])
    frames = (mixed * jax.nn.sigmoid(mixed)).astype(jnp.bfloat16)
    fade = fade_ref[0]
    shape = (share, spatial * wide)
    current = nn_dot(picker(shape, lambda row: row // FR * wide + FADE + row % FR), frames)

    def faded(row):
        return jnp.where(row % FR < fade, row // FR * wide + FADE - fade + row % FR, -1)

    previous = nn_dot(picker(shape, faded), frames)
    frame = lax.broadcasted_iota(jnp.int32, (share, out_ref.shape[2]), 0) % FR
    fade_float = jnp.full(frame.shape, fade, jnp.int32).astype(jnp.float32)
    weight = (frame.astype(jnp.float32) + 1.0) / (fade_float + 1.0)
    weight = jnp.where((frame < fade) & (position > 0), weight, 1.0)
    out_ref[0] = (weight * current + (1.0 - weight) * previous).astype(jnp.bfloat16)


def project(finished, w_in):
    axes = ("mp", "seq")
    parts = lax.axis_size(axes)
    _, rows, depth = finished.shape
    channels = w_in.shape[1]
    chunks = -(-depth // (2 * HD))
    return plain_call(
        functools.partial(project_kernel, axes),
        "project",
        [jax.ShapeDtypeStruct((rows // parts, channels), jnp.bfloat16)] * parts,
        2 * rows * depth * channels,
        (finished, w_in),
        [HBM_SPEC] * 2,
        scratch=[
            pltpu.VMEM((rows, depth), jnp.bfloat16),
            pltpu.VMEM((depth, channels), jnp.bfloat16),
            pltpu.SemaphoreType.DMA((chunks,)),
            pltpu.SemaphoreType.DMA((chunks,)),
        ],
        limit=VMEM_ALL,
    )


def gather(parts, rows):
    share, channels = parts[0].shape
    tail_rows = share // FR * (KT - 1 + FADE)
    return plain_call(
        gather_kernel,
        "gather",
        [jax.ShapeDtypeStruct((count, channels), jnp.bfloat16) for count in (share, tail_rows)],
        rows * channels,
        parts,
    )


def decode(hidden, tail, conv_w, fade_count):
    share, channels = hidden.shape
    return plain_call(
        decode_kernel,
        "decode",
        [jax.ShapeDtypeStruct((1, share, channels), jnp.bfloat16)],
        2 * share * KT * channels * channels,
        (fade_count, hidden, tail, conv_w),
        [SMEM_SPEC],
    )[0]


def per_device(
    query, noisy_kv, clean_kv, causal_mask, step_index, finished, w_in, conv_w, fade_count
):
    steps, _, rows, columns = query.shape
    heads = columns // HD
    row_count = steps * rows
    span = lax.axis_size("span")
    axes = ("mp", "seq")
    acc_shape = jax.ShapeDtypeStruct((heads, HD, row_count), jnp.float32)
    stat_shape = jax.ShapeDtypeStruct((heads, row_count), jnp.float32)
    pair_flops = 4 * row_count * rows * columns

    near = hop(clean_kv, "span", 1)
    pieces = project(finished, w_in)
    parts = [pieces[0]] + [swap(p, axes, offset + 1) for offset, p in enumerate(pieces[1:])]
    if span == 4:
        direct = send(after(clean_kv, pieces[0]), [(0, 3)])
    carry = plain_call(
        own_kernel,
        "own",
        [acc_shape, stat_shape, stat_shape],
        pair_flops,
        (step_index, query, noisy_kv),
        [SMEM_SPEC] + [HBM_SPEC] * 2,
        scratch=[
            pltpu.VMEM((steps, rows, columns), jnp.bfloat16),
            pltpu.VMEM((steps, 2, rows, columns), jnp.bfloat16),
            pltpu.SemaphoreType.DMA((heads,)),
            pltpu.SemaphoreType.DMA((heads,)),
        ],
        limit=VMEM_ALL,
    )
    hidden, tail = gather(parts, rows)
    tail = hop(tail, "span", 1)
    if span == 4:
        near = after(near, carry[0], hidden)
        early = [(near, delivered(span, 1)), (direct, {3: 0})]
        first = lax.axis_index("span") == 0
        passed = [jnp.where(first, clean_kv[which], near[which]) for which in range(2)]
        keys, values = [send(block, [(0, 2), (2, 3)]) for block in passed]
        last_plan = {2: 0, 3: 1}
    else:
        ring = [near]
        for _ in range(2, span):
            ring.append(hop(ring[-1], "span", 1))
        early = [(block, delivered(span, back + 1)) for back, block in enumerate(ring[:-1])]
        keys, values = ring[-1][0], ring[-1][1]
        last_plan = delivered(span, span - 1)
    decoded = decode(hidden, tail, conv_w, fade_count)
    carry = [carry[0], after(carry[1], decoded), carry[2]]
    for first in range(0, len(early), 2):
        group = early[first : first + 2]
        carry = plain_call(
            functools.partial(mid_kernel, [plan for _, plan in group]),
            "middle",
            [acc_shape, stat_shape, stat_shape],
            len(group) * pair_flops,
            (step_index, causal_mask, query, *[block for block, _ in group], *carry),
            [SMEM_SPEC] * 2,
        )
    acc, weights = plain_call(
        functools.partial(score_kernel, last_plan),
        "score",
        [acc_shape, jax.ShapeDtypeStruct((heads, rows, row_count), jnp.bfloat16)],
        pair_flops // 2,
        (step_index, causal_mask, query, keys, *carry),
        [SMEM_SPEC] * 2,
    )
    averaged, squares = plain_call(
        average_kernel,
        "average",
        [acc_shape, jax.ShapeDtypeStruct((1, row_count), jnp.float32)],
        pair_flops // 2,
        (acc, weights, values),
    )
    others = [swap(squares, axes, offset) for offset in range(1, lax.axis_size(axes))]
    turned = plain_call(
        turn_kernel,
        "turn",
        [jax.ShapeDtypeStruct((steps, rows, columns), jnp.float32)],
        row_count * columns,
        (averaged,),
    )[0]
    attended = plain_call(
        functools.partial(scale_kernel, columns * lax.axis_size(axes)),
        "scale",
        jax.ShapeDtypeStruct(query.shape, jnp.bfloat16),
        row_count * columns,
        (turned, squares, *others),
        out_specs=HBM_SPEC,
        scratch=[
            pltpu.VMEM((steps, rows, columns), jnp.bfloat16),
            pltpu.SemaphoreType.DMA((steps,)),
        ],
    )
    return (attended, decoded)


def solution(mesh):
    placed = (
        P(None, ("groups", "span"), None, ("mp", "seq")),
        P(None, None, ("groups", "span"), None, ("mp", "seq")),
        P(None, ("groups", "span"), None, ("mp", "seq")),
        P("groups", None),
        P("groups", None),
        P(("groups", "span"), None, ("mp", "seq")),
        P(("mp", "seq"), None),
        P(),
        P(("groups", "span")),
    )
    return jax.shard_map(
        per_device,
        mesh=mesh,
        in_specs=placed,
        out_specs=(
            P(None, ("groups", "span"), None, ("mp", "seq")),
            P(("groups", "span"), ("mp", "seq"), None),
        ),
        check_vma=False,
    )
```

```python
import functools
import math

import jax
import jax.numpy as jnp
from jax import lax
from jax.experimental import pallas as pl
from jax.experimental.pallas import tpu as pltpu
from jax.sharding import PartitionSpec as P

FR = 6
HD = 128
KT = 3
FADE = 2
NSTEPS = 64
LOG2E = 1.4426950408889634
VMEM_LIMIT = 24 * 1024 * 1024
VMEM_ALL = 60 * 1024 * 1024

SMEM_SPEC = pl.BlockSpec(memory_space=pltpu.SMEM)
VMEM_SPEC = pl.BlockSpec(memory_space=pltpu.VMEM)
HBM_SPEC = pl.BlockSpec(memory_space=pltpu.HBM)


def cost(flops, nbytes):
    return pl.CostEstimate(flops=flops, bytes_accessed=nbytes, transcendentals=0)


def hop(value, axis, steps):
    count = lax.axis_size(axis)
    return lax.ppermute(value, axis, [(source, source + steps) for source in range(count - steps)])


def swap(value, axes, offset):
    count = lax.axis_size(axes)
    if count & (count - 1) == 0:
        pairs = [(source, source ^ offset) for source in range(count)]
    else:
        pairs = [(source, (source + offset) % count) for source in range(count)]
    return lax.ppermute(value, axes, pairs)


def target_of(axes, offset):
    count = lax.axis_size(axes)
    mine = lax.axis_index(axes)
    if count & (count - 1) == 0:
        return mine ^ offset
    return lax.rem(mine + offset, count)


def after(value, *earlier):
    return lax.optimization_barrier((value, *earlier))[0]


def nt_dot(left, right):
    return lax.dot_general(left, right, (((1,), (1,)), ((), ())), preferred_element_type=jnp.float32)


def tn_dot(left, right):
    return lax.dot_general(left, right, (((0,), (0,)), ((), ())), preferred_element_type=jnp.float32)


def nn_dot(left, right):
    return jnp.dot(left, right, preferred_element_type=jnp.float32)


def row_factors(step_ref, position, steps, rows):
    lane = lax.broadcasted_iota(jnp.int32, (1, steps * rows), 1)
    index = jnp.full(lane.shape, step_ref[position, 0], jnp.int32)
    for step in range(1, steps):
        index = jnp.where(lane >= step * rows, step_ref[position, step], index)
    fraction = 1.0 - index.astype(jnp.float32) / NSTEPS
    level = 3.0 * fraction / (1.0 + 2.0 * fraction)
    return (0.5 + level) * (LOG2E / math.sqrt(HD))


def lane_windows(steps, rows):
    total = steps * rows
    return [
        (step * rows // HD * HD, min(total, -(-(step + 1) * rows // HD) * HD))
        for step in range(steps)
    ]


def join_steps(pieces, windows, rows):
    total = windows[-1][1]
    tiles = []
    for first in range(0, total, HD):
        stop = min(first + HD, total)
        tile = None
        for step, (begin, end) in enumerate(windows):
            if begin <= first and stop <= end and step * rows < stop and first < (step + 1) * rows:
                part = pieces[step][:, first - begin : stop - begin]
                if tile is None:
                    tile = part
                else:
                    lane = lax.broadcasted_iota(jnp.int32, part.shape, 1) + first
                    tile = jnp.where(lane >= step * rows, part, tile)
        tiles.append(tile)
    return jnp.concatenate(tiles, 1)


def own_kernel(step_ref, q_hbm, kv_hbm, acc_ref, top_ref, total_ref, q_ref, kv_ref, q_sem, kv_sem):
    position = lax.axis_index("span")
    steps, rows, columns = q_ref.shape
    heads = columns // HD
    copies = []
    for step in range(steps):
        copies.append(pltpu.make_async_copy(q_hbm.at[step, 0], q_ref.at[step], q_sem.at[step]))
        copies.append(pltpu.make_async_copy(kv_hbm.at[step, :, 0], kv_ref.at[step], kv_sem.at[step]))
    for copy in copies:
        copy.start()
    factors = row_factors(step_ref, position, steps, rows)
    windows = lane_windows(steps, rows)
    for copy in copies:
        copy.wait()
    for head in range(heads):
        cut = slice(head * HD, (head + 1) * HD)
        queries = q_ref[:, :, cut].reshape(steps * rows, HD)
        scores = join_steps(
            [nt_dot(kv_ref[s, 0, :, cut], queries[a:b]) for s, (a, b) in enumerate(windows)],
            windows,
            rows,
        )
        scores = scores * factors
        top = jnp.max(scores, axis=0, keepdims=True)
        weights = jnp.exp2(scores - top)
        rounded = weights.astype(jnp.bfloat16)
        acc_ref[head] = join_steps(
            [tn_dot(kv_ref[s, 1, :, cut], rounded[:, a:b]) for s, (a, b) in enumerate(windows)],
            windows,
            rows,
        )
        top_ref[head : head + 1] = top
        total_ref[head : head + 1] = jnp.sum(weights, axis=0, keepdims=True)


def absorb(queries, keys, values, factors, acc, top, total):
    scores = nt_dot(keys, queries) * factors
    newest = jnp.maximum(top, jnp.max(scores, axis=0, keepdims=True))
    weights = jnp.exp2(scores - newest)
    shrink = jnp.exp2(top - newest)
    total = total * shrink + jnp.sum(weights, axis=0, keepdims=True)
    acc = acc * shrink + tn_dot(values, weights.astype(jnp.bfloat16))
    return acc, newest, total


def visible(mask_ref, position, blocks):
    seen = False
    for place, block in blocks.items():
        seen = seen | ((position == place) & (mask_ref[place, block] > 0))
    return seen


def mid_kernel(plans, step_ref, mask_ref, q_ref, *refs):
    block_refs = refs[: len(plans)]
    acc_in, top_in, total_in, acc_ref, top_ref, total_ref = refs[len(plans) :]
    position = lax.axis_index("span")
    steps, _, rows, columns = q_ref.shape
    acc_ref[...] = acc_in[...]
    top_ref[...] = top_in[...]
    total_ref[...] = total_in[...]
    for blocks, block_ref in zip(plans, block_refs):

        @pl.when(visible(mask_ref, position, blocks))
        def _(block_ref=block_ref):
            factors = row_factors(step_ref, position, steps, rows)
            for head in range(columns // HD):
                cut = slice(head * HD, (head + 1) * HD)
                queries = q_ref[:, 0, :, cut].reshape(steps * rows, HD)
                acc, top, total = absorb(
                    queries,
                    block_ref[0, 0, :, cut],
                    block_ref[1, 0, :, cut],
                    factors,
                    acc_ref[head],
                    top_ref[head : head + 1],
                    total_ref[head : head + 1],
                )
                acc_ref[head] = acc
                top_ref[head : head + 1] = top
                total_ref[head : head + 1] = total


def score_kernel(plan, step_ref, mask_ref, q_ref, key_ref, acc_in, top_in, total_in, acc_ref, w_ref):
    position = lax.axis_index("span")
    steps, _, rows, columns = q_ref.shape
    seen = visible(mask_ref, position, plan)

    @pl.when(seen)
    def _():
        factors = row_factors(step_ref, position, steps, rows)
        for head in range(columns // HD):
            cut = slice(head * HD, (head + 1) * HD)
            queries = q_ref[:, 0, :, cut].reshape(steps * rows, HD)
            scores = nt_dot(key_ref[0, :, cut], queries) * factors
            top = top_in[head : head + 1]
            newest = jnp.maximum(top, jnp.max(scores, axis=0, keepdims=True))
            weights = jnp.exp2(scores - newest)
            shrink = jnp.exp2(top - newest)
            total = total_in[head : head + 1] * shrink + jnp.sum(weights, axis=0, keepdims=True)
            inverse = 1.0 / total
            w_ref[head] = (weights * inverse).astype(jnp.bfloat16)
            acc_ref[head] = acc_in[head] * (shrink * inverse)

    @pl.when(jnp.logical_not(seen))
    def _():
        w_ref[...] = jnp.zeros_like(w_ref)
        for head in range(columns // HD):
            acc_ref[head] = acc_in[head] * (1.0 / total_in[head : head + 1])


def average_kernel(acc_ref, w_ref, value_ref, average_ref, square_ref):
    squares = jnp.zeros(square_ref.shape, jnp.float32)
    for head in range(acc_ref.shape[0]):
        values = value_ref[0, :, head * HD : (head + 1) * HD]
        average = acc_ref[head] + tn_dot(values, w_ref[head])
        average_ref[head] = average
        squares = squares + jnp.sum(average * average, axis=0, keepdims=True)
    square_ref[...] = squares


def turn_kernel(in_ref, out_ref):
    heads = in_ref.shape[0]
    steps, rows, _ = out_ref.shape
    for head in range(heads):
        out_ref[:, :, head * HD : (head + 1) * HD] = in_ref[head].T.reshape(steps, rows, HD)


def scale_kernel(width, average_ref, *refs):
    part_refs, (out_hbm, out_ref, sem) = refs[:-3], refs[-3:]
    total = part_refs[0][...]
    for ref in part_refs[1:]:
        total = total + ref[...]
    inverse = lax.rsqrt(total / width + 1e-06)
    steps, rows, columns = average_ref.shape
    spread = jnp.broadcast_to(inverse, (HD, steps * rows)).T
    copies = []
    for step in range(steps):
        factor = spread[step * rows : (step + 1) * rows]
        for first in range(0, columns, HD):
            cut = slice(first, first + HD)
            out_ref[step, :, cut] = (average_ref[step, :, cut] * factor).astype(jnp.bfloat16)
        copies.append(pltpu.make_async_copy(out_ref.at[step], out_hbm.at[step, 0], sem.at[step]))
        copies[-1].start()
    for copy in copies:
        copy.wait()


def send(value, pairs):
    return lax.ppermute(value, "span", pairs)


def delivered(span, back):
    return {place: place - back for place in range(back, span)}


def plain_call(kernel, name, out_shape, flops, operands, in_specs=(), out_specs=None, scratch=(), limit=VMEM_LIMIT):
    nbytes = sum(math.prod(o.shape) * o.dtype.itemsize for o in operands)
    if out_specs is None:
        out_specs = [VMEM_SPEC] * len(out_shape)
    return pl.pallas_call(
        kernel,
        in_specs=list(in_specs) + [VMEM_SPEC] * (len(operands) - len(in_specs)),
        out_specs=out_specs,
        out_shape=out_shape,
        scratch_shapes=list(scratch),
        compiler_params=pltpu.CompilerParams(vmem_limit_bytes=limit),
        cost_estimate=cost(flops, nbytes),
        name=name,
    )(*operands)


def picker(shape, wanted):
    row = lax.broadcasted_iota(jnp.int32, shape, 0)
    column = lax.broadcasted_iota(jnp.int32, shape, 1)
    return jnp.where(column == wanted(row), 1.0, 0.0).astype(jnp.bfloat16)


def project_kernel(axes, x_hbm, w_hbm, *refs):
    out_refs, (x_ref, w_ref, x_sem, w_sem) = refs[:-4], refs[-4:]
    rows, depth = x_ref.shape
    share = out_refs[0].shape[0]
    x_copy = pltpu.make_async_copy(x_hbm.at[0], x_ref, x_sem)
    x_copy.start()
    copies = []
    for place, first in enumerate(range(0, depth, 2 * HD)):
        cut = slice(first, min(first + 2 * HD, depth))
        copies.append((cut, pltpu.make_async_copy(w_hbm.at[cut], w_ref.at[cut], w_sem.at[place])))
        copies[-1][1].start()
    total = jnp.zeros((rows, w_ref.shape[1]), jnp.float32)
    x_copy.wait()
    for cut, w_copy in copies:
        w_copy.wait()
        total = total + nn_dot(x_ref[:, cut], w_ref[cut])
    projected = total.astype(jnp.bfloat16)
    for offset, out_ref in enumerate(out_refs):
        first = target_of(axes, offset) * share
        chosen = picker((share, rows), lambda row: row + first)
        out_ref[...] = nn_dot(chosen, projected).astype(jnp.bfloat16)


def gather_kernel(*refs):
    hidden_ref, tail_ref = refs[-2:]
    total = refs[0][...].astype(jnp.float32)
    for ref in refs[1:-2]:
        total = total + ref[...].astype(jnp.float32)
    hidden = total.astype(jnp.bfloat16)
    hidden_ref[...] = hidden
    kept = KT - 1 + FADE
    shape = (tail_ref.shape[0], hidden.shape[0])
    chosen = picker(shape, lambda row: row // kept * FR + FR - kept + row % kept)
    tail_ref[...] = nn_dot(chosen, hidden).astype(jnp.bfloat16)


def decode_kernel(fade_ref, hidden_ref, tail_ref, conv_ref, out_ref):
    position = lax.axis_index("span")
    share = hidden_ref.shape[0]
    spatial = share // FR
    kept = KT - 1 + FADE
    wide = FADE + FR
    hidden, tail = hidden_ref[...], tail_ref[...]
    mixed = jnp.zeros((spatial * wide, out_ref.shape[2]), jnp.float32)
    for tap in range(KT):
        def from_tail(row):
            place = row % wide + KT - 1 - tap
            return jnp.where(place < kept, row // wide * kept + place, -1)

        def from_hidden(row):
            place = row % wide + KT - 1 - tap
            return jnp.where(place >= kept, row // wide * FR + place - kept, -1)

        window = nn_dot(picker((spatial * wide, tail.shape[0]), from_tail), tail)
        window = window + nn_dot(picker((spatial * wide, share), from_hidden), hidden)
        mixed = mixed + nn_dot(window.astype(jnp.bfloat16), conv_ref[tap])
    frames = (mixed * jax.nn.sigmoid(mixed)).astype(jnp.bfloat16)
    fade = fade_ref[0]
    shape = (share, spatial * wide)
    current = nn_dot(picker(shape, lambda row: row // FR * wide + FADE + row % FR), frames)

    def faded(row):
        return jnp.where(row % FR < fade, row // FR * wide + FADE - fade + row % FR, -1)

    previous = nn_dot(picker(shape, faded), frames)
    frame = lax.broadcasted_iota(jnp.int32, (share, out_ref.shape[2]), 0) % FR
    fade_float = jnp.full(frame.shape, fade, jnp.int32).astype(jnp.float32)
    weight = (frame.astype(jnp.float32) + 1.0) / (fade_float + 1.0)
    weight = jnp.where((frame < fade) & (position > 0), weight, 1.0)
    out_ref[0] = (weight * current + (1.0 - weight) * previous).astype(jnp.bfloat16)


def project(finished, w_in):
    axes = ("mp", "seq")
    parts = lax.axis_size(axes)
    _, rows, depth = finished.shape
    channels = w_in.shape[1]
    chunks = -(-depth // (2 * HD))
    return plain_call(
        functools.partial(project_kernel, axes),
        "project",
        [jax.ShapeDtypeStruct((rows // parts, channels), jnp.bfloat16)] * parts,
        2 * rows * depth * channels,
        (finished, w_in),
        [HBM_SPEC] * 2,
        scratch=[
            pltpu.VMEM((rows, depth), jnp.bfloat16),
            pltpu.VMEM((depth, channels), jnp.bfloat16),
            pltpu.SemaphoreType.DMA,
            pltpu.SemaphoreType.DMA((chunks,)),
        ],
        limit=VMEM_ALL,
    )


def gather(parts, rows):
    share, channels = parts[0].shape
    tail_rows = share // FR * (KT - 1 + FADE)
    return plain_call(
        gather_kernel,
        "gather",
        [jax.ShapeDtypeStruct((count, channels), jnp.bfloat16) for count in (share, tail_rows)],
        rows * channels,
        parts,
    )


def decode(hidden, tail, conv_w, fade_count):
    share, channels = hidden.shape
    return plain_call(
        decode_kernel,
        "decode",
        [jax.ShapeDtypeStruct((1, share, channels), jnp.bfloat16)],
        2 * share * KT * channels * channels,
        (fade_count, hidden, tail, conv_w),
        [SMEM_SPEC],
    )[0]


def per_device(
    query, noisy_kv, clean_kv, causal_mask, step_index, finished, w_in, conv_w, fade_count
):
    steps, _, rows, columns = query.shape
    heads = columns // HD
    row_count = steps * rows
    span = lax.axis_size("span")
    axes = ("mp", "seq")
    acc_shape = jax.ShapeDtypeStruct((heads, HD, row_count), jnp.float32)
    stat_shape = jax.ShapeDtypeStruct((heads, row_count), jnp.float32)
    pair_flops = 4 * row_count * rows * columns

    first_pairs = [(0, 2), (2, 3)] if span == 4 else [(c, c + 1) for c in range(span - 1)]
    near = send(clean_kv, first_pairs)
    pieces = project(finished, w_in)
    parts = [pieces[0]] + [swap(p, axes, offset + 1) for offset, p in enumerate(pieces[1:])]
    if span == 4:
        direct = send(after(clean_kv, pieces[0]), [(1, 3)])
    carry = plain_call(
        own_kernel,
        "own",
        [acc_shape, stat_shape, stat_shape],
        pair_flops,
        (step_index, query, noisy_kv),
        [SMEM_SPEC] + [HBM_SPEC] * 2,
        scratch=[
            pltpu.VMEM((steps, rows, columns), jnp.bfloat16),
            pltpu.VMEM((steps, 2, rows, columns), jnp.bfloat16),
            pltpu.SemaphoreType.DMA((steps,)),
            pltpu.SemaphoreType.DMA((steps,)),
        ],
        limit=VMEM_ALL,
    )
    hidden, tail = gather(parts, rows)
    tail = hop(tail, "span", 1)
    if span == 4:
        near = after(near, carry[0], hidden)
        early = [(near, {2: 0, 3: 2}), (direct, {3: 1})]
        forwards = lax.axis_index("span") == 2
        passed = [jnp.where(forwards, near[which], clean_kv[which]) for which in range(2)]
        keys, values = [hop(block, "span", 1) for block in passed]
        last_plan = {1: 0, 2: 1, 3: 0}
    else:
        ring = [near]
        for _ in range(2, span):
            ring.append(hop(ring[-1], "span", 1))
        early = [(block, delivered(span, back + 1)) for back, block in enumerate(ring[:-1])]
        keys, values = ring[-1][0], ring[-1][1]
        last_plan = delivered(span, span - 1)
    decoded = decode(hidden, tail, conv_w, fade_count)
    for first in range(0, len(early), 2):
        group = early[first : first + 2]
        carry = plain_call(
            functools.partial(mid_kernel, [plan for _, plan in group]),
            "middle",
            [acc_shape, stat_shape, stat_shape],
            len(group) * pair_flops,
            (step_index, causal_mask, query, *[block for block, _ in group], *carry),
            [SMEM_SPEC] * 2,
        )
    acc, weights = plain_call(
        functools.partial(score_kernel, last_plan),
        "score",
        [acc_shape, jax.ShapeDtypeStruct((heads, rows, row_count), jnp.bfloat16)],
        pair_flops // 2,
        (step_index, causal_mask, query, keys, *carry),
        [SMEM_SPEC] * 2,
    )
    averaged, squares = plain_call(
        average_kernel,
        "average",
        [acc_shape, jax.ShapeDtypeStruct((1, row_count), jnp.float32)],
        pair_flops // 2,
        (acc, weights, values),
    )
    others = [swap(squares, axes, offset) for offset in range(1, lax.axis_size(axes))]
    turned = plain_call(
        turn_kernel,
        "turn",
        [jax.ShapeDtypeStruct((steps, rows, columns), jnp.float32)],
        row_count * columns,
        (averaged,),
    )[0]
    attended = plain_call(
        functools.partial(scale_kernel, columns * lax.axis_size(axes)),
        "scale",
        jax.ShapeDtypeStruct(query.shape, jnp.bfloat16),
        row_count * columns,
        (turned, squares, *others),
        out_specs=HBM_SPEC,
        scratch=[
            pltpu.VMEM((steps, rows, columns), jnp.bfloat16),
            pltpu.SemaphoreType.DMA((steps,)),
        ],
    )
    return (attended, decoded)


def solution(mesh):
    placed = (
        P(None, ("groups", "span"), None, ("mp", "seq")),
        P(None, None, ("groups", "span"), None, ("mp", "seq")),
        P(None, ("groups", "span"), None, ("mp", "seq")),
        P("groups", None),
        P("groups", None),
        P(("groups", "span"), None, ("mp", "seq")),
        P(("mp", "seq"), None),
        P(),
        P(("groups", "span")),
    )
    return jax.shard_map(
        per_device,
        mesh=mesh,
        in_specs=placed,
        out_specs=(
            P(None, ("groups", "span"), None, ("mp", "seq")),
            P(("groups", "span"), ("mp", "seq"), None),
        ),
        check_vma=False,
    )
```

```python
import functools
import math

import jax
import jax.numpy as jnp
from jax import lax
from jax.experimental import pallas as pl
from jax.experimental.pallas import tpu as pltpu
from jax.sharding import PartitionSpec as P

FR = 6
HD = 128
KT = 3
FADE = 2
NSTEPS = 64
LOG2E = 1.4426950408889634
VMEM_LIMIT = 24 * 1024 * 1024
VMEM_ALL = 60 * 1024 * 1024

SMEM_SPEC = pl.BlockSpec(memory_space=pltpu.SMEM)
VMEM_SPEC = pl.BlockSpec(memory_space=pltpu.VMEM)
HBM_SPEC = pl.BlockSpec(memory_space=pltpu.HBM)


def cost(flops, nbytes):
    return pl.CostEstimate(flops=flops, bytes_accessed=nbytes, transcendentals=0)


def hop(value, axis, steps):
    count = lax.axis_size(axis)
    return lax.ppermute(value, axis, [(source, source + steps) for source in range(count - steps)])


def swap(value, axes, offset):
    count = lax.axis_size(axes)
    if count & (count - 1) == 0:
        pairs = [(source, source ^ offset) for source in range(count)]
    else:
        pairs = [(source, (source + offset) % count) for source in range(count)]
    return lax.ppermute(value, axes, pairs)


def target_of(axes, offset):
    count = lax.axis_size(axes)
    mine = lax.axis_index(axes)
    if count & (count - 1) == 0:
        return mine ^ offset
    return lax.rem(mine + offset, count)


def after(value, *earlier):
    return lax.optimization_barrier((value, *earlier))[0]


def nt_dot(left, right):
    return lax.dot_general(left, right, (((1,), (1,)), ((), ())), preferred_element_type=jnp.float32)


def tn_dot(left, right):
    return lax.dot_general(left, right, (((0,), (0,)), ((), ())), preferred_element_type=jnp.float32)


def nn_dot(left, right):
    return jnp.dot(left, right, preferred_element_type=jnp.float32)


def row_factors(step_ref, position, steps, rows):
    lane = lax.broadcasted_iota(jnp.int32, (1, steps * rows), 1)
    index = jnp.full(lane.shape, step_ref[position, 0], jnp.int32)
    for step in range(1, steps):
        index = jnp.where(lane >= step * rows, step_ref[position, step], index)
    fraction = 1.0 - index.astype(jnp.float32) / NSTEPS
    level = 3.0 * fraction / (1.0 + 2.0 * fraction)
    return (0.5 + level) * (LOG2E / math.sqrt(HD))


def lane_windows(steps, rows):
    total = steps * rows
    return [
        (step * rows // HD * HD, min(total, -(-(step + 1) * rows // HD) * HD))
        for step in range(steps)
    ]


def join_steps(pieces, windows, rows):
    total = windows[-1][1]
    tiles = []
    for first in range(0, total, HD):
        stop = min(first + HD, total)
        tile = None
        for step, (begin, end) in enumerate(windows):
            if begin <= first and stop <= end and step * rows < stop and first < (step + 1) * rows:
                part = pieces[step][:, first - begin : stop - begin]
                if tile is None:
                    tile = part
                else:
                    lane = lax.broadcasted_iota(jnp.int32, part.shape, 1) + first
                    tile = jnp.where(lane >= step * rows, part, tile)
        tiles.append(tile)
    return jnp.concatenate(tiles, 1)


def own_kernel(step_ref, q_ref, kv_ref, acc_ref, top_ref, total_ref):
    position = lax.axis_index("span")
    steps, _, rows, columns = q_ref.shape
    factors = row_factors(step_ref, position, steps, rows)
    windows = lane_windows(steps, rows)
    for head in range(columns // HD):
        cut = slice(head * HD, (head + 1) * HD)
        queries = q_ref[:, 0, :, cut].reshape(steps * rows, HD)
        scores = join_steps(
            [nt_dot(kv_ref[s, 0, 0, :, cut], queries[a:b]) for s, (a, b) in enumerate(windows)],
            windows,
            rows,
        )
        scores = scores * factors
        top = jnp.max(scores, axis=0, keepdims=True)
        weights = jnp.exp2(scores - top)
        rounded = weights.astype(jnp.bfloat16)
        acc_ref[head] = join_steps(
            [tn_dot(kv_ref[s, 1, 0, :, cut], rounded[:, a:b]) for s, (a, b) in enumerate(windows)],
            windows,
            rows,
        )
        top_ref[head : head + 1] = top
        total_ref[head : head + 1] = jnp.sum(weights, axis=0, keepdims=True)


def absorb(queries, keys, values, factors, acc, top, total):
    scores = nt_dot(keys, queries) * factors
    newest = jnp.maximum(top, jnp.max(scores, axis=0, keepdims=True))
    weights = jnp.exp2(scores - newest)
    shrink = jnp.exp2(top - newest)
    total = total * shrink + jnp.sum(weights, axis=0, keepdims=True)
    acc = acc * shrink + tn_dot(values, weights.astype(jnp.bfloat16))
    return acc, newest, total


def visible(mask_ref, position, blocks):
    seen = False
    for place, block in blocks.items():
        seen = seen | ((position == place) & (mask_ref[place, block] > 0))
    return seen


def half(ref, which, cut):
    return ref[which, 0, :, cut] if len(ref.shape) == 4 else ref[0, :, cut]


def mid_kernel(plan, step_ref, mask_ref, q_ref, *refs):
    block_refs, (acc_in, top_in, total_in, acc_ref, top_ref, total_ref) = refs[:-6], refs[-6:]
    position = lax.axis_index("span")
    steps, _, rows, columns = q_ref.shape
    seen = visible(mask_ref, position, plan)

    @pl.when(seen)
    def _():
        factors = row_factors(step_ref, position, steps, rows)
        for head in range(columns // HD):
            cut = slice(head * HD, (head + 1) * HD)
            queries = q_ref[:, 0, :, cut].reshape(steps * rows, HD)
            acc, top, total = absorb(
                queries,
                half(block_refs[0], 0, cut),
                half(block_refs[-1], 1, cut),
                factors,
                acc_in[head],
                top_in[head : head + 1],
                total_in[head : head + 1],
            )
            acc_ref[head] = acc
            top_ref[head : head + 1] = top
            total_ref[head : head + 1] = total

    @pl.when(jnp.logical_not(seen))
    def _():
        acc_ref[...] = acc_in[...]
        top_ref[...] = top_in[...]
        total_ref[...] = total_in[...]


def score_kernel(plans, step_ref, mask_ref, q_ref, *refs):
    key_refs, (acc_in, top_in, total_in, acc_ref, w_ref) = refs[:-5], refs[-5:]
    position = lax.axis_index("span")
    steps, _, rows, columns = q_ref.shape

    def finish(key_ref):
        factors = row_factors(step_ref, position, steps, rows)
        for head in range(columns // HD):
            cut = slice(head * HD, (head + 1) * HD)
            queries = q_ref[:, 0, :, cut].reshape(steps * rows, HD)
            scores = nt_dot(half(key_ref, 0, cut), queries) * factors
            top = top_in[head : head + 1]
            newest = jnp.maximum(top, jnp.max(scores, axis=0, keepdims=True))
            weights = jnp.exp2(scores - newest)
            shrink = jnp.exp2(top - newest)
            total = total_in[head : head + 1] * shrink + jnp.sum(weights, axis=0, keepdims=True)
            inverse = 1.0 / total
            w_ref[head] = (weights * inverse).astype(jnp.bfloat16)
            acc_ref[head] = acc_in[head] * (shrink * inverse)

    rest = True
    for plan, key_ref in zip(plans, key_refs):
        seen = visible(mask_ref, position, plan)
        rest = jnp.logical_and(rest, jnp.logical_not(seen))
        pl.when(seen)(functools.partial(finish, key_ref))

    @pl.when(rest)
    def _():
        w_ref[...] = jnp.zeros_like(w_ref)
        for head in range(columns // HD):
            acc_ref[head] = acc_in[head] * (1.0 / total_in[head : head + 1])


def average_kernel(plans, acc_ref, w_ref, *refs):
    value_refs, (average_ref, square_ref) = refs[:-2], refs[-2:]
    position = lax.axis_index("span")

    def finish(value_ref):
        squares = jnp.zeros(square_ref.shape, jnp.float32)
        for head in range(acc_ref.shape[0]):
            average = acc_ref[head]
            if value_ref is not None:
                values = half(value_ref, 1, slice(head * HD, (head + 1) * HD))
                average = average + tn_dot(values, w_ref[head])
            average_ref[head] = average
            squares = squares + jnp.sum(average * average, axis=0, keepdims=True)
        square_ref[...] = squares

    rest = True
    for plan, value_ref in zip(plans, value_refs):
        here = functools.reduce(jnp.logical_or, [position == place for place in plan])
        rest = jnp.logical_and(rest, jnp.logical_not(here))
        pl.when(here)(functools.partial(finish, value_ref))
    pl.when(rest)(functools.partial(finish, None))


def turn_kernel(in_ref, out_ref):
    heads = in_ref.shape[0]
    steps, rows, _ = out_ref.shape
    for head in range(heads):
        out_ref[:, :, head * HD : (head + 1) * HD] = in_ref[head].T.reshape(steps, rows, HD)


def scale_kernel(width, average_ref, *refs):
    part_refs, (out_hbm, out_ref, sem) = refs[:-3], refs[-3:]
    total = part_refs[0][...]
    for ref in part_refs[1:]:
        total = total + ref[...]
    inverse = lax.rsqrt(total / width + 1e-06)
    steps, rows, columns = average_ref.shape
    spread = jnp.broadcast_to(inverse, (HD, steps * rows)).T
    copies = []
    for step in range(steps):
        factor = spread[step * rows : (step + 1) * rows]
        for first in range(0, columns, HD):
            cut = slice(first, first + HD)
            out_ref[step, :, cut] = (average_ref[step, :, cut] * factor).astype(jnp.bfloat16)
        copies.append(pltpu.make_async_copy(out_ref.at[step], out_hbm.at[step, 0], sem.at[step]))
        copies[-1].start()
    for copy in copies:
        copy.wait()


def send(value, pairs):
    return lax.ppermute(value, "span", pairs)


def delivered(span, back):
    return {place: place - back for place in range(back, span)}


def plain_call(kernel, name, out_shape, flops, operands, in_specs=(), out_specs=None, scratch=(), limit=VMEM_LIMIT):
    nbytes = sum(math.prod(o.shape) * o.dtype.itemsize for o in operands)
    if out_specs is None:
        out_specs = [VMEM_SPEC] * len(out_shape)
    return pl.pallas_call(
        kernel,
        in_specs=list(in_specs) + [VMEM_SPEC] * (len(operands) - len(in_specs)),
        out_specs=out_specs,
        out_shape=out_shape,
        scratch_shapes=list(scratch),
        compiler_params=pltpu.CompilerParams(vmem_limit_bytes=limit),
        cost_estimate=cost(flops, nbytes),
        name=name,
    )(*operands)


def picker(shape, wanted):
    row = lax.broadcasted_iota(jnp.int32, shape, 0)
    column = lax.broadcasted_iota(jnp.int32, shape, 1)
    return jnp.where(column == wanted(row), 1.0, 0.0).astype(jnp.bfloat16)


def project_kernel(axes, x_hbm, w_hbm, *refs):
    out_refs, (x_ref, w_ref, x_sem, w_sem) = refs[:-4], refs[-4:]
    rows, depth = x_ref.shape
    share = out_refs[0].shape[0]
    x_copy = pltpu.make_async_copy(x_hbm.at[0], x_ref, x_sem)
    x_copy.start()
    copies = []
    for place, first in enumerate(range(0, depth, 2 * HD)):
        cut = slice(first, min(first + 2 * HD, depth))
        copies.append((cut, pltpu.make_async_copy(w_hbm.at[cut], w_ref.at[cut], w_sem.at[place])))
        copies[-1][1].start()
    total = jnp.zeros((rows, w_ref.shape[1]), jnp.float32)
    x_copy.wait()
    for cut, w_copy in copies:
        w_copy.wait()
        total = total + nn_dot(x_ref[:, cut], w_ref[cut])
    projected = total.astype(jnp.bfloat16)
    for offset, out_ref in enumerate(out_refs):
        first = target_of(axes, offset) * share
        chosen = picker((share, rows), lambda row: row + first)
        out_ref[...] = nn_dot(chosen, projected).astype(jnp.bfloat16)


def gather_kernel(*refs):
    hidden_ref, tail_ref = refs[-2:]
    total = refs[0][...].astype(jnp.float32)
    for ref in refs[1:-2]:
        total = total + ref[...].astype(jnp.float32)
    hidden = total.astype(jnp.bfloat16)
    hidden_ref[...] = hidden
    kept = KT - 1 + FADE
    shape = (tail_ref.shape[0], hidden.shape[0])
    chosen = picker(shape, lambda row: row // kept * FR + FR - kept + row % kept)
    tail_ref[...] = nn_dot(chosen, hidden).astype(jnp.bfloat16)


def decode_kernel(fade_ref, hidden_ref, tail_ref, conv_ref, out_ref):
    position = lax.axis_index("span")
    share = hidden_ref.shape[0]
    spatial = share // FR
    kept = KT - 1 + FADE
    wide = FADE + FR
    hidden, tail = hidden_ref[...], tail_ref[...]
    mixed = jnp.zeros((spatial * wide, out_ref.shape[2]), jnp.float32)
    for tap in range(KT):
        def from_tail(row):
            place = row % wide + KT - 1 - tap
            return jnp.where(place < kept, row // wide * kept + place, -1)

        def from_hidden(row):
            place = row % wide + KT - 1 - tap
            return jnp.where(place >= kept, row // wide * FR + place - kept, -1)

        window = nn_dot(picker((spatial * wide, tail.shape[0]), from_tail), tail)
        window = window + nn_dot(picker((spatial * wide, share), from_hidden), hidden)
        mixed = mixed + nn_dot(window.astype(jnp.bfloat16), conv_ref[tap])
    frames = (mixed * jax.nn.sigmoid(mixed)).astype(jnp.bfloat16)
    fade = fade_ref[0]
    shape = (share, spatial * wide)
    current = nn_dot(picker(shape, lambda row: row // FR * wide + FADE + row % FR), frames)

    def faded(row):
        return jnp.where(row % FR < fade, row // FR * wide + FADE - fade + row % FR, -1)

    previous = nn_dot(picker(shape, faded), frames)
    frame = lax.broadcasted_iota(jnp.int32, (share, out_ref.shape[2]), 0) % FR
    fade_float = jnp.full(frame.shape, fade, jnp.int32).astype(jnp.float32)
    weight = (frame.astype(jnp.float32) + 1.0) / (fade_float + 1.0)
    weight = jnp.where((frame < fade) & (position > 0), weight, 1.0)
    out_ref[0] = (weight * current + (1.0 - weight) * previous).astype(jnp.bfloat16)


def project(finished, w_in):
    axes = ("mp", "seq")
    parts = lax.axis_size(axes)
    _, rows, depth = finished.shape
    channels = w_in.shape[1]
    chunks = -(-depth // (2 * HD))
    return plain_call(
        functools.partial(project_kernel, axes),
        "project",
        [jax.ShapeDtypeStruct((rows // parts, channels), jnp.bfloat16)] * parts,
        2 * rows * depth * channels,
        (finished, w_in),
        [HBM_SPEC] * 2,
        scratch=[
            pltpu.VMEM((rows, depth), jnp.bfloat16),
            pltpu.VMEM((depth, channels), jnp.bfloat16),
            pltpu.SemaphoreType.DMA,
            pltpu.SemaphoreType.DMA((chunks,)),
        ],
        limit=VMEM_ALL,
    )


def gather(parts, rows):
    share, channels = parts[0].shape
    tail_rows = share // FR * (KT - 1 + FADE)
    return plain_call(
        gather_kernel,
        "gather",
        [jax.ShapeDtypeStruct((count, channels), jnp.bfloat16) for count in (share, tail_rows)],
        rows * channels,
        parts,
    )


def decode(hidden, tail, conv_w, fade_count):
    share, channels = hidden.shape
    return plain_call(
        decode_kernel,
        "decode",
        [jax.ShapeDtypeStruct((1, share, channels), jnp.bfloat16)],
        2 * share * KT * channels * channels,
        (fade_count, hidden, tail, conv_w),
        [SMEM_SPEC],
    )[0]


def per_device(
    query, noisy_kv, clean_kv, causal_mask, step_index, finished, w_in, conv_w, fade_count
):
    steps, _, rows, columns = query.shape
    heads = columns // HD
    row_count = steps * rows
    span = lax.axis_size("span")
    axes = ("mp", "seq")
    acc_shape = jax.ShapeDtypeStruct((heads, HD, row_count), jnp.float32)
    stat_shape = jax.ShapeDtypeStruct((heads, row_count), jnp.float32)
    pair_flops = 4 * row_count * rows * columns

    first_pairs = [(0, 2), (2, 3)] if span == 4 else [(c, c + 1) for c in range(span - 1)]
    near = send(clean_kv, first_pairs)

    def absorb_block(carry, block, plan):
        return plain_call(
            functools.partial(mid_kernel, plan),
            "middle",
            [acc_shape, stat_shape, stat_shape],
            pair_flops,
            (step_index, causal_mask, query, *block, *carry),
            [SMEM_SPEC] * 2,
        )

    pieces = project(finished, w_in)
    parts = [pieces[0]] + [swap(p, axes, offset + 1) for offset, p in enumerate(pieces[1:])]
    first_step = step_index
    if span == 4:
        own_keys = after(clean_kv, pieces[0])[0]
        direct = send(own_keys, [(1, 3)])
        first_step = after(step_index, own_keys)
    carry = plain_call(
        own_kernel,
        "own",
        [acc_shape, stat_shape, stat_shape],
        pair_flops,
        (first_step, query, noisy_kv),
        [SMEM_SPEC],
    )
    hidden, tail = gather(parts, rows)
    tail = hop(tail, "span", 1)
    if span == 4:
        near = after(near, carry[0], hidden)
        forwards = lax.axis_index("span") == 2
        passed = [jnp.where(forwards, near[which], clean_kv[1 - which]) for which in range(2)]
        passed = [hop(block, "span", 1) for block in passed]
        early = [(passed, {3: 0})]
        carry = [carry[0], after(carry[1], direct), carry[2]]
        carry = absorb_block(carry, (near,), {2: 0, 3: 2})
        final = send(after(passed[0], carry[1]), [(2, 3)])
        keys = [(passed[1], {1: 0, 2: 1}), (direct, {3: 1})]
        values = [(passed[0], {1: 0, 2: 1}), (final, {3: 1})]
    else:
        ring = [near]
        for _ in range(2, span):
            ring.append(hop(ring[-1], "span", 1))
        early = [((block,), delivered(span, back + 1)) for back, block in enumerate(ring[:-1])]
        keys = values = [(ring[-1], delivered(span, span - 1))]
    decoded = decode(hidden, tail, conv_w, fade_count)
    for block, plan in early:
        carry = absorb_block(carry, block, plan)
    acc, weights = plain_call(
        functools.partial(score_kernel, [plan for _, plan in keys]),
        "score",
        [acc_shape, jax.ShapeDtypeStruct((heads, rows, row_count), jnp.bfloat16)],
        pair_flops // 2,
        (step_index, causal_mask, query, *[block for block, _ in keys], *carry),
        [SMEM_SPEC] * 2,
    )
    averaged, squares = plain_call(
        functools.partial(average_kernel, [plan for _, plan in values]),
        "average",
        [acc_shape, jax.ShapeDtypeStruct((1, row_count), jnp.float32)],
        pair_flops // 2,
        (acc, weights, *[block for block, _ in values]),
    )
    others = [swap(squares, axes, offset) for offset in range(1, lax.axis_size(axes))]
    turned = plain_call(
        turn_kernel,
        "turn",
        [jax.ShapeDtypeStruct((steps, rows, columns), jnp.float32)],
        row_count * columns,
        (averaged,),
    )[0]
    attended = plain_call(
        functools.partial(scale_kernel, columns * lax.axis_size(axes)),
        "scale",
        jax.ShapeDtypeStruct(query.shape, jnp.bfloat16),
        row_count * columns,
        (turned, squares, *others),
        out_specs=HBM_SPEC,
        scratch=[
            pltpu.VMEM((steps, rows, columns), jnp.bfloat16),
            pltpu.SemaphoreType.DMA((steps,)),
        ],
    )
    return (attended, decoded)


def solution(mesh):
    placed = (
        P(None, ("groups", "span"), None, ("mp", "seq")),
        P(None, None, ("groups", "span"), None, ("mp", "seq")),
        P(None, ("groups", "span"), None, ("mp", "seq")),
        P("groups", None),
        P("groups", None),
        P(("groups", "span"), None, ("mp", "seq")),
        P(("mp", "seq"), None),
        P(),
        P(("groups", "span")),
    )
    return jax.shard_map(
        per_device,
        mesh=mesh,
        in_specs=placed,
        out_specs=(
            P(None, ("groups", "span"), None, ("mp", "seq")),
            P(("groups", "span"), ("mp", "seq"), None),
        ),
        check_vma=False,
    )
```

```python
import functools
import math

import jax
import jax.numpy as jnp
from jax import lax
from jax.experimental import pallas as pl
from jax.experimental.pallas import tpu as pltpu
from jax.sharding import PartitionSpec as P

FR = 6
HD = 128
KT = 3
FADE = 2
NSTEPS = 64
LOG2E = 1.4426950408889634
VMEM_LIMIT = 24 * 1024 * 1024
VMEM_ALL = 60 * 1024 * 1024

SMEM_SPEC = pl.BlockSpec(memory_space=pltpu.SMEM)
VMEM_SPEC = pl.BlockSpec(memory_space=pltpu.VMEM)
HBM_SPEC = pl.BlockSpec(memory_space=pltpu.HBM)


def cost(flops, nbytes):
    return pl.CostEstimate(flops=flops, bytes_accessed=nbytes, transcendentals=0)


def hop(value, axis, steps):
    count = lax.axis_size(axis)
    return lax.ppermute(value, axis, [(source, source + steps) for source in range(count - steps)])


def swap(value, axes, offset):
    count = lax.axis_size(axes)
    if count & (count - 1) == 0:
        pairs = [(source, source ^ offset) for source in range(count)]
    else:
        pairs = [(source, (source + offset) % count) for source in range(count)]
    return lax.ppermute(value, axes, pairs)


def target_of(axes, offset):
    count = lax.axis_size(axes)
    mine = lax.axis_index(axes)
    if count & (count - 1) == 0:
        return mine ^ offset
    return lax.rem(mine + offset, count)


def after(value, *earlier):
    return lax.optimization_barrier((value, *earlier))[0]


def nt_dot(left, right):
    return lax.dot_general(left, right, (((1,), (1,)), ((), ())), preferred_element_type=jnp.float32)


def tn_dot(left, right):
    return lax.dot_general(left, right, (((0,), (0,)), ((), ())), preferred_element_type=jnp.float32)


def nn_dot(left, right):
    return jnp.dot(left, right, preferred_element_type=jnp.float32)


def row_factors(step_ref, position, steps, rows):
    lane = lax.broadcasted_iota(jnp.int32, (1, steps * rows), 1)
    index = jnp.full(lane.shape, step_ref[position, 0], jnp.int32)
    for step in range(1, steps):
        index = jnp.where(lane >= step * rows, step_ref[position, step], index)
    fraction = 1.0 - index.astype(jnp.float32) / NSTEPS
    level = 3.0 * fraction / (1.0 + 2.0 * fraction)
    return (0.5 + level) * (LOG2E / math.sqrt(HD))


def lane_windows(steps, rows):
    total = steps * rows
    return [
        (step * rows // HD * HD, min(total, -(-(step + 1) * rows // HD) * HD))
        for step in range(steps)
    ]


def join_steps(pieces, windows, rows):
    total = windows[-1][1]
    tiles = []
    for first in range(0, total, HD):
        stop = min(first + HD, total)
        tile = None
        for step, (begin, end) in enumerate(windows):
            if begin <= first and stop <= end and step * rows < stop and first < (step + 1) * rows:
                part = pieces[step][:, first - begin : stop - begin]
                if tile is None:
                    tile = part
                else:
                    lane = lax.broadcasted_iota(jnp.int32, part.shape, 1) + first
                    tile = jnp.where(lane >= step * rows, part, tile)
        tiles.append(tile)
    return jnp.concatenate(tiles, 1)


def own_kernel(step_ref, q_ref, kv_ref, acc_ref, top_ref, total_ref):
    position = lax.axis_index("span")
    steps, _, rows, columns = q_ref.shape
    factors = row_factors(step_ref, position, steps, rows)
    windows = lane_windows(steps, rows)
    for head in range(columns // HD):
        cut = slice(head * HD, (head + 1) * HD)
        queries = q_ref[:, 0, :, cut].reshape(steps * rows, HD)
        scores = join_steps(
            [nt_dot(kv_ref[s, 0, 0, :, cut], queries[a:b]) for s, (a, b) in enumerate(windows)],
            windows,
            rows,
        )
        scores = scores * factors
        top = jnp.max(scores, axis=0, keepdims=True)
        weights = jnp.exp2(scores - top)
        rounded = weights.astype(jnp.bfloat16)
        acc_ref[head] = join_steps(
            [tn_dot(kv_ref[s, 1, 0, :, cut], rounded[:, a:b]) for s, (a, b) in enumerate(windows)],
            windows,
            rows,
        )
        top_ref[head : head + 1] = top
        total_ref[head : head + 1] = jnp.sum(weights, axis=0, keepdims=True)


def absorb(queries, keys, values, factors, acc, top, total):
    scores = nt_dot(keys, queries) * factors
    newest = jnp.maximum(top, jnp.max(scores, axis=0, keepdims=True))
    weights = jnp.exp2(scores - newest)
    shrink = jnp.exp2(top - newest)
    total = total * shrink + jnp.sum(weights, axis=0, keepdims=True)
    acc = acc * shrink + tn_dot(values, weights.astype(jnp.bfloat16))
    return acc, newest, total


def visible(mask_ref, position, blocks):
    seen = False
    for place, block in blocks.items():
        seen = seen | ((position == place) & (mask_ref[place, block] > 0))
    return seen


def half(ref, which, cut):
    return ref[which, 0, :, cut] if len(ref.shape) == 4 else ref[0, :, cut]


def mid_kernel(plan, step_ref, mask_ref, q_ref, *refs):
    block_refs, (acc_in, top_in, total_in, acc_ref, top_ref, total_ref) = refs[:-6], refs[-6:]
    position = lax.axis_index("span")
    steps, _, rows, columns = q_ref.shape
    seen = visible(mask_ref, position, plan)

    @pl.when(seen)
    def _():
        factors = row_factors(step_ref, position, steps, rows)
        for head in range(columns // HD):
            cut = slice(head * HD, (head + 1) * HD)
            queries = q_ref[:, 0, :, cut].reshape(steps * rows, HD)
            acc, top, total = absorb(
                queries,
                half(block_refs[0], 0, cut),
                half(block_refs[-1], 1, cut),
                factors,
                acc_in[head],
                top_in[head : head + 1],
                total_in[head : head + 1],
            )
            acc_ref[head] = acc
            top_ref[head : head + 1] = top
            total_ref[head : head + 1] = total

    @pl.when(jnp.logical_not(seen))
    def _():
        acc_ref[...] = acc_in[...]
        top_ref[...] = top_in[...]
        total_ref[...] = total_in[...]


def score_kernel(plans, step_ref, mask_ref, q_ref, *refs):
    key_refs, (acc_in, top_in, total_in, acc_ref, w_ref) = refs[:-5], refs[-5:]
    position = lax.axis_index("span")
    steps, _, rows, columns = q_ref.shape

    def finish(key_ref):
        factors = row_factors(step_ref, position, steps, rows)
        for head in range(columns // HD):
            cut = slice(head * HD, (head + 1) * HD)
            queries = q_ref[:, 0, :, cut].reshape(steps * rows, HD)
            scores = nt_dot(half(key_ref, 0, cut), queries) * factors
            top = top_in[head : head + 1]
            newest = jnp.maximum(top, jnp.max(scores, axis=0, keepdims=True))
            weights = jnp.exp2(scores - newest)
            shrink = jnp.exp2(top - newest)
            total = total_in[head : head + 1] * shrink + jnp.sum(weights, axis=0, keepdims=True)
            inverse = 1.0 / total
            w_ref[head] = (weights * inverse).astype(jnp.bfloat16)
            acc_ref[head] = acc_in[head] * (shrink * inverse)

    rest = True
    for plan, key_ref in zip(plans, key_refs):
        seen = visible(mask_ref, position, plan)
        rest = jnp.logical_and(rest, jnp.logical_not(seen))
        pl.when(seen)(functools.partial(finish, key_ref))

    @pl.when(rest)
    def _():
        w_ref[...] = jnp.zeros_like(w_ref)
        for head in range(columns // HD):
            acc_ref[head] = acc_in[head] * (1.0 / total_in[head : head + 1])


def average_kernel(plans, acc_ref, w_ref, *refs):
    value_refs, (average_ref, square_ref) = refs[:-2], refs[-2:]
    position = lax.axis_index("span")

    def finish(value_ref):
        squares = jnp.zeros(square_ref.shape, jnp.float32)
        for head in range(acc_ref.shape[0]):
            average = acc_ref[head]
            if value_ref is not None:
                values = half(value_ref, 1, slice(head * HD, (head + 1) * HD))
                average = average + tn_dot(values, w_ref[head])
            average_ref[head] = average
            squares = squares + jnp.sum(average * average, axis=0, keepdims=True)
        square_ref[...] = squares

    rest = True
    for plan, value_ref in zip(plans, value_refs):
        here = functools.reduce(jnp.logical_or, [position == place for place in plan])
        rest = jnp.logical_and(rest, jnp.logical_not(here))
        pl.when(here)(functools.partial(finish, value_ref))
    pl.when(rest)(functools.partial(finish, None))


def turn_kernel(in_ref, out_ref):
    heads = in_ref.shape[0]
    steps, rows, _ = out_ref.shape
    for head in range(heads):
        out_ref[:, :, head * HD : (head + 1) * HD] = in_ref[head].T.reshape(steps, rows, HD)


def scale_kernel(width, average_ref, *refs):
    part_refs, (out_hbm, out_ref, sem) = refs[:-3], refs[-3:]
    total = part_refs[0][...]
    for ref in part_refs[1:]:
        total = total + ref[...]
    inverse = lax.rsqrt(total / width + 1e-06)
    steps, rows, columns = average_ref.shape
    spread = jnp.broadcast_to(inverse, (HD, steps * rows)).T
    copies = []
    for step in range(steps):
        factor = spread[step * rows : (step + 1) * rows]
        for first in range(0, columns, HD):
            cut = slice(first, first + HD)
            out_ref[step, :, cut] = (average_ref[step, :, cut] * factor).astype(jnp.bfloat16)
        copies.append(pltpu.make_async_copy(out_ref.at[step], out_hbm.at[step, 0], sem.at[step]))
        copies[-1].start()
    for copy in copies:
        copy.wait()


def send(value, pairs):
    return lax.ppermute(value, "span", pairs)


def delivered(span, back):
    return {place: place - back for place in range(back, span)}


def plain_call(kernel, name, out_shape, flops, operands, in_specs=(), out_specs=None, scratch=(), limit=VMEM_LIMIT):
    nbytes = sum(math.prod(o.shape) * o.dtype.itemsize for o in operands)
    if out_specs is None:
        out_specs = [VMEM_SPEC] * len(out_shape)
    return pl.pallas_call(
        kernel,
        in_specs=list(in_specs) + [VMEM_SPEC] * (len(operands) - len(in_specs)),
        out_specs=out_specs,
        out_shape=out_shape,
        scratch_shapes=list(scratch),
        compiler_params=pltpu.CompilerParams(vmem_limit_bytes=limit),
        cost_estimate=cost(flops, nbytes),
        name=name,
    )(*operands)


def picker(shape, wanted):
    row = lax.broadcasted_iota(jnp.int32, shape, 0)
    column = lax.broadcasted_iota(jnp.int32, shape, 1)
    return jnp.where(column == wanted(row), 1.0, 0.0).astype(jnp.bfloat16)


def project_kernel(axes, x_hbm, w_hbm, *refs):
    out_refs, (x_ref, w_ref, x_sem, w_sem) = refs[:-4], refs[-4:]
    rows, depth = x_ref.shape
    share = out_refs[0].shape[0]
    x_copy = pltpu.make_async_copy(x_hbm.at[0], x_ref, x_sem)
    x_copy.start()
    copies = []
    for place, first in enumerate(range(0, depth, 2 * HD)):
        cut = slice(first, min(first + 2 * HD, depth))
        copies.append((cut, pltpu.make_async_copy(w_hbm.at[cut], w_ref.at[cut], w_sem.at[place])))
        copies[-1][1].start()
    total = jnp.zeros((rows, w_ref.shape[1]), jnp.float32)
    x_copy.wait()
    for cut, w_copy in copies:
        w_copy.wait()
        total = total + nn_dot(x_ref[:, cut], w_ref[cut])
    projected = total.astype(jnp.bfloat16)
    for offset, out_ref in enumerate(out_refs):
        first = target_of(axes, offset) * share
        chosen = picker((share, rows), lambda row: row + first)
        out_ref[...] = nn_dot(chosen, projected).astype(jnp.bfloat16)


def gather_kernel(*refs):
    hidden_ref, tail_ref = refs[-2:]
    total = refs[0][...].astype(jnp.float32)
    for ref in refs[1:-2]:
        total = total + ref[...].astype(jnp.float32)
    hidden = total.astype(jnp.bfloat16)
    hidden_ref[...] = hidden
    kept = KT - 1 + FADE
    shape = (tail_ref.shape[0], hidden.shape[0])
    chosen = picker(shape, lambda row: row // kept * FR + FR - kept + row % kept)
    tail_ref[...] = nn_dot(chosen, hidden).astype(jnp.bfloat16)


def decode_kernel(fade_ref, hidden_ref, tail_ref, conv_ref, out_ref):
    position = lax.axis_index("span")
    share = hidden_ref.shape[0]
    spatial = share // FR
    kept = KT - 1 + FADE
    wide = FADE + FR
    hidden, tail = hidden_ref[...], tail_ref[...]
    mixed = jnp.zeros((spatial * wide, out_ref.shape[2]), jnp.float32)
    for tap in range(KT):
        def from_tail(row):
            place = row % wide + KT - 1 - tap
            return jnp.where(place < kept, row // wide * kept + place, -1)

        def from_hidden(row):
            place = row % wide + KT - 1 - tap
            return jnp.where(place >= kept, row // wide * FR + place - kept, -1)

        window = nn_dot(picker((spatial * wide, tail.shape[0]), from_tail), tail)
        window = window + nn_dot(picker((spatial * wide, share), from_hidden), hidden)
        mixed = mixed + nn_dot(window.astype(jnp.bfloat16), conv_ref[tap])
    frames = (mixed * jax.nn.sigmoid(mixed)).astype(jnp.bfloat16)
    fade = fade_ref[0]
    shape = (share, spatial * wide)
    current = nn_dot(picker(shape, lambda row: row // FR * wide + FADE + row % FR), frames)

    def faded(row):
        return jnp.where(row % FR < fade, row // FR * wide + FADE - fade + row % FR, -1)

    previous = nn_dot(picker(shape, faded), frames)
    frame = lax.broadcasted_iota(jnp.int32, (share, out_ref.shape[2]), 0) % FR
    fade_float = jnp.full(frame.shape, fade, jnp.int32).astype(jnp.float32)
    weight = (frame.astype(jnp.float32) + 1.0) / (fade_float + 1.0)
    weight = jnp.where((frame < fade) & (position > 0), weight, 1.0)
    out_ref[0] = (weight * current + (1.0 - weight) * previous).astype(jnp.bfloat16)


def project(finished, w_in):
    axes = ("mp", "seq")
    parts = lax.axis_size(axes)
    _, rows, depth = finished.shape
    channels = w_in.shape[1]
    chunks = -(-depth // (2 * HD))
    return plain_call(
        functools.partial(project_kernel, axes),
        "project",
        [jax.ShapeDtypeStruct((rows // parts, channels), jnp.bfloat16)] * parts,
        2 * rows * depth * channels,
        (finished, w_in),
        [HBM_SPEC] * 2,
        scratch=[
            pltpu.VMEM((rows, depth), jnp.bfloat16),
            pltpu.VMEM((depth, channels), jnp.bfloat16),
            pltpu.SemaphoreType.DMA,
            pltpu.SemaphoreType.DMA((chunks,)),
        ],
        limit=VMEM_ALL,
    )


def gather(parts, rows):
    share, channels = parts[0].shape
    tail_rows = share // FR * (KT - 1 + FADE)
    return plain_call(
        gather_kernel,
        "gather",
        [jax.ShapeDtypeStruct((count, channels), jnp.bfloat16) for count in (share, tail_rows)],
        rows * channels,
        parts,
    )


def decode(hidden, tail, conv_w, fade_count):
    share, channels = hidden.shape
    return plain_call(
        decode_kernel,
        "decode",
        [jax.ShapeDtypeStruct((1, share, channels), jnp.bfloat16)],
        2 * share * KT * channels * channels,
        (fade_count, hidden, tail, conv_w),
        [SMEM_SPEC],
    )[0]


def per_device(
    query, noisy_kv, clean_kv, causal_mask, step_index, finished, w_in, conv_w, fade_count
):
    steps, _, rows, columns = query.shape
    heads = columns // HD
    row_count = steps * rows
    span = lax.axis_size("span")
    axes = ("mp", "seq")
    acc_shape = jax.ShapeDtypeStruct((heads, HD, row_count), jnp.float32)
    stat_shape = jax.ShapeDtypeStruct((heads, row_count), jnp.float32)
    pair_flops = 4 * row_count * rows * columns

    first_pairs = [(0, 2), (2, 3)] if span == 4 else [(c, c + 1) for c in range(span - 1)]
    near = send(clean_kv, first_pairs)
    pieces = project(finished, w_in)
    parts = [pieces[0]] + [swap(p, axes, offset + 1) for offset, p in enumerate(pieces[1:])]
    if span == 4:
        direct = send(after(clean_kv, pieces[0]), [(1, 3)])
    carry = plain_call(
        own_kernel,
        "own",
        [acc_shape, stat_shape, stat_shape],
        pair_flops,
        (step_index, query, noisy_kv),
        [SMEM_SPEC],
    )
    hidden, tail = gather(parts, rows)
    tail = hop(tail, "span", 1)
    if span == 4:
        near = after(near, carry[0], hidden)
        forwards = lax.axis_index("span") == 2
        passed = [jnp.where(forwards, near[which], clean_kv[which]) for which in range(2)]
        passed = [hop(block, "span", 1) for block in passed]
        early = [(near, {2: 0, 3: 2}), (direct, {3: 1})]
        keys, values = passed
        last_plan = {1: 0, 2: 1, 3: 0}
    else:
        ring = [near]
        for _ in range(2, span):
            ring.append(hop(ring[-1], "span", 1))
        early = [(block, delivered(span, back + 1)) for back, block in enumerate(ring[:-1])]
        keys = values = ring[-1]
        last_plan = delivered(span, span - 1)
    for block, plan in early:
        carry = plain_call(
            functools.partial(mid_kernel, plan),
            "middle",
            [acc_shape, stat_shape, stat_shape],
            pair_flops,
            (step_index, causal_mask, query, block, *carry),
            [SMEM_SPEC] * 2,
        )
    acc, weights = plain_call(
        functools.partial(score_kernel, [last_plan]),
        "score",
        [acc_shape, jax.ShapeDtypeStruct((heads, rows, row_count), jnp.bfloat16)],
        pair_flops // 2,
        (step_index, causal_mask, query, keys, *carry),
        [SMEM_SPEC] * 2,
    )
    decoded = decode(after(hidden, weights), tail, conv_w, fade_count)
    averaged, squares = plain_call(
        functools.partial(average_kernel, [last_plan]),
        "average",
        [acc_shape, jax.ShapeDtypeStruct((1, row_count), jnp.float32)],
        pair_flops // 2,
        (after(acc, decoded), weights, values),
    )
    others = [swap(squares, axes, offset) for offset in range(1, lax.axis_size(axes))]
    turned = plain_call(
        turn_kernel,
        "turn",
        [jax.ShapeDtypeStruct((steps, rows, columns), jnp.float32)],
        row_count * columns,
        (averaged,),
    )[0]
    attended = plain_call(
        functools.partial(scale_kernel, columns * lax.axis_size(axes)),
        "scale",
        jax.ShapeDtypeStruct(query.shape, jnp.bfloat16),
        row_count * columns,
        (turned, squares, *others),
        out_specs=HBM_SPEC,
        scratch=[
            pltpu.VMEM((steps, rows, columns), jnp.bfloat16),
            pltpu.SemaphoreType.DMA((steps,)),
        ],
    )
    return (attended, decoded)


def solution(mesh):
    placed = (
        P(None, ("groups", "span"), None, ("mp", "seq")),
        P(None, None, ("groups", "span"), None, ("mp", "seq")),
        P(None, ("groups", "span"), None, ("mp", "seq")),
        P("groups", None),
        P("groups", None),
        P(("groups", "span"), None, ("mp", "seq")),
        P(("mp", "seq"), None),
        P(),
        P(("groups", "span")),
    )
    return jax.shard_map(
        per_device,
        mesh=mesh,
        in_specs=placed,
        out_specs=(
            P(None, ("groups", "span"), None, ("mp", "seq")),
            P(("groups", "span"), ("mp", "seq"), None),
        ),
        check_vma=False,
    )
```

```python
import functools
import math

import jax
import jax.numpy as jnp
from jax import lax
from jax.experimental import pallas as pl
from jax.experimental.pallas import tpu as pltpu
from jax.sharding import PartitionSpec as P

FR = 6
HD = 128
KT = 3
FADE = 2
NSTEPS = 64
LOG2E = 1.4426950408889634
VMEM_LIMIT = 24 * 1024 * 1024
VMEM_ALL = 60 * 1024 * 1024

SMEM_SPEC = pl.BlockSpec(memory_space=pltpu.SMEM)
VMEM_SPEC = pl.BlockSpec(memory_space=pltpu.VMEM)
HBM_SPEC = pl.BlockSpec(memory_space=pltpu.HBM)


def cost(flops, nbytes):
    return pl.CostEstimate(flops=flops, bytes_accessed=nbytes, transcendentals=0)


def hop(value, axis, steps):
    count = lax.axis_size(axis)
    return lax.ppermute(value, axis, [(source, source + steps) for source in range(count - steps)])


def swap(value, axes, offset):
    count = lax.axis_size(axes)
    if count & (count - 1) == 0:
        pairs = [(source, source ^ offset) for source in range(count)]
    else:
        pairs = [(source, (source + offset) % count) for source in range(count)]
    return lax.ppermute(value, axes, pairs)


def target_of(axes, offset):
    count = lax.axis_size(axes)
    mine = lax.axis_index(axes)
    if count & (count - 1) == 0:
        return mine ^ offset
    return lax.rem(mine + offset, count)


def after(value, *earlier):
    return lax.optimization_barrier((value, *earlier))[0]


def nt_dot(left, right):
    return lax.dot_general(left, right, (((1,), (1,)), ((), ())), preferred_element_type=jnp.float32)


def tn_dot(left, right):
    return lax.dot_general(left, right, (((0,), (0,)), ((), ())), preferred_element_type=jnp.float32)


def nn_dot(left, right):
    return jnp.dot(left, right, preferred_element_type=jnp.float32)


def row_factors(step_ref, position, steps, rows):
    lane = lax.broadcasted_iota(jnp.int32, (1, steps * rows), 1)
    index = jnp.full(lane.shape, step_ref[position, 0], jnp.int32)
    for step in range(1, steps):
        index = jnp.where(lane >= step * rows, step_ref[position, step], index)
    fraction = 1.0 - index.astype(jnp.float32) / NSTEPS
    level = 3.0 * fraction / (1.0 + 2.0 * fraction)
    return (0.5 + level) * (LOG2E / math.sqrt(HD))


def lane_windows(steps, rows):
    total = steps * rows
    return [
        (step * rows // HD * HD, min(total, -(-(step + 1) * rows // HD) * HD))
        for step in range(steps)
    ]


def join_steps(pieces, windows, rows):
    total = windows[-1][1]
    tiles = []
    for first in range(0, total, HD):
        stop = min(first + HD, total)
        tile = None
        for step, (begin, end) in enumerate(windows):
            if begin <= first and stop <= end and step * rows < stop and first < (step + 1) * rows:
                part = pieces[step][:, first - begin : stop - begin]
                if tile is None:
                    tile = part
                else:
                    lane = lax.broadcasted_iota(jnp.int32, part.shape, 1) + first
                    tile = jnp.where(lane >= step * rows, part, tile)
        tiles.append(tile)
    return jnp.concatenate(tiles, 1)


def own_kernel(step_ref, q_ref, kv_ref, acc_ref, top_ref, total_ref):
    position = lax.axis_index("span")
    steps, _, rows, columns = q_ref.shape
    factors = row_factors(step_ref, position, steps, rows)
    windows = lane_windows(steps, rows)
    for head in range(columns // HD):
        cut = slice(head * HD, (head + 1) * HD)
        queries = q_ref[:, 0, :, cut].reshape(steps * rows, HD)
        scores = join_steps(
            [nt_dot(kv_ref[s, 0, 0, :, cut], queries[a:b]) for s, (a, b) in enumerate(windows)],
            windows,
            rows,
        )
        scores = scores * factors
        top = jnp.max(scores, axis=0, keepdims=True)
        weights = jnp.exp2(scores - top)
        rounded = weights.astype(jnp.bfloat16)
        acc_ref[head] = join_steps(
            [tn_dot(kv_ref[s, 1, 0, :, cut], rounded[:, a:b]) for s, (a, b) in enumerate(windows)],
            windows,
            rows,
        )
        top_ref[head : head + 1] = top
        total_ref[head : head + 1] = jnp.sum(weights, axis=0, keepdims=True)


def absorb(queries, keys, values, factors, acc, top, total):
    scores = nt_dot(keys, queries) * factors
    newest = jnp.maximum(top, jnp.max(scores, axis=0, keepdims=True))
    weights = jnp.exp2(scores - newest)
    shrink = jnp.exp2(top - newest)
    total = total * shrink + jnp.sum(weights, axis=0, keepdims=True)
    acc = acc * shrink + tn_dot(values, weights.astype(jnp.bfloat16))
    return acc, newest, total


def visible(mask_ref, position, blocks):
    seen = False
    for place, block in blocks.items():
        seen = seen | ((position == place) & (mask_ref[place, block] > 0))
    return seen


def half(ref, which, cut):
    return ref[which, 0, :, cut] if len(ref.shape) == 4 else ref[0, :, cut]


def mid_kernel(plan, step_ref, mask_ref, q_ref, *refs):
    block_refs, (acc_in, top_in, total_in, acc_ref, top_ref, total_ref) = refs[:-6], refs[-6:]
    position = lax.axis_index("span")
    steps, _, rows, columns = q_ref.shape
    seen = visible(mask_ref, position, plan)

    @pl.when(seen)
    def _():
        factors = row_factors(step_ref, position, steps, rows)
        for head in range(columns // HD):
            cut = slice(head * HD, (head + 1) * HD)
            queries = q_ref[:, 0, :, cut].reshape(steps * rows, HD)
            acc, top, total = absorb(
                queries,
                half(block_refs[0], 0, cut),
                half(block_refs[-1], 1, cut),
                factors,
                acc_in[head],
                top_in[head : head + 1],
                total_in[head : head + 1],
            )
            acc_ref[head] = acc
            top_ref[head : head + 1] = top
            total_ref[head : head + 1] = total

    @pl.when(jnp.logical_not(seen))
    def _():
        acc_ref[...] = acc_in[...]
        top_ref[...] = top_in[...]
        total_ref[...] = total_in[...]


def score_kernel(plans, step_ref, mask_ref, q_ref, *refs):
    key_refs, (acc_in, top_in, total_in, acc_ref, w_ref) = refs[:-5], refs[-5:]
    position = lax.axis_index("span")
    steps, _, rows, columns = q_ref.shape

    def finish(key_ref):
        factors = row_factors(step_ref, position, steps, rows)
        for head in range(columns // HD):
            cut = slice(head * HD, (head + 1) * HD)
            queries = q_ref[:, 0, :, cut].reshape(steps * rows, HD)
            scores = nt_dot(half(key_ref, 0, cut), queries) * factors
            top = top_in[head : head + 1]
            newest = jnp.maximum(top, jnp.max(scores, axis=0, keepdims=True))
            weights = jnp.exp2(scores - newest)
            shrink = jnp.exp2(top - newest)
            total = total_in[head : head + 1] * shrink + jnp.sum(weights, axis=0, keepdims=True)
            inverse = 1.0 / total
            w_ref[head] = (weights * inverse).astype(jnp.bfloat16)
            acc_ref[head] = acc_in[head] * (shrink * inverse)

    rest = True
    for plan, key_ref in zip(plans, key_refs):
        seen = visible(mask_ref, position, plan)
        rest = jnp.logical_and(rest, jnp.logical_not(seen))
        pl.when(seen)(functools.partial(finish, key_ref))

    @pl.when(rest)
    def _():
        w_ref[...] = jnp.zeros_like(w_ref)
        for head in range(columns // HD):
            acc_ref[head] = acc_in[head] * (1.0 / total_in[head : head + 1])


def average_kernel(plans, acc_ref, w_ref, *refs):
    value_refs, (average_ref, square_ref) = refs[:-2], refs[-2:]
    position = lax.axis_index("span")

    def finish(value_ref):
        squares = jnp.zeros(square_ref.shape[1:], jnp.float32)
        for head in range(acc_ref.shape[0]):
            average = acc_ref[head]
            if value_ref is not None:
                values = half(value_ref, 1, slice(head * HD, (head + 1) * HD))
                average = average + tn_dot(values, w_ref[head])
            average_ref[head] = average
            squares = squares + jnp.sum(average * average, axis=0, keepdims=True)
        square_ref[...] = jnp.broadcast_to(squares, square_ref.shape)

    rest = True
    for plan, value_ref in zip(plans, value_refs):
        here = functools.reduce(jnp.logical_or, [position == place for place in plan])
        rest = jnp.logical_and(rest, jnp.logical_not(here))
        pl.when(here)(functools.partial(finish, value_ref))
    pl.when(rest)(functools.partial(finish, None))


def turn_kernel(in_ref, out_ref):
    heads = in_ref.shape[0]
    steps, rows, _ = out_ref.shape
    for head in range(heads):
        out_ref[:, :, head * HD : (head + 1) * HD] = in_ref[head].T.reshape(steps, rows, HD)


def scale_kernel(width, average_ref, square_ref, out_hbm, out_ref, sem):
    total = jnp.sum(square_ref[...], axis=0)
    inverse = lax.rsqrt(total / width + 1e-06)
    steps, rows, columns = average_ref.shape
    spread = jnp.broadcast_to(inverse, (HD, steps * rows)).T
    copies = []
    for step in range(steps):
        factor = spread[step * rows : (step + 1) * rows]
        for first in range(0, columns, HD):
            cut = slice(first, first + HD)
            out_ref[step, :, cut] = (average_ref[step, :, cut] * factor).astype(jnp.bfloat16)
        copies.append(pltpu.make_async_copy(out_ref.at[step], out_hbm.at[step, 0], sem.at[step]))
        copies[-1].start()
    for copy in copies:
        copy.wait()


def send(value, pairs):
    return lax.ppermute(value, "span", pairs)


def delivered(span, back):
    return {place: place - back for place in range(back, span)}


def plain_call(kernel, name, out_shape, flops, operands, in_specs=(), out_specs=None, scratch=(), limit=VMEM_LIMIT):
    nbytes = sum(math.prod(o.shape) * o.dtype.itemsize for o in operands)
    if out_specs is None:
        out_specs = [VMEM_SPEC] * len(out_shape)
    return pl.pallas_call(
        kernel,
        in_specs=list(in_specs) + [VMEM_SPEC] * (len(operands) - len(in_specs)),
        out_specs=out_specs,
        out_shape=out_shape,
        scratch_shapes=list(scratch),
        compiler_params=pltpu.CompilerParams(vmem_limit_bytes=limit),
        cost_estimate=cost(flops, nbytes),
        name=name,
    )(*operands)


def picker(shape, wanted):
    row = lax.broadcasted_iota(jnp.int32, shape, 0)
    column = lax.broadcasted_iota(jnp.int32, shape, 1)
    return jnp.where(column == wanted(row), 1.0, 0.0).astype(jnp.bfloat16)


def project_kernel(axes, x_hbm, w_hbm, *refs):
    out_refs, (x_ref, w_ref, x_sem, w_sem) = refs[:-4], refs[-4:]
    rows, depth = x_ref.shape
    share = out_refs[0].shape[0]
    x_copy = pltpu.make_async_copy(x_hbm.at[0], x_ref, x_sem)
    x_copy.start()
    copies = []
    for place, first in enumerate(range(0, depth, 2 * HD)):
        cut = slice(first, min(first + 2 * HD, depth))
        copies.append((cut, pltpu.make_async_copy(w_hbm.at[cut], w_ref.at[cut], w_sem.at[place])))
        copies[-1][1].start()
    total = jnp.zeros((rows, w_ref.shape[1]), jnp.float32)
    x_copy.wait()
    for cut, w_copy in copies:
        w_copy.wait()
        total = total + nn_dot(x_ref[:, cut], w_ref[cut])
    projected = total.astype(jnp.bfloat16)
    for offset, out_ref in enumerate(out_refs):
        first = target_of(axes, offset) * share
        chosen = picker((share, rows), lambda row: row + first)
        out_ref[...] = nn_dot(chosen, projected).astype(jnp.bfloat16)


def gather_kernel(*refs):
    hidden_ref, tail_ref = refs[-2:]
    total = refs[0][...].astype(jnp.float32)
    for ref in refs[1:-2]:
        total = total + ref[...].astype(jnp.float32)
    hidden = total.astype(jnp.bfloat16)
    hidden_ref[...] = hidden
    kept = KT - 1 + FADE
    shape = (tail_ref.shape[0], hidden.shape[0])
    chosen = picker(shape, lambda row: row // kept * FR + FR - kept + row % kept)
    tail_ref[...] = nn_dot(chosen, hidden).astype(jnp.bfloat16)


def decode_kernel(fade_ref, hidden_ref, tail_ref, conv_ref, out_ref):
    position = lax.axis_index("span")
    share = hidden_ref.shape[0]
    spatial = share // FR
    kept = KT - 1 + FADE
    wide = FADE + FR
    hidden, tail = hidden_ref[...], tail_ref[...]
    mixed = jnp.zeros((spatial * wide, out_ref.shape[2]), jnp.float32)
    for tap in range(KT):
        def from_tail(row):
            place = row % wide + KT - 1 - tap
            return jnp.where(place < kept, row // wide * kept + place, -1)

        def from_hidden(row):
            place = row % wide + KT - 1 - tap
            return jnp.where(place >= kept, row // wide * FR + place - kept, -1)

        window = nn_dot(picker((spatial * wide, tail.shape[0]), from_tail), tail)
        window = window + nn_dot(picker((spatial * wide, share), from_hidden), hidden)
        mixed = mixed + nn_dot(window.astype(jnp.bfloat16), conv_ref[tap])
    frames = (mixed * jax.nn.sigmoid(mixed)).astype(jnp.bfloat16)
    fade = fade_ref[0]
    shape = (share, spatial * wide)
    current = nn_dot(picker(shape, lambda row: row // FR * wide + FADE + row % FR), frames)

    def faded(row):
        return jnp.where(row % FR < fade, row // FR * wide + FADE - fade + row % FR, -1)

    previous = nn_dot(picker(shape, faded), frames)
    frame = lax.broadcasted_iota(jnp.int32, (share, out_ref.shape[2]), 0) % FR
    fade_float = jnp.full(frame.shape, fade, jnp.int32).astype(jnp.float32)
    weight = (frame.astype(jnp.float32) + 1.0) / (fade_float + 1.0)
    weight = jnp.where((frame < fade) & (position > 0), weight, 1.0)
    out_ref[0] = (weight * current + (1.0 - weight) * previous).astype(jnp.bfloat16)


def project(finished, w_in):
    axes = ("mp", "seq")
    parts = lax.axis_size(axes)
    _, rows, depth = finished.shape
    channels = w_in.shape[1]
    chunks = -(-depth // (2 * HD))
    return plain_call(
        functools.partial(project_kernel, axes),
        "project",
        [jax.ShapeDtypeStruct((rows // parts, channels), jnp.bfloat16)] * parts,
        2 * rows * depth * channels,
        (finished, w_in),
        [HBM_SPEC] * 2,
        scratch=[
            pltpu.VMEM((rows, depth), jnp.bfloat16),
            pltpu.VMEM((depth, channels), jnp.bfloat16),
            pltpu.SemaphoreType.DMA,
            pltpu.SemaphoreType.DMA((chunks,)),
        ],
        limit=VMEM_ALL,
    )


def gather(parts, rows):
    share, channels = parts[0].shape
    tail_rows = share // FR * (KT - 1 + FADE)
    return plain_call(
        gather_kernel,
        "gather",
        [jax.ShapeDtypeStruct((count, channels), jnp.bfloat16) for count in (share, tail_rows)],
        rows * channels,
        parts,
    )


def decode(hidden, tail, conv_w, fade_count):
    share, channels = hidden.shape
    return plain_call(
        decode_kernel,
        "decode",
        [jax.ShapeDtypeStruct((1, share, channels), jnp.bfloat16)],
        2 * share * KT * channels * channels,
        (fade_count, hidden, tail, conv_w),
        [SMEM_SPEC],
    )[0]


def per_device(
    query, noisy_kv, clean_kv, causal_mask, step_index, finished, w_in, conv_w, fade_count
):
    steps, _, rows, columns = query.shape
    heads = columns // HD
    row_count = steps * rows
    span = lax.axis_size("span")
    axes = ("mp", "seq")
    acc_shape = jax.ShapeDtypeStruct((heads, HD, row_count), jnp.float32)
    stat_shape = jax.ShapeDtypeStruct((heads, row_count), jnp.float32)
    pair_flops = 4 * row_count * rows * columns

    first_pairs = [(0, 2), (2, 3)] if span == 4 else [(c, c + 1) for c in range(span - 1)]
    near = send(clean_kv, first_pairs)
    pieces = project(finished, w_in)
    parts = [pieces[0]] + [swap(p, axes, offset + 1) for offset, p in enumerate(pieces[1:])]
    if span == 4:
        direct = send(after(clean_kv, pieces[0]), [(1, 3)])
    carry = plain_call(
        own_kernel,
        "own",
        [acc_shape, stat_shape, stat_shape],
        pair_flops,
        (step_index, query, noisy_kv),
        [SMEM_SPEC],
    )
    hidden, tail = gather(parts, rows)
    tail = hop(tail, "span", 1)
    if span == 4:
        near = after(near, carry[0], hidden)
        forwards = lax.axis_index("span") == 2
        passed = [jnp.where(forwards, near[which], clean_kv[which]) for which in range(2)]
        passed = [hop(block, "span", 1) for block in passed]
        early = [(near, {2: 0, 3: 2}), (direct, {3: 1})]
        keys, values = passed
        last_plan = {1: 0, 2: 1, 3: 0}
    else:
        ring = [near]
        for _ in range(2, span):
            ring.append(hop(ring[-1], "span", 1))
        early = [(block, delivered(span, back + 1)) for back, block in enumerate(ring[:-1])]
        keys = values = ring[-1]
        last_plan = delivered(span, span - 1)
    for block, plan in early:
        carry = plain_call(
            functools.partial(mid_kernel, plan),
            "middle",
            [acc_shape, stat_shape, stat_shape],
            pair_flops,
            (step_index, causal_mask, query, block, *carry),
            [SMEM_SPEC] * 2,
        )
    acc, weights = plain_call(
        functools.partial(score_kernel, [last_plan]),
        "score",
        [acc_shape, jax.ShapeDtypeStruct((heads, rows, row_count), jnp.bfloat16)],
        pair_flops // 2,
        (step_index, causal_mask, query, keys, *carry),
        [SMEM_SPEC] * 2,
    )
    averaged, squares = plain_call(
        functools.partial(average_kernel, [last_plan]),
        "average",
        [acc_shape, jax.ShapeDtypeStruct((lax.axis_size(axes), 1, row_count), jnp.float32)],
        pair_flops // 2,
        (acc, weights, values),
    )
    decoded = decode(after(hidden, squares), tail, conv_w, fade_count)
    parts = lax.axis_size(axes)
    shared = lax.all_to_all(squares, axes, 0, 0, tiled=True)
    turned = plain_call(
        turn_kernel,
        "turn",
        [jax.ShapeDtypeStruct((steps, rows, columns), jnp.float32)],
        row_count * columns,
        (averaged,),
    )[0]
    attended = plain_call(
        functools.partial(scale_kernel, columns * parts),
        "scale",
        jax.ShapeDtypeStruct(query.shape, jnp.bfloat16),
        row_count * columns,
        (turned, shared),
        out_specs=HBM_SPEC,
        scratch=[
            pltpu.VMEM((steps, rows, columns), jnp.bfloat16),
            pltpu.SemaphoreType.DMA((steps,)),
        ],
    )
    return (attended, decoded)


def solution(mesh):
    placed = (
        P(None, ("groups", "span"), None, ("mp", "seq")),
        P(None, None, ("groups", "span"), None, ("mp", "seq")),
        P(None, ("groups", "span"), None, ("mp", "seq")),
        P("groups", None),
        P("groups", None),
        P(("groups", "span"), None, ("mp", "seq")),
        P(("mp", "seq"), None),
        P(),
        P(("groups", "span")),
    )
    return jax.shard_map(
        per_device,
        mesh=mesh,
        in_specs=placed,
        out_specs=(
            P(None, ("groups", "span"), None, ("mp", "seq")),
            P(("groups", "span"), ("mp", "seq"), None),
        ),
        check_vma=False,
    )
```

```python
import functools
import math

import jax
import jax.numpy as jnp
from jax import lax
from jax.experimental import pallas as pl
from jax.experimental.pallas import tpu as pltpu
from jax.sharding import PartitionSpec as P

FR = 6
HD = 128
KT = 3
FADE = 2
NSTEPS = 64
LOG2E = 1.4426950408889634
VMEM_LIMIT = 24 * 1024 * 1024
VMEM_ALL = 60 * 1024 * 1024

SMEM_SPEC = pl.BlockSpec(memory_space=pltpu.SMEM)
VMEM_SPEC = pl.BlockSpec(memory_space=pltpu.VMEM)
HBM_SPEC = pl.BlockSpec(memory_space=pltpu.HBM)


def cost(flops, nbytes):
    return pl.CostEstimate(flops=flops, bytes_accessed=nbytes, transcendentals=0)


def hop(value, axis, steps):
    count = lax.axis_size(axis)
    return lax.ppermute(value, axis, [(source, source + steps) for source in range(count - steps)])


def swap(value, axes, offset):
    count = lax.axis_size(axes)
    if count & (count - 1) == 0:
        pairs = [(source, source ^ offset) for source in range(count)]
    else:
        pairs = [(source, (source + offset) % count) for source in range(count)]
    return lax.ppermute(value, axes, pairs)


def target_of(axes, offset):
    count = lax.axis_size(axes)
    mine = lax.axis_index(axes)
    if count & (count - 1) == 0:
        return mine ^ offset
    return lax.rem(mine + offset, count)


def after(value, *earlier):
    return lax.optimization_barrier((value, *earlier))[0]


def nt_dot(left, right):
    return lax.dot_general(left, right, (((1,), (1,)), ((), ())), preferred_element_type=jnp.float32)


def tn_dot(left, right):
    return lax.dot_general(left, right, (((0,), (0,)), ((), ())), preferred_element_type=jnp.float32)


def nn_dot(left, right):
    return jnp.dot(left, right, preferred_element_type=jnp.float32)


def row_factors(step_ref, position, steps, rows):
    lane = lax.broadcasted_iota(jnp.int32, (1, steps * rows), 1)
    index = jnp.full(lane.shape, step_ref[position, 0], jnp.int32)
    for step in range(1, steps):
        index = jnp.where(lane >= step * rows, step_ref[position, step], index)
    fraction = 1.0 - index.astype(jnp.float32) / NSTEPS
    level = 3.0 * fraction / (1.0 + 2.0 * fraction)
    return (0.5 + level) * (LOG2E / math.sqrt(HD))


def lane_windows(steps, rows):
    total = steps * rows
    return [
        (step * rows // HD * HD, min(total, -(-(step + 1) * rows // HD) * HD))
        for step in range(steps)
    ]


def join_steps(pieces, windows, rows):
    total = windows[-1][1]
    tiles = []
    for first in range(0, total, HD):
        stop = min(first + HD, total)
        tile = None
        for step, (begin, end) in enumerate(windows):
            if begin <= first and stop <= end and step * rows < stop and first < (step + 1) * rows:
                part = pieces[step][:, first - begin : stop - begin]
                if tile is None:
                    tile = part
                else:
                    lane = lax.broadcasted_iota(jnp.int32, part.shape, 1) + first
                    tile = jnp.where(lane >= step * rows, part, tile)
        tiles.append(tile)
    return jnp.concatenate(tiles, 1)


def own_kernel(step_ref, q_ref, kv_ref, acc_ref, top_ref, total_ref):
    position = lax.axis_index("span")
    steps, _, rows, columns = q_ref.shape
    factors = row_factors(step_ref, position, steps, rows)
    windows = lane_windows(steps, rows)
    for head in range(columns // HD):
        cut = slice(head * HD, (head + 1) * HD)
        queries = q_ref[:, 0, :, cut].reshape(steps * rows, HD)
        scores = join_steps(
            [nt_dot(kv_ref[s, 0, 0, :, cut], queries[a:b]) for s, (a, b) in enumerate(windows)],
            windows,
            rows,
        )
        scores = scores * factors
        top = jnp.max(scores, axis=0, keepdims=True)
        weights = jnp.exp2(scores - top)
        rounded = weights.astype(jnp.bfloat16)
        acc_ref[head] = join_steps(
            [tn_dot(kv_ref[s, 1, 0, :, cut], rounded[:, a:b]) for s, (a, b) in enumerate(windows)],
            windows,
            rows,
        )
        top_ref[head : head + 1] = top
        total_ref[head : head + 1] = jnp.sum(weights, axis=0, keepdims=True)


def absorb(queries, keys, values, factors, acc, top, total):
    scores = nt_dot(keys, queries) * factors
    newest = jnp.maximum(top, jnp.max(scores, axis=0, keepdims=True))
    weights = jnp.exp2(scores - newest)
    shrink = jnp.exp2(top - newest)
    total = total * shrink + jnp.sum(weights, axis=0, keepdims=True)
    acc = acc * shrink + tn_dot(values, weights.astype(jnp.bfloat16))
    return acc, newest, total


def visible(mask_ref, position, blocks):
    seen = False
    for place, block in blocks.items():
        seen = seen | ((position == place) & (mask_ref[place, block] > 0))
    return seen


def half(ref, which, cut):
    return ref[which, 0, :, cut] if len(ref.shape) == 4 else ref[0, :, cut]


def mid_kernel(plan, step_ref, mask_ref, q_ref, *refs):
    block_refs, (acc_in, top_in, total_in, acc_ref, top_ref, total_ref) = refs[:-6], refs[-6:]
    position = lax.axis_index("span")
    steps, _, rows, columns = q_ref.shape
    seen = visible(mask_ref, position, plan)

    @pl.when(seen)
    def _():
        factors = row_factors(step_ref, position, steps, rows)
        for head in range(columns // HD):
            cut = slice(head * HD, (head + 1) * HD)
            queries = q_ref[:, 0, :, cut].reshape(steps * rows, HD)
            acc, top, total = absorb(
                queries,
                half(block_refs[0], 0, cut),
                half(block_refs[-1], 1, cut),
                factors,
                acc_in[head],
                top_in[head : head + 1],
                total_in[head : head + 1],
            )
            acc_ref[head] = acc
            top_ref[head : head + 1] = top
            total_ref[head : head + 1] = total

    @pl.when(jnp.logical_not(seen))
    def _():
        acc_ref[...] = acc_in[...]
        top_ref[...] = top_in[...]
        total_ref[...] = total_in[...]


def score_kernel(plans, step_ref, mask_ref, q_ref, *refs):
    key_refs, (acc_in, top_in, total_in, acc_ref, w_ref) = refs[:-5], refs[-5:]
    position = lax.axis_index("span")
    steps, _, rows, columns = q_ref.shape

    def finish(key_ref):
        factors = row_factors(step_ref, position, steps, rows)
        for head in range(columns // HD):
            cut = slice(head * HD, (head + 1) * HD)
            queries = q_ref[:, 0, :, cut].reshape(steps * rows, HD)
            scores = nt_dot(half(key_ref, 0, cut), queries) * factors
            top = top_in[head : head + 1]
            newest = jnp.maximum(top, jnp.max(scores, axis=0, keepdims=True))
            weights = jnp.exp2(scores - newest)
            shrink = jnp.exp2(top - newest)
            total = total_in[head : head + 1] * shrink + jnp.sum(weights, axis=0, keepdims=True)
            inverse = 1.0 / total
            w_ref[head] = (weights * inverse).astype(jnp.bfloat16)
            acc_ref[head] = acc_in[head] * (shrink * inverse)

    rest = True
    for plan, key_ref in zip(plans, key_refs):
        seen = visible(mask_ref, position, plan)
        rest = jnp.logical_and(rest, jnp.logical_not(seen))
        pl.when(seen)(functools.partial(finish, key_ref))

    @pl.when(rest)
    def _():
        w_ref[...] = jnp.zeros_like(w_ref)
        for head in range(columns // HD):
            acc_ref[head] = acc_in[head] * (1.0 / total_in[head : head + 1])


def average_kernel(plans, acc_ref, w_ref, *refs):
    value_refs, (average_ref, square_ref) = refs[:-2], refs[-2:]
    position = lax.axis_index("span")

    def finish(value_ref):
        squares = jnp.zeros(square_ref.shape, jnp.float32)
        for head in range(acc_ref.shape[0]):
            average = acc_ref[head]
            if value_ref is not None:
                values = half(value_ref, 1, slice(head * HD, (head + 1) * HD))
                average = average + tn_dot(values, w_ref[head])
            average_ref[head] = average
            squares = squares + jnp.sum(average * average, axis=0, keepdims=True)
        square_ref[...] = squares

    rest = True
    for plan, value_ref in zip(plans, value_refs):
        here = functools.reduce(jnp.logical_or, [position == place for place in plan])
        rest = jnp.logical_and(rest, jnp.logical_not(here))
        pl.when(here)(functools.partial(finish, value_ref))
    pl.when(rest)(functools.partial(finish, None))


def turn_kernel(in_ref, out_ref):
    heads = in_ref.shape[0]
    steps, rows, _ = out_ref.shape
    for head in range(heads):
        out_ref[:, :, head * HD : (head + 1) * HD] = in_ref[head].T.reshape(steps, rows, HD)


def scale_kernel(width, average_ref, *refs):
    part_refs, (out_hbm, out_ref, sem) = refs[:-3], refs[-3:]
    total = part_refs[0][...]
    for ref in part_refs[1:]:
        total = total + ref[...]
    inverse = lax.rsqrt(total / width + 1e-06)
    steps, rows, columns = average_ref.shape
    spread = jnp.broadcast_to(inverse, (HD, steps * rows)).T
    copies = []
    for step in range(steps):
        factor = spread[step * rows : (step + 1) * rows]
        for first in range(0, columns, HD):
            cut = slice(first, first + HD)
            out_ref[step, :, cut] = (average_ref[step, :, cut] * factor).astype(jnp.bfloat16)
        copies.append(pltpu.make_async_copy(out_ref.at[step], out_hbm.at[step, 0], sem.at[step]))
        copies[-1].start()
    for copy in copies:
        copy.wait()


def send(value, pairs):
    return lax.ppermute(value, "span", pairs)


def delivered(span, back):
    return {place: place - back for place in range(back, span)}


def plain_call(kernel, name, out_shape, flops, operands, in_specs=(), out_specs=None, scratch=(), limit=VMEM_LIMIT):
    nbytes = sum(math.prod(o.shape) * o.dtype.itemsize for o in operands)
    if out_specs is None:
        out_specs = [VMEM_SPEC] * len(out_shape)
    return pl.pallas_call(
        kernel,
        in_specs=list(in_specs) + [VMEM_SPEC] * (len(operands) - len(in_specs)),
        out_specs=out_specs,
        out_shape=out_shape,
        scratch_shapes=list(scratch),
        compiler_params=pltpu.CompilerParams(vmem_limit_bytes=limit),
        cost_estimate=cost(flops, nbytes),
        name=name,
    )(*operands)


def picker(shape, wanted):
    row = lax.broadcasted_iota(jnp.int32, shape, 0)
    column = lax.broadcasted_iota(jnp.int32, shape, 1)
    return jnp.where(column == wanted(row), 1.0, 0.0).astype(jnp.bfloat16)


def project_kernel(axes, x_hbm, w_hbm, *refs):
    out_refs, (x_ref, w_ref, x_sem, w_sem) = refs[:-4], refs[-4:]
    rows, depth = x_ref.shape
    share = out_refs[0].shape[0]
    x_copy = pltpu.make_async_copy(x_hbm.at[0], x_ref, x_sem)
    x_copy.start()
    copies = []
    for place, first in enumerate(range(0, depth, 2 * HD)):
        cut = slice(first, min(first + 2 * HD, depth))
        copies.append((cut, pltpu.make_async_copy(w_hbm.at[cut], w_ref.at[cut], w_sem.at[place])))
        copies[-1][1].start()
    total = jnp.zeros((rows, w_ref.shape[1]), jnp.float32)
    x_copy.wait()
    for cut, w_copy in copies:
        w_copy.wait()
        total = total + nn_dot(x_ref[:, cut], w_ref[cut])
    projected = total.astype(jnp.bfloat16)
    for offset, out_ref in enumerate(out_refs):
        first = target_of(axes, offset) * share
        chosen = picker((share, rows), lambda row: row + first)
        out_ref[...] = nn_dot(chosen, projected).astype(jnp.bfloat16)


def gather_kernel(*refs):
    hidden_ref, tail_ref = refs[-2:]
    total = refs[0][...].astype(jnp.float32)
    for ref in refs[1:-2]:
        total = total + ref[...].astype(jnp.float32)
    hidden = total.astype(jnp.bfloat16)
    hidden_ref[...] = hidden
    kept = KT - 1 + FADE
    shape = (tail_ref.shape[0], hidden.shape[0])
    chosen = picker(shape, lambda row: row // kept * FR + FR - kept + row % kept)
    tail_ref[...] = nn_dot(chosen, hidden).astype(jnp.bfloat16)


def decode_kernel(fade_ref, hidden_ref, tail_ref, conv_ref, out_ref):
    position = lax.axis_index("span")
    share = hidden_ref.shape[0]
    spatial = share // FR
    kept = KT - 1 + FADE
    wide = FADE + FR
    hidden, tail = hidden_ref[...], tail_ref[...]
    mixed = jnp.zeros((spatial * wide, out_ref.shape[2]), jnp.float32)
    for tap in range(KT):
        def from_tail(row):
            place = row % wide + KT - 1 - tap
            return jnp.where(place < kept, row // wide * kept + place, -1)

        def from_hidden(row):
            place = row % wide + KT - 1 - tap
            return jnp.where(place >= kept, row // wide * FR + place - kept, -1)

        window = nn_dot(picker((spatial * wide, tail.shape[0]), from_tail), tail)
        window = window + nn_dot(picker((spatial * wide, share), from_hidden), hidden)
        mixed = mixed + nn_dot(window.astype(jnp.bfloat16), conv_ref[tap])
    frames = (mixed * jax.nn.sigmoid(mixed)).astype(jnp.bfloat16)
    fade = fade_ref[0]
    shape = (share, spatial * wide)
    current = nn_dot(picker(shape, lambda row: row // FR * wide + FADE + row % FR), frames)

    def faded(row):
        return jnp.where(row % FR < fade, row // FR * wide + FADE - fade + row % FR, -1)

    previous = nn_dot(picker(shape, faded), frames)
    frame = lax.broadcasted_iota(jnp.int32, (share, out_ref.shape[2]), 0) % FR
    fade_float = jnp.full(frame.shape, fade, jnp.int32).astype(jnp.float32)
    weight = (frame.astype(jnp.float32) + 1.0) / (fade_float + 1.0)
    weight = jnp.where((frame < fade) & (position > 0), weight, 1.0)
    out_ref[0] = (weight * current + (1.0 - weight) * previous).astype(jnp.bfloat16)


def project(finished, w_in):
    axes = ("mp", "seq")
    parts = lax.axis_size(axes)
    _, rows, depth = finished.shape
    channels = w_in.shape[1]
    chunks = -(-depth // (2 * HD))
    return plain_call(
        functools.partial(project_kernel, axes),
        "project",
        [jax.ShapeDtypeStruct((rows // parts, channels), jnp.bfloat16)] * parts,
        2 * rows * depth * channels,
        (finished, w_in),
        [HBM_SPEC] * 2,
        scratch=[
            pltpu.VMEM((rows, depth), jnp.bfloat16),
            pltpu.VMEM((depth, channels), jnp.bfloat16),
            pltpu.SemaphoreType.DMA,
            pltpu.SemaphoreType.DMA((chunks,)),
        ],
        limit=VMEM_ALL,
    )


def gather(parts, rows):
    share, channels = parts[0].shape
    tail_rows = share // FR * (KT - 1 + FADE)
    return plain_call(
        gather_kernel,
        "gather",
        [jax.ShapeDtypeStruct((count, channels), jnp.bfloat16) for count in (share, tail_rows)],
        rows * channels,
        parts,
    )


def decode(hidden, tail, conv_w, fade_count):
    share, channels = hidden.shape
    return plain_call(
        decode_kernel,
        "decode",
        [jax.ShapeDtypeStruct((1, share, channels), jnp.bfloat16)],
        2 * share * KT * channels * channels,
        (fade_count, hidden, tail, conv_w),
        [SMEM_SPEC],
    )[0]


def per_device(
    query, noisy_kv, clean_kv, causal_mask, step_index, finished, w_in, conv_w, fade_count
):
    steps, _, rows, columns = query.shape
    heads = columns // HD
    row_count = steps * rows
    span = lax.axis_size("span")
    axes = ("mp", "seq")
    acc_shape = jax.ShapeDtypeStruct((heads, HD, row_count), jnp.float32)
    stat_shape = jax.ShapeDtypeStruct((heads, row_count), jnp.float32)
    pair_flops = 4 * row_count * rows * columns

    first_pairs = [(0, 2), (2, 3)] if span == 4 else [(c, c + 1) for c in range(span - 1)]
    near = send(clean_kv, first_pairs)
    pieces = project(finished, w_in)
    parts = [pieces[0]] + [swap(p, axes, offset + 1) for offset, p in enumerate(pieces[1:])]
    if span == 4:
        direct = send(after(clean_kv, pieces[0]), [(1, 3)])
    carry = plain_call(
        own_kernel,
        "own",
        [acc_shape, stat_shape, stat_shape],
        pair_flops,
        (step_index, query, noisy_kv),
        [SMEM_SPEC],
    )
    hidden, tail = gather(parts, rows)
    tail = hop(tail, "span", 1)
    if span == 4:
        near = after(near, carry[0], hidden)
        forwards = lax.axis_index("span") == 2
        passed = [jnp.where(forwards, near[which], clean_kv[which]) for which in range(2)]
        passed = [hop(block, "span", 1) for block in passed]
        early = [(near, {2: 0, 3: 2}), (direct, {3: 1})]
        keys, values = passed
        last_plan = {1: 0, 2: 1, 3: 0}
    else:
        ring = [near]
        for _ in range(2, span):
            ring.append(hop(ring[-1], "span", 1))
        early = [(block, delivered(span, back + 1)) for back, block in enumerate(ring[:-1])]
        keys = values = ring[-1]
        last_plan = delivered(span, span - 1)
    for block, plan in early:
        carry = plain_call(
            functools.partial(mid_kernel, plan),
            "middle",
            [acc_shape, stat_shape, stat_shape],
            pair_flops,
            (step_index, causal_mask, query, block, *carry),
            [SMEM_SPEC] * 2,
        )
    acc, weights = plain_call(
        functools.partial(score_kernel, [last_plan]),
        "score",
        [acc_shape, jax.ShapeDtypeStruct((heads, rows, row_count), jnp.bfloat16)],
        pair_flops // 2,
        (step_index, causal_mask, query, keys, *carry),
        [SMEM_SPEC] * 2,
    )
    averaged, squares = plain_call(
        functools.partial(average_kernel, [last_plan]),
        "average",
        [acc_shape, jax.ShapeDtypeStruct((1, row_count), jnp.float32)],
        pair_flops // 2,
        (acc, weights, values),
    )
    decoded = decode(after(hidden, squares), tail, conv_w, fade_count)
    others = [swap(squares, axes, offset) for offset in range(1, lax.axis_size(axes))]
    turned = plain_call(
        turn_kernel,
        "turn",
        [jax.ShapeDtypeStruct((steps, rows, columns), jnp.float32)],
        row_count * columns,
        (averaged,),
    )[0]
    attended = plain_call(
        functools.partial(scale_kernel, columns * lax.axis_size(axes)),
        "scale",
        jax.ShapeDtypeStruct(query.shape, jnp.bfloat16),
        row_count * columns,
        (turned, squares, *others),
        out_specs=HBM_SPEC,
        scratch=[
            pltpu.VMEM((steps, rows, columns), jnp.bfloat16),
            pltpu.SemaphoreType.DMA((steps,)),
        ],
    )
    return (attended, decoded)


def solution(mesh):
    placed = (
        P(None, ("groups", "span"), None, ("mp", "seq")),
        P(None, None, ("groups", "span"), None, ("mp", "seq")),
        P(None, ("groups", "span"), None, ("mp", "seq")),
        P("groups", None),
        P("groups", None),
        P(("groups", "span"), None, ("mp", "seq")),
        P(("mp", "seq"), None),
        P(),
        P(("groups", "span")),
    )
    return jax.shard_map(
        per_device,
        mesh=mesh,
        in_specs=placed,
        out_specs=(
            P(None, ("groups", "span"), None, ("mp", "seq")),
            P(("groups", "span"), ("mp", "seq"), None),
        ),
        check_vma=False,
    )
```

```python
import functools
import math

import jax
import jax.numpy as jnp
from jax import lax
from jax.experimental import pallas as pl
from jax.experimental.pallas import tpu as pltpu
from jax.sharding import PartitionSpec as P

FR = 6
HD = 128
KT = 3
FADE = 2
NSTEPS = 64
LOG2E = 1.4426950408889634
VMEM_LIMIT = 24 * 1024 * 1024
VMEM_ALL = 60 * 1024 * 1024

SMEM_SPEC = pl.BlockSpec(memory_space=pltpu.SMEM)
VMEM_SPEC = pl.BlockSpec(memory_space=pltpu.VMEM)
HBM_SPEC = pl.BlockSpec(memory_space=pltpu.HBM)


def cost(flops, nbytes):
    return pl.CostEstimate(flops=flops, bytes_accessed=nbytes, transcendentals=0)


def hop(value, axis, steps):
    count = lax.axis_size(axis)
    return lax.ppermute(value, axis, [(source, source + steps) for source in range(count - steps)])


def swap(value, axes, offset):
    count = lax.axis_size(axes)
    if count & (count - 1) == 0:
        pairs = [(source, source ^ offset) for source in range(count)]
    else:
        pairs = [(source, (source + offset) % count) for source in range(count)]
    return lax.ppermute(value, axes, pairs)


def target_of(axes, offset):
    count = lax.axis_size(axes)
    mine = lax.axis_index(axes)
    if count & (count - 1) == 0:
        return mine ^ offset
    return lax.rem(mine + offset, count)


def after(value, *earlier):
    return lax.optimization_barrier((value, *earlier))[0]


def nt_dot(left, right):
    return lax.dot_general(left, right, (((1,), (1,)), ((), ())), preferred_element_type=jnp.float32)


def tn_dot(left, right):
    return lax.dot_general(left, right, (((0,), (0,)), ((), ())), preferred_element_type=jnp.float32)


def nn_dot(left, right):
    return jnp.dot(left, right, preferred_element_type=jnp.float32)


def row_factors(step_ref, position, steps, rows):
    lane = lax.broadcasted_iota(jnp.int32, (1, steps * rows), 1)
    index = jnp.full(lane.shape, step_ref[position, 0], jnp.int32)
    for step in range(1, steps):
        index = jnp.where(lane >= step * rows, step_ref[position, step], index)
    fraction = 1.0 - index.astype(jnp.float32) / NSTEPS
    level = 3.0 * fraction / (1.0 + 2.0 * fraction)
    return (0.5 + level) * (LOG2E / math.sqrt(HD))


def lane_windows(steps, rows):
    total = steps * rows
    return [
        (step * rows // HD * HD, min(total, -(-(step + 1) * rows // HD) * HD))
        for step in range(steps)
    ]


def join_steps(pieces, windows, rows):
    total = windows[-1][1]
    tiles = []
    for first in range(0, total, HD):
        stop = min(first + HD, total)
        tile = None
        for step, (begin, end) in enumerate(windows):
            if begin <= first and stop <= end and step * rows < stop and first < (step + 1) * rows:
                part = pieces[step][:, first - begin : stop - begin]
                if tile is None:
                    tile = part
                else:
                    lane = lax.broadcasted_iota(jnp.int32, part.shape, 1) + first
                    tile = jnp.where(lane >= step * rows, part, tile)
        tiles.append(tile)
    return jnp.concatenate(tiles, 1)


def own_kernel(step_ref, q_ref, kv_ref, acc_ref, top_ref, total_ref):
    position = lax.axis_index("span")
    steps, _, rows, columns = q_ref.shape
    factors = row_factors(step_ref, position, steps, rows)
    windows = lane_windows(steps, rows)
    for head in range(columns // HD):
        cut = slice(head * HD, (head + 1) * HD)
        queries = q_ref[:, 0, :, cut].reshape(steps * rows, HD)
        scores = join_steps(
            [nt_dot(kv_ref[s, 0, 0, :, cut], queries[a:b]) for s, (a, b) in enumerate(windows)],
            windows,
            rows,
        )
        scores = scores * factors
        top = jnp.max(scores, axis=0, keepdims=True)
        weights = jnp.exp2(scores - top)
        rounded = weights.astype(jnp.bfloat16)
        acc_ref[head] = join_steps(
            [tn_dot(kv_ref[s, 1, 0, :, cut], rounded[:, a:b]) for s, (a, b) in enumerate(windows)],
            windows,
            rows,
        )
        top_ref[head : head + 1] = top
        total_ref[head : head + 1] = jnp.sum(weights, axis=0, keepdims=True)


def absorb(queries, keys, values, factors, acc, top, total):
    scores = nt_dot(keys, queries) * factors
    newest = jnp.maximum(top, jnp.max(scores, axis=0, keepdims=True))
    weights = jnp.exp2(scores - newest)
    shrink = jnp.exp2(top - newest)
    total = total * shrink + jnp.sum(weights, axis=0, keepdims=True)
    acc = acc * shrink + tn_dot(values, weights.astype(jnp.bfloat16))
    return acc, newest, total


def visible(mask_ref, position, blocks):
    seen = False
    for place, block in blocks.items():
        seen = seen | ((position == place) & (mask_ref[place, block] > 0))
    return seen


def half(ref, which, cut):
    return ref[which, 0, :, cut] if len(ref.shape) == 4 else ref[0, :, cut]


def mid_kernel(plan, step_ref, mask_ref, q_ref, *refs):
    block_refs, (acc_in, top_in, total_in, acc_ref, top_ref, total_ref) = refs[:-6], refs[-6:]
    position = lax.axis_index("span")
    steps, _, rows, columns = q_ref.shape
    seen = visible(mask_ref, position, plan)

    @pl.when(seen)
    def _():
        factors = row_factors(step_ref, position, steps, rows)
        for head in range(columns // HD):
            cut = slice(head * HD, (head + 1) * HD)
            queries = q_ref[:, 0, :, cut].reshape(steps * rows, HD)
            acc, top, total = absorb(
                queries,
                half(block_refs[0], 0, cut),
                half(block_refs[-1], 1, cut),
                factors,
                acc_in[head],
                top_in[head : head + 1],
                total_in[head : head + 1],
            )
            acc_ref[head] = acc
            top_ref[head : head + 1] = top
            total_ref[head : head + 1] = total

    @pl.when(jnp.logical_not(seen))
    def _():
        acc_ref[...] = acc_in[...]
        top_ref[...] = top_in[...]
        total_ref[...] = total_in[...]


def score_kernel(plans, step_ref, mask_ref, q_ref, *refs):
    key_refs, (acc_in, top_in, total_in, acc_ref, w_ref) = refs[:-5], refs[-5:]
    position = lax.axis_index("span")
    steps, _, rows, columns = q_ref.shape

    def finish(key_ref):
        factors = row_factors(step_ref, position, steps, rows)
        for head in range(columns // HD):
            cut = slice(head * HD, (head + 1) * HD)
            queries = q_ref[:, 0, :, cut].reshape(steps * rows, HD)
            scores = nt_dot(half(key_ref, 0, cut), queries) * factors
            top = top_in[head : head + 1]
            newest = jnp.maximum(top, jnp.max(scores, axis=0, keepdims=True))
            weights = jnp.exp2(scores - newest)
            shrink = jnp.exp2(top - newest)
            total = total_in[head : head + 1] * shrink + jnp.sum(weights, axis=0, keepdims=True)
            inverse = 1.0 / total
            w_ref[head] = (weights * inverse).astype(jnp.bfloat16)
            acc_ref[head] = acc_in[head] * (shrink * inverse)

    rest = True
    for plan, key_ref in zip(plans, key_refs):
        seen = visible(mask_ref, position, plan)
        rest = jnp.logical_and(rest, jnp.logical_not(seen))
        pl.when(seen)(functools.partial(finish, key_ref))

    @pl.when(rest)
    def _():
        w_ref[...] = jnp.zeros_like(w_ref)
        for head in range(columns // HD):
            acc_ref[head] = acc_in[head] * (1.0 / total_in[head : head + 1])


def average_head(head, acc_ref, w_ref, value_ref, first):
    if value_ref.shape[-1] == acc_ref.shape[0] * HD:
        first = 0
    cut = slice((head - first) * HD, (head - first + 1) * HD)
    return acc_ref[head] + tn_dot(half(value_ref, 1, cut), w_ref[head])


def average_kernel(begin, end, acc_ref, w_ref, value_ref, average_ref, square_ref):
    squares = jnp.zeros(square_ref.shape, jnp.float32)
    for head in range(begin, end):
        average = average_head(head, acc_ref, w_ref, value_ref, begin)
        squares = squares + jnp.sum(average * average, axis=0, keepdims=True)
        average_ref[:, :, (head - begin) * HD : (head - begin + 1) * HD] = average.T.reshape(
            average_ref.shape[:2] + (HD,)
        )
    square_ref[...] = squares


def rest_kernel(begin, end, acc_ref, w_ref, value_ref, before_ref, average_ref, square_ref):
    squares = before_ref[...]
    for head in range(begin, end):
        average = average_head(head, acc_ref, w_ref, value_ref, begin)
        squares = squares + jnp.sum(average * average, axis=0, keepdims=True)
        average_ref[head - begin] = average
    square_ref[...] = squares


def turn_kernel(in_ref, square_in, out_ref, square_ref):
    steps, rows, _ = out_ref.shape
    for head in range(in_ref.shape[0]):
        out_ref[:, :, head * HD : (head + 1) * HD] = in_ref[head].T.reshape(steps, rows, HD)
    square_ref[...] = square_in[...]


def scale_kernel(width, front_ref, back_ref, *refs):
    part_refs, (out_hbm, out_ref, sem) = refs[:-3], refs[-3:]
    total = part_refs[0][...]
    for ref in part_refs[1:]:
        total = total + ref[...]
    inverse = lax.rsqrt(total / width + 1e-06)
    steps, rows, columns = out_ref.shape
    spread = jnp.broadcast_to(inverse, (HD, steps * rows)).T
    copies = []
    for step in range(steps):
        factor = spread[step * rows : (step + 1) * rows]
        place = 0
        for ref in (front_ref, back_ref):
            for first in range(0, ref.shape[2], HD):
                average = ref[step, :, first : first + HD]
                out_ref[step, :, place : place + HD] = (average * factor).astype(jnp.bfloat16)
                place += HD
        copies.append(pltpu.make_async_copy(out_ref.at[step], out_hbm.at[step, 0], sem.at[step]))
        copies[-1].start()
    for copy in copies:
        copy.wait()


def send(value, pairs):
    return lax.ppermute(value, "span", pairs)


def delivered(span, back):
    return {place: place - back for place in range(back, span)}


def plain_call(kernel, name, out_shape, flops, operands, in_specs=(), out_specs=None, scratch=(), limit=VMEM_LIMIT):
    nbytes = sum(math.prod(o.shape) * o.dtype.itemsize for o in operands)
    if out_specs is None:
        out_specs = [VMEM_SPEC] * len(out_shape)
    return pl.pallas_call(
        kernel,
        in_specs=list(in_specs) + [VMEM_SPEC] * (len(operands) - len(in_specs)),
        out_specs=out_specs,
        out_shape=out_shape,
        scratch_shapes=list(scratch),
        compiler_params=pltpu.CompilerParams(vmem_limit_bytes=limit),
        cost_estimate=cost(flops, nbytes),
        name=name,
    )(*operands)


def picker(shape, wanted):
    row = lax.broadcasted_iota(jnp.int32, shape, 0)
    column = lax.broadcasted_iota(jnp.int32, shape, 1)
    return jnp.where(column == wanted(row), 1.0, 0.0).astype(jnp.bfloat16)


def project_kernel(axes, x_hbm, w_hbm, *refs):
    out_refs, (x_ref, w_ref, x_sem, w_sem) = refs[:-4], refs[-4:]
    rows, depth = x_ref.shape
    share = out_refs[0].shape[0]
    x_copy = pltpu.make_async_copy(x_hbm.at[0], x_ref, x_sem)
    x_copy.start()
    copies = []
    for place, first in enumerate(range(0, depth, 2 * HD)):
        cut = slice(first, min(first + 2 * HD, depth))
        copies.append((cut, pltpu.make_async_copy(w_hbm.at[cut], w_ref.at[cut], w_sem.at[place])))
        copies[-1][1].start()
    total = jnp.zeros((rows, w_ref.shape[1]), jnp.float32)
    x_copy.wait()
    for cut, w_copy in copies:
        w_copy.wait()
        total = total + nn_dot(x_ref[:, cut], w_ref[cut])
    projected = total.astype(jnp.bfloat16)
    for offset, out_ref in enumerate(out_refs):
        first = target_of(axes, offset) * share
        chosen = picker((share, rows), lambda row: row + first)
        out_ref[...] = nn_dot(chosen, projected).astype(jnp.bfloat16)


def gather_kernel(*refs):
    hidden_ref, tail_ref = refs[-2:]
    total = refs[0][...].astype(jnp.float32)
    for ref in refs[1:-2]:
        total = total + ref[...].astype(jnp.float32)
    hidden = total.astype(jnp.bfloat16)
    hidden_ref[...] = hidden
    kept = KT - 1 + FADE
    shape = (tail_ref.shape[0], hidden.shape[0])
    chosen = picker(shape, lambda row: row // kept * FR + FR - kept + row % kept)
    tail_ref[...] = nn_dot(chosen, hidden).astype(jnp.bfloat16)


def decode_kernel(fade_ref, hidden_ref, tail_ref, conv_ref, out_ref):
    position = lax.axis_index("span")
    share = hidden_ref.shape[0]
    spatial = share // FR
    kept = KT - 1 + FADE
    wide = FADE + FR
    hidden, tail = hidden_ref[...], tail_ref[...]
    mixed = jnp.zeros((spatial * wide, out_ref.shape[2]), jnp.float32)
    for tap in range(KT):
        def from_tail(row):
            place = row % wide + KT - 1 - tap
            return jnp.where(place < kept, row // wide * kept + place, -1)

        def from_hidden(row):
            place = row % wide + KT - 1 - tap
            return jnp.where(place >= kept, row // wide * FR + place - kept, -1)

        window = nn_dot(picker((spatial * wide, tail.shape[0]), from_tail), tail)
        window = window + nn_dot(picker((spatial * wide, share), from_hidden), hidden)
        mixed = mixed + nn_dot(window.astype(jnp.bfloat16), conv_ref[tap])
    frames = (mixed * jax.nn.sigmoid(mixed)).astype(jnp.bfloat16)
    fade = fade_ref[0]
    shape = (share, spatial * wide)
    current = nn_dot(picker(shape, lambda row: row // FR * wide + FADE + row % FR), frames)

    def faded(row):
        return jnp.where(row % FR < fade, row // FR * wide + FADE - fade + row % FR, -1)

    previous = nn_dot(picker(shape, faded), frames)
    frame = lax.broadcasted_iota(jnp.int32, (share, out_ref.shape[2]), 0) % FR
    fade_float = jnp.full(frame.shape, fade, jnp.int32).astype(jnp.float32)
    weight = (frame.astype(jnp.float32) + 1.0) / (fade_float + 1.0)
    weight = jnp.where((frame < fade) & (position > 0), weight, 1.0)
    out_ref[0] = (weight * current + (1.0 - weight) * previous).astype(jnp.bfloat16)


def project(finished, w_in):
    axes = ("mp", "seq")
    parts = lax.axis_size(axes)
    _, rows, depth = finished.shape
    channels = w_in.shape[1]
    chunks = -(-depth // (2 * HD))
    return plain_call(
        functools.partial(project_kernel, axes),
        "project",
        [jax.ShapeDtypeStruct((rows // parts, channels), jnp.bfloat16)] * parts,
        2 * rows * depth * channels,
        (finished, w_in),
        [HBM_SPEC] * 2,
        scratch=[
            pltpu.VMEM((rows, depth), jnp.bfloat16),
            pltpu.VMEM((depth, channels), jnp.bfloat16),
            pltpu.SemaphoreType.DMA,
            pltpu.SemaphoreType.DMA((chunks,)),
        ],
        limit=VMEM_ALL,
    )


def gather(parts, rows):
    share, channels = parts[0].shape
    tail_rows = share // FR * (KT - 1 + FADE)
    return plain_call(
        gather_kernel,
        "gather",
        [jax.ShapeDtypeStruct((count, channels), jnp.bfloat16) for count in (share, tail_rows)],
        rows * channels,
        parts,
    )


def decode(hidden, tail, conv_w, fade_count):
    share, channels = hidden.shape
    return plain_call(
        decode_kernel,
        "decode",
        [jax.ShapeDtypeStruct((1, share, channels), jnp.bfloat16)],
        2 * share * KT * channels * channels,
        (fade_count, hidden, tail, conv_w),
        [SMEM_SPEC],
    )[0]


def per_device(
    query, noisy_kv, clean_kv, causal_mask, step_index, finished, w_in, conv_w, fade_count
):
    steps, _, rows, columns = query.shape
    heads = columns // HD
    middle = (heads + 1) // 2 * HD
    row_count = steps * rows
    span = lax.axis_size("span")
    axes = ("mp", "seq")
    acc_shape = jax.ShapeDtypeStruct((heads, HD, row_count), jnp.float32)
    stat_shape = jax.ShapeDtypeStruct((heads, row_count), jnp.float32)
    pair_flops = 4 * row_count * rows * columns

    first_pairs = [(0, 2), (2, 3)] if span == 4 else [(c, c + 1) for c in range(span - 1)]
    near = send(clean_kv, first_pairs)
    pieces = project(finished, w_in)
    parts = [pieces[0]] + [swap(p, axes, offset + 1) for offset, p in enumerate(pieces[1:])]
    if span == 4:
        direct = send(after(clean_kv, pieces[0]), [(1, 3)])
    carry = plain_call(
        own_kernel,
        "own",
        [acc_shape, stat_shape, stat_shape],
        pair_flops,
        (step_index, query, noisy_kv),
        [SMEM_SPEC],
    )
    hidden, tail = gather(parts, rows)
    tail = hop(tail, "span", 1)
    if span == 4:
        near = after(near, carry[0], hidden)
        forwards = lax.axis_index("span") == 2
        passed = [jnp.where(forwards, near[which], clean_kv[which]) for which in range(2)]
        passed = [passed[0], passed[1][:, :, :middle], passed[1][:, :, middle:]]
        passed = [hop(block, "span", 1) for block in passed]
        early = [(near, {2: 0, 3: 2}), (direct, {3: 1})]
        keys, *values = passed
        last_plan = {1: 0, 2: 1, 3: 0}
    else:
        ring = [near]
        for _ in range(2, span):
            ring.append(hop(ring[-1], "span", 1))
        early = [(block, delivered(span, back + 1)) for back, block in enumerate(ring[:-1])]
        keys, values = ring[-1], ring[-1:] * 2
        last_plan = delivered(span, span - 1)
    for block, plan in early:
        carry = plain_call(
            functools.partial(mid_kernel, plan),
            "middle",
            [acc_shape, stat_shape, stat_shape],
            pair_flops,
            (step_index, causal_mask, query, block, *carry),
            [SMEM_SPEC] * 2,
        )
    acc, weights = plain_call(
        functools.partial(score_kernel, [last_plan]),
        "score",
        [acc_shape, jax.ShapeDtypeStruct((heads, rows, row_count), jnp.bfloat16)],
        pair_flops // 2,
        (step_index, causal_mask, query, keys, *carry),
        [SMEM_SPEC] * 2,
    )
    square_shape = jax.ShapeDtypeStruct((1, row_count), jnp.float32)
    front, squares = plain_call(
        functools.partial(average_kernel, 0, middle // HD),
        "average",
        [jax.ShapeDtypeStruct((steps, rows, middle), jnp.float32), square_shape],
        pair_flops // 4,
        (acc, weights, values[0]),
    )
    averaged, squares = plain_call(
        functools.partial(rest_kernel, middle // HD, heads),
        "rest",
        [jax.ShapeDtypeStruct((heads - middle // HD, HD, row_count), jnp.float32), square_shape],
        pair_flops // 4,
        (acc, weights, values[1], squares),
    )
    others = [swap(squares, axes, offset) for offset in range(2, lax.axis_size(axes))]
    back, squares = plain_call(
        turn_kernel,
        "turn",
        [jax.ShapeDtypeStruct((steps, rows, columns - middle), jnp.float32), square_shape],
        row_count * columns,
        (averaged, squares),
    )
    others.append(swap(squares, axes, 1))
    decoded = decode(after(hidden, back), tail, conv_w, fade_count)
    attended = plain_call(
        functools.partial(scale_kernel, columns * lax.axis_size(axes)),
        "scale",
        jax.ShapeDtypeStruct(query.shape, jnp.bfloat16),
        row_count * columns,
        (front, back, squares, *others),
        out_specs=HBM_SPEC,
        scratch=[
            pltpu.VMEM((steps, rows, columns), jnp.bfloat16),
            pltpu.SemaphoreType.DMA((steps,)),
        ],
    )
    return (attended, decoded)


def solution(mesh):
    placed = (
        P(None, ("groups", "span"), None, ("mp", "seq")),
        P(None, None, ("groups", "span"), None, ("mp", "seq")),
        P(None, ("groups", "span"), None, ("mp", "seq")),
        P("groups", None),
        P("groups", None),
        P(("groups", "span"), None, ("mp", "seq")),
        P(("mp", "seq"), None),
        P(),
        P(("groups", "span")),
    )
    return jax.shard_map(
        per_device,
        mesh=mesh,
        in_specs=placed,
        out_specs=(
            P(None, ("groups", "span"), None, ("mp", "seq")),
            P(("groups", "span"), ("mp", "seq"), None),
        ),
        check_vma=False,
    )
```

```python
import functools
import math

import jax
import jax.numpy as jnp
from jax import lax
from jax.experimental import pallas as pl
from jax.experimental.pallas import tpu as pltpu
from jax.sharding import PartitionSpec as P

FR = 6
HD = 128
KT = 3
FADE = 2
NSTEPS = 64
LOG2E = 1.4426950408889634
VMEM_LIMIT = 24 * 1024 * 1024
VMEM_ALL = 60 * 1024 * 1024

SMEM_SPEC = pl.BlockSpec(memory_space=pltpu.SMEM)
VMEM_SPEC = pl.BlockSpec(memory_space=pltpu.VMEM)
HBM_SPEC = pl.BlockSpec(memory_space=pltpu.HBM)


def cost(flops, nbytes):
    return pl.CostEstimate(flops=flops, bytes_accessed=nbytes, transcendentals=0)


def hop(value, axis, steps):
    count = lax.axis_size(axis)
    return lax.ppermute(value, axis, [(source, source + steps) for source in range(count - steps)])


def swap(value, axes, offset):
    count = lax.axis_size(axes)
    if count & (count - 1) == 0:
        pairs = [(source, source ^ offset) for source in range(count)]
    else:
        pairs = [(source, (source + offset) % count) for source in range(count)]
    return lax.ppermute(value, axes, pairs)


def target_of(axes, offset):
    count = lax.axis_size(axes)
    mine = lax.axis_index(axes)
    if count & (count - 1) == 0:
        return mine ^ offset
    return lax.rem(mine + offset, count)


def after(value, *earlier):
    return lax.optimization_barrier((value, *earlier))[0]


def nt_dot(left, right):
    return lax.dot_general(left, right, (((1,), (1,)), ((), ())), preferred_element_type=jnp.float32)


def tn_dot(left, right):
    return lax.dot_general(left, right, (((0,), (0,)), ((), ())), preferred_element_type=jnp.float32)


def nn_dot(left, right):
    return jnp.dot(left, right, preferred_element_type=jnp.float32)


def row_factors(step_ref, position, steps, rows):
    lane = lax.broadcasted_iota(jnp.int32, (1, steps * rows), 1)
    index = jnp.full(lane.shape, step_ref[position, 0], jnp.int32)
    for step in range(1, steps):
        index = jnp.where(lane >= step * rows, step_ref[position, step], index)
    fraction = 1.0 - index.astype(jnp.float32) / NSTEPS
    level = 3.0 * fraction / (1.0 + 2.0 * fraction)
    return (0.5 + level) * (LOG2E / math.sqrt(HD))


def lane_windows(steps, rows):
    total = steps * rows
    return [
        (step * rows // HD * HD, min(total, -(-(step + 1) * rows // HD) * HD))
        for step in range(steps)
    ]


def join_steps(pieces, windows, rows):
    total = windows[-1][1]
    tiles = []
    for first in range(0, total, HD):
        stop = min(first + HD, total)
        tile = None
        for step, (begin, end) in enumerate(windows):
            if begin <= first and stop <= end and step * rows < stop and first < (step + 1) * rows:
                part = pieces[step][:, first - begin : stop - begin]
                if tile is None:
                    tile = part
                else:
                    lane = lax.broadcasted_iota(jnp.int32, part.shape, 1) + first
                    tile = jnp.where(lane >= step * rows, part, tile)
        tiles.append(tile)
    return jnp.concatenate(tiles, 1)


def own_kernel(step_ref, q_ref, kv_ref, acc_ref, top_ref, total_ref):
    position = lax.axis_index("span")
    steps, _, rows, columns = q_ref.shape
    factors = row_factors(step_ref, position, steps, rows)
    windows = lane_windows(steps, rows)
    for head in range(columns // HD):
        cut = slice(head * HD, (head + 1) * HD)
        queries = q_ref[:, 0, :, cut].reshape(steps * rows, HD)
        scores = join_steps(
            [nt_dot(kv_ref[s, 0, 0, :, cut], queries[a:b]) for s, (a, b) in enumerate(windows)],
            windows,
            rows,
        )
        scores = scores * factors
        top = jnp.max(scores, axis=0, keepdims=True)
        weights = jnp.exp2(scores - top)
        rounded = weights.astype(jnp.bfloat16)
        acc_ref[head] = join_steps(
            [tn_dot(kv_ref[s, 1, 0, :, cut], rounded[:, a:b]) for s, (a, b) in enumerate(windows)],
            windows,
            rows,
        )
        top_ref[head : head + 1] = top
        total_ref[head : head + 1] = jnp.sum(weights, axis=0, keepdims=True)


def absorb(queries, keys, values, factors, acc, top, total):
    scores = nt_dot(keys, queries) * factors
    newest = jnp.maximum(top, jnp.max(scores, axis=0, keepdims=True))
    weights = jnp.exp2(scores - newest)
    shrink = jnp.exp2(top - newest)
    total = total * shrink + jnp.sum(weights, axis=0, keepdims=True)
    acc = acc * shrink + tn_dot(values, weights.astype(jnp.bfloat16))
    return acc, newest, total


def visible(mask_ref, position, blocks):
    seen = False
    for place, block in blocks.items():
        seen = seen | ((position == place) & (mask_ref[place, block] > 0))
    return seen


def half(ref, which, cut):
    return ref[which, 0, :, cut] if len(ref.shape) == 4 else ref[0, :, cut]


def mid_kernel(plan, step_ref, mask_ref, q_ref, *refs):
    block_refs, (acc_in, top_in, total_in, acc_ref, top_ref, total_ref) = refs[:-6], refs[-6:]
    position = lax.axis_index("span")
    steps, _, rows, columns = q_ref.shape
    seen = visible(mask_ref, position, plan)

    @pl.when(seen)
    def _():
        factors = row_factors(step_ref, position, steps, rows)
        for head in range(columns // HD):
            cut = slice(head * HD, (head + 1) * HD)
            queries = q_ref[:, 0, :, cut].reshape(steps * rows, HD)
            acc, top, total = absorb(
                queries,
                half(block_refs[0], 0, cut),
                half(block_refs[-1], 1, cut),
                factors,
                acc_in[head],
                top_in[head : head + 1],
                total_in[head : head + 1],
            )
            acc_ref[head] = acc
            top_ref[head : head + 1] = top
            total_ref[head : head + 1] = total

    @pl.when(jnp.logical_not(seen))
    def _():
        acc_ref[...] = acc_in[...]
        top_ref[...] = top_in[...]
        total_ref[...] = total_in[...]


def score_kernel(plans, step_ref, mask_ref, q_ref, *refs):
    key_refs, (acc_in, top_in, total_in, acc_ref, w_ref) = refs[:-5], refs[-5:]
    position = lax.axis_index("span")
    steps, _, rows, columns = q_ref.shape

    def finish(key_ref):
        factors = row_factors(step_ref, position, steps, rows)
        for head in range(columns // HD):
            cut = slice(head * HD, (head + 1) * HD)
            queries = q_ref[:, 0, :, cut].reshape(steps * rows, HD)
            scores = nt_dot(half(key_ref, 0, cut), queries) * factors
            top = top_in[head : head + 1]
            newest = jnp.maximum(top, jnp.max(scores, axis=0, keepdims=True))
            weights = jnp.exp2(scores - newest)
            shrink = jnp.exp2(top - newest)
            total = total_in[head : head + 1] * shrink + jnp.sum(weights, axis=0, keepdims=True)
            inverse = 1.0 / total
            w_ref[head] = (weights * inverse).astype(jnp.bfloat16)
            acc_ref[head] = acc_in[head] * (shrink * inverse)

    rest = True
    for plan, key_ref in zip(plans, key_refs):
        seen = visible(mask_ref, position, plan)
        rest = jnp.logical_and(rest, jnp.logical_not(seen))
        pl.when(seen)(functools.partial(finish, key_ref))

    @pl.when(rest)
    def _():
        w_ref[...] = jnp.zeros_like(w_ref)
        for head in range(columns // HD):
            acc_ref[head] = acc_in[head] * (1.0 / total_in[head : head + 1])


def average_head(head, acc_ref, w_ref, value_ref, first):
    if value_ref.shape[-1] == acc_ref.shape[0] * HD:
        first = 0
    cut = slice((head - first) * HD, (head - first + 1) * HD)
    return acc_ref[head] + tn_dot(half(value_ref, 1, cut), w_ref[head])


def average_kernel(begin, end, acc_ref, w_ref, value_ref, average_ref, square_ref):
    squares = jnp.zeros(square_ref.shape, jnp.float32)
    for head in range(begin, end):
        average = average_head(head, acc_ref, w_ref, value_ref, begin)
        squares = squares + jnp.sum(average * average, axis=0, keepdims=True)
        average_ref[:, :, (head - begin) * HD : (head - begin + 1) * HD] = average.T.reshape(
            average_ref.shape[:2] + (HD,)
        )
    square_ref[...] = squares


def rest_kernel(begin, end, acc_ref, w_ref, value_ref, before_ref, average_ref, square_ref):
    squares = before_ref[...]
    for head in range(begin, end):
        average = average_head(head, acc_ref, w_ref, value_ref, begin)
        squares = squares + jnp.sum(average * average, axis=0, keepdims=True)
        average_ref[head - begin] = average
    square_ref[...] = squares


def turn_kernel(in_ref, square_in, out_ref, square_ref):
    steps, rows, _ = out_ref.shape
    for head in range(in_ref.shape[0]):
        out_ref[:, :, head * HD : (head + 1) * HD] = in_ref[head].T.reshape(steps, rows, HD)
    square_ref[...] = square_in[...]


def scale_kernel(width, front_ref, back_ref, *refs):
    part_refs, (out_hbm, out_ref, sem) = refs[:-3], refs[-3:]
    total = part_refs[0][...]
    for ref in part_refs[1:]:
        total = total + ref[...]
    inverse = lax.rsqrt(total / width + 1e-06)
    steps, rows, columns = out_ref.shape
    spread = jnp.broadcast_to(inverse, (HD, steps * rows)).T
    copies = []
    for step in range(steps):
        factor = spread[step * rows : (step + 1) * rows]
        place = 0
        for ref in (front_ref, back_ref):
            for first in range(0, ref.shape[2], HD):
                average = ref[step, :, first : first + HD]
                out_ref[step, :, place : place + HD] = (average * factor).astype(jnp.bfloat16)
                place += HD
        copies.append(pltpu.make_async_copy(out_ref.at[step], out_hbm.at[step, 0], sem.at[step]))
        copies[-1].start()
    for copy in copies:
        copy.wait()


def send(value, pairs):
    return lax.ppermute(value, "span", pairs)


def delivered(span, back):
    return {place: place - back for place in range(back, span)}


def plain_call(kernel, name, out_shape, flops, operands, in_specs=(), out_specs=None, scratch=(), limit=VMEM_LIMIT):
    nbytes = sum(math.prod(o.shape) * o.dtype.itemsize for o in operands)
    if out_specs is None:
        out_specs = [VMEM_SPEC] * len(out_shape)
    return pl.pallas_call(
        kernel,
        in_specs=list(in_specs) + [VMEM_SPEC] * (len(operands) - len(in_specs)),
        out_specs=out_specs,
        out_shape=out_shape,
        scratch_shapes=list(scratch),
        compiler_params=pltpu.CompilerParams(vmem_limit_bytes=limit),
        cost_estimate=cost(flops, nbytes),
        name=name,
    )(*operands)


def picker(shape, wanted):
    row = lax.broadcasted_iota(jnp.int32, shape, 0)
    column = lax.broadcasted_iota(jnp.int32, shape, 1)
    return jnp.where(column == wanted(row), 1.0, 0.0).astype(jnp.bfloat16)


def project_kernel(axes, x_hbm, w_hbm, *refs):
    out_refs, (x_ref, w_ref, x_sem, w_sem) = refs[:-4], refs[-4:]
    rows, depth = x_ref.shape
    share = out_refs[0].shape[0]
    x_copy = pltpu.make_async_copy(x_hbm.at[0], x_ref, x_sem)
    x_copy.start()
    copies = []
    for place, first in enumerate(range(0, depth, 2 * HD)):
        cut = slice(first, min(first + 2 * HD, depth))
        copies.append((cut, pltpu.make_async_copy(w_hbm.at[cut], w_ref.at[cut], w_sem.at[place])))
        copies[-1][1].start()
    total = jnp.zeros((rows, w_ref.shape[1]), jnp.float32)
    x_copy.wait()
    for cut, w_copy in copies:
        w_copy.wait()
        total = total + nn_dot(x_ref[:, cut], w_ref[cut])
    projected = total.astype(jnp.bfloat16)
    for offset, out_ref in enumerate(out_refs):
        first = target_of(axes, offset) * share
        chosen = picker((share, rows), lambda row: row + first)
        out_ref[...] = nn_dot(chosen, projected).astype(jnp.bfloat16)


def gather_kernel(*refs):
    hidden_ref, tail_ref = refs[-2:]
    total = refs[0][...].astype(jnp.float32)
    for ref in refs[1:-2]:
        total = total + ref[...].astype(jnp.float32)
    hidden = total.astype(jnp.bfloat16)
    hidden_ref[...] = hidden
    kept = KT - 1 + FADE
    shape = (tail_ref.shape[0], hidden.shape[0])
    chosen = picker(shape, lambda row: row // kept * FR + FR - kept + row % kept)
    tail_ref[...] = nn_dot(chosen, hidden).astype(jnp.bfloat16)


def decode_kernel(fade_ref, hidden_ref, tail_ref, conv_ref, out_ref):
    position = lax.axis_index("span")
    share = hidden_ref.shape[0]
    spatial = share // FR
    kept = KT - 1 + FADE
    wide = FADE + FR
    hidden, tail = hidden_ref[...], tail_ref[...]
    mixed = jnp.zeros((spatial * wide, out_ref.shape[2]), jnp.float32)
    for tap in range(KT):
        def from_tail(row):
            place = row % wide + KT - 1 - tap
            return jnp.where(place < kept, row // wide * kept + place, -1)

        def from_hidden(row):
            place = row % wide + KT - 1 - tap
            return jnp.where(place >= kept, row // wide * FR + place - kept, -1)

        window = nn_dot(picker((spatial * wide, tail.shape[0]), from_tail), tail)
        window = window + nn_dot(picker((spatial * wide, share), from_hidden), hidden)
        mixed = mixed + nn_dot(window.astype(jnp.bfloat16), conv_ref[tap])
    frames = (mixed * jax.nn.sigmoid(mixed)).astype(jnp.bfloat16)
    fade = fade_ref[0]
    shape = (share, spatial * wide)
    current = nn_dot(picker(shape, lambda row: row // FR * wide + FADE + row % FR), frames)

    def faded(row):
        return jnp.where(row % FR < fade, row // FR * wide + FADE - fade + row % FR, -1)

    previous = nn_dot(picker(shape, faded), frames)
    frame = lax.broadcasted_iota(jnp.int32, (share, out_ref.shape[2]), 0) % FR
    fade_float = jnp.full(frame.shape, fade, jnp.int32).astype(jnp.float32)
    weight = (frame.astype(jnp.float32) + 1.0) / (fade_float + 1.0)
    weight = jnp.where((frame < fade) & (position > 0), weight, 1.0)
    out_ref[0] = (weight * current + (1.0 - weight) * previous).astype(jnp.bfloat16)


def project(finished, w_in):
    axes = ("mp", "seq")
    parts = lax.axis_size(axes)
    _, rows, depth = finished.shape
    channels = w_in.shape[1]
    chunks = -(-depth // (2 * HD))
    return plain_call(
        functools.partial(project_kernel, axes),
        "project",
        [jax.ShapeDtypeStruct((rows // parts, channels), jnp.bfloat16)] * parts,
        2 * rows * depth * channels,
        (finished, w_in),
        [HBM_SPEC] * 2,
        scratch=[
            pltpu.VMEM((rows, depth), jnp.bfloat16),
            pltpu.VMEM((depth, channels), jnp.bfloat16),
            pltpu.SemaphoreType.DMA,
            pltpu.SemaphoreType.DMA((chunks,)),
        ],
        limit=VMEM_ALL,
    )


def gather(parts, rows):
    share, channels = parts[0].shape
    tail_rows = share // FR * (KT - 1 + FADE)
    return plain_call(
        gather_kernel,
        "gather",
        [jax.ShapeDtypeStruct((count, channels), jnp.bfloat16) for count in (share, tail_rows)],
        rows * channels,
        parts,
    )


def decode(hidden, tail, conv_w, fade_count):
    share, channels = hidden.shape
    return plain_call(
        decode_kernel,
        "decode",
        [jax.ShapeDtypeStruct((1, share, channels), jnp.bfloat16)],
        2 * share * KT * channels * channels,
        (fade_count, hidden, tail, conv_w),
        [SMEM_SPEC],
    )[0]


def per_device(
    query, noisy_kv, clean_kv, causal_mask, step_index, finished, w_in, conv_w, fade_count
):
    steps, _, rows, columns = query.shape
    heads = columns // HD
    middle = (heads + 1) // 2 * HD
    row_count = steps * rows
    span = lax.axis_size("span")
    axes = ("mp", "seq")
    acc_shape = jax.ShapeDtypeStruct((heads, HD, row_count), jnp.float32)
    stat_shape = jax.ShapeDtypeStruct((heads, row_count), jnp.float32)
    pair_flops = 4 * row_count * rows * columns

    first_pairs = [(0, 2), (2, 3)] if span == 4 else [(c, c + 1) for c in range(span - 1)]
    near = send(clean_kv, first_pairs)
    pieces = project(finished, w_in)
    parts = [pieces[0]] + [swap(p, axes, offset + 1) for offset, p in enumerate(pieces[1:])]
    if span == 4:
        direct = send(clean_kv, [(1, 3)])
    carry = plain_call(
        own_kernel,
        "own",
        [acc_shape, stat_shape, stat_shape],
        pair_flops,
        (step_index, query, noisy_kv),
        [SMEM_SPEC],
    )
    hidden, tail = gather(parts, rows)
    tail = hop(tail, "span", 1)
    if span == 4:
        near = after(near, carry[0], hidden)
        forwards = lax.axis_index("span") == 2
        passed = [jnp.where(forwards, near[which], clean_kv[which]) for which in range(2)]
        passed = [passed[0], passed[1][:, :, :middle], passed[1][:, :, middle:]]
        passed = [hop(block, "span", 1) for block in passed]
        early = [(near, {2: 0, 3: 2}), (direct, {3: 1})]
        keys, *values = passed
        last_plan = {1: 0, 2: 1, 3: 0}
    else:
        ring = [near]
        for _ in range(2, span):
            ring.append(hop(ring[-1], "span", 1))
        early = [(block, delivered(span, back + 1)) for back, block in enumerate(ring[:-1])]
        keys, values = ring[-1], ring[-1:] * 2
        last_plan = delivered(span, span - 1)
    for block, plan in early:
        carry = plain_call(
            functools.partial(mid_kernel, plan),
            "middle",
            [acc_shape, stat_shape, stat_shape],
            pair_flops,
            (step_index, causal_mask, query, block, *carry),
            [SMEM_SPEC] * 2,
        )
    acc, weights = plain_call(
        functools.partial(score_kernel, [last_plan]),
        "score",
        [acc_shape, jax.ShapeDtypeStruct((heads, rows, row_count), jnp.bfloat16)],
        pair_flops // 2,
        (step_index, causal_mask, query, keys, *carry),
        [SMEM_SPEC] * 2,
    )
    square_shape = jax.ShapeDtypeStruct((1, row_count), jnp.float32)
    front, squares = plain_call(
        functools.partial(average_kernel, 0, middle // HD),
        "average",
        [jax.ShapeDtypeStruct((steps, rows, middle), jnp.float32), square_shape],
        pair_flops // 4,
        (acc, weights, values[0]),
    )
    averaged, squares = plain_call(
        functools.partial(rest_kernel, middle // HD, heads),
        "rest",
        [jax.ShapeDtypeStruct((heads - middle // HD, HD, row_count), jnp.float32), square_shape],
        pair_flops // 4,
        (acc, weights, values[1], squares),
    )
    others = [swap(squares, axes, offset) for offset in range(2, lax.axis_size(axes))]
    back, squares = plain_call(
        turn_kernel,
        "turn",
        [jax.ShapeDtypeStruct((steps, rows, columns - middle), jnp.float32), square_shape],
        row_count * columns,
        (averaged, squares),
    )
    others.append(swap(squares, axes, 1))
    decoded = decode(after(hidden, back), tail, conv_w, fade_count)
    attended = plain_call(
        functools.partial(scale_kernel, columns * lax.axis_size(axes)),
        "scale",
        jax.ShapeDtypeStruct(query.shape, jnp.bfloat16),
        row_count * columns,
        (front, back, squares, *others),
        out_specs=HBM_SPEC,
        scratch=[
            pltpu.VMEM((steps, rows, columns), jnp.bfloat16),
            pltpu.SemaphoreType.DMA((steps,)),
        ],
    )
    return (attended, decoded)


def solution(mesh):
    placed = (
        P(None, ("groups", "span"), None, ("mp", "seq")),
        P(None, None, ("groups", "span"), None, ("mp", "seq")),
        P(None, ("groups", "span"), None, ("mp", "seq")),
        P("groups", None),
        P("groups", None),
        P(("groups", "span"), None, ("mp", "seq")),
        P(("mp", "seq"), None),
        P(),
        P(("groups", "span")),
    )
    return jax.shard_map(
        per_device,
        mesh=mesh,
        in_specs=placed,
        out_specs=(
            P(None, ("groups", "span"), None, ("mp", "seq")),
            P(("groups", "span"), ("mp", "seq"), None),
        ),
        check_vma=False,
    )
```

```python
import functools
import math

import jax
import jax.numpy as jnp
from jax import lax
from jax.experimental import pallas as pl
from jax.experimental.pallas import tpu as pltpu
from jax.sharding import PartitionSpec as P

FR = 6
HD = 128
KT = 3
FADE = 2
NSTEPS = 64
LOG2E = 1.4426950408889634
VMEM_LIMIT = 24 * 1024 * 1024
VMEM_ALL = 60 * 1024 * 1024

SMEM_SPEC = pl.BlockSpec(memory_space=pltpu.SMEM)
VMEM_SPEC = pl.BlockSpec(memory_space=pltpu.VMEM)
HBM_SPEC = pl.BlockSpec(memory_space=pltpu.HBM)


def cost(flops, nbytes):
    return pl.CostEstimate(flops=flops, bytes_accessed=nbytes, transcendentals=0)


def hop(value, axis, steps):
    count = lax.axis_size(axis)
    return lax.ppermute(value, axis, [(source, source + steps) for source in range(count - steps)])


def swap(value, axes, offset):
    count = lax.axis_size(axes)
    if count & (count - 1) == 0:
        pairs = [(source, source ^ offset) for source in range(count)]
    else:
        pairs = [(source, (source + offset) % count) for source in range(count)]
    return lax.ppermute(value, axes, pairs)


def target_of(axes, offset):
    count = lax.axis_size(axes)
    mine = lax.axis_index(axes)
    if count & (count - 1) == 0:
        return mine ^ offset
    return lax.rem(mine + offset, count)


def after(value, *earlier):
    return lax.optimization_barrier((value, *earlier))[0]


def nt_dot(left, right):
    return lax.dot_general(left, right, (((1,), (1,)), ((), ())), preferred_element_type=jnp.float32)


def tn_dot(left, right):
    return lax.dot_general(left, right, (((0,), (0,)), ((), ())), preferred_element_type=jnp.float32)


def nn_dot(left, right):
    return jnp.dot(left, right, preferred_element_type=jnp.float32)


def row_factors(step_ref, position, steps, rows):
    lane = lax.broadcasted_iota(jnp.int32, (1, steps * rows), 1)
    index = jnp.full(lane.shape, step_ref[position, 0], jnp.int32)
    for step in range(1, steps):
        index = jnp.where(lane >= step * rows, step_ref[position, step], index)
    fraction = 1.0 - index.astype(jnp.float32) / NSTEPS
    level = 3.0 * fraction / (1.0 + 2.0 * fraction)
    return (0.5 + level) * (LOG2E / math.sqrt(HD))


def lane_windows(steps, rows):
    total = steps * rows
    return [
        (step * rows // HD * HD, min(total, -(-(step + 1) * rows // HD) * HD))
        for step in range(steps)
    ]


def join_steps(pieces, windows, rows):
    total = windows[-1][1]
    tiles = []
    for first in range(0, total, HD):
        stop = min(first + HD, total)
        tile = None
        for step, (begin, end) in enumerate(windows):
            if begin <= first and stop <= end and step * rows < stop and first < (step + 1) * rows:
                part = pieces[step][:, first - begin : stop - begin]
                if tile is None:
                    tile = part
                else:
                    lane = lax.broadcasted_iota(jnp.int32, part.shape, 1) + first
                    tile = jnp.where(lane >= step * rows, part, tile)
        tiles.append(tile)
    return jnp.concatenate(tiles, 1)


def own_kernel(step_ref, q_ref, kv_ref, acc_ref, top_ref, total_ref):
    position = lax.axis_index("span")
    steps, _, rows, columns = q_ref.shape
    factors = row_factors(step_ref, position, steps, rows)
    windows = lane_windows(steps, rows)
    for head in range(columns // HD):
        cut = slice(head * HD, (head + 1) * HD)
        queries = q_ref[:, 0, :, cut].reshape(steps * rows, HD)
        scores = join_steps(
            [nt_dot(kv_ref[s, 0, 0, :, cut], queries[a:b]) for s, (a, b) in enumerate(windows)],
            windows,
            rows,
        )
        scores = scores * factors
        top = jnp.max(scores, axis=0, keepdims=True)
        weights = jnp.exp2(scores - top)
        rounded = weights.astype(jnp.bfloat16)
        acc_ref[head] = join_steps(
            [tn_dot(kv_ref[s, 1, 0, :, cut], rounded[:, a:b]) for s, (a, b) in enumerate(windows)],
            windows,
            rows,
        )
        top_ref[head : head + 1] = top
        total_ref[head : head + 1] = jnp.sum(weights, axis=0, keepdims=True)


def absorb(queries, keys, values, factors, acc, top, total):
    scores = nt_dot(keys, queries) * factors
    newest = jnp.maximum(top, jnp.max(scores, axis=0, keepdims=True))
    weights = jnp.exp2(scores - newest)
    shrink = jnp.exp2(top - newest)
    total = total * shrink + jnp.sum(weights, axis=0, keepdims=True)
    acc = acc * shrink + tn_dot(values, weights.astype(jnp.bfloat16))
    return acc, newest, total


def visible(mask_ref, position, plan):
    odd = lax.rem(lax.axis_index("seq"), 2)
    seen = False
    for parity, blocks in enumerate(plan):
        for place, block in blocks.items():
            here = (odd == parity) & (position == place)
            seen = seen | (here & (mask_ref[place, block] > 0))
    return seen


def half(ref, which, cut):
    return ref[which, 0, :, cut] if len(ref.shape) == 4 else ref[0, :, cut]


def mid_kernel(plan, step_ref, mask_ref, q_ref, *refs):
    block_refs, (acc_in, top_in, total_in, acc_ref, top_ref, total_ref) = refs[:-6], refs[-6:]
    position = lax.axis_index("span")
    steps, _, rows, columns = q_ref.shape
    seen = visible(mask_ref, position, plan)

    @pl.when(seen)
    def _():
        factors = row_factors(step_ref, position, steps, rows)
        for head in range(columns // HD):
            cut = slice(head * HD, (head + 1) * HD)
            queries = q_ref[:, 0, :, cut].reshape(steps * rows, HD)
            acc, top, total = absorb(
                queries,
                half(block_refs[0], 0, cut),
                half(block_refs[-1], 1, cut),
                factors,
                acc_in[head],
                top_in[head : head + 1],
                total_in[head : head + 1],
            )
            acc_ref[head] = acc
            top_ref[head : head + 1] = top
            total_ref[head : head + 1] = total

    @pl.when(jnp.logical_not(seen))
    def _():
        acc_ref[...] = acc_in[...]
        top_ref[...] = top_in[...]
        total_ref[...] = total_in[...]


def score_kernel(plans, step_ref, mask_ref, q_ref, *refs):
    key_refs, (acc_in, top_in, total_in, acc_ref, w_ref) = refs[:-5], refs[-5:]
    position = lax.axis_index("span")
    steps, _, rows, columns = q_ref.shape

    def finish(key_ref):
        factors = row_factors(step_ref, position, steps, rows)
        for head in range(columns // HD):
            cut = slice(head * HD, (head + 1) * HD)
            queries = q_ref[:, 0, :, cut].reshape(steps * rows, HD)
            scores = nt_dot(half(key_ref, 0, cut), queries) * factors
            top = top_in[head : head + 1]
            newest = jnp.maximum(top, jnp.max(scores, axis=0, keepdims=True))
            weights = jnp.exp2(scores - newest)
            shrink = jnp.exp2(top - newest)
            total = total_in[head : head + 1] * shrink + jnp.sum(weights, axis=0, keepdims=True)
            inverse = 1.0 / total
            w_ref[head] = (weights * inverse).astype(jnp.bfloat16)
            acc_ref[head] = acc_in[head] * (shrink * inverse)

    rest = True
    for plan, key_ref in zip(plans, key_refs):
        seen = visible(mask_ref, position, plan)
        rest = jnp.logical_and(rest, jnp.logical_not(seen))
        pl.when(seen)(functools.partial(finish, key_ref))

    @pl.when(rest)
    def _():
        w_ref[...] = jnp.zeros_like(w_ref)
        for head in range(columns // HD):
            acc_ref[head] = acc_in[head] * (1.0 / total_in[head : head + 1])


def average_head(head, acc_ref, w_ref, value_ref, first):
    if value_ref.shape[-1] == acc_ref.shape[0] * HD:
        first = 0
    cut = slice((head - first) * HD, (head - first + 1) * HD)
    return acc_ref[head] + tn_dot(half(value_ref, 1, cut), w_ref[head])


def average_kernel(begin, end, acc_ref, w_ref, value_ref, average_ref, square_ref):
    squares = jnp.zeros(square_ref.shape, jnp.float32)
    for head in range(begin, end):
        average = average_head(head, acc_ref, w_ref, value_ref, begin)
        squares = squares + jnp.sum(average * average, axis=0, keepdims=True)
        average_ref[:, :, (head - begin) * HD : (head - begin + 1) * HD] = average.T.reshape(
            average_ref.shape[:2] + (HD,)
        )
    square_ref[...] = squares


def rest_kernel(begin, end, acc_ref, w_ref, value_ref, before_ref, average_ref, square_ref):
    squares = before_ref[...]
    for head in range(begin, end):
        average = average_head(head, acc_ref, w_ref, value_ref, begin)
        squares = squares + jnp.sum(average * average, axis=0, keepdims=True)
        average_ref[head - begin] = average
    square_ref[...] = squares


def turn_kernel(in_ref, square_in, out_ref, square_ref):
    steps, rows, _ = out_ref.shape
    for head in range(in_ref.shape[0]):
        out_ref[:, :, head * HD : (head + 1) * HD] = in_ref[head].T.reshape(steps, rows, HD)
    square_ref[...] = square_in[...]


def scale_kernel(width, front_ref, back_ref, *refs):
    part_refs, (out_hbm, out_ref, sem) = refs[:-3], refs[-3:]
    total = part_refs[0][...]
    for ref in part_refs[1:]:
        total = total + ref[...]
    inverse = lax.rsqrt(total / width + 1e-06)
    steps, rows, columns = out_ref.shape
    spread = jnp.broadcast_to(inverse, (HD, steps * rows)).T
    copies = []
    for step in range(steps):
        factor = spread[step * rows : (step + 1) * rows]
        place = 0
        for ref in (front_ref, back_ref):
            for first in range(0, ref.shape[2], HD):
                average = ref[step, :, first : first + HD]
                out_ref[step, :, place : place + HD] = (average * factor).astype(jnp.bfloat16)
                place += HD
        copies.append(pltpu.make_async_copy(out_ref.at[step], out_hbm.at[step, 0], sem.at[step]))
        copies[-1].start()
    for copy in copies:
        copy.wait()


def send(value, pairs):
    cores = lax.axis_size("seq")
    flat = [
        (source * cores + core, target * cores + core)
        for core in range(cores)
        for source, target in pairs[core % 2]
    ]
    return lax.ppermute(value, ("span", "seq"), flat)


def delivered(span, back):
    return [{place: place - back for place in range(back, span)}] * 2


def plain_call(kernel, name, out_shape, flops, operands, in_specs=(), out_specs=None, scratch=(), limit=VMEM_LIMIT):
    nbytes = sum(math.prod(o.shape) * o.dtype.itemsize for o in operands)
    if out_specs is None:
        out_specs = [VMEM_SPEC] * len(out_shape)
    return pl.pallas_call(
        kernel,
        in_specs=list(in_specs) + [VMEM_SPEC] * (len(operands) - len(in_specs)),
        out_specs=out_specs,
        out_shape=out_shape,
        scratch_shapes=list(scratch),
        compiler_params=pltpu.CompilerParams(vmem_limit_bytes=limit),
        cost_estimate=cost(flops, nbytes),
        name=name,
    )(*operands)


def picker(shape, wanted):
    row = lax.broadcasted_iota(jnp.int32, shape, 0)
    column = lax.broadcasted_iota(jnp.int32, shape, 1)
    return jnp.where(column == wanted(row), 1.0, 0.0).astype(jnp.bfloat16)


def project_kernel(axes, x_hbm, w_hbm, *refs):
    out_refs, (x_ref, w_ref, x_sem, w_sem) = refs[:-4], refs[-4:]
    rows, depth = x_ref.shape
    share = out_refs[0].shape[0]
    x_copy = pltpu.make_async_copy(x_hbm.at[0], x_ref, x_sem)
    x_copy.start()
    copies = []
    for place, first in enumerate(range(0, depth, 2 * HD)):
        cut = slice(first, min(first + 2 * HD, depth))
        copies.append((cut, pltpu.make_async_copy(w_hbm.at[cut], w_ref.at[cut], w_sem.at[place])))
        copies[-1][1].start()
    total = jnp.zeros((rows, w_ref.shape[1]), jnp.float32)
    x_copy.wait()
    for cut, w_copy in copies:
        w_copy.wait()
        total = total + nn_dot(x_ref[:, cut], w_ref[cut])
    projected = total.astype(jnp.bfloat16)
    for offset, out_ref in enumerate(out_refs):
        first = target_of(axes, offset) * share
        chosen = picker((share, rows), lambda row: row + first)
        out_ref[...] = nn_dot(chosen, projected).astype(jnp.bfloat16)


def gather_kernel(*refs):
    hidden_ref, tail_ref = refs[-2:]
    total = refs[0][...].astype(jnp.float32)
    for ref in refs[1:-2]:
        total = total + ref[...].astype(jnp.float32)
    hidden = total.astype(jnp.bfloat16)
    hidden_ref[...] = hidden
    kept = KT - 1 + FADE
    shape = (tail_ref.shape[0], hidden.shape[0])
    chosen = picker(shape, lambda row: row // kept * FR + FR - kept + row % kept)
    tail_ref[...] = nn_dot(chosen, hidden).astype(jnp.bfloat16)


def decode_kernel(fade_ref, hidden_ref, tail_ref, conv_ref, out_ref):
    position = lax.axis_index("span")
    share = hidden_ref.shape[0]
    spatial = share // FR
    kept = KT - 1 + FADE
    wide = FADE + FR
    hidden, tail = hidden_ref[...], tail_ref[...]
    mixed = jnp.zeros((spatial * wide, out_ref.shape[2]), jnp.float32)
    for tap in range(KT):
        def from_tail(row):
            place = row % wide + KT - 1 - tap
            return jnp.where(place < kept, row // wide * kept + place, -1)

        def from_hidden(row):
            place = row % wide + KT - 1 - tap
            return jnp.where(place >= kept, row // wide * FR + place - kept, -1)

        window = nn_dot(picker((spatial * wide, tail.shape[0]), from_tail), tail)
        window = window + nn_dot(picker((spatial * wide, share), from_hidden), hidden)
        mixed = mixed + nn_dot(window.astype(jnp.bfloat16), conv_ref[tap])
    frames = (mixed * jax.nn.sigmoid(mixed)).astype(jnp.bfloat16)
    fade = fade_ref[0]
    shape = (share, spatial * wide)
    current = nn_dot(picker(shape, lambda row: row // FR * wide + FADE + row % FR), frames)

    def faded(row):
        return jnp.where(row % FR < fade, row // FR * wide + FADE - fade + row % FR, -1)

    previous = nn_dot(picker(shape, faded), frames)
    frame = lax.broadcasted_iota(jnp.int32, (share, out_ref.shape[2]), 0) % FR
    fade_float = jnp.full(frame.shape, fade, jnp.int32).astype(jnp.float32)
    weight = (frame.astype(jnp.float32) + 1.0) / (fade_float + 1.0)
    weight = jnp.where((frame < fade) & (position > 0), weight, 1.0)
    out_ref[0] = (weight * current + (1.0 - weight) * previous).astype(jnp.bfloat16)


def project(finished, w_in):
    axes = ("mp", "seq")
    parts = lax.axis_size(axes)
    _, rows, depth = finished.shape
    channels = w_in.shape[1]
    chunks = -(-depth // (2 * HD))
    return plain_call(
        functools.partial(project_kernel, axes),
        "project",
        [jax.ShapeDtypeStruct((rows // parts, channels), jnp.bfloat16)] * parts,
        2 * rows * depth * channels,
        (finished, w_in),
        [HBM_SPEC] * 2,
        scratch=[
            pltpu.VMEM((rows, depth), jnp.bfloat16),
            pltpu.VMEM((depth, channels), jnp.bfloat16),
            pltpu.SemaphoreType.DMA,
            pltpu.SemaphoreType.DMA((chunks,)),
        ],
        limit=VMEM_ALL,
    )


def gather(parts, rows):
    share, channels = parts[0].shape
    tail_rows = share // FR * (KT - 1 + FADE)
    return plain_call(
        gather_kernel,
        "gather",
        [jax.ShapeDtypeStruct((count, channels), jnp.bfloat16) for count in (share, tail_rows)],
        rows * channels,
        parts,
    )


def decode(hidden, tail, conv_w, fade_count):
    share, channels = hidden.shape
    return plain_call(
        decode_kernel,
        "decode",
        [jax.ShapeDtypeStruct((1, share, channels), jnp.bfloat16)],
        2 * share * KT * channels * channels,
        (fade_count, hidden, tail, conv_w),
        [SMEM_SPEC],
    )[0]


def per_device(
    query, noisy_kv, clean_kv, causal_mask, step_index, finished, w_in, conv_w, fade_count
):
    steps, _, rows, columns = query.shape
    heads = columns // HD
    middle = (heads + 1) // 2 * HD
    row_count = steps * rows
    span = lax.axis_size("span")
    axes = ("mp", "seq")
    acc_shape = jax.ShapeDtypeStruct((heads, HD, row_count), jnp.float32)
    stat_shape = jax.ShapeDtypeStruct((heads, row_count), jnp.float32)
    pair_flops = 4 * row_count * rows * columns

    shift = [(place, place + 1) for place in range(span - 1)]
    near = send(clean_kv, [[(0, 2), (2, 3)] if span == 4 else shift, shift])
    pieces = project(finished, w_in)
    parts = [pieces[0]] + [swap(p, axes, offset + 1) for offset, p in enumerate(pieces[1:])]
    if span == 4:
        direct = send(after(clean_kv, pieces[0]), [[(1, 3)], [(0, 3)]])
    carry = plain_call(
        own_kernel,
        "own",
        [acc_shape, stat_shape, stat_shape],
        pair_flops,
        (step_index, query, noisy_kv),
        [SMEM_SPEC],
    )
    hidden, tail = gather(parts, rows)
    tail = hop(tail, "span", 1)
    if span == 4:
        near = after(near, carry[0], hidden)
        forwards = lax.axis_index("span") == 2
        passed = [jnp.where(forwards, near[which], clean_kv[which]) for which in range(2)]
        passed = [passed[0], passed[1][:, :, :middle], passed[1][:, :, middle:]]
        passed = [send(block, [shift, [(0, 2), (2, 3)]]) for block in passed]
        early = [(near, [{2: 0, 3: 2}, {1: 0, 2: 1, 3: 2}]), (direct, [{3: 1}, {3: 0}])]
        keys, *values = passed
        last_plan = [{1: 0, 2: 1, 3: 0}, {2: 0, 3: 1}]
    else:
        ring = [near]
        for _ in range(2, span):
            ring.append(hop(ring[-1], "span", 1))
        early = [(block, delivered(span, back + 1)) for back, block in enumerate(ring[:-1])]
        keys, values = ring[-1], ring[-1:] * 2
        last_plan = delivered(span, span - 1)
    for block, plan in early:
        carry = plain_call(
            functools.partial(mid_kernel, plan),
            "middle",
            [acc_shape, stat_shape, stat_shape],
            pair_flops,
            (step_index, causal_mask, query, block, *carry),
            [SMEM_SPEC] * 2,
        )
    acc, weights = plain_call(
        functools.partial(score_kernel, [last_plan]),
        "score",
        [acc_shape, jax.ShapeDtypeStruct((heads, rows, row_count), jnp.bfloat16)],
        pair_flops // 2,
        (step_index, causal_mask, query, keys, *carry),
        [SMEM_SPEC] * 2,
    )
    square_shape = jax.ShapeDtypeStruct((1, row_count), jnp.float32)
    front, squares = plain_call(
        functools.partial(average_kernel, 0, middle // HD),
        "average",
        [jax.ShapeDtypeStruct((steps, rows, middle), jnp.float32), square_shape],
        pair_flops // 4,
        (acc, weights, values[0]),
    )
    averaged, squares = plain_call(
        functools.partial(rest_kernel, middle // HD, heads),
        "rest",
        [jax.ShapeDtypeStruct((heads - middle // HD, HD, row_count), jnp.float32), square_shape],
        pair_flops // 4,
        (acc, weights, values[1], squares),
    )
    others = [swap(squares, axes, offset) for offset in range(2, lax.axis_size(axes))]
    back, squares = plain_call(
        turn_kernel,
        "turn",
        [jax.ShapeDtypeStruct((steps, rows, columns - middle), jnp.float32), square_shape],
        row_count * columns,
        (averaged, squares),
    )
    others.append(swap(squares, axes, 1))
    decoded = decode(after(hidden, back), tail, conv_w, fade_count)
    attended = plain_call(
        functools.partial(scale_kernel, columns * lax.axis_size(axes)),
        "scale",
        jax.ShapeDtypeStruct(query.shape, jnp.bfloat16),
        row_count * columns,
        (front, back, squares, *others),
        out_specs=HBM_SPEC,
        scratch=[
            pltpu.VMEM((steps, rows, columns), jnp.bfloat16),
            pltpu.SemaphoreType.DMA((steps,)),
        ],
    )
    return (attended, decoded)


def solution(mesh):
    placed = (
        P(None, ("groups", "span"), None, ("mp", "seq")),
        P(None, None, ("groups", "span"), None, ("mp", "seq")),
        P(None, ("groups", "span"), None, ("mp", "seq")),
        P("groups", None),
        P("groups", None),
        P(("groups", "span"), None, ("mp", "seq")),
        P(("mp", "seq"), None),
        P(),
        P(("groups", "span")),
    )
    return jax.shard_map(
        per_device,
        mesh=mesh,
        in_specs=placed,
        out_specs=(
            P(None, ("groups", "span"), None, ("mp", "seq")),
            P(("groups", "span"), ("mp", "seq"), None),
        ),
        check_vma=False,
    )
```

```python
import functools
import math

import jax
import jax.numpy as jnp
from jax import lax
from jax.experimental import pallas as pl
from jax.experimental.pallas import tpu as pltpu
from jax.sharding import PartitionSpec as P

FR = 6
HD = 128
KT = 3
FADE = 2
NSTEPS = 64
LOG2E = 1.4426950408889634
VMEM_LIMIT = 24 * 1024 * 1024
VMEM_ALL = 60 * 1024 * 1024

SMEM_SPEC = pl.BlockSpec(memory_space=pltpu.SMEM)
VMEM_SPEC = pl.BlockSpec(memory_space=pltpu.VMEM)
HBM_SPEC = pl.BlockSpec(memory_space=pltpu.HBM)


def cost(flops, nbytes):
    return pl.CostEstimate(flops=flops, bytes_accessed=nbytes, transcendentals=0)


def hop(value, axis, steps):
    count = lax.axis_size(axis)
    return lax.ppermute(value, axis, [(source, source + steps) for source in range(count - steps)])


def swap(value, axes, offset):
    count = lax.axis_size(axes)
    if count & (count - 1) == 0:
        pairs = [(source, source ^ offset) for source in range(count)]
    else:
        pairs = [(source, (source + offset) % count) for source in range(count)]
    return lax.ppermute(value, axes, pairs)


def target_of(axes, offset):
    count = lax.axis_size(axes)
    mine = lax.axis_index(axes)
    if count & (count - 1) == 0:
        return mine ^ offset
    return lax.rem(mine + offset, count)


def after(value, *earlier):
    return lax.optimization_barrier((value, *earlier))[0]


def nt_dot(left, right):
    return lax.dot_general(left, right, (((1,), (1,)), ((), ())), preferred_element_type=jnp.float32)


def tn_dot(left, right):
    return lax.dot_general(left, right, (((0,), (0,)), ((), ())), preferred_element_type=jnp.float32)


def nn_dot(left, right):
    return jnp.dot(left, right, preferred_element_type=jnp.float32)


def row_factors(step_ref, position, steps, rows):
    lane = lax.broadcasted_iota(jnp.int32, (1, steps * rows), 1)
    index = jnp.full(lane.shape, step_ref[position, 0], jnp.int32)
    for step in range(1, steps):
        index = jnp.where(lane >= step * rows, step_ref[position, step], index)
    fraction = 1.0 - index.astype(jnp.float32) / NSTEPS
    level = 3.0 * fraction / (1.0 + 2.0 * fraction)
    return (0.5 + level) * (LOG2E / math.sqrt(HD))


def lane_windows(steps, rows):
    total = steps * rows
    return [
        (step * rows // HD * HD, min(total, -(-(step + 1) * rows // HD) * HD))
        for step in range(steps)
    ]


def join_steps(pieces, windows, rows):
    total = windows[-1][1]
    tiles = []
    for first in range(0, total, HD):
        stop = min(first + HD, total)
        tile = None
        for step, (begin, end) in enumerate(windows):
            if begin <= first and stop <= end and step * rows < stop and first < (step + 1) * rows:
                part = pieces[step][:, first - begin : stop - begin]
                if tile is None:
                    tile = part
                else:
                    lane = lax.broadcasted_iota(jnp.int32, part.shape, 1) + first
                    tile = jnp.where(lane >= step * rows, part, tile)
        tiles.append(tile)
    return jnp.concatenate(tiles, 1)


def own_kernel(step_ref, q_ref, kv_ref, acc_ref, top_ref, total_ref):
    position = lax.axis_index("span")
    steps, _, rows, columns = q_ref.shape
    factors = row_factors(step_ref, position, steps, rows)
    windows = lane_windows(steps, rows)
    for head in range(columns // HD):
        cut = slice(head * HD, (head + 1) * HD)
        queries = q_ref[:, 0, :, cut].reshape(steps * rows, HD)
        scores = join_steps(
            [nt_dot(kv_ref[s, 0, 0, :, cut], queries[a:b]) for s, (a, b) in enumerate(windows)],
            windows,
            rows,
        )
        scores = scores * factors
        top = jnp.max(scores, axis=0, keepdims=True)
        weights = jnp.exp2(scores - top)
        rounded = weights.astype(jnp.bfloat16)
        acc_ref[head] = join_steps(
            [tn_dot(kv_ref[s, 1, 0, :, cut], rounded[:, a:b]) for s, (a, b) in enumerate(windows)],
            windows,
            rows,
        )
        top_ref[head : head + 1] = top
        total_ref[head : head + 1] = jnp.sum(weights, axis=0, keepdims=True)


def absorb(queries, keys, values, factors, acc, top, total):
    scores = nt_dot(keys, queries) * factors
    newest = jnp.maximum(top, jnp.max(scores, axis=0, keepdims=True))
    weights = jnp.exp2(scores - newest)
    shrink = jnp.exp2(top - newest)
    total = total * shrink + jnp.sum(weights, axis=0, keepdims=True)
    acc = acc * shrink + tn_dot(values, weights.astype(jnp.bfloat16))
    return acc, newest, total


def visible(mask_ref, position, plan):
    odd = lax.rem(lax.axis_index("seq"), 2)
    seen = False
    for parity, blocks in enumerate(plan):
        for place, block in blocks.items():
            here = (odd == parity) & (position == place)
            seen = seen | (here & (mask_ref[place, block] > 0))
    return seen


def half(ref, which, cut):
    return ref[which, 0, :, cut] if len(ref.shape) == 4 else ref[0, :, cut]


def mid_kernel(plans, step_ref, mask_ref, q_ref, *refs):
    block_refs, (acc_in, top_in, total_in, acc_ref, top_ref, total_ref) = refs[:-6], refs[-6:]
    position = lax.axis_index("span")
    steps, _, rows, columns = q_ref.shape

    def take(block_ref):
        factors = row_factors(step_ref, position, steps, rows)
        for head in range(columns // HD):
            cut = slice(head * HD, (head + 1) * HD)
            queries = q_ref[:, 0, :, cut].reshape(steps * rows, HD)
            acc, top, total = absorb(
                queries,
                half(block_ref, 0, cut),
                half(block_ref, 1, cut),
                factors,
                acc_in[head],
                top_in[head : head + 1],
                total_in[head : head + 1],
            )
            acc_ref[head] = acc
            top_ref[head : head + 1] = top
            total_ref[head : head + 1] = total

    rest = True
    for plan, block_ref in zip(plans, block_refs):
        seen = visible(mask_ref, position, plan)
        rest = jnp.logical_and(rest, jnp.logical_not(seen))
        pl.when(seen)(functools.partial(take, block_ref))

    @pl.when(rest)
    def _():
        acc_ref[...] = acc_in[...]
        top_ref[...] = top_in[...]
        total_ref[...] = total_in[...]


def score_kernel(plans, step_ref, mask_ref, q_ref, *refs):
    key_refs, (acc_in, top_in, total_in, acc_ref, w_ref) = refs[:-5], refs[-5:]
    position = lax.axis_index("span")
    steps, _, rows, columns = q_ref.shape

    def finish(key_ref):
        factors = row_factors(step_ref, position, steps, rows)
        for head in range(columns // HD):
            cut = slice(head * HD, (head + 1) * HD)
            queries = q_ref[:, 0, :, cut].reshape(steps * rows, HD)
            scores = nt_dot(half(key_ref, 0, cut), queries) * factors
            top = top_in[head : head + 1]
            newest = jnp.maximum(top, jnp.max(scores, axis=0, keepdims=True))
            weights = jnp.exp2(scores - newest)
            shrink = jnp.exp2(top - newest)
            total = total_in[head : head + 1] * shrink + jnp.sum(weights, axis=0, keepdims=True)
            inverse = 1.0 / total
            w_ref[head] = (weights * inverse).astype(jnp.bfloat16)
            acc_ref[head] = acc_in[head] * (shrink * inverse)

    rest = True
    for plan, key_ref in zip(plans, key_refs):
        seen = visible(mask_ref, position, plan)
        rest = jnp.logical_and(rest, jnp.logical_not(seen))
        pl.when(seen)(functools.partial(finish, key_ref))

    @pl.when(rest)
    def _():
        w_ref[...] = jnp.zeros_like(w_ref)
        for head in range(columns // HD):
            acc_ref[head] = acc_in[head] * (1.0 / total_in[head : head + 1])


def average_head(head, acc_ref, w_ref, value_ref, first):
    if value_ref.shape[-1] == acc_ref.shape[0] * HD:
        first = 0
    cut = slice((head - first) * HD, (head - first + 1) * HD)
    return acc_ref[head] + tn_dot(half(value_ref, 1, cut), w_ref[head])


def average_kernel(begin, end, acc_ref, w_ref, value_ref, average_ref, square_ref):
    squares = jnp.zeros(square_ref.shape, jnp.float32)
    for head in range(begin, end):
        average = average_head(head, acc_ref, w_ref, value_ref, begin)
        squares = squares + jnp.sum(average * average, axis=0, keepdims=True)
        average_ref[:, :, (head - begin) * HD : (head - begin + 1) * HD] = average.T.reshape(
            average_ref.shape[:2] + (HD,)
        )
    square_ref[...] = squares


def rest_kernel(begin, end, acc_ref, w_ref, value_ref, before_ref, average_ref, square_ref):
    squares = before_ref[...]
    for head in range(begin, end):
        average = average_head(head, acc_ref, w_ref, value_ref, begin)
        squares = squares + jnp.sum(average * average, axis=0, keepdims=True)
        average_ref[head - begin] = average
    square_ref[...] = squares


def turn_kernel(in_ref, square_in, out_ref, square_ref):
    steps, rows, _ = out_ref.shape
    for head in range(in_ref.shape[0]):
        out_ref[:, :, head * HD : (head + 1) * HD] = in_ref[head].T.reshape(steps, rows, HD)
    square_ref[...] = square_in[...]


def scale_kernel(width, front_ref, back_ref, *refs):
    part_refs, (out_hbm, out_ref, sem) = refs[:-3], refs[-3:]
    total = part_refs[0][...]
    for ref in part_refs[1:]:
        total = total + ref[...]
    inverse = lax.rsqrt(total / width + 1e-06)
    steps, rows, columns = out_ref.shape
    spread = jnp.broadcast_to(inverse, (HD, steps * rows)).T
    copies = []
    for step in range(steps):
        factor = spread[step * rows : (step + 1) * rows]
        place = 0
        for ref in (front_ref, back_ref):
            for first in range(0, ref.shape[2], HD):
                average = ref[step, :, first : first + HD]
                out_ref[step, :, place : place + HD] = (average * factor).astype(jnp.bfloat16)
                place += HD
        copies.append(pltpu.make_async_copy(out_ref.at[step], out_hbm.at[step, 0], sem.at[step]))
        copies[-1].start()
    for copy in copies:
        copy.wait()


def send(value, pairs):
    cores = lax.axis_size("seq")
    flat = [
        (source * cores + core, target * cores + core)
        for core in range(cores)
        for source, target in pairs[core % 2]
    ]
    return lax.ppermute(value, ("span", "seq"), flat)


def delivered(span, back):
    return [{place: place - back for place in range(back, span)}] * 2


def plain_call(kernel, name, out_shape, flops, operands, in_specs=(), out_specs=None, scratch=(), limit=VMEM_LIMIT):
    nbytes = sum(math.prod(o.shape) * o.dtype.itemsize for o in operands)
    if out_specs is None:
        out_specs = [VMEM_SPEC] * len(out_shape)
    return pl.pallas_call(
        kernel,
        in_specs=list(in_specs) + [VMEM_SPEC] * (len(operands) - len(in_specs)),
        out_specs=out_specs,
        out_shape=out_shape,
        scratch_shapes=list(scratch),
        compiler_params=pltpu.CompilerParams(vmem_limit_bytes=limit),
        cost_estimate=cost(flops, nbytes),
        name=name,
    )(*operands)


def picker(shape, wanted):
    row = lax.broadcasted_iota(jnp.int32, shape, 0)
    column = lax.broadcasted_iota(jnp.int32, shape, 1)
    return jnp.where(column == wanted(row), 1.0, 0.0).astype(jnp.bfloat16)


def project_kernel(axes, x_hbm, w_hbm, *refs):
    out_refs, (x_ref, w_ref, x_sem, w_sem) = refs[:-4], refs[-4:]
    rows, depth = x_ref.shape
    share = out_refs[0].shape[0]
    x_copy = pltpu.make_async_copy(x_hbm.at[0], x_ref, x_sem)
    x_copy.start()
    copies = []
    for place, first in enumerate(range(0, depth, 2 * HD)):
        cut = slice(first, min(first + 2 * HD, depth))
        copies.append((cut, pltpu.make_async_copy(w_hbm.at[cut], w_ref.at[cut], w_sem.at[place])))
        copies[-1][1].start()
    total = jnp.zeros((rows, w_ref.shape[1]), jnp.float32)
    x_copy.wait()
    for cut, w_copy in copies:
        w_copy.wait()
        total = total + nn_dot(x_ref[:, cut], w_ref[cut])
    projected = total.astype(jnp.bfloat16)
    for offset, out_ref in enumerate(out_refs):
        first = target_of(axes, offset) * share
        chosen = picker((share, rows), lambda row: row + first)
        out_ref[...] = nn_dot(chosen, projected).astype(jnp.bfloat16)


def gather_kernel(*refs):
    hidden_ref, tail_ref = refs[-2:]
    total = refs[0][...].astype(jnp.float32)
    for ref in refs[1:-2]:
        total = total + ref[...].astype(jnp.float32)
    hidden = total.astype(jnp.bfloat16)
    hidden_ref[...] = hidden
    kept = KT - 1 + FADE
    shape = (tail_ref.shape[0], hidden.shape[0])
    chosen = picker(shape, lambda row: row // kept * FR + FR - kept + row % kept)
    tail_ref[...] = nn_dot(chosen, hidden).astype(jnp.bfloat16)


def decode_kernel(fade_ref, hidden_ref, tail_ref, conv_ref, out_ref):
    position = lax.axis_index("span")
    share = hidden_ref.shape[0]
    spatial = share // FR
    kept = KT - 1 + FADE
    wide = FADE + FR
    hidden, tail = hidden_ref[...], tail_ref[...]
    mixed = jnp.zeros((spatial * wide, out_ref.shape[2]), jnp.float32)
    for tap in range(KT):
        def from_tail(row):
            place = row % wide + KT - 1 - tap
            return jnp.where(place < kept, row // wide * kept + place, -1)

        def from_hidden(row):
            place = row % wide + KT - 1 - tap
            return jnp.where(place >= kept, row // wide * FR + place - kept, -1)

        window = nn_dot(picker((spatial * wide, tail.shape[0]), from_tail), tail)
        window = window + nn_dot(picker((spatial * wide, share), from_hidden), hidden)
        mixed = mixed + nn_dot(window.astype(jnp.bfloat16), conv_ref[tap])
    frames = (mixed * jax.nn.sigmoid(mixed)).astype(jnp.bfloat16)
    fade = fade_ref[0]
    shape = (share, spatial * wide)
    current = nn_dot(picker(shape, lambda row: row // FR * wide + FADE + row % FR), frames)

    def faded(row):
        return jnp.where(row % FR < fade, row // FR * wide + FADE - fade + row % FR, -1)

    previous = nn_dot(picker(shape, faded), frames)
    frame = lax.broadcasted_iota(jnp.int32, (share, out_ref.shape[2]), 0) % FR
    fade_float = jnp.full(frame.shape, fade, jnp.int32).astype(jnp.float32)
    weight = (frame.astype(jnp.float32) + 1.0) / (fade_float + 1.0)
    weight = jnp.where((frame < fade) & (position > 0), weight, 1.0)
    out_ref[0] = (weight * current + (1.0 - weight) * previous).astype(jnp.bfloat16)


def project(finished, w_in):
    axes = ("mp", "seq")
    parts = lax.axis_size(axes)
    _, rows, depth = finished.shape
    channels = w_in.shape[1]
    chunks = -(-depth // (2 * HD))
    return plain_call(
        functools.partial(project_kernel, axes),
        "project",
        [jax.ShapeDtypeStruct((rows // parts, channels), jnp.bfloat16)] * parts,
        2 * rows * depth * channels,
        (finished, w_in),
        [HBM_SPEC] * 2,
        scratch=[
            pltpu.VMEM((rows, depth), jnp.bfloat16),
            pltpu.VMEM((depth, channels), jnp.bfloat16),
            pltpu.SemaphoreType.DMA,
            pltpu.SemaphoreType.DMA((chunks,)),
        ],
        limit=VMEM_ALL,
    )


def gather(parts, rows):
    share, channels = parts[0].shape
    tail_rows = share // FR * (KT - 1 + FADE)
    return plain_call(
        gather_kernel,
        "gather",
        [jax.ShapeDtypeStruct((count, channels), jnp.bfloat16) for count in (share, tail_rows)],
        rows * channels,
        parts,
    )


def decode(hidden, tail, conv_w, fade_count):
    share, channels = hidden.shape
    return plain_call(
        decode_kernel,
        "decode",
        [jax.ShapeDtypeStruct((1, share, channels), jnp.bfloat16)],
        2 * share * KT * channels * channels,
        (fade_count, hidden, tail, conv_w),
        [SMEM_SPEC],
    )[0]


def per_device(
    query, noisy_kv, clean_kv, causal_mask, step_index, finished, w_in, conv_w, fade_count
):
    steps, _, rows, columns = query.shape
    heads = columns // HD
    middle = (heads + 1) // 2 * HD
    row_count = steps * rows
    span = lax.axis_size("span")
    axes = ("mp", "seq")
    acc_shape = jax.ShapeDtypeStruct((heads, HD, row_count), jnp.float32)
    stat_shape = jax.ShapeDtypeStruct((heads, row_count), jnp.float32)
    pair_flops = 4 * row_count * rows * columns

    shift = [(place, place + 1) for place in range(span - 1)]
    if span == 4:
        near = send(clean_kv, [[(0, 2)], [(0, 1), (1, 2)]])
        filler = send(clean_kv, [[(2, 3)]] * 2)
    else:
        near = send(clean_kv, [shift] * 2)
    carry = plain_call(
        own_kernel,
        "own",
        [acc_shape, stat_shape, stat_shape],
        pair_flops,
        (step_index, query, noisy_kv),
        [SMEM_SPEC],
    )
    pieces = project(after(finished, carry[1]), w_in)
    parts = [pieces[0]] + [swap(p, axes, offset + 1) for offset, p in enumerate(pieces[1:])]
    if span == 4:
        direct = send(clean_kv, [[(1, 3)], [(0, 3)]])
    hidden, tail = gather(parts, rows)
    tail = hop(tail, "span", 1)
    if span == 4:
        near = after(near, carry[0], pieces[0])
        forwards = lax.axis_index("span") == 2
        passed = [jnp.where(forwards, near[which], clean_kv[which]) for which in range(2)]
        passed = [passed[0], passed[1][:, :, :middle], passed[1][:, :, middle:]]
        passed = [send(block, [shift, [(0, 2), (2, 3)]]) for block in passed]
        early = [
            [(near, [{2: 0}, {1: 0, 2: 1}]), (filler, [{3: 2}] * 2)],
            [(direct, [{3: 1}, {3: 0}])],
        ]
        keys, *values = passed
        last_plan = [{1: 0, 2: 1, 3: 0}, {2: 0, 3: 1}]
    else:
        ring = [near]
        for _ in range(2, span):
            ring.append(hop(ring[-1], "span", 1))
        early = [[(block, delivered(span, back + 1))] for back, block in enumerate(ring[:-1])]
        keys, values = ring[-1], ring[-1:] * 2
        last_plan = delivered(span, span - 1)
    for choice in early:
        carry = plain_call(
            functools.partial(mid_kernel, [plan for _, plan in choice]),
            "middle",
            [acc_shape, stat_shape, stat_shape],
            pair_flops,
            (step_index, causal_mask, query, *[block for block, _ in choice], *carry),
            [SMEM_SPEC] * 2,
        )
    acc, weights = plain_call(
        functools.partial(score_kernel, [last_plan]),
        "score",
        [acc_shape, jax.ShapeDtypeStruct((heads, rows, row_count), jnp.bfloat16)],
        pair_flops // 2,
        (step_index, causal_mask, query, keys, *carry),
        [SMEM_SPEC] * 2,
    )
    square_shape = jax.ShapeDtypeStruct((1, row_count), jnp.float32)
    front, squares = plain_call(
        functools.partial(average_kernel, 0, middle // HD),
        "average",
        [jax.ShapeDtypeStruct((steps, rows, middle), jnp.float32), square_shape],
        pair_flops // 4,
        (acc, weights, values[0]),
    )
    averaged, squares = plain_call(
        functools.partial(rest_kernel, middle // HD, heads),
        "rest",
        [jax.ShapeDtypeStruct((heads - middle // HD, HD, row_count), jnp.float32), square_shape],
        pair_flops // 4,
        (acc, weights, values[1], squares),
    )
    others = [swap(squares, axes, offset) for offset in range(2, lax.axis_size(axes))]
    back, squares = plain_call(
        turn_kernel,
        "turn",
        [jax.ShapeDtypeStruct((steps, rows, columns - middle), jnp.float32), square_shape],
        row_count * columns,
        (averaged, squares),
    )
    others.append(swap(squares, axes, 1))
    decoded = decode(after(hidden, back), tail, conv_w, fade_count)
    attended = plain_call(
        functools.partial(scale_kernel, columns * lax.axis_size(axes)),
        "scale",
        jax.ShapeDtypeStruct(query.shape, jnp.bfloat16),
        row_count * columns,
        (front, back, squares, *others),
        out_specs=HBM_SPEC,
        scratch=[
            pltpu.VMEM((steps, rows, columns), jnp.bfloat16),
            pltpu.SemaphoreType.DMA((steps,)),
        ],
    )
    return (attended, decoded)


def solution(mesh):
    placed = (
        P(None, ("groups", "span"), None, ("mp", "seq")),
        P(None, None, ("groups", "span"), None, ("mp", "seq")),
        P(None, ("groups", "span"), None, ("mp", "seq")),
        P("groups", None),
        P("groups", None),
        P(("groups", "span"), None, ("mp", "seq")),
        P(("mp", "seq"), None),
        P(),
        P(("groups", "span")),
    )
    return jax.shard_map(
        per_device,
        mesh=mesh,
        in_specs=placed,
        out_specs=(
            P(None, ("groups", "span"), None, ("mp", "seq")),
            P(("groups", "span"), ("mp", "seq"), None),
        ),
        check_vma=False,
    )
```

```python
import functools
import math

import jax
import jax.numpy as jnp
from jax import lax
from jax.experimental import pallas as pl
from jax.experimental.pallas import tpu as pltpu
from jax.sharding import PartitionSpec as P

FR = 6
HD = 128
KT = 3
FADE = 2
NSTEPS = 64
LOG2E = 1.4426950408889634
VMEM_LIMIT = 24 * 1024 * 1024
VMEM_ALL = 60 * 1024 * 1024

SMEM_SPEC = pl.BlockSpec(memory_space=pltpu.SMEM)
VMEM_SPEC = pl.BlockSpec(memory_space=pltpu.VMEM)
HBM_SPEC = pl.BlockSpec(memory_space=pltpu.HBM)


def cost(flops, nbytes):
    return pl.CostEstimate(flops=flops, bytes_accessed=nbytes, transcendentals=0)


def hop(value, axis, steps):
    count = lax.axis_size(axis)
    return lax.ppermute(value, axis, [(source, source + steps) for source in range(count - steps)])


def swap(value, axes, offset):
    count = lax.axis_size(axes)
    if count & (count - 1) == 0:
        pairs = [(source, source ^ offset) for source in range(count)]
    else:
        pairs = [(source, (source + offset) % count) for source in range(count)]
    return lax.ppermute(value, axes, pairs)


def target_of(axes, offset):
    count = lax.axis_size(axes)
    mine = lax.axis_index(axes)
    if count & (count - 1) == 0:
        return mine ^ offset
    return lax.rem(mine + offset, count)


def after(value, *earlier):
    return lax.optimization_barrier((value, *earlier))[0]


def nt_dot(left, right):
    return lax.dot_general(left, right, (((1,), (1,)), ((), ())), preferred_element_type=jnp.float32)


def tn_dot(left, right):
    return lax.dot_general(left, right, (((0,), (0,)), ((), ())), preferred_element_type=jnp.float32)


def nn_dot(left, right):
    return jnp.dot(left, right, preferred_element_type=jnp.float32)


def row_factors(step_ref, position, steps, rows):
    lane = lax.broadcasted_iota(jnp.int32, (1, steps * rows), 1)
    index = jnp.full(lane.shape, step_ref[position, 0], jnp.int32)
    for step in range(1, steps):
        index = jnp.where(lane >= step * rows, step_ref[position, step], index)
    fraction = 1.0 - index.astype(jnp.float32) / NSTEPS
    level = 3.0 * fraction / (1.0 + 2.0 * fraction)
    return (0.5 + level) * (LOG2E / math.sqrt(HD))


def lane_windows(steps, rows):
    total = steps * rows
    return [
        (step * rows // HD * HD, min(total, -(-(step + 1) * rows // HD) * HD))
        for step in range(steps)
    ]


def join_steps(pieces, windows, rows):
    total = windows[-1][1]
    tiles = []
    for first in range(0, total, HD):
        stop = min(first + HD, total)
        tile = None
        for step, (begin, end) in enumerate(windows):
            if begin <= first and stop <= end and step * rows < stop and first < (step + 1) * rows:
                part = pieces[step][:, first - begin : stop - begin]
                if tile is None:
                    tile = part
                else:
                    lane = lax.broadcasted_iota(jnp.int32, part.shape, 1) + first
                    tile = jnp.where(lane >= step * rows, part, tile)
        tiles.append(tile)
    return jnp.concatenate(tiles, 1)


def own_kernel(step_ref, q_ref, kv_ref, acc_ref, top_ref, total_ref):
    position = lax.axis_index("span")
    steps, _, rows, columns = q_ref.shape
    factors = row_factors(step_ref, position, steps, rows)
    windows = lane_windows(steps, rows)
    for head in range(columns // HD):
        cut = slice(head * HD, (head + 1) * HD)
        queries = q_ref[:, 0, :, cut].reshape(steps * rows, HD)
        scores = join_steps(
            [nt_dot(kv_ref[s, 0, 0, :, cut], queries[a:b]) for s, (a, b) in enumerate(windows)],
            windows,
            rows,
        )
        scores = scores * factors
        top = jnp.max(scores, axis=0, keepdims=True)
        weights = jnp.exp2(scores - top)
        rounded = weights.astype(jnp.bfloat16)
        acc_ref[head] = join_steps(
            [tn_dot(kv_ref[s, 1, 0, :, cut], rounded[:, a:b]) for s, (a, b) in enumerate(windows)],
            windows,
            rows,
        )
        top_ref[head : head + 1] = top
        total_ref[head : head + 1] = jnp.sum(weights, axis=0, keepdims=True)


def absorb(queries, keys, values, factors, acc, top, total):
    scores = nt_dot(keys, queries) * factors
    newest = jnp.maximum(top, jnp.max(scores, axis=0, keepdims=True))
    weights = jnp.exp2(scores - newest)
    shrink = jnp.exp2(top - newest)
    total = total * shrink + jnp.sum(weights, axis=0, keepdims=True)
    acc = acc * shrink + tn_dot(values, weights.astype(jnp.bfloat16))
    return acc, newest, total


def visible(mask_ref, position, blocks):
    seen = False
    for place, block in blocks.items():
        seen = seen | ((position == place) & (mask_ref[place, block] > 0))
    return seen


def half(ref, which, cut):
    return ref[which, 0, :, cut] if len(ref.shape) == 4 else ref[0, :, cut]


def mid_kernel(plan, step_ref, mask_ref, q_ref, *refs):
    block_refs, (acc_in, top_in, total_in, acc_ref, top_ref, total_ref) = refs[:-6], refs[-6:]
    position = lax.axis_index("span")
    steps, _, rows, columns = q_ref.shape
    seen = visible(mask_ref, position, plan)

    @pl.when(seen)
    def _():
        factors = row_factors(step_ref, position, steps, rows)
        for head in range(columns // HD):
            cut = slice(head * HD, (head + 1) * HD)
            queries = q_ref[:, 0, :, cut].reshape(steps * rows, HD)
            acc, top, total = absorb(
                queries,
                half(block_refs[0], 0, cut),
                half(block_refs[-1], 1, cut),
                factors,
                acc_in[head],
                top_in[head : head + 1],
                total_in[head : head + 1],
            )
            acc_ref[head] = acc
            top_ref[head : head + 1] = top
            total_ref[head : head + 1] = total

    @pl.when(jnp.logical_not(seen))
    def _():
        acc_ref[...] = acc_in[...]
        top_ref[...] = top_in[...]
        total_ref[...] = total_in[...]


def score_kernel(plans, step_ref, mask_ref, q_ref, *refs):
    key_refs, (acc_in, top_in, total_in, acc_ref, w_ref) = refs[:-5], refs[-5:]
    position = lax.axis_index("span")
    steps, _, rows, columns = q_ref.shape

    def finish(key_ref):
        factors = row_factors(step_ref, position, steps, rows)
        for head in range(columns // HD):
            cut = slice(head * HD, (head + 1) * HD)
            queries = q_ref[:, 0, :, cut].reshape(steps * rows, HD)
            scores = nt_dot(half(key_ref, 0, cut), queries) * factors
            top = top_in[head : head + 1]
            newest = jnp.maximum(top, jnp.max(scores, axis=0, keepdims=True))
            weights = jnp.exp2(scores - newest)
            shrink = jnp.exp2(top - newest)
            total = total_in[head : head + 1] * shrink + jnp.sum(weights, axis=0, keepdims=True)
            inverse = 1.0 / total
            w_ref[head] = (weights * inverse).astype(jnp.bfloat16)
            acc_ref[head] = acc_in[head] * (shrink * inverse)

    rest = True
    for plan, key_ref in zip(plans, key_refs):
        seen = visible(mask_ref, position, plan)
        rest = jnp.logical_and(rest, jnp.logical_not(seen))
        pl.when(seen)(functools.partial(finish, key_ref))

    @pl.when(rest)
    def _():
        w_ref[...] = jnp.zeros_like(w_ref)
        for head in range(columns // HD):
            acc_ref[head] = acc_in[head] * (1.0 / total_in[head : head + 1])


def average_head(head, acc_ref, w_ref, value_ref, first):
    if value_ref.shape[-1] == acc_ref.shape[0] * HD:
        first = 0
    cut = slice((head - first) * HD, (head - first + 1) * HD)
    return acc_ref[head] + tn_dot(half(value_ref, 1, cut), w_ref[head])


def average_kernel(begin, end, acc_ref, w_ref, value_ref, average_ref, square_ref):
    squares = jnp.zeros(square_ref.shape, jnp.float32)
    for head in range(begin, end):
        average = average_head(head, acc_ref, w_ref, value_ref, begin)
        squares = squares + jnp.sum(average * average, axis=0, keepdims=True)
        average_ref[:, :, (head - begin) * HD : (head - begin + 1) * HD] = average.T.reshape(
            average_ref.shape[:2] + (HD,)
        )
    square_ref[...] = squares


def rest_kernel(begin, end, acc_ref, w_ref, value_ref, before_ref, average_ref, square_ref):
    squares = before_ref[...]
    for head in range(begin, end):
        average = average_head(head, acc_ref, w_ref, value_ref, begin)
        squares = squares + jnp.sum(average * average, axis=0, keepdims=True)
        average_ref[head - begin] = average
    square_ref[...] = squares


def turn_kernel(in_ref, square_in, out_ref, square_ref):
    steps, rows, _ = out_ref.shape
    for head in range(in_ref.shape[0]):
        out_ref[:, :, head * HD : (head + 1) * HD] = in_ref[head].T.reshape(steps, rows, HD)
    square_ref[...] = square_in[...]


def scale_kernel(width, front_ref, back_ref, *refs):
    part_refs, (out_hbm, out_ref, sem) = refs[:-3], refs[-3:]
    total = part_refs[0][...]
    for ref in part_refs[1:]:
        total = total + ref[...]
    inverse = lax.rsqrt(total / width + 1e-06)
    steps, rows, columns = out_ref.shape
    copies = []
    for step in range(steps):
        own = inverse[:, step * rows : (step + 1) * rows]
        factor = jnp.broadcast_to(own, (HD, rows)).T
        place = 0
        for ref in (front_ref, back_ref):
            for first in range(0, ref.shape[2], HD):
                average = ref[step, :, first : first + HD]
                out_ref[step, :, place : place + HD] = (average * factor).astype(jnp.bfloat16)
                place += HD
        copies.append(pltpu.make_async_copy(out_ref.at[step], out_hbm.at[step, 0], sem.at[step]))
        copies[-1].start()
    for copy in copies:
        copy.wait()


def send(value, pairs):
    return lax.ppermute(value, "span", pairs)


def delivered(span, back):
    return {place: place - back for place in range(back, span)}


def plain_call(kernel, name, out_shape, flops, operands, in_specs=(), out_specs=None, scratch=(), limit=VMEM_LIMIT):
    nbytes = sum(math.prod(o.shape) * o.dtype.itemsize for o in operands)
    if out_specs is None:
        out_specs = [VMEM_SPEC] * len(out_shape)
    return pl.pallas_call(
        kernel,
        in_specs=list(in_specs) + [VMEM_SPEC] * (len(operands) - len(in_specs)),
        out_specs=out_specs,
        out_shape=out_shape,
        scratch_shapes=list(scratch),
        compiler_params=pltpu.CompilerParams(vmem_limit_bytes=limit),
        cost_estimate=cost(flops, nbytes),
        name=name,
    )(*operands)


def picker(shape, wanted):
    row = lax.broadcasted_iota(jnp.int32, shape, 0)
    column = lax.broadcasted_iota(jnp.int32, shape, 1)
    return jnp.where(column == wanted(row), 1.0, 0.0).astype(jnp.bfloat16)


def project_kernel(axes, x_hbm, w_hbm, *refs):
    out_refs, (x_ref, w_ref, x_sem, w_sem) = refs[:-4], refs[-4:]
    rows, depth = x_ref.shape
    share = out_refs[0].shape[0]
    x_copy = pltpu.make_async_copy(x_hbm.at[0], x_ref, x_sem)
    x_copy.start()
    copies = []
    for place, first in enumerate(range(0, depth, 2 * HD)):
        cut = slice(first, min(first + 2 * HD, depth))
        copies.append((cut, pltpu.make_async_copy(w_hbm.at[cut], w_ref.at[cut], w_sem.at[place])))
        copies[-1][1].start()
    total = jnp.zeros((rows, w_ref.shape[1]), jnp.float32)
    x_copy.wait()
    for cut, w_copy in copies:
        w_copy.wait()
        total = total + nn_dot(x_ref[:, cut], w_ref[cut])
    projected = total.astype(jnp.bfloat16)
    for offset, out_ref in enumerate(out_refs):
        first = target_of(axes, offset) * share
        chosen = picker((share, rows), lambda row: row + first)
        out_ref[...] = nn_dot(chosen, projected).astype(jnp.bfloat16)


def gather_kernel(*refs):
    hidden_ref, tail_ref = refs[-2:]
    total = refs[0][...].astype(jnp.float32)
    for ref in refs[1:-2]:
        total = total + ref[...].astype(jnp.float32)
    hidden = total.astype(jnp.bfloat16)
    hidden_ref[...] = hidden
    kept = KT - 1 + FADE
    shape = (tail_ref.shape[0], hidden.shape[0])
    chosen = picker(shape, lambda row: row // kept * FR + FR - kept + row % kept)
    tail_ref[...] = nn_dot(chosen, hidden).astype(jnp.bfloat16)


def decode_kernel(fade_ref, hidden_ref, tail_ref, conv_ref, out_ref):
    position = lax.axis_index("span")
    share = hidden_ref.shape[0]
    spatial = share // FR
    kept = KT - 1 + FADE
    wide = FADE + FR
    hidden, tail = hidden_ref[...], tail_ref[...]
    mixed = jnp.zeros((spatial * wide, out_ref.shape[2]), jnp.float32)
    for tap in range(KT):
        def from_tail(row):
            place = row % wide + KT - 1 - tap
            return jnp.where(place < kept, row // wide * kept + place, -1)

        def from_hidden(row):
            place = row % wide + KT - 1 - tap
            return jnp.where(place >= kept, row // wide * FR + place - kept, -1)

        window = nn_dot(picker((spatial * wide, tail.shape[0]), from_tail), tail)
        window = window + nn_dot(picker((spatial * wide, share), from_hidden), hidden)
        mixed = mixed + nn_dot(window.astype(jnp.bfloat16), conv_ref[tap])
    frames = (mixed * jax.nn.sigmoid(mixed)).astype(jnp.bfloat16)
    fade = fade_ref[0]
    shape = (share, spatial * wide)
    current = nn_dot(picker(shape, lambda row: row // FR * wide + FADE + row % FR), frames)

    def faded(row):
        return jnp.where(row % FR < fade, row // FR * wide + FADE - fade + row % FR, -1)

    previous = nn_dot(picker(shape, faded), frames)
    frame = lax.broadcasted_iota(jnp.int32, (share, out_ref.shape[2]), 0) % FR
    fade_float = jnp.full(frame.shape, fade, jnp.int32).astype(jnp.float32)
    weight = (frame.astype(jnp.float32) + 1.0) / (fade_float + 1.0)
    weight = jnp.where((frame < fade) & (position > 0), weight, 1.0)
    out_ref[0] = (weight * current + (1.0 - weight) * previous).astype(jnp.bfloat16)


def project(finished, w_in):
    axes = ("mp", "seq")
    parts = lax.axis_size(axes)
    _, rows, depth = finished.shape
    channels = w_in.shape[1]
    chunks = -(-depth // (2 * HD))
    return plain_call(
        functools.partial(project_kernel, axes),
        "project",
        [jax.ShapeDtypeStruct((rows // parts, channels), jnp.bfloat16)] * parts,
        2 * rows * depth * channels,
        (finished, w_in),
        [HBM_SPEC] * 2,
        scratch=[
            pltpu.VMEM((rows, depth), jnp.bfloat16),
            pltpu.VMEM((depth, channels), jnp.bfloat16),
            pltpu.SemaphoreType.DMA,
            pltpu.SemaphoreType.DMA((chunks,)),
        ],
        limit=VMEM_ALL,
    )


def gather(parts, rows):
    share, channels = parts[0].shape
    tail_rows = share // FR * (KT - 1 + FADE)
    return plain_call(
        gather_kernel,
        "gather",
        [jax.ShapeDtypeStruct((count, channels), jnp.bfloat16) for count in (share, tail_rows)],
        rows * channels,
        parts,
    )


def decode(hidden, tail, conv_w, fade_count):
    share, channels = hidden.shape
    return plain_call(
        decode_kernel,
        "decode",
        [jax.ShapeDtypeStruct((1, share, channels), jnp.bfloat16)],
        2 * share * KT * channels * channels,
        (fade_count, hidden, tail, conv_w),
        [SMEM_SPEC],
    )[0]


def per_device(
    query, noisy_kv, clean_kv, causal_mask, step_index, finished, w_in, conv_w, fade_count
):
    steps, _, rows, columns = query.shape
    heads = columns // HD
    middle = -(-2 * heads // 3) * HD
    row_count = steps * rows
    span = lax.axis_size("span")
    axes = ("mp", "seq")
    acc_shape = jax.ShapeDtypeStruct((heads, HD, row_count), jnp.float32)
    stat_shape = jax.ShapeDtypeStruct((heads, row_count), jnp.float32)
    pair_flops = 4 * row_count * rows * columns

    first_pairs = [(0, 2), (2, 3)] if span == 4 else [(c, c + 1) for c in range(span - 1)]
    near = send(clean_kv, first_pairs)
    pieces = project(finished, w_in)
    parts = [pieces[0]] + [swap(p, axes, offset + 1) for offset, p in enumerate(pieces[1:])]
    if span == 4:
        direct = send(clean_kv, [(1, 3)])
    carry = plain_call(
        own_kernel,
        "own",
        [acc_shape, stat_shape, stat_shape],
        pair_flops,
        (step_index, query, noisy_kv),
        [SMEM_SPEC],
    )
    hidden, tail = gather(parts, rows)
    tail = hop(tail, "span", 1)
    if span == 4:
        near = after(near, carry[0], hidden)
        forwards = lax.axis_index("span") == 2
        passed = [jnp.where(forwards, near[which], clean_kv[which]) for which in range(2)]
        passed = [passed[0], passed[1][:, :, :middle], passed[1][:, :, middle:]]
        passed = [hop(block, "span", 1) for block in passed]
        early = [(near, {2: 0, 3: 2}), (direct, {3: 1})]
        keys, *values = passed
        last_plan = {1: 0, 2: 1, 3: 0}
    else:
        ring = [near]
        for _ in range(2, span):
            ring.append(hop(ring[-1], "span", 1))
        early = [(block, delivered(span, back + 1)) for back, block in enumerate(ring[:-1])]
        keys, values = ring[-1], ring[-1:] * 2
        last_plan = delivered(span, span - 1)
    for block, plan in early:
        carry = plain_call(
            functools.partial(mid_kernel, plan),
            "middle",
            [acc_shape, stat_shape, stat_shape],
            pair_flops,
            (step_index, causal_mask, query, block, *carry),
            [SMEM_SPEC] * 2,
        )
    acc, weights = plain_call(
        functools.partial(score_kernel, [last_plan]),
        "score",
        [acc_shape, jax.ShapeDtypeStruct((heads, rows, row_count), jnp.bfloat16)],
        pair_flops // 2,
        (step_index, causal_mask, query, keys, *carry),
        [SMEM_SPEC] * 2,
    )
    square_shape = jax.ShapeDtypeStruct((1, row_count), jnp.float32)
    front, squares = plain_call(
        functools.partial(average_kernel, 0, middle // HD),
        "average",
        [jax.ShapeDtypeStruct((steps, rows, middle), jnp.float32), square_shape],
        pair_flops // 4,
        (acc, weights, values[0]),
    )
    averaged, squares = plain_call(
        functools.partial(rest_kernel, middle // HD, heads),
        "rest",
        [jax.ShapeDtypeStruct((heads - middle // HD, HD, row_count), jnp.float32), square_shape],
        pair_flops // 4,
        (acc, weights, values[1], squares),
    )
    others = [swap(squares, axes, offset) for offset in range(2, lax.axis_size(axes))]
    back, squares = plain_call(
        turn_kernel,
        "turn",
        [jax.ShapeDtypeStruct((steps, rows, columns - middle), jnp.float32), square_shape],
        row_count * columns,
        (averaged, squares),
    )
    others.append(swap(squares, axes, 1))
    decoded = decode(after(hidden, back), tail, conv_w, fade_count)
    attended = plain_call(
        functools.partial(scale_kernel, columns * lax.axis_size(axes)),
        "scale",
        jax.ShapeDtypeStruct(query.shape, jnp.bfloat16),
        row_count * columns,
        (front, back, squares, *others),
        out_specs=HBM_SPEC,
        scratch=[
            pltpu.VMEM((steps, rows, columns), jnp.bfloat16),
            pltpu.SemaphoreType.DMA((steps,)),
        ],
    )
    return (attended, decoded)


def solution(mesh):
    placed = (
        P(None, ("groups", "span"), None, ("mp", "seq")),
        P(None, None, ("groups", "span"), None, ("mp", "seq")),
        P(None, ("groups", "span"), None, ("mp", "seq")),
        P("groups", None),
        P("groups", None),
        P(("groups", "span"), None, ("mp", "seq")),
        P(("mp", "seq"), None),
        P(),
        P(("groups", "span")),
    )
    return jax.shard_map(
        per_device,
        mesh=mesh,
        in_specs=placed,
        out_specs=(
            P(None, ("groups", "span"), None, ("mp", "seq")),
            P(("groups", "span"), ("mp", "seq"), None),
        ),
        check_vma=False,
    )
```

```python
import functools
import math

import jax
import jax.numpy as jnp
from jax import lax
from jax.experimental import pallas as pl
from jax.experimental.pallas import tpu as pltpu
from jax.sharding import PartitionSpec as P

FR = 6
HD = 128
KT = 3
FADE = 2
NSTEPS = 64
LOG2E = 1.4426950408889634
VMEM_LIMIT = 24 * 1024 * 1024
VMEM_ALL = 60 * 1024 * 1024

SMEM_SPEC = pl.BlockSpec(memory_space=pltpu.SMEM)
VMEM_SPEC = pl.BlockSpec(memory_space=pltpu.VMEM)
HBM_SPEC = pl.BlockSpec(memory_space=pltpu.HBM)


def cost(flops, nbytes):
    return pl.CostEstimate(flops=flops, bytes_accessed=nbytes, transcendentals=0)


def hop(value, axis, steps):
    count = lax.axis_size(axis)
    return lax.ppermute(value, axis, [(source, source + steps) for source in range(count - steps)])


def swap(value, axes, offset):
    count = lax.axis_size(axes)
    if count & (count - 1) == 0:
        pairs = [(source, source ^ offset) for source in range(count)]
    else:
        pairs = [(source, (source + offset) % count) for source in range(count)]
    return lax.ppermute(value, axes, pairs)


def target_of(axes, offset):
    count = lax.axis_size(axes)
    mine = lax.axis_index(axes)
    if count & (count - 1) == 0:
        return mine ^ offset
    return lax.rem(mine + offset, count)


def after(value, *earlier):
    return lax.optimization_barrier((value, *earlier))[0]


def nt_dot(left, right):
    return lax.dot_general(left, right, (((1,), (1,)), ((), ())), preferred_element_type=jnp.float32)


def tn_dot(left, right):
    return lax.dot_general(left, right, (((0,), (0,)), ((), ())), preferred_element_type=jnp.float32)


def nn_dot(left, right):
    return jnp.dot(left, right, preferred_element_type=jnp.float32)


def row_factors(step_ref, position, steps, rows):
    lane = lax.broadcasted_iota(jnp.int32, (1, steps * rows), 1)
    index = jnp.full(lane.shape, step_ref[position, 0], jnp.int32)
    for step in range(1, steps):
        index = jnp.where(lane >= step * rows, step_ref[position, step], index)
    fraction = 1.0 - index.astype(jnp.float32) / NSTEPS
    level = 3.0 * fraction / (1.0 + 2.0 * fraction)
    return (0.5 + level) * (LOG2E / math.sqrt(HD))


def lane_windows(steps, rows):
    total = steps * rows
    return [
        (step * rows // HD * HD, min(total, -(-(step + 1) * rows // HD) * HD))
        for step in range(steps)
    ]


def join_steps(pieces, windows, rows):
    total = windows[-1][1]
    tiles = []
    for first in range(0, total, HD):
        stop = min(first + HD, total)
        tile = None
        for step, (begin, end) in enumerate(windows):
            if begin <= first and stop <= end and step * rows < stop and first < (step + 1) * rows:
                part = pieces[step][:, first - begin : stop - begin]
                if tile is None:
                    tile = part
                else:
                    lane = lax.broadcasted_iota(jnp.int32, part.shape, 1) + first
                    tile = jnp.where(lane >= step * rows, part, tile)
        tiles.append(tile)
    return jnp.concatenate(tiles, 1)


def own_kernel(step_ref, q_ref, kv_ref, acc_ref, top_ref, total_ref):
    position = lax.axis_index("span")
    steps, _, rows, columns = q_ref.shape
    factors = row_factors(step_ref, position, steps, rows)
    windows = lane_windows(steps, rows)
    for head in range(columns // HD):
        cut = slice(head * HD, (head + 1) * HD)
        queries = q_ref[:, 0, :, cut].reshape(steps * rows, HD)
        scores = join_steps(
            [nt_dot(kv_ref[s, 0, 0, :, cut], queries[a:b]) for s, (a, b) in enumerate(windows)],
            windows,
            rows,
        )
        scores = scores * factors
        top = jnp.max(scores, axis=0, keepdims=True)
        weights = jnp.exp2(scores - top)
        rounded = weights.astype(jnp.bfloat16)
        acc_ref[head] = join_steps(
            [tn_dot(kv_ref[s, 1, 0, :, cut], rounded[:, a:b]) for s, (a, b) in enumerate(windows)],
            windows,
            rows,
        )
        top_ref[head : head + 1] = top
        total_ref[head : head + 1] = jnp.sum(weights, axis=0, keepdims=True)


def absorb(queries, keys, values, factors, acc, top, total):
    scores = nt_dot(keys, queries) * factors
    newest = jnp.maximum(top, jnp.max(scores, axis=0, keepdims=True))
    weights = jnp.exp2(scores - newest)
    shrink = jnp.exp2(top - newest)
    total = total * shrink + jnp.sum(weights, axis=0, keepdims=True)
    acc = acc * shrink + tn_dot(values, weights.astype(jnp.bfloat16))
    return acc, newest, total


def visible(mask_ref, position, blocks):
    seen = False
    for place, block in blocks.items():
        seen = seen | ((position == place) & (mask_ref[place, block] > 0))
    return seen


def half(ref, which, cut):
    return ref[which, 0, :, cut] if len(ref.shape) == 4 else ref[0, :, cut]


def mid_kernel(plan, step_ref, mask_ref, q_ref, *refs):
    block_refs, (acc_in, top_in, total_in, acc_ref, top_ref, total_ref) = refs[:-6], refs[-6:]
    position = lax.axis_index("span")
    steps, _, rows, columns = q_ref.shape
    seen = visible(mask_ref, position, plan)

    @pl.when(seen)
    def _():
        factors = row_factors(step_ref, position, steps, rows)
        for head in range(columns // HD):
            cut = slice(head * HD, (head + 1) * HD)
            queries = q_ref[:, 0, :, cut].reshape(steps * rows, HD)
            acc, top, total = absorb(
                queries,
                half(block_refs[0], 0, cut),
                half(block_refs[-1], 1, cut),
                factors,
                acc_in[head],
                top_in[head : head + 1],
                total_in[head : head + 1],
            )
            acc_ref[head] = acc
            top_ref[head : head + 1] = top
            total_ref[head : head + 1] = total

    @pl.when(jnp.logical_not(seen))
    def _():
        acc_ref[...] = acc_in[...]
        top_ref[...] = top_in[...]
        total_ref[...] = total_in[...]


def score_kernel(plans, step_ref, mask_ref, q_ref, *refs):
    key_refs, (acc_in, top_in, total_in, acc_ref, w_ref) = refs[:-5], refs[-5:]
    position = lax.axis_index("span")
    steps, _, rows, columns = q_ref.shape

    def finish(key_ref):
        factors = row_factors(step_ref, position, steps, rows)
        for head in range(columns // HD):
            cut = slice(head * HD, (head + 1) * HD)
            queries = q_ref[:, 0, :, cut].reshape(steps * rows, HD)
            scores = nt_dot(half(key_ref, 0, cut), queries) * factors
            top = top_in[head : head + 1]
            newest = jnp.maximum(top, jnp.max(scores, axis=0, keepdims=True))
            weights = jnp.exp2(scores - newest)
            shrink = jnp.exp2(top - newest)
            total = total_in[head : head + 1] * shrink + jnp.sum(weights, axis=0, keepdims=True)
            inverse = 1.0 / total
            w_ref[head] = (weights * inverse).astype(jnp.bfloat16)
            acc_ref[head] = acc_in[head] * (shrink * inverse)

    rest = True
    for plan, key_ref in zip(plans, key_refs):
        seen = visible(mask_ref, position, plan)
        rest = jnp.logical_and(rest, jnp.logical_not(seen))
        pl.when(seen)(functools.partial(finish, key_ref))

    @pl.when(rest)
    def _():
        w_ref[...] = jnp.zeros_like(w_ref)
        for head in range(columns // HD):
            acc_ref[head] = acc_in[head] * (1.0 / total_in[head : head + 1])


def average_head(head, acc_ref, w_ref, value_ref, first):
    if value_ref.shape[-1] == acc_ref.shape[0] * HD:
        first = 0
    cut = slice((head - first) * HD, (head - first + 1) * HD)
    return acc_ref[head] + tn_dot(half(value_ref, 1, cut), w_ref[head])


def average_kernel(begin, end, acc_ref, w_ref, value_ref, average_ref, square_ref):
    squares = jnp.zeros(square_ref.shape, jnp.float32)
    for head in range(begin, end):
        average = average_head(head, acc_ref, w_ref, value_ref, begin)
        squares = squares + jnp.sum(average * average, axis=0, keepdims=True)
        average_ref[:, :, (head - begin) * HD : (head - begin + 1) * HD] = average.T.reshape(
            average_ref.shape[:2] + (HD,)
        )
    square_ref[...] = squares


def rest_kernel(begin, end, acc_ref, w_ref, value_ref, before_ref, average_ref, square_ref):
    squares = before_ref[...]
    for head in range(begin, end):
        average = average_head(head, acc_ref, w_ref, value_ref, begin)
        squares = squares + jnp.sum(average * average, axis=0, keepdims=True)
        average_ref[head - begin] = average
    square_ref[...] = squares


def turn_kernel(in_ref, *refs):
    square_refs, (out_ref, square_ref) = refs[:-2], refs[-2:]
    steps, rows, _ = out_ref.shape
    squares = square_refs[0][...]
    for ref in square_refs[1:]:
        squares = squares + ref[...]
    square_ref[...] = squares
    for head in range(in_ref.shape[0]):
        out_ref[:, :, head * HD : (head + 1) * HD] = in_ref[head].T.reshape(steps, rows, HD)


def scale_kernel(width, front_ref, back_ref, *refs):
    part_refs, (out_hbm, out_ref, sem) = refs[:-3], refs[-3:]
    total = part_refs[0][...]
    for ref in part_refs[1:]:
        total = total + ref[...]
    inverse = lax.rsqrt(total / width + 1e-06)
    steps, rows, columns = out_ref.shape
    copies = []
    for step in range(steps):
        own = inverse[:, step * rows : (step + 1) * rows]
        factor = jnp.broadcast_to(own, (HD, rows)).T
        place = 0
        for ref in (front_ref, back_ref):
            for first in range(0, ref.shape[2], HD):
                average = ref[step, :, first : first + HD]
                out_ref[step, :, place : place + HD] = (average * factor).astype(jnp.bfloat16)
                place += HD
        copies.append(pltpu.make_async_copy(out_ref.at[step], out_hbm.at[step, 0], sem.at[step]))
        copies[-1].start()
    for copy in copies:
        copy.wait()


def send(value, pairs):
    return lax.ppermute(value, "span", pairs)


def delivered(span, back):
    return {place: place - back for place in range(back, span)}


def plain_call(kernel, name, out_shape, flops, operands, in_specs=(), out_specs=None, scratch=(), limit=VMEM_LIMIT):
    nbytes = sum(math.prod(o.shape) * o.dtype.itemsize for o in operands)
    if out_specs is None:
        out_specs = [VMEM_SPEC] * len(out_shape)
    return pl.pallas_call(
        kernel,
        in_specs=list(in_specs) + [VMEM_SPEC] * (len(operands) - len(in_specs)),
        out_specs=out_specs,
        out_shape=out_shape,
        scratch_shapes=list(scratch),
        compiler_params=pltpu.CompilerParams(vmem_limit_bytes=limit),
        cost_estimate=cost(flops, nbytes),
        name=name,
    )(*operands)


def picker(shape, wanted):
    row = lax.broadcasted_iota(jnp.int32, shape, 0)
    column = lax.broadcasted_iota(jnp.int32, shape, 1)
    return jnp.where(column == wanted(row), 1.0, 0.0).astype(jnp.bfloat16)


def project_kernel(axes, x_hbm, w_hbm, *refs):
    out_refs, (x_ref, w_ref, x_sem, w_sem) = refs[:-4], refs[-4:]
    rows, depth = x_ref.shape
    share = out_refs[0].shape[0]
    x_copy = pltpu.make_async_copy(x_hbm.at[0], x_ref, x_sem)
    x_copy.start()
    copies = []
    for place, first in enumerate(range(0, depth, 2 * HD)):
        cut = slice(first, min(first + 2 * HD, depth))
        copies.append((cut, pltpu.make_async_copy(w_hbm.at[cut], w_ref.at[cut], w_sem.at[place])))
        copies[-1][1].start()
    total = jnp.zeros((rows, w_ref.shape[1]), jnp.float32)
    x_copy.wait()
    for cut, w_copy in copies:
        w_copy.wait()
        total = total + nn_dot(x_ref[:, cut], w_ref[cut])
    projected = total.astype(jnp.bfloat16)
    for offset, out_ref in enumerate(out_refs):
        first = target_of(axes, offset) * share
        chosen = picker((share, rows), lambda row: row + first)
        out_ref[...] = nn_dot(chosen, projected).astype(jnp.bfloat16)


def gather_kernel(*refs):
    hidden_ref, tail_ref = refs[-2:]
    total = refs[0][...].astype(jnp.float32)
    for ref in refs[1:-2]:
        total = total + ref[...].astype(jnp.float32)
    hidden = total.astype(jnp.bfloat16)
    hidden_ref[...] = hidden
    kept = KT - 1 + FADE
    shape = (tail_ref.shape[0], hidden.shape[0])
    chosen = picker(shape, lambda row: row // kept * FR + FR - kept + row % kept)
    tail_ref[...] = nn_dot(chosen, hidden).astype(jnp.bfloat16)


def decode_kernel(fade_ref, hidden_ref, tail_ref, conv_ref, out_ref):
    position = lax.axis_index("span")
    share = hidden_ref.shape[0]
    spatial = share // FR
    kept = KT - 1 + FADE
    wide = FADE + FR
    hidden, tail = hidden_ref[...], tail_ref[...]
    mixed = jnp.zeros((spatial * wide, out_ref.shape[2]), jnp.float32)
    for tap in range(KT):
        def from_tail(row):
            place = row % wide + KT - 1 - tap
            return jnp.where(place < kept, row // wide * kept + place, -1)

        def from_hidden(row):
            place = row % wide + KT - 1 - tap
            return jnp.where(place >= kept, row // wide * FR + place - kept, -1)

        window = nn_dot(picker((spatial * wide, tail.shape[0]), from_tail), tail)
        window = window + nn_dot(picker((spatial * wide, share), from_hidden), hidden)
        mixed = mixed + nn_dot(window.astype(jnp.bfloat16), conv_ref[tap])
    frames = (mixed * jax.nn.sigmoid(mixed)).astype(jnp.bfloat16)
    fade = fade_ref[0]
    shape = (share, spatial * wide)
    current = nn_dot(picker(shape, lambda row: row // FR * wide + FADE + row % FR), frames)

    def faded(row):
        return jnp.where(row % FR < fade, row // FR * wide + FADE - fade + row % FR, -1)

    previous = nn_dot(picker(shape, faded), frames)
    frame = lax.broadcasted_iota(jnp.int32, (share, out_ref.shape[2]), 0) % FR
    fade_float = jnp.full(frame.shape, fade, jnp.int32).astype(jnp.float32)
    weight = (frame.astype(jnp.float32) + 1.0) / (fade_float + 1.0)
    weight = jnp.where((frame < fade) & (position > 0), weight, 1.0)
    out_ref[0] = (weight * current + (1.0 - weight) * previous).astype(jnp.bfloat16)


def project(finished, w_in):
    axes = ("mp", "seq")
    parts = lax.axis_size(axes)
    _, rows, depth = finished.shape
    channels = w_in.shape[1]
    chunks = -(-depth // (2 * HD))
    return plain_call(
        functools.partial(project_kernel, axes),
        "project",
        [jax.ShapeDtypeStruct((rows // parts, channels), jnp.bfloat16)] * parts,
        2 * rows * depth * channels,
        (finished, w_in),
        [HBM_SPEC] * 2,
        scratch=[
            pltpu.VMEM((rows, depth), jnp.bfloat16),
            pltpu.VMEM((depth, channels), jnp.bfloat16),
            pltpu.SemaphoreType.DMA,
            pltpu.SemaphoreType.DMA((chunks,)),
        ],
        limit=VMEM_ALL,
    )


def gather(parts, rows):
    share, channels = parts[0].shape
    tail_rows = share // FR * (KT - 1 + FADE)
    return plain_call(
        gather_kernel,
        "gather",
        [jax.ShapeDtypeStruct((count, channels), jnp.bfloat16) for count in (share, tail_rows)],
        rows * channels,
        parts,
    )


def decode(hidden, tail, conv_w, fade_count):
    share, channels = hidden.shape
    return plain_call(
        decode_kernel,
        "decode",
        [jax.ShapeDtypeStruct((1, share, channels), jnp.bfloat16)],
        2 * share * KT * channels * channels,
        (fade_count, hidden, tail, conv_w),
        [SMEM_SPEC],
    )[0]


def per_device(
    query, noisy_kv, clean_kv, causal_mask, step_index, finished, w_in, conv_w, fade_count
):
    steps, _, rows, columns = query.shape
    heads = columns // HD
    middle = (heads - max(1, heads // 3)) * HD
    row_count = steps * rows
    span = lax.axis_size("span")
    axes = ("mp", "seq")
    acc_shape = jax.ShapeDtypeStruct((heads, HD, row_count), jnp.float32)
    stat_shape = jax.ShapeDtypeStruct((heads, row_count), jnp.float32)
    pair_flops = 4 * row_count * rows * columns

    first_pairs = [(0, 2), (2, 3)] if span == 4 else [(c, c + 1) for c in range(span - 1)]
    near = send(clean_kv, first_pairs)
    pieces = project(finished, w_in)
    parts = [pieces[0]] + [swap(p, axes, offset + 1) for offset, p in enumerate(pieces[1:])]
    if span == 4:
        direct = send(clean_kv, [(1, 3)])
    carry = plain_call(
        own_kernel,
        "own",
        [acc_shape, stat_shape, stat_shape],
        pair_flops,
        (step_index, query, noisy_kv),
        [SMEM_SPEC],
    )
    hidden, tail = gather(parts, rows)
    tail = hop(tail, "span", 1)
    if span == 4:
        near = after(near, carry[0], hidden)
        forwards = lax.axis_index("span") == 2
        passed = [jnp.where(forwards, near[which], clean_kv[which]) for which in range(2)]
        passed = [passed[0], passed[1][:, :, :middle], passed[1][:, :, middle:]]
        passed = [hop(block, "span", 1) for block in passed]
        early = [(near, {2: 0, 3: 2}), (direct, {3: 1})]
        keys, *values = passed
        last_plan = {1: 0, 2: 1, 3: 0}
    else:
        ring = [near]
        for _ in range(2, span):
            ring.append(hop(ring[-1], "span", 1))
        early = [(block, delivered(span, back + 1)) for back, block in enumerate(ring[:-1])]
        keys, values = ring[-1], ring[-1:] * 2
        last_plan = delivered(span, span - 1)
    for block, plan in early:
        carry = plain_call(
            functools.partial(mid_kernel, plan),
            "middle",
            [acc_shape, stat_shape, stat_shape],
            pair_flops,
            (step_index, causal_mask, query, block, *carry),
            [SMEM_SPEC] * 2,
        )
    acc, weights = plain_call(
        functools.partial(score_kernel, [last_plan]),
        "score",
        [acc_shape, jax.ShapeDtypeStruct((heads, rows, row_count), jnp.bfloat16)],
        pair_flops // 2,
        (step_index, causal_mask, query, keys, *carry),
        [SMEM_SPEC] * 2,
    )
    square_shape = jax.ShapeDtypeStruct((1, row_count), jnp.float32)
    front, squares = plain_call(
        functools.partial(average_kernel, 0, middle // HD),
        "average",
        [jax.ShapeDtypeStruct((steps, rows, middle), jnp.float32), square_shape],
        pair_flops // 4,
        (acc, weights, values[0]),
    )
    averaged, squares = plain_call(
        functools.partial(rest_kernel, middle // HD, heads),
        "rest",
        [jax.ShapeDtypeStruct((heads - middle // HD, HD, row_count), jnp.float32), square_shape],
        pair_flops // 4,
        (acc, weights, values[1], squares),
    )
    within = [swap(squares, "seq", offset) for offset in range(1, lax.axis_size("seq"))]
    back, squares = plain_call(
        turn_kernel,
        "turn",
        [jax.ShapeDtypeStruct((steps, rows, columns - middle), jnp.float32), square_shape],
        row_count * columns,
        (averaged, squares, *within),
    )
    others = [swap(squares, "mp", offset) for offset in range(1, lax.axis_size("mp"))]
    decoded = decode(after(hidden, back), tail, conv_w, fade_count)
    attended = plain_call(
        functools.partial(scale_kernel, columns * lax.axis_size(axes)),
        "scale",
        jax.ShapeDtypeStruct(query.shape, jnp.bfloat16),
        row_count * columns,
        (front, back, squares, *others),
        out_specs=HBM_SPEC,
        scratch=[
            pltpu.VMEM((steps, rows, columns), jnp.bfloat16),
            pltpu.SemaphoreType.DMA((steps,)),
        ],
    )
    return (attended, decoded)


def solution(mesh):
    placed = (
        P(None, ("groups", "span"), None, ("mp", "seq")),
        P(None, None, ("groups", "span"), None, ("mp", "seq")),
        P(None, ("groups", "span"), None, ("mp", "seq")),
        P("groups", None),
        P("groups", None),
        P(("groups", "span"), None, ("mp", "seq")),
        P(("mp", "seq"), None),
        P(),
        P(("groups", "span")),
    )
    return jax.shard_map(
        per_device,
        mesh=mesh,
        in_specs=placed,
        out_specs=(
            P(None, ("groups", "span"), None, ("mp", "seq")),
            P(("groups", "span"), ("mp", "seq"), None),
        ),
        check_vma=False,
    )
```

```python
import functools
import math

import jax
import jax.numpy as jnp
from jax import lax
from jax.experimental import pallas as pl
from jax.experimental.pallas import tpu as pltpu
from jax.sharding import PartitionSpec as P

FR = 6
HD = 128
KT = 3
FADE = 2
NSTEPS = 64
LOG2E = 1.4426950408889634
VMEM_LIMIT = 24 * 1024 * 1024
VMEM_ALL = 60 * 1024 * 1024

SMEM_SPEC = pl.BlockSpec(memory_space=pltpu.SMEM)
VMEM_SPEC = pl.BlockSpec(memory_space=pltpu.VMEM)
HBM_SPEC = pl.BlockSpec(memory_space=pltpu.HBM)


def cost(flops, nbytes):
    return pl.CostEstimate(flops=flops, bytes_accessed=nbytes, transcendentals=0)


def hop(value, axis, steps):
    count = lax.axis_size(axis)
    return lax.ppermute(value, axis, [(source, source + steps) for source in range(count - steps)])


def swap(value, axes, offset):
    count = lax.axis_size(axes)
    if count & (count - 1) == 0:
        pairs = [(source, source ^ offset) for source in range(count)]
    else:
        pairs = [(source, (source + offset) % count) for source in range(count)]
    return lax.ppermute(value, axes, pairs)


def target_of(axes, offset):
    count = lax.axis_size(axes)
    mine = lax.axis_index(axes)
    if count & (count - 1) == 0:
        return mine ^ offset
    return lax.rem(mine + offset, count)


def after(value, *earlier):
    return lax.optimization_barrier((value, *earlier))[0]


def nt_dot(left, right):
    return lax.dot_general(left, right, (((1,), (1,)), ((), ())), preferred_element_type=jnp.float32)


def tn_dot(left, right):
    return lax.dot_general(left, right, (((0,), (0,)), ((), ())), preferred_element_type=jnp.float32)


def nn_dot(left, right):
    return jnp.dot(left, right, preferred_element_type=jnp.float32)


def row_factors(step_ref, position, steps, rows):
    lane = lax.broadcasted_iota(jnp.int32, (1, steps * rows), 1)
    index = jnp.full(lane.shape, step_ref[position, 0], jnp.int32)
    for step in range(1, steps):
        index = jnp.where(lane >= step * rows, step_ref[position, step], index)
    fraction = 1.0 - index.astype(jnp.float32) / NSTEPS
    level = 3.0 * fraction / (1.0 + 2.0 * fraction)
    return (0.5 + level) * (LOG2E / math.sqrt(HD))


def lane_windows(steps, rows):
    total = steps * rows
    return [
        (step * rows // HD * HD, min(total, -(-(step + 1) * rows // HD) * HD))
        for step in range(steps)
    ]


def join_steps(pieces, windows, rows):
    total = windows[-1][1]
    tiles = []
    for first in range(0, total, HD):
        stop = min(first + HD, total)
        tile = None
        for step, (begin, end) in enumerate(windows):
            if begin <= first and stop <= end and step * rows < stop and first < (step + 1) * rows:
                part = pieces[step][:, first - begin : stop - begin]
                if tile is None:
                    tile = part
                else:
                    lane = lax.broadcasted_iota(jnp.int32, part.shape, 1) + first
                    tile = jnp.where(lane >= step * rows, part, tile)
        tiles.append(tile)
    return jnp.concatenate(tiles, 1)


def own_kernel(step_ref, q_ref, kv_ref, acc_ref, top_ref, total_ref):
    position = lax.axis_index("span")
    steps, _, rows, columns = q_ref.shape
    factors = row_factors(step_ref, position, steps, rows)
    windows = lane_windows(steps, rows)
    for head in range(columns // HD):
        cut = slice(head * HD, (head + 1) * HD)
        queries = q_ref[:, 0, :, cut].reshape(steps * rows, HD)
        scores = join_steps(
            [nt_dot(kv_ref[s, 0, 0, :, cut], queries[a:b]) for s, (a, b) in enumerate(windows)],
            windows,
            rows,
        )
        scores = scores * factors
        top = jnp.max(scores, axis=0, keepdims=True)
        weights = jnp.exp2(scores - top)
        rounded = weights.astype(jnp.bfloat16)
        acc_ref[head] = join_steps(
            [tn_dot(kv_ref[s, 1, 0, :, cut], rounded[:, a:b]) for s, (a, b) in enumerate(windows)],
            windows,
            rows,
        )
        top_ref[head : head + 1] = top
        total_ref[head : head + 1] = jnp.sum(weights, axis=0, keepdims=True)


def absorb(queries, keys, values, factors, acc, top, total):
    scores = nt_dot(keys, queries) * factors
    newest = jnp.maximum(top, jnp.max(scores, axis=0, keepdims=True))
    weights = jnp.exp2(scores - newest)
    shrink = jnp.exp2(top - newest)
    total = total * shrink + jnp.sum(weights, axis=0, keepdims=True)
    acc = acc * shrink + tn_dot(values, weights.astype(jnp.bfloat16))
    return acc, newest, total


def visible(mask_ref, position, blocks):
    seen = False
    for place, block in blocks.items():
        seen = seen | ((position == place) & (mask_ref[place, block] > 0))
    return seen


def half(ref, which, cut):
    return ref[which, 0, :, cut] if len(ref.shape) == 4 else ref[0, :, cut]


def mid_kernel(plan, step_ref, mask_ref, q_ref, *refs):
    block_refs, (acc_in, top_in, total_in, acc_ref, top_ref, total_ref) = refs[:-6], refs[-6:]
    position = lax.axis_index("span")
    steps, _, rows, columns = q_ref.shape
    seen = visible(mask_ref, position, plan)

    @pl.when(seen)
    def _():
        factors = row_factors(step_ref, position, steps, rows)
        for head in range(columns // HD):
            cut = slice(head * HD, (head + 1) * HD)
            queries = q_ref[:, 0, :, cut].reshape(steps * rows, HD)
            acc, top, total = absorb(
                queries,
                half(block_refs[0], 0, cut),
                half(block_refs[-1], 1, cut),
                factors,
                acc_in[head],
                top_in[head : head + 1],
                total_in[head : head + 1],
            )
            acc_ref[head] = acc
            top_ref[head : head + 1] = top
            total_ref[head : head + 1] = total

    @pl.when(jnp.logical_not(seen))
    def _():
        acc_ref[...] = acc_in[...]
        top_ref[...] = top_in[...]
        total_ref[...] = total_in[...]


def score_kernel(plans, step_ref, mask_ref, q_ref, *refs):
    key_refs, (acc_in, top_in, total_in, acc_ref, w_ref) = refs[:-5], refs[-5:]
    position = lax.axis_index("span")
    steps, _, rows, columns = q_ref.shape

    def finish(key_ref):
        factors = row_factors(step_ref, position, steps, rows)
        for head in range(columns // HD):
            cut = slice(head * HD, (head + 1) * HD)
            queries = q_ref[:, 0, :, cut].reshape(steps * rows, HD)
            scores = nt_dot(half(key_ref, 0, cut), queries) * factors
            top = top_in[head : head + 1]
            newest = jnp.maximum(top, jnp.max(scores, axis=0, keepdims=True))
            weights = jnp.exp2(scores - newest)
            shrink = jnp.exp2(top - newest)
            total = total_in[head : head + 1] * shrink + jnp.sum(weights, axis=0, keepdims=True)
            inverse = 1.0 / total
            w_ref[head] = (weights * inverse).astype(jnp.bfloat16)
            acc_ref[head] = acc_in[head] * (shrink * inverse)

    rest = True
    for plan, key_ref in zip(plans, key_refs):
        seen = visible(mask_ref, position, plan)
        rest = jnp.logical_and(rest, jnp.logical_not(seen))
        pl.when(seen)(functools.partial(finish, key_ref))

    @pl.when(rest)
    def _():
        w_ref[...] = jnp.zeros_like(w_ref)
        for head in range(columns // HD):
            acc_ref[head] = acc_in[head] * (1.0 / total_in[head : head + 1])


def average_head(head, acc_ref, w_ref, value_ref, first):
    if value_ref.shape[-1] == acc_ref.shape[0] * HD:
        first = 0
    cut = slice((head - first) * HD, (head - first + 1) * HD)
    return acc_ref[head] + tn_dot(half(value_ref, 1, cut), w_ref[head])


def average_kernel(begin, end, acc_ref, w_ref, value_ref, average_ref, square_ref):
    squares = jnp.zeros(square_ref.shape, jnp.float32)
    for head in range(begin, end):
        average = average_head(head, acc_ref, w_ref, value_ref, begin)
        squares = squares + jnp.sum(average * average, axis=0, keepdims=True)
        average_ref[:, :, (head - begin) * HD : (head - begin + 1) * HD] = average.T.reshape(
            average_ref.shape[:2] + (HD,)
        )
    square_ref[...] = squares


def rest_kernel(begin, end, acc_ref, w_ref, value_ref, before_ref, average_ref, square_ref):
    squares = before_ref[...]
    for head in range(begin, end):
        average = average_head(head, acc_ref, w_ref, value_ref, begin)
        squares = squares + jnp.sum(average * average, axis=0, keepdims=True)
        average_ref[head - begin] = average
    square_ref[...] = squares


def turn_kernel(in_ref, square_in, out_ref, square_ref):
    steps, rows, _ = out_ref.shape
    for head in range(in_ref.shape[0]):
        out_ref[:, :, head * HD : (head + 1) * HD] = in_ref[head].T.reshape(steps, rows, HD)
    square_ref[...] = square_in[...]


def scale_kernel(width, front_ref, back_ref, *refs):
    part_refs, (out_hbm, out_ref, sem) = refs[:-3], refs[-3:]
    total = part_refs[0][...]
    for ref in part_refs[1:]:
        total = total + ref[...]
    inverse = lax.rsqrt(total / width + 1e-06)
    steps, rows, columns = out_ref.shape
    copies = []
    for step in range(steps):
        own = inverse[:, step * rows : (step + 1) * rows]
        factor = jnp.broadcast_to(own, (HD, rows)).T
        place = 0
        for ref in (front_ref, back_ref):
            for first in range(0, ref.shape[2], HD):
                average = ref[step, :, first : first + HD]
                out_ref[step, :, place : place + HD] = (average * factor).astype(jnp.bfloat16)
                place += HD
        copies.append(pltpu.make_async_copy(out_ref.at[step], out_hbm.at[step, 0], sem.at[step]))
        copies[-1].start()
    for copy in copies:
        copy.wait()


def send(value, pairs):
    return lax.ppermute(value, "span", pairs)


def delivered(span, back):
    return {place: place - back for place in range(back, span)}


def plain_call(kernel, name, out_shape, flops, operands, in_specs=(), out_specs=None, scratch=(), limit=VMEM_LIMIT):
    nbytes = sum(math.prod(o.shape) * o.dtype.itemsize for o in operands)
    if out_specs is None:
        out_specs = [VMEM_SPEC] * len(out_shape)
    return pl.pallas_call(
        kernel,
        in_specs=list(in_specs) + [VMEM_SPEC] * (len(operands) - len(in_specs)),
        out_specs=out_specs,
        out_shape=out_shape,
        scratch_shapes=list(scratch),
        compiler_params=pltpu.CompilerParams(vmem_limit_bytes=limit),
        cost_estimate=cost(flops, nbytes),
        name=name,
    )(*operands)


def picker(shape, wanted):
    row = lax.broadcasted_iota(jnp.int32, shape, 0)
    column = lax.broadcasted_iota(jnp.int32, shape, 1)
    return jnp.where(column == wanted(row), 1.0, 0.0).astype(jnp.bfloat16)


def project_kernel(axes, x_hbm, w_hbm, *refs):
    out_refs, (x_ref, w_ref, x_sem, w_sem) = refs[:-4], refs[-4:]
    rows, depth = x_ref.shape
    share = out_refs[0].shape[0]
    x_copy = pltpu.make_async_copy(x_hbm.at[0], x_ref, x_sem)
    x_copy.start()
    copies = []
    for place, first in enumerate(range(0, depth, 2 * HD)):
        cut = slice(first, min(first + 2 * HD, depth))
        copies.append((cut, pltpu.make_async_copy(w_hbm.at[cut], w_ref.at[cut], w_sem.at[place])))
        copies[-1][1].start()
    total = jnp.zeros((rows, w_ref.shape[1]), jnp.float32)
    x_copy.wait()
    for cut, w_copy in copies:
        w_copy.wait()
        total = total + nn_dot(x_ref[:, cut], w_ref[cut])
    projected = total.astype(jnp.bfloat16)
    for offset, out_ref in enumerate(out_refs):
        first = target_of(axes, offset) * share
        chosen = picker((share, rows), lambda row: row + first)
        out_ref[...] = nn_dot(chosen, projected).astype(jnp.bfloat16)


def gather_kernel(*refs):
    hidden_ref, tail_ref = refs[-2:]
    total = refs[0][...].astype(jnp.float32)
    for ref in refs[1:-2]:
        total = total + ref[...].astype(jnp.float32)
    hidden = total.astype(jnp.bfloat16)
    hidden_ref[...] = hidden
    kept = KT - 1 + FADE
    shape = (tail_ref.shape[0], hidden.shape[0])
    chosen = picker(shape, lambda row: row // kept * FR + FR - kept + row % kept)
    tail_ref[...] = nn_dot(chosen, hidden).astype(jnp.bfloat16)


def decode_kernel(fade_ref, hidden_ref, tail_ref, conv_ref, out_ref):
    position = lax.axis_index("span")
    share = hidden_ref.shape[0]
    spatial = share // FR
    kept = KT - 1 + FADE
    wide = FADE + FR
    hidden, tail = hidden_ref[...], tail_ref[...]
    mixed = jnp.zeros((spatial * wide, out_ref.shape[2]), jnp.float32)
    for tap in range(KT):
        def from_tail(row):
            place = row % wide + KT - 1 - tap
            return jnp.where(place < kept, row // wide * kept + place, -1)

        def from_hidden(row):
            place = row % wide + KT - 1 - tap
            return jnp.where(place >= kept, row // wide * FR + place - kept, -1)

        window = nn_dot(picker((spatial * wide, tail.shape[0]), from_tail), tail)
        window = window + nn_dot(picker((spatial * wide, share), from_hidden), hidden)
        mixed = mixed + nn_dot(window.astype(jnp.bfloat16), conv_ref[tap])
    frames = (mixed * jax.nn.sigmoid(mixed)).astype(jnp.bfloat16)
    fade = fade_ref[0]
    shape = (share, spatial * wide)
    current = nn_dot(picker(shape, lambda row: row // FR * wide + FADE + row % FR), frames)

    def faded(row):
        return jnp.where(row % FR < fade, row // FR * wide + FADE - fade + row % FR, -1)

    previous = nn_dot(picker(shape, faded), frames)
    frame = lax.broadcasted_iota(jnp.int32, (share, out_ref.shape[2]), 0) % FR
    fade_float = jnp.full(frame.shape, fade, jnp.int32).astype(jnp.float32)
    weight = (frame.astype(jnp.float32) + 1.0) / (fade_float + 1.0)
    weight = jnp.where((frame < fade) & (position > 0), weight, 1.0)
    out_ref[0] = (weight * current + (1.0 - weight) * previous).astype(jnp.bfloat16)


def project(finished, w_in):
    axes = ("mp", "seq")
    parts = lax.axis_size(axes)
    _, rows, depth = finished.shape
    channels = w_in.shape[1]
    chunks = -(-depth // (2 * HD))
    return plain_call(
        functools.partial(project_kernel, axes),
        "project",
        [jax.ShapeDtypeStruct((rows // parts, channels), jnp.bfloat16)] * parts,
        2 * rows * depth * channels,
        (finished, w_in),
        [HBM_SPEC] * 2,
        scratch=[
            pltpu.VMEM((rows, depth), jnp.bfloat16),
            pltpu.VMEM((depth, channels), jnp.bfloat16),
            pltpu.SemaphoreType.DMA,
            pltpu.SemaphoreType.DMA((chunks,)),
        ],
        limit=VMEM_ALL,
    )


def gather(parts, rows):
    share, channels = parts[0].shape
    tail_rows = share // FR * (KT - 1 + FADE)
    return plain_call(
        gather_kernel,
        "gather",
        [jax.ShapeDtypeStruct((count, channels), jnp.bfloat16) for count in (share, tail_rows)],
        rows * channels,
        parts,
    )


def decode(hidden, tail, conv_w, fade_count):
    share, channels = hidden.shape
    return plain_call(
        decode_kernel,
        "decode",
        [jax.ShapeDtypeStruct((1, share, channels), jnp.bfloat16)],
        2 * share * KT * channels * channels,
        (fade_count, hidden, tail, conv_w),
        [SMEM_SPEC],
    )[0]


def per_device(
    query, noisy_kv, clean_kv, causal_mask, step_index, finished, w_in, conv_w, fade_count
):
    steps, _, rows, columns = query.shape
    heads = columns // HD
    middle = (heads - max(1, heads // 3)) * HD
    row_count = steps * rows
    span = lax.axis_size("span")
    axes = ("mp", "seq")
    acc_shape = jax.ShapeDtypeStruct((heads, HD, row_count), jnp.float32)
    stat_shape = jax.ShapeDtypeStruct((heads, row_count), jnp.float32)
    pair_flops = 4 * row_count * rows * columns

    first_pairs = [(0, 2), (2, 3)] if span == 4 else [(c, c + 1) for c in range(span - 1)]
    near = send(clean_kv, first_pairs)
    pieces = project(finished, w_in)
    parts = [pieces[0]] + [swap(p, axes, offset + 1) for offset, p in enumerate(pieces[1:])]
    if span == 4:
        direct = send(clean_kv, [(1, 3)])
    carry = plain_call(
        own_kernel,
        "own",
        [acc_shape, stat_shape, stat_shape],
        pair_flops,
        (step_index, query, noisy_kv),
        [SMEM_SPEC],
    )
    hidden, tail = gather(parts, rows)
    tail = hop(tail, "span", 1)
    if span == 4:
        near = after(near, carry[0], hidden)
        forwards = lax.axis_index("span") == 2
        passed = [jnp.where(forwards, near[which], clean_kv[which]) for which in range(2)]
        passed = [passed[0], passed[1][:, :, :middle], passed[1][:, :, middle:]]
        passed = [hop(block, "span", 1) for block in passed]
        early = [(near, {2: 0, 3: 2}), (direct, {3: 1})]
        keys, *values = passed
        last_plan = {1: 0, 2: 1, 3: 0}
    else:
        ring = [near]
        for _ in range(2, span):
            ring.append(hop(ring[-1], "span", 1))
        early = [(block, delivered(span, back + 1)) for back, block in enumerate(ring[:-1])]
        keys, values = ring[-1], ring[-1:] * 2
        last_plan = delivered(span, span - 1)
    for block, plan in early:
        carry = plain_call(
            functools.partial(mid_kernel, plan),
            "middle",
            [acc_shape, stat_shape, stat_shape],
            pair_flops,
            (step_index, causal_mask, query, block, *carry),
            [SMEM_SPEC] * 2,
        )
    acc, weights = plain_call(
        functools.partial(score_kernel, [last_plan]),
        "score",
        [acc_shape, jax.ShapeDtypeStruct((heads, rows, row_count), jnp.bfloat16)],
        pair_flops // 2,
        (step_index, causal_mask, query, keys, *carry),
        [SMEM_SPEC] * 2,
    )
    square_shape = jax.ShapeDtypeStruct((1, row_count), jnp.float32)
    front, squares = plain_call(
        functools.partial(average_kernel, 0, middle // HD),
        "average",
        [jax.ShapeDtypeStruct((steps, rows, middle), jnp.float32), square_shape],
        pair_flops // 4,
        (acc, weights, values[0]),
    )
    averaged, squares = plain_call(
        functools.partial(rest_kernel, middle // HD, heads),
        "rest",
        [jax.ShapeDtypeStruct((heads - middle // HD, HD, row_count), jnp.float32), square_shape],
        pair_flops // 4,
        (acc, weights, values[1], squares),
    )
    others = [swap(squares, axes, offset) for offset in range(lax.axis_size(axes) - 1, 1, -1)]
    back, squares = plain_call(
        turn_kernel,
        "turn",
        [jax.ShapeDtypeStruct((steps, rows, columns - middle), jnp.float32), square_shape],
        row_count * columns,
        (averaged, squares),
    )
    others.append(swap(squares, axes, 1))
    decoded = decode(after(hidden, back), tail, conv_w, fade_count)
    attended = plain_call(
        functools.partial(scale_kernel, columns * lax.axis_size(axes)),
        "scale",
        jax.ShapeDtypeStruct(query.shape, jnp.bfloat16),
        row_count * columns,
        (front, back, squares, *others),
        out_specs=HBM_SPEC,
        scratch=[
            pltpu.VMEM((steps, rows, columns), jnp.bfloat16),
            pltpu.SemaphoreType.DMA((steps,)),
        ],
    )
    return (attended, decoded)


def solution(mesh):
    placed = (
        P(None, ("groups", "span"), None, ("mp", "seq")),
        P(None, None, ("groups", "span"), None, ("mp", "seq")),
        P(None, ("groups", "span"), None, ("mp", "seq")),
        P("groups", None),
        P("groups", None),
        P(("groups", "span"), None, ("mp", "seq")),
        P(("mp", "seq"), None),
        P(),
        P(("groups", "span")),
    )
    return jax.shard_map(
        per_device,
        mesh=mesh,
        in_specs=placed,
        out_specs=(
            P(None, ("groups", "span"), None, ("mp", "seq")),
            P(("groups", "span"), ("mp", "seq"), None),
        ),
        check_vma=False,
    )
```

```python
import functools
import math

import jax
import jax.numpy as jnp
from jax import lax
from jax.experimental import pallas as pl
from jax.experimental.pallas import tpu as pltpu
from jax.sharding import PartitionSpec as P

FR = 6
HD = 128
KT = 3
FADE = 2
NSTEPS = 64
LOG2E = 1.4426950408889634
VMEM_LIMIT = 24 * 1024 * 1024
VMEM_ALL = 60 * 1024 * 1024

SMEM_SPEC = pl.BlockSpec(memory_space=pltpu.SMEM)
VMEM_SPEC = pl.BlockSpec(memory_space=pltpu.VMEM)
HBM_SPEC = pl.BlockSpec(memory_space=pltpu.HBM)


def cost(flops, nbytes):
    return pl.CostEstimate(flops=flops, bytes_accessed=nbytes, transcendentals=0)


def hop(value, axis, steps):
    count = lax.axis_size(axis)
    return lax.ppermute(value, axis, [(source, source + steps) for source in range(count - steps)])


def swap(value, axes, offset):
    count = lax.axis_size(axes)
    if count & (count - 1) == 0:
        pairs = [(source, source ^ offset) for source in range(count)]
    else:
        pairs = [(source, (source + offset) % count) for source in range(count)]
    return lax.ppermute(value, axes, pairs)


def target_of(axes, offset):
    count = lax.axis_size(axes)
    mine = lax.axis_index(axes)
    if count & (count - 1) == 0:
        return mine ^ offset
    return lax.rem(mine + offset, count)


def after(value, *earlier):
    return lax.optimization_barrier((value, *earlier))[0]


def nt_dot(left, right):
    return lax.dot_general(left, right, (((1,), (1,)), ((), ())), preferred_element_type=jnp.float32)


def tn_dot(left, right):
    return lax.dot_general(left, right, (((0,), (0,)), ((), ())), preferred_element_type=jnp.float32)


def nn_dot(left, right):
    return jnp.dot(left, right, preferred_element_type=jnp.float32)


def row_factors(step_ref, position, steps, rows):
    lane = lax.broadcasted_iota(jnp.int32, (1, steps * rows), 1)
    index = jnp.full(lane.shape, step_ref[position, 0], jnp.int32)
    for step in range(1, steps):
        index = jnp.where(lane >= step * rows, step_ref[position, step], index)
    fraction = 1.0 - index.astype(jnp.float32) / NSTEPS
    level = 3.0 * fraction / (1.0 + 2.0 * fraction)
    return (0.5 + level) * (LOG2E / math.sqrt(HD))


def lane_windows(steps, rows):
    total = steps * rows
    return [
        (step * rows // HD * HD, min(total, -(-(step + 1) * rows // HD) * HD))
        for step in range(steps)
    ]


def join_steps(pieces, windows, rows):
    total = windows[-1][1]
    tiles = []
    for first in range(0, total, HD):
        stop = min(first + HD, total)
        tile = None
        for step, (begin, end) in enumerate(windows):
            if begin <= first and stop <= end and step * rows < stop and first < (step + 1) * rows:
                part = pieces[step][:, first - begin : stop - begin]
                if tile is None:
                    tile = part
                else:
                    lane = lax.broadcasted_iota(jnp.int32, part.shape, 1) + first
                    tile = jnp.where(lane >= step * rows, part, tile)
        tiles.append(tile)
    return jnp.concatenate(tiles, 1)


def own_kernel(step_ref, q_ref, kv_ref, acc_ref, top_ref, total_ref):
    position = lax.axis_index("span")
    steps, _, rows, columns = q_ref.shape
    factors = row_factors(step_ref, position, steps, rows)
    windows = lane_windows(steps, rows)
    for head in range(columns // HD):
        cut = slice(head * HD, (head + 1) * HD)
        queries = q_ref[:, 0, :, cut].reshape(steps * rows, HD)
        scores = join_steps(
            [nt_dot(kv_ref[s, 0, 0, :, cut], queries[a:b]) for s, (a, b) in enumerate(windows)],
            windows,
            rows,
        )
        scores = scores * factors
        top = jnp.max(scores, axis=0, keepdims=True)
        weights = jnp.exp2(scores - top)
        rounded = weights.astype(jnp.bfloat16)
        acc_ref[head] = join_steps(
            [tn_dot(kv_ref[s, 1, 0, :, cut], rounded[:, a:b]) for s, (a, b) in enumerate(windows)],
            windows,
            rows,
        )
        top_ref[head : head + 1] = top
        total_ref[head : head + 1] = jnp.sum(weights, axis=0, keepdims=True)


def absorb(queries, keys, values, factors, acc, top, total):
    scores = nt_dot(keys, queries) * factors
    newest = jnp.maximum(top, jnp.max(scores, axis=0, keepdims=True))
    weights = jnp.exp2(scores - newest)
    shrink = jnp.exp2(top - newest)
    total = total * shrink + jnp.sum(weights, axis=0, keepdims=True)
    acc = acc * shrink + tn_dot(values, weights.astype(jnp.bfloat16))
    return acc, newest, total


def visible(mask_ref, position, plan):
    odd = lax.rem(lax.axis_index("seq"), 2)
    seen = False
    for parity, blocks in enumerate(plan):
        for place, block in blocks.items():
            here = (odd == parity) & (position == place)
            seen = seen | (here & (mask_ref[place, block] > 0))
    return seen


def half(ref, which, cut):
    return ref[which, 0, :, cut] if len(ref.shape) == 4 else ref[0, :, cut]


def mid_kernel(plan, step_ref, mask_ref, q_ref, *refs):
    block_refs, (acc_in, top_in, total_in, acc_ref, top_ref, total_ref) = refs[:-6], refs[-6:]
    position = lax.axis_index("span")
    steps, _, rows, columns = q_ref.shape
    seen = visible(mask_ref, position, plan)

    @pl.when(seen)
    def _():
        factors = row_factors(step_ref, position, steps, rows)
        for head in range(columns // HD):
            cut = slice(head * HD, (head + 1) * HD)
            queries = q_ref[:, 0, :, cut].reshape(steps * rows, HD)
            acc, top, total = absorb(
                queries,
                half(block_refs[0], 0, cut),
                half(block_refs[-1], 1, cut),
                factors,
                acc_in[head],
                top_in[head : head + 1],
                total_in[head : head + 1],
            )
            acc_ref[head] = acc
            top_ref[head : head + 1] = top
            total_ref[head : head + 1] = total

    @pl.when(jnp.logical_not(seen))
    def _():
        acc_ref[...] = acc_in[...]
        top_ref[...] = top_in[...]
        total_ref[...] = total_in[...]


def score_kernel(plans, step_ref, mask_ref, q_ref, *refs):
    key_refs, (acc_in, top_in, total_in, acc_ref, w_ref) = refs[:-5], refs[-5:]
    position = lax.axis_index("span")
    steps, _, rows, columns = q_ref.shape

    def finish(key_ref):
        factors = row_factors(step_ref, position, steps, rows)
        for head in range(columns // HD):
            cut = slice(head * HD, (head + 1) * HD)
            queries = q_ref[:, 0, :, cut].reshape(steps * rows, HD)
            scores = nt_dot(half(key_ref, 0, cut), queries) * factors
            top = top_in[head : head + 1]
            newest = jnp.maximum(top, jnp.max(scores, axis=0, keepdims=True))
            weights = jnp.exp2(scores - newest)
            shrink = jnp.exp2(top - newest)
            total = total_in[head : head + 1] * shrink + jnp.sum(weights, axis=0, keepdims=True)
            inverse = 1.0 / total
            w_ref[head] = (weights * inverse).astype(jnp.bfloat16)
            acc_ref[head] = acc_in[head] * (shrink * inverse)

    rest = True
    for plan, key_ref in zip(plans, key_refs):
        seen = visible(mask_ref, position, plan)
        rest = jnp.logical_and(rest, jnp.logical_not(seen))
        pl.when(seen)(functools.partial(finish, key_ref))

    @pl.when(rest)
    def _():
        w_ref[...] = jnp.zeros_like(w_ref)
        for head in range(columns // HD):
            acc_ref[head] = acc_in[head] * (1.0 / total_in[head : head + 1])


def average_head(head, acc_ref, w_ref, value_ref, first):
    if value_ref.shape[-1] == acc_ref.shape[0] * HD:
        first = 0
    cut = slice((head - first) * HD, (head - first + 1) * HD)
    return acc_ref[head] + tn_dot(half(value_ref, 1, cut), w_ref[head])


def average_kernel(begin, end, acc_ref, w_ref, value_ref, average_ref, square_ref):
    squares = jnp.zeros(square_ref.shape, jnp.float32)
    for head in range(begin, end):
        average = average_head(head, acc_ref, w_ref, value_ref, begin)
        squares = squares + jnp.sum(average * average, axis=0, keepdims=True)
        average_ref[:, :, (head - begin) * HD : (head - begin + 1) * HD] = average.T.reshape(
            average_ref.shape[:2] + (HD,)
        )
    square_ref[...] = squares


def rest_kernel(begin, end, acc_ref, w_ref, value_ref, before_ref, average_ref, square_ref):
    squares = before_ref[...]
    for head in range(begin, end):
        average = average_head(head, acc_ref, w_ref, value_ref, begin)
        squares = squares + jnp.sum(average * average, axis=0, keepdims=True)
        average_ref[head - begin] = average
    square_ref[...] = squares


def turn_kernel(in_ref, square_in, out_ref, square_ref):
    steps, rows, _ = out_ref.shape
    for head in range(in_ref.shape[0]):
        out_ref[:, :, head * HD : (head + 1) * HD] = in_ref[head].T.reshape(steps, rows, HD)
    square_ref[...] = square_in[...]


def scale_kernel(width, front_ref, back_ref, *refs):
    part_refs, (out_hbm, out_ref, sem) = refs[:-3], refs[-3:]
    total = part_refs[0][...]
    for ref in part_refs[1:]:
        total = total + ref[...]
    inverse = lax.rsqrt(total / width + 1e-06)
    steps, rows, columns = out_ref.shape
    spread = jnp.broadcast_to(inverse, (HD, steps * rows)).T
    copies = []
    for step in range(steps):
        factor = spread[step * rows : (step + 1) * rows]
        place = 0
        for ref in (front_ref, back_ref):
            for first in range(0, ref.shape[2], HD):
                average = ref[step, :, first : first + HD]
                out_ref[step, :, place : place + HD] = (average * factor).astype(jnp.bfloat16)
                place += HD
        copies.append(pltpu.make_async_copy(out_ref.at[step], out_hbm.at[step, 0], sem.at[step]))
        copies[-1].start()
    for copy in copies:
        copy.wait()


def send(value, pairs):
    cores = lax.axis_size("seq")
    flat = [
        (source * cores + core, target * cores + core)
        for core in range(cores)
        for source, target in pairs[core % 2]
    ]
    return lax.ppermute(value, ("span", "seq"), flat)


def delivered(span, back):
    return [{place: place - back for place in range(back, span)}] * 2


def plain_call(kernel, name, out_shape, flops, operands, in_specs=(), out_specs=None, scratch=(), limit=VMEM_LIMIT):
    nbytes = sum(math.prod(o.shape) * o.dtype.itemsize for o in operands)
    if out_specs is None:
        out_specs = [VMEM_SPEC] * len(out_shape)
    return pl.pallas_call(
        kernel,
        in_specs=list(in_specs) + [VMEM_SPEC] * (len(operands) - len(in_specs)),
        out_specs=out_specs,
        out_shape=out_shape,
        scratch_shapes=list(scratch),
        compiler_params=pltpu.CompilerParams(vmem_limit_bytes=limit),
        cost_estimate=cost(flops, nbytes),
        name=name,
    )(*operands)


def picker(shape, wanted):
    row = lax.broadcasted_iota(jnp.int32, shape, 0)
    column = lax.broadcasted_iota(jnp.int32, shape, 1)
    return jnp.where(column == wanted(row), 1.0, 0.0).astype(jnp.bfloat16)


def project_kernel(axes, x_hbm, w_hbm, *refs):
    out_refs, (x_ref, w_ref, x_sem, w_sem) = refs[:-4], refs[-4:]
    rows, depth = x_ref.shape
    share = out_refs[0].shape[0]
    x_copy = pltpu.make_async_copy(x_hbm.at[0], x_ref, x_sem)
    x_copy.start()
    copies = []
    for place, first in enumerate(range(0, depth, 2 * HD)):
        cut = slice(first, min(first + 2 * HD, depth))
        copies.append((cut, pltpu.make_async_copy(w_hbm.at[cut], w_ref.at[cut], w_sem.at[place])))
        copies[-1][1].start()
    total = jnp.zeros((rows, w_ref.shape[1]), jnp.float32)
    x_copy.wait()
    for cut, w_copy in copies:
        w_copy.wait()
        total = total + nn_dot(x_ref[:, cut], w_ref[cut])
    projected = total.astype(jnp.bfloat16)
    for offset, out_ref in enumerate(out_refs):
        first = target_of(axes, offset) * share
        chosen = picker((share, rows), lambda row: row + first)
        out_ref[...] = nn_dot(chosen, projected).astype(jnp.bfloat16)


def gather_kernel(*refs):
    hidden_ref, tail_ref = refs[-2:]
    total = refs[0][...].astype(jnp.float32)
    for ref in refs[1:-2]:
        total = total + ref[...].astype(jnp.float32)
    hidden = total.astype(jnp.bfloat16)
    hidden_ref[...] = hidden
    kept = KT - 1 + FADE
    shape = (tail_ref.shape[0], hidden.shape[0])
    chosen = picker(shape, lambda row: row // kept * FR + FR - kept + row % kept)
    tail_ref[...] = nn_dot(chosen, hidden).astype(jnp.bfloat16)


def decode_kernel(fade_ref, hidden_ref, tail_ref, conv_ref, out_ref):
    position = lax.axis_index("span")
    share = hidden_ref.shape[0]
    spatial = share // FR
    kept = KT - 1 + FADE
    wide = FADE + FR
    hidden, tail = hidden_ref[...], tail_ref[...]
    mixed = jnp.zeros((spatial * wide, out_ref.shape[2]), jnp.float32)
    for tap in range(KT):
        def from_tail(row):
            place = row % wide + KT - 1 - tap
            return jnp.where(place < kept, row // wide * kept + place, -1)

        def from_hidden(row):
            place = row % wide + KT - 1 - tap
            return jnp.where(place >= kept, row // wide * FR + place - kept, -1)

        window = nn_dot(picker((spatial * wide, tail.shape[0]), from_tail), tail)
        window = window + nn_dot(picker((spatial * wide, share), from_hidden), hidden)
        mixed = mixed + nn_dot(window.astype(jnp.bfloat16), conv_ref[tap])
    frames = (mixed * jax.nn.sigmoid(mixed)).astype(jnp.bfloat16)
    fade = fade_ref[0]
    shape = (share, spatial * wide)
    current = nn_dot(picker(shape, lambda row: row // FR * wide + FADE + row % FR), frames)

    def faded(row):
        return jnp.where(row % FR < fade, row // FR * wide + FADE - fade + row % FR, -1)

    previous = nn_dot(picker(shape, faded), frames)
    frame = lax.broadcasted_iota(jnp.int32, (share, out_ref.shape[2]), 0) % FR
    fade_float = jnp.full(frame.shape, fade, jnp.int32).astype(jnp.float32)
    weight = (frame.astype(jnp.float32) + 1.0) / (fade_float + 1.0)
    weight = jnp.where((frame < fade) & (position > 0), weight, 1.0)
    out_ref[0] = (weight * current + (1.0 - weight) * previous).astype(jnp.bfloat16)


def project(finished, w_in):
    axes = ("mp", "seq")
    parts = lax.axis_size(axes)
    _, rows, depth = finished.shape
    channels = w_in.shape[1]
    chunks = -(-depth // (2 * HD))
    return plain_call(
        functools.partial(project_kernel, axes),
        "project",
        [jax.ShapeDtypeStruct((rows // parts, channels), jnp.bfloat16)] * parts,
        2 * rows * depth * channels,
        (finished, w_in),
        [HBM_SPEC] * 2,
        scratch=[
            pltpu.VMEM((rows, depth), jnp.bfloat16),
            pltpu.VMEM((depth, channels), jnp.bfloat16),
            pltpu.SemaphoreType.DMA,
            pltpu.SemaphoreType.DMA((chunks,)),
        ],
        limit=VMEM_ALL,
    )


def gather(parts, rows):
    share, channels = parts[0].shape
    tail_rows = share // FR * (KT - 1 + FADE)
    return plain_call(
        gather_kernel,
        "gather",
        [jax.ShapeDtypeStruct((count, channels), jnp.bfloat16) for count in (share, tail_rows)],
        rows * channels,
        parts,
    )


def decode(hidden, tail, conv_w, fade_count):
    share, channels = hidden.shape
    return plain_call(
        decode_kernel,
        "decode",
        [jax.ShapeDtypeStruct((1, share, channels), jnp.bfloat16)],
        2 * share * KT * channels * channels,
        (fade_count, hidden, tail, conv_w),
        [SMEM_SPEC],
    )[0]


def per_device(
    query, noisy_kv, clean_kv, causal_mask, step_index, finished, w_in, conv_w, fade_count
):
    steps, _, rows, columns = query.shape
    heads = columns // HD
    middle = (heads - max(1, heads // 3)) * HD
    row_count = steps * rows
    span = lax.axis_size("span")
    axes = ("mp", "seq")
    acc_shape = jax.ShapeDtypeStruct((heads, HD, row_count), jnp.float32)
    stat_shape = jax.ShapeDtypeStruct((heads, row_count), jnp.float32)
    pair_flops = 4 * row_count * rows * columns

    shift = [(place, place + 1) for place in range(span - 1)]
    near = send(clean_kv, [[(0, 2), (2, 3)] if span == 4 else shift, shift])
    pieces = project(finished, w_in)
    parts = [pieces[0]] + [swap(p, axes, offset + 1) for offset, p in enumerate(pieces[1:])]
    hidden, tail = gather(parts, rows)
    gate = after(clean_kv, hidden)
    if span == 4:
        direct = send(gate, [[(1, 3)], [(0, 3)]])
    carry = plain_call(
        own_kernel,
        "own",
        [acc_shape, stat_shape, stat_shape],
        pair_flops,
        (after(step_index, gate), query, noisy_kv),
        [SMEM_SPEC],
    )
    tail = hop(tail, "span", 1)
    if span == 4:
        near = after(near, carry[0], hidden)
        forwards = lax.axis_index("span") == 2
        passed = [jnp.where(forwards, near[which], clean_kv[which]) for which in range(2)]
        passed = [passed[0], passed[1][:, :, :middle], passed[1][:, :, middle:]]
        passed = [send(block, [shift, [(0, 2), (2, 3)]]) for block in passed]
        early = [(near, [{2: 0, 3: 2}, {1: 0, 2: 1, 3: 2}]), (direct, [{3: 1}, {3: 0}])]
        keys, *values = passed
        last_plan = [{1: 0, 2: 1, 3: 0}, {2: 0, 3: 1}]
    else:
        ring = [near]
        for _ in range(2, span):
            ring.append(hop(ring[-1], "span", 1))
        early = [(block, delivered(span, back + 1)) for back, block in enumerate(ring[:-1])]
        keys, values = ring[-1], ring[-1:] * 2
        last_plan = delivered(span, span - 1)
    for block, plan in early:
        carry = plain_call(
            functools.partial(mid_kernel, plan),
            "middle",
            [acc_shape, stat_shape, stat_shape],
            pair_flops,
            (step_index, causal_mask, query, block, *carry),
            [SMEM_SPEC] * 2,
        )
    acc, weights = plain_call(
        functools.partial(score_kernel, [last_plan]),
        "score",
        [acc_shape, jax.ShapeDtypeStruct((heads, rows, row_count), jnp.bfloat16)],
        pair_flops // 2,
        (step_index, causal_mask, query, keys, *carry),
        [SMEM_SPEC] * 2,
    )
    square_shape = jax.ShapeDtypeStruct((1, row_count), jnp.float32)
    front, squares = plain_call(
        functools.partial(average_kernel, 0, middle // HD),
        "average",
        [jax.ShapeDtypeStruct((steps, rows, middle), jnp.float32), square_shape],
        pair_flops // 4,
        (acc, weights, values[0]),
    )
    averaged, squares = plain_call(
        functools.partial(rest_kernel, middle // HD, heads),
        "rest",
        [jax.ShapeDtypeStruct((heads - middle // HD, HD, row_count), jnp.float32), square_shape],
        pair_flops // 4,
        (acc, weights, values[1], squares),
    )
    others = [swap(squares, axes, offset) for offset in range(2, lax.axis_size(axes))]
    back, squares = plain_call(
        turn_kernel,
        "turn",
        [jax.ShapeDtypeStruct((steps, rows, columns - middle), jnp.float32), square_shape],
        row_count * columns,
        (averaged, squares),
    )
    others.append(swap(squares, axes, 1))
    decoded = decode(after(hidden, back), tail, conv_w, fade_count)
    attended = plain_call(
        functools.partial(scale_kernel, columns * lax.axis_size(axes)),
        "scale",
        jax.ShapeDtypeStruct(query.shape, jnp.bfloat16),
        row_count * columns,
        (front, back, squares, *others),
        out_specs=HBM_SPEC,
        scratch=[
            pltpu.VMEM((steps, rows, columns), jnp.bfloat16),
            pltpu.SemaphoreType.DMA((steps,)),
        ],
    )
    return (attended, decoded)


def solution(mesh):
    placed = (
        P(None, ("groups", "span"), None, ("mp", "seq")),
        P(None, None, ("groups", "span"), None, ("mp", "seq")),
        P(None, ("groups", "span"), None, ("mp", "seq")),
        P("groups", None),
        P("groups", None),
        P(("groups", "span"), None, ("mp", "seq")),
        P(("mp", "seq"), None),
        P(),
        P(("groups", "span")),
    )
    return jax.shard_map(
        per_device,
        mesh=mesh,
        in_specs=placed,
        out_specs=(
            P(None, ("groups", "span"), None, ("mp", "seq")),
            P(("groups", "span"), ("mp", "seq"), None),
        ),
        check_vma=False,
    )
```

```python
import functools
import math

import jax
import jax.numpy as jnp
from jax import lax
from jax.experimental import pallas as pl
from jax.experimental.pallas import tpu as pltpu
from jax.sharding import PartitionSpec as P

FR = 6
HD = 128
KT = 3
FADE = 2
NSTEPS = 64
LOG2E = 1.4426950408889634
VMEM_LIMIT = 24 * 1024 * 1024
VMEM_ALL = 60 * 1024 * 1024

SMEM_SPEC = pl.BlockSpec(memory_space=pltpu.SMEM)
VMEM_SPEC = pl.BlockSpec(memory_space=pltpu.VMEM)
HBM_SPEC = pl.BlockSpec(memory_space=pltpu.HBM)


def cost(flops, nbytes):
    return pl.CostEstimate(flops=flops, bytes_accessed=nbytes, transcendentals=0)


def hop(value, axis, steps):
    count = lax.axis_size(axis)
    return lax.ppermute(value, axis, [(source, source + steps) for source in range(count - steps)])


def swap(value, axes, offset):
    count = lax.axis_size(axes)
    if count & (count - 1) == 0:
        pairs = [(source, source ^ offset) for source in range(count)]
    else:
        pairs = [(source, (source + offset) % count) for source in range(count)]
    return lax.ppermute(value, axes, pairs)


def target_of(axes, offset):
    count = lax.axis_size(axes)
    mine = lax.axis_index(axes)
    if count & (count - 1) == 0:
        return mine ^ offset
    return lax.rem(mine + offset, count)


def after(value, *earlier):
    return lax.optimization_barrier((value, *earlier))[0]


def nt_dot(left, right):
    return lax.dot_general(left, right, (((1,), (1,)), ((), ())), preferred_element_type=jnp.float32)


def tn_dot(left, right):
    return lax.dot_general(left, right, (((0,), (0,)), ((), ())), preferred_element_type=jnp.float32)


def nn_dot(left, right):
    return jnp.dot(left, right, preferred_element_type=jnp.float32)


def row_factors(step_ref, position, steps, rows):
    lane = lax.broadcasted_iota(jnp.int32, (1, steps * rows), 1)
    index = jnp.full(lane.shape, step_ref[position, 0], jnp.int32)
    for step in range(1, steps):
        index = jnp.where(lane >= step * rows, step_ref[position, step], index)
    fraction = 1.0 - index.astype(jnp.float32) / NSTEPS
    level = 3.0 * fraction / (1.0 + 2.0 * fraction)
    return (0.5 + level) * (LOG2E / math.sqrt(HD))


def lane_windows(steps, rows):
    total = steps * rows
    return [
        (step * rows // HD * HD, min(total, -(-(step + 1) * rows // HD) * HD))
        for step in range(steps)
    ]


def join_steps(pieces, windows, rows):
    total = windows[-1][1]
    tiles = []
    for first in range(0, total, HD):
        stop = min(first + HD, total)
        tile = None
        for step, (begin, end) in enumerate(windows):
            if begin <= first and stop <= end and step * rows < stop and first < (step + 1) * rows:
                part = pieces[step][:, first - begin : stop - begin]
                if tile is None:
                    tile = part
                else:
                    lane = lax.broadcasted_iota(jnp.int32, part.shape, 1) + first
                    tile = jnp.where(lane >= step * rows, part, tile)
        tiles.append(tile)
    return jnp.concatenate(tiles, 1)


def own_kernel(step_ref, q_ref, kv_ref, acc_ref, top_ref, total_ref):
    position = lax.axis_index("span")
    steps, _, rows, columns = q_ref.shape
    factors = row_factors(step_ref, position, steps, rows)
    windows = lane_windows(steps, rows)
    for head in range(columns // HD):
        cut = slice(head * HD, (head + 1) * HD)
        queries = q_ref[:, 0, :, cut].reshape(steps * rows, HD)
        scores = join_steps(
            [nt_dot(kv_ref[s, 0, 0, :, cut], queries[a:b]) for s, (a, b) in enumerate(windows)],
            windows,
            rows,
        )
        scores = scores * factors
        top = jnp.max(scores, axis=0, keepdims=True)
        weights = jnp.exp2(scores - top)
        rounded = weights.astype(jnp.bfloat16)
        acc_ref[head] = join_steps(
            [tn_dot(kv_ref[s, 1, 0, :, cut], rounded[:, a:b]) for s, (a, b) in enumerate(windows)],
            windows,
            rows,
        )
        top_ref[head : head + 1] = top
        total_ref[head : head + 1] = jnp.sum(weights, axis=0, keepdims=True)


def absorb(queries, keys, values, factors, acc, top, total):
    scores = nt_dot(keys, queries) * factors
    newest = jnp.maximum(top, jnp.max(scores, axis=0, keepdims=True))
    weights = jnp.exp2(scores - newest)
    shrink = jnp.exp2(top - newest)
    total = total * shrink + jnp.sum(weights, axis=0, keepdims=True)
    acc = acc * shrink + tn_dot(values, weights.astype(jnp.bfloat16))
    return acc, newest, total


def visible(mask_ref, position, blocks):
    seen = False
    for place, block in blocks.items():
        seen = seen | ((position == place) & (mask_ref[place, block] > 0))
    return seen


def half(ref, which, cut):
    return ref[which, 0, :, cut] if len(ref.shape) == 4 else ref[0, :, cut]


def mid_kernel(plan, step_ref, mask_ref, q_ref, *refs):
    block_refs, (acc_in, top_in, total_in, acc_ref, top_ref, total_ref) = refs[:-6], refs[-6:]
    position = lax.axis_index("span")
    steps, _, rows, columns = q_ref.shape
    seen = visible(mask_ref, position, plan)

    @pl.when(seen)
    def _():
        factors = row_factors(step_ref, position, steps, rows)
        for head in range(columns // HD):
            cut = slice(head * HD, (head + 1) * HD)
            queries = q_ref[:, 0, :, cut].reshape(steps * rows, HD)
            acc, top, total = absorb(
                queries,
                half(block_refs[0], 0, cut),
                half(block_refs[-1], 1, cut),
                factors,
                acc_in[head],
                top_in[head : head + 1],
                total_in[head : head + 1],
            )
            acc_ref[head] = acc
            top_ref[head : head + 1] = top
            total_ref[head : head + 1] = total

    @pl.when(jnp.logical_not(seen))
    def _():
        acc_ref[...] = acc_in[...]
        top_ref[...] = top_in[...]
        total_ref[...] = total_in[...]


def score_kernel(plans, step_ref, mask_ref, q_ref, *refs):
    key_refs, (acc_in, top_in, total_in, acc_ref, w_ref) = refs[:-5], refs[-5:]
    position = lax.axis_index("span")
    steps, _, rows, columns = q_ref.shape

    def finish(key_ref):
        factors = row_factors(step_ref, position, steps, rows)
        for head in range(columns // HD):
            cut = slice(head * HD, (head + 1) * HD)
            queries = q_ref[:, 0, :, cut].reshape(steps * rows, HD)
            scores = nt_dot(half(key_ref, 0, cut), queries) * factors
            top = top_in[head : head + 1]
            newest = jnp.maximum(top, jnp.max(scores, axis=0, keepdims=True))
            weights = jnp.exp2(scores - newest)
            shrink = jnp.exp2(top - newest)
            total = total_in[head : head + 1] * shrink + jnp.sum(weights, axis=0, keepdims=True)
            inverse = 1.0 / total
            w_ref[head] = (weights * inverse).astype(jnp.bfloat16)
            acc_ref[head] = acc_in[head] * (shrink * inverse)

    rest = True
    for plan, key_ref in zip(plans, key_refs):
        seen = visible(mask_ref, position, plan)
        rest = jnp.logical_and(rest, jnp.logical_not(seen))
        pl.when(seen)(functools.partial(finish, key_ref))

    @pl.when(rest)
    def _():
        w_ref[...] = jnp.zeros_like(w_ref)
        for head in range(columns // HD):
            acc_ref[head] = acc_in[head] * (1.0 / total_in[head : head + 1])


def average_head(head, acc_ref, w_ref, value_ref, first):
    if value_ref.shape[-1] == acc_ref.shape[0] * HD:
        first = 0
    cut = slice((head - first) * HD, (head - first + 1) * HD)
    return acc_ref[head] + tn_dot(half(value_ref, 1, cut), w_ref[head])


def average_kernel(begin, end, acc_ref, w_ref, value_ref, average_ref, square_ref):
    squares = jnp.zeros(square_ref.shape, jnp.float32)
    for head in range(begin, end):
        average = average_head(head, acc_ref, w_ref, value_ref, begin)
        squares = squares + jnp.sum(average * average, axis=0, keepdims=True)
        average_ref[:, :, (head - begin) * HD : (head - begin + 1) * HD] = average.T.reshape(
            average_ref.shape[:2] + (HD,)
        )
    square_ref[...] = squares


def rest_kernel(begin, end, acc_ref, w_ref, value_ref, before_ref, average_ref, square_ref):
    squares = before_ref[...]
    for head in range(begin, end):
        average = average_head(head, acc_ref, w_ref, value_ref, begin)
        squares = squares + jnp.sum(average * average, axis=0, keepdims=True)
        average_ref[head - begin] = average
    square_ref[...] = squares


def turn_kernel(in_ref, square_in, out_ref, square_ref):
    steps, rows, _ = out_ref.shape
    for head in range(in_ref.shape[0]):
        out_ref[:, :, head * HD : (head + 1) * HD] = in_ref[head].T.reshape(steps, rows, HD)
    square_ref[...] = square_in[...]


def scale_kernel(width, front_ref, back_ref, *refs):
    part_refs, (out_hbm, out_ref, sem) = refs[:-3], refs[-3:]
    total = part_refs[0][...]
    for ref in part_refs[1:]:
        total = total + ref[...]
    inverse = lax.rsqrt(total / width + 1e-06)
    steps, rows, columns = out_ref.shape
    copies = []
    for step in range(steps):
        own = inverse[:, step * rows : (step + 1) * rows]
        factor = jnp.broadcast_to(own, (HD, rows)).T
        place = 0
        for ref in (front_ref, back_ref):
            for first in range(0, ref.shape[2], HD):
                average = ref[step, :, first : first + HD]
                out_ref[step, :, place : place + HD] = (average * factor).astype(jnp.bfloat16)
                place += HD
        copies.append(pltpu.make_async_copy(out_ref.at[step], out_hbm.at[step, 0], sem.at[step]))
        copies[-1].start()
    for copy in copies:
        copy.wait()


def send(value, pairs):
    return lax.ppermute(value, "span", pairs)


def delivered(span, back):
    return {place: place - back for place in range(back, span)}


def plain_call(kernel, name, out_shape, flops, operands, in_specs=(), out_specs=None, scratch=(), limit=VMEM_LIMIT):
    nbytes = sum(math.prod(o.shape) * o.dtype.itemsize for o in operands)
    if out_specs is None:
        out_specs = [VMEM_SPEC] * len(out_shape)
    return pl.pallas_call(
        kernel,
        in_specs=list(in_specs) + [VMEM_SPEC] * (len(operands) - len(in_specs)),
        out_specs=out_specs,
        out_shape=out_shape,
        scratch_shapes=list(scratch),
        compiler_params=pltpu.CompilerParams(vmem_limit_bytes=limit),
        cost_estimate=cost(flops, nbytes),
        name=name,
    )(*operands)


def picker(shape, wanted):
    row = lax.broadcasted_iota(jnp.int32, shape, 0)
    column = lax.broadcasted_iota(jnp.int32, shape, 1)
    return jnp.where(column == wanted(row), 1.0, 0.0).astype(jnp.bfloat16)


def project_kernel(axes, x_hbm, w_hbm, *refs):
    out_refs, (x_ref, w_ref, x_sem, w_sem) = refs[:-4], refs[-4:]
    rows, depth = x_ref.shape
    share = out_refs[0].shape[0]
    x_copy = pltpu.make_async_copy(x_hbm.at[0], x_ref, x_sem)
    x_copy.start()
    copies = []
    for place, first in enumerate(range(0, depth, 2 * HD)):
        cut = slice(first, min(first + 2 * HD, depth))
        copies.append((cut, pltpu.make_async_copy(w_hbm.at[cut], w_ref.at[cut], w_sem.at[place])))
        copies[-1][1].start()
    total = jnp.zeros((rows, w_ref.shape[1]), jnp.float32)
    x_copy.wait()
    for cut, w_copy in copies:
        w_copy.wait()
        total = total + nn_dot(x_ref[:, cut], w_ref[cut])
    projected = total.astype(jnp.bfloat16)
    for offset, out_ref in enumerate(out_refs):
        first = target_of(axes, offset) * share
        chosen = picker((share, rows), lambda row: row + first)
        out_ref[...] = nn_dot(chosen, projected).astype(jnp.bfloat16)


def gather_kernel(*refs):
    hidden_ref, tail_ref = refs[-2:]
    total = refs[0][...].astype(jnp.float32)
    for ref in refs[1:-2]:
        total = total + ref[...].astype(jnp.float32)
    hidden = total.astype(jnp.bfloat16)
    hidden_ref[...] = hidden
    kept = KT - 1 + FADE
    shape = (tail_ref.shape[0], hidden.shape[0])
    chosen = picker(shape, lambda row: row // kept * FR + FR - kept + row % kept)
    tail_ref[...] = nn_dot(chosen, hidden).astype(jnp.bfloat16)


def decode_kernel(fade_ref, hidden_ref, tail_ref, conv_ref, out_ref):
    position = lax.axis_index("span")
    share = hidden_ref.shape[0]
    spatial = share // FR
    kept = KT - 1 + FADE
    wide = FADE + FR
    hidden, tail = hidden_ref[...], tail_ref[...]
    mixed = jnp.zeros((spatial * wide, out_ref.shape[2]), jnp.float32)
    for tap in range(KT):
        def from_tail(row):
            place = row % wide + KT - 1 - tap
            return jnp.where(place < kept, row // wide * kept + place, -1)

        def from_hidden(row):
            place = row % wide + KT - 1 - tap
            return jnp.where(place >= kept, row // wide * FR + place - kept, -1)

        window = nn_dot(picker((spatial * wide, tail.shape[0]), from_tail), tail)
        window = window + nn_dot(picker((spatial * wide, share), from_hidden), hidden)
        mixed = mixed + nn_dot(window.astype(jnp.bfloat16), conv_ref[tap])
    frames = (mixed * jax.nn.sigmoid(mixed)).astype(jnp.bfloat16)
    fade = fade_ref[0]
    shape = (share, spatial * wide)
    current = nn_dot(picker(shape, lambda row: row // FR * wide + FADE + row % FR), frames)

    def faded(row):
        return jnp.where(row % FR < fade, row // FR * wide + FADE - fade + row % FR, -1)

    previous = nn_dot(picker(shape, faded), frames)
    frame = lax.broadcasted_iota(jnp.int32, (share, out_ref.shape[2]), 0) % FR
    fade_float = jnp.full(frame.shape, fade, jnp.int32).astype(jnp.float32)
    weight = (frame.astype(jnp.float32) + 1.0) / (fade_float + 1.0)
    weight = jnp.where((frame < fade) & (position > 0), weight, 1.0)
    out_ref[0] = (weight * current + (1.0 - weight) * previous).astype(jnp.bfloat16)


def project(finished, w_in):
    axes = ("mp", "seq")
    parts = lax.axis_size(axes)
    _, rows, depth = finished.shape
    channels = w_in.shape[1]
    chunks = -(-depth // (2 * HD))
    return plain_call(
        functools.partial(project_kernel, axes),
        "project",
        [jax.ShapeDtypeStruct((rows // parts, channels), jnp.bfloat16)] * parts,
        2 * rows * depth * channels,
        (finished, w_in),
        [HBM_SPEC] * 2,
        scratch=[
            pltpu.VMEM((rows, depth), jnp.bfloat16),
            pltpu.VMEM((depth, channels), jnp.bfloat16),
            pltpu.SemaphoreType.DMA,
            pltpu.SemaphoreType.DMA((chunks,)),
        ],
    )


def gather(parts, rows):
    share, channels = parts[0].shape
    tail_rows = share // FR * (KT - 1 + FADE)
    return plain_call(
        gather_kernel,
        "gather",
        [jax.ShapeDtypeStruct((count, channels), jnp.bfloat16) for count in (share, tail_rows)],
        rows * channels,
        parts,
    )


def decode(hidden, tail, conv_w, fade_count):
    share, channels = hidden.shape
    return plain_call(
        decode_kernel,
        "decode",
        [jax.ShapeDtypeStruct((1, share, channels), jnp.bfloat16)],
        2 * share * KT * channels * channels,
        (fade_count, hidden, tail, conv_w),
        [SMEM_SPEC],
    )[0]


def per_device(
    query, noisy_kv, clean_kv, causal_mask, step_index, finished, w_in, conv_w, fade_count
):
    steps, _, rows, columns = query.shape
    heads = columns // HD
    middle = (heads - max(1, heads // 3)) * HD
    row_count = steps * rows
    span = lax.axis_size("span")
    axes = ("mp", "seq")
    acc_shape = jax.ShapeDtypeStruct((heads, HD, row_count), jnp.float32)
    stat_shape = jax.ShapeDtypeStruct((heads, row_count), jnp.float32)
    pair_flops = 4 * row_count * rows * columns

    first_pairs = [(0, 2), (2, 3)] if span == 4 else [(c, c + 1) for c in range(span - 1)]
    near = send(clean_kv, first_pairs)
    if span == 4:
        direct = send(clean_kv, [(1, 3)])
    carry = plain_call(
        own_kernel,
        "own",
        [acc_shape, stat_shape, stat_shape],
        pair_flops,
        (step_index, query, noisy_kv),
        [SMEM_SPEC],
    )
    pieces = project(after(finished, carry[1]), w_in)
    parts = [pieces[0]] + [swap(p, axes, offset + 1) for offset, p in enumerate(pieces[1:])]
    hidden, tail = gather(parts, rows)
    tail = hop(tail, "span", 1)
    if span == 4:
        near = after(near, hidden)
        forwards = lax.axis_index("span") == 2
        passed = [jnp.where(forwards, near[which], clean_kv[which]) for which in range(2)]
        passed = [passed[0], passed[1][:, :, :middle], passed[1][:, :, middle:]]
        passed = [hop(block, "span", 1) for block in passed]
        early = [(near, {2: 0, 3: 2}), (direct, {3: 1})]
        keys, *values = passed
        last_plan = {1: 0, 2: 1, 3: 0}
    else:
        ring = [near]
        for _ in range(2, span):
            ring.append(hop(ring[-1], "span", 1))
        early = [(block, delivered(span, back + 1)) for back, block in enumerate(ring[:-1])]
        keys, values = ring[-1], ring[-1:] * 2
        last_plan = delivered(span, span - 1)
    for block, plan in early:
        carry = plain_call(
            functools.partial(mid_kernel, plan),
            "middle",
            [acc_shape, stat_shape, stat_shape],
            pair_flops,
            (step_index, causal_mask, query, block, *carry),
            [SMEM_SPEC] * 2,
        )
    acc, weights = plain_call(
        functools.partial(score_kernel, [last_plan]),
        "score",
        [acc_shape, jax.ShapeDtypeStruct((heads, rows, row_count), jnp.bfloat16)],
        pair_flops // 2,
        (step_index, causal_mask, query, keys, *carry),
        [SMEM_SPEC] * 2,
    )
    square_shape = jax.ShapeDtypeStruct((1, row_count), jnp.float32)
    front, squares = plain_call(
        functools.partial(average_kernel, 0, middle // HD),
        "average",
        [jax.ShapeDtypeStruct((steps, rows, middle), jnp.float32), square_shape],
        pair_flops // 4,
        (acc, weights, values[0]),
    )
    averaged, squares = plain_call(
        functools.partial(rest_kernel, middle // HD, heads),
        "rest",
        [jax.ShapeDtypeStruct((heads - middle // HD, HD, row_count), jnp.float32), square_shape],
        pair_flops // 4,
        (acc, weights, values[1], squares),
    )
    others = [swap(squares, axes, offset) for offset in range(2, lax.axis_size(axes))]
    back, squares = plain_call(
        turn_kernel,
        "turn",
        [jax.ShapeDtypeStruct((steps, rows, columns - middle), jnp.float32), square_shape],
        row_count * columns,
        (averaged, squares),
    )
    others.append(swap(squares, axes, 1))
    decoded = decode(after(hidden, back), tail, conv_w, fade_count)
    attended = plain_call(
        functools.partial(scale_kernel, columns * lax.axis_size(axes)),
        "scale",
        jax.ShapeDtypeStruct(query.shape, jnp.bfloat16),
        row_count * columns,
        (front, back, squares, *others),
        out_specs=HBM_SPEC,
        scratch=[
            pltpu.VMEM((steps, rows, columns), jnp.bfloat16),
            pltpu.SemaphoreType.DMA((steps,)),
        ],
    )
    return (attended, decoded)


def solution(mesh):
    placed = (
        P(None, ("groups", "span"), None, ("mp", "seq")),
        P(None, None, ("groups", "span"), None, ("mp", "seq")),
        P(None, ("groups", "span"), None, ("mp", "seq")),
        P("groups", None),
        P("groups", None),
        P(("groups", "span"), None, ("mp", "seq")),
        P(("mp", "seq"), None),
        P(),
        P(("groups", "span")),
    )
    return jax.shard_map(
        per_device,
        mesh=mesh,
        in_specs=placed,
        out_specs=(
            P(None, ("groups", "span"), None, ("mp", "seq")),
            P(("groups", "span"), ("mp", "seq"), None),
        ),
        check_vma=False,
    )
```

```python
import functools
import math

import jax
import jax.numpy as jnp
from jax import lax
from jax.experimental import pallas as pl
from jax.experimental.pallas import tpu as pltpu
from jax.sharding import PartitionSpec as P

FR = 6
HD = 128
KT = 3
FADE = 2
NSTEPS = 64
LOG2E = 1.4426950408889634
VMEM_LIMIT = 24 * 1024 * 1024
VMEM_ALL = 60 * 1024 * 1024

SMEM_SPEC = pl.BlockSpec(memory_space=pltpu.SMEM)
VMEM_SPEC = pl.BlockSpec(memory_space=pltpu.VMEM)
HBM_SPEC = pl.BlockSpec(memory_space=pltpu.HBM)


def cost(flops, nbytes):
    return pl.CostEstimate(flops=flops, bytes_accessed=nbytes, transcendentals=0)


def hop(value, axis, steps):
    count = lax.axis_size(axis)
    return lax.ppermute(value, axis, [(source, source + steps) for source in range(count - steps)])


def swap(value, axes, offset):
    count = lax.axis_size(axes)
    if count & (count - 1) == 0:
        pairs = [(source, source ^ offset) for source in range(count)]
    else:
        pairs = [(source, (source + offset) % count) for source in range(count)]
    return lax.ppermute(value, axes, pairs)


def target_of(axes, offset):
    count = lax.axis_size(axes)
    mine = lax.axis_index(axes)
    if count & (count - 1) == 0:
        return mine ^ offset
    return lax.rem(mine + offset, count)


def after(value, *earlier):
    return lax.optimization_barrier((value, *earlier))[0]


def nt_dot(left, right):
    return lax.dot_general(left, right, (((1,), (1,)), ((), ())), preferred_element_type=jnp.float32)


def tn_dot(left, right):
    return lax.dot_general(left, right, (((0,), (0,)), ((), ())), preferred_element_type=jnp.float32)


def nn_dot(left, right):
    return jnp.dot(left, right, preferred_element_type=jnp.float32)


def row_factors(step_ref, position, steps, rows):
    lane = lax.broadcasted_iota(jnp.int32, (1, steps * rows), 1)
    index = jnp.full(lane.shape, step_ref[position, 0], jnp.int32)
    for step in range(1, steps):
        index = jnp.where(lane >= step * rows, step_ref[position, step], index)
    fraction = 1.0 - index.astype(jnp.float32) / NSTEPS
    level = 3.0 * fraction / (1.0 + 2.0 * fraction)
    return (0.5 + level) * (LOG2E / math.sqrt(HD))


def lane_windows(steps, rows):
    total = steps * rows
    return [
        (step * rows // HD * HD, min(total, -(-(step + 1) * rows // HD) * HD))
        for step in range(steps)
    ]


def join_steps(pieces, windows, rows):
    total = windows[-1][1]
    tiles = []
    for first in range(0, total, HD):
        stop = min(first + HD, total)
        tile = None
        for step, (begin, end) in enumerate(windows):
            if begin <= first and stop <= end and step * rows < stop and first < (step + 1) * rows:
                part = pieces[step][:, first - begin : stop - begin]
                if tile is None:
                    tile = part
                else:
                    lane = lax.broadcasted_iota(jnp.int32, part.shape, 1) + first
                    tile = jnp.where(lane >= step * rows, part, tile)
        tiles.append(tile)
    return jnp.concatenate(tiles, 1)


def own_kernel(step_ref, q_ref, kv_ref, acc_ref, top_ref, total_ref):
    position = lax.axis_index("span")
    steps, _, rows, columns = q_ref.shape
    factors = row_factors(step_ref, position, steps, rows)
    windows = lane_windows(steps, rows)
    for head in range(columns // HD):
        cut = slice(head * HD, (head + 1) * HD)
        queries = q_ref[:, 0, :, cut].reshape(steps * rows, HD)
        scores = join_steps(
            [nt_dot(kv_ref[s, 0, 0, :, cut], queries[a:b]) for s, (a, b) in enumerate(windows)],
            windows,
            rows,
        )
        scores = scores * factors
        top = jnp.max(scores, axis=0, keepdims=True)
        weights = jnp.exp2(scores - top)
        rounded = weights.astype(jnp.bfloat16)
        acc_ref[head] = join_steps(
            [tn_dot(kv_ref[s, 1, 0, :, cut], rounded[:, a:b]) for s, (a, b) in enumerate(windows)],
            windows,
            rows,
        )
        top_ref[head : head + 1] = top
        total_ref[head : head + 1] = jnp.sum(weights, axis=0, keepdims=True)


def absorb(queries, keys, values, factors, acc, top, total):
    scores = nt_dot(keys, queries) * factors
    newest = jnp.maximum(top, jnp.max(scores, axis=0, keepdims=True))
    weights = jnp.exp2(scores - newest)
    shrink = jnp.exp2(top - newest)
    total = total * shrink + jnp.sum(weights, axis=0, keepdims=True)
    acc = acc * shrink + tn_dot(values, weights.astype(jnp.bfloat16))
    return acc, newest, total


def visible(mask_ref, position, blocks):
    seen = False
    for place, block in blocks.items():
        seen = seen | ((position == place) & (mask_ref[place, block] > 0))
    return seen


def half(ref, which, cut):
    return ref[which, 0, :, cut] if len(ref.shape) == 4 else ref[0, :, cut]


def mid_kernel(plan, step_ref, mask_ref, q_ref, *refs):
    block_refs, (acc_in, top_in, total_in, acc_ref, top_ref, total_ref) = refs[:-6], refs[-6:]
    position = lax.axis_index("span")
    steps, _, rows, columns = q_ref.shape
    seen = visible(mask_ref, position, plan)

    @pl.when(seen)
    def _():
        factors = row_factors(step_ref, position, steps, rows)
        for head in range(columns // HD):
            cut = slice(head * HD, (head + 1) * HD)
            queries = q_ref[:, 0, :, cut].reshape(steps * rows, HD)
            acc, top, total = absorb(
                queries,
                half(block_refs[0], 0, cut),
                half(block_refs[-1], 1, cut),
                factors,
                acc_in[head],
                top_in[head : head + 1],
                total_in[head : head + 1],
            )
            acc_ref[head] = acc
            top_ref[head : head + 1] = top
            total_ref[head : head + 1] = total

    @pl.when(jnp.logical_not(seen))
    def _():
        acc_ref[...] = acc_in[...]
        top_ref[...] = top_in[...]
        total_ref[...] = total_in[...]


def score_kernel(plans, step_ref, mask_ref, q_ref, *refs):
    key_refs, (acc_in, top_in, total_in, acc_ref, w_ref) = refs[:-5], refs[-5:]
    position = lax.axis_index("span")
    steps, _, rows, columns = q_ref.shape

    def finish(key_ref):
        factors = row_factors(step_ref, position, steps, rows)
        for head in range(columns // HD):
            cut = slice(head * HD, (head + 1) * HD)
            queries = q_ref[:, 0, :, cut].reshape(steps * rows, HD)
            scores = nt_dot(half(key_ref, 0, cut), queries) * factors
            top = top_in[head : head + 1]
            newest = jnp.maximum(top, jnp.max(scores, axis=0, keepdims=True))
            weights = jnp.exp2(scores - newest)
            shrink = jnp.exp2(top - newest)
            total = total_in[head : head + 1] * shrink + jnp.sum(weights, axis=0, keepdims=True)
            inverse = 1.0 / total
            w_ref[head] = (weights * inverse).astype(jnp.bfloat16)
            acc_ref[head] = acc_in[head] * (shrink * inverse)

    rest = True
    for plan, key_ref in zip(plans, key_refs):
        seen = visible(mask_ref, position, plan)
        rest = jnp.logical_and(rest, jnp.logical_not(seen))
        pl.when(seen)(functools.partial(finish, key_ref))

    @pl.when(rest)
    def _():
        w_ref[...] = jnp.zeros_like(w_ref)
        for head in range(columns // HD):
            acc_ref[head] = acc_in[head] * (1.0 / total_in[head : head + 1])


def average_head(head, acc_ref, w_ref, value_ref, first):
    if value_ref.shape[-1] == acc_ref.shape[0] * HD:
        first = 0
    cut = slice((head - first) * HD, (head - first + 1) * HD)
    return acc_ref[head] + tn_dot(half(value_ref, 1, cut), w_ref[head])


def average_kernel(begin, end, acc_ref, w_ref, value_ref, average_ref, square_ref):
    squares = jnp.zeros(square_ref.shape, jnp.float32)
    for head in range(begin, end):
        average = average_head(head, acc_ref, w_ref, value_ref, begin)
        squares = squares + jnp.sum(average * average, axis=0, keepdims=True)
        average_ref[:, :, (head - begin) * HD : (head - begin + 1) * HD] = average.T.reshape(
            average_ref.shape[:2] + (HD,)
        )
    square_ref[...] = squares


def rest_kernel(begin, end, acc_ref, w_ref, value_ref, before_ref, average_ref, square_ref):
    squares = before_ref[...]
    for head in range(begin, end):
        average = average_head(head, acc_ref, w_ref, value_ref, begin)
        squares = squares + jnp.sum(average * average, axis=0, keepdims=True)
        average_ref[head - begin] = average
    square_ref[...] = squares


def turn_kernel(in_ref, square_in, out_ref, square_ref):
    steps, rows, _ = out_ref.shape
    for head in range(in_ref.shape[0]):
        out_ref[:, :, head * HD : (head + 1) * HD] = in_ref[head].T.reshape(steps, rows, HD)
    square_ref[...] = square_in[...]


def scale_kernel(width, front_ref, back_ref, *refs):
    part_refs, (out_hbm, out_ref, sem) = refs[:-3], refs[-3:]
    total = part_refs[0][...]
    for ref in part_refs[1:]:
        total = total + ref[...]
    inverse = lax.rsqrt(total / width + 1e-06)
    steps, rows, columns = out_ref.shape
    copies = []
    for step in range(steps):
        own = inverse[:, step * rows : (step + 1) * rows]
        factor = jnp.broadcast_to(own, (HD, rows)).T
        place = 0
        for ref in (front_ref, back_ref):
            for first in range(0, ref.shape[2], HD):
                average = ref[step, :, first : first + HD]
                out_ref[step, :, place : place + HD] = (average * factor).astype(jnp.bfloat16)
                place += HD
        copies.append(pltpu.make_async_copy(out_ref.at[step], out_hbm.at[step, 0], sem.at[step]))
        copies[-1].start()
    for copy in copies:
        copy.wait()


def send(value, pairs):
    return lax.ppermute(value, "span", pairs)


def delivered(span, back):
    return {place: place - back for place in range(back, span)}


def plain_call(kernel, name, out_shape, flops, operands, in_specs=(), out_specs=None, scratch=(), limit=VMEM_LIMIT):
    nbytes = sum(math.prod(o.shape) * o.dtype.itemsize for o in operands)
    if out_specs is None:
        out_specs = [VMEM_SPEC] * len(out_shape)
    return pl.pallas_call(
        kernel,
        in_specs=list(in_specs) + [VMEM_SPEC] * (len(operands) - len(in_specs)),
        out_specs=out_specs,
        out_shape=out_shape,
        scratch_shapes=list(scratch),
        compiler_params=pltpu.CompilerParams(vmem_limit_bytes=limit),
        cost_estimate=cost(flops, nbytes),
        name=name,
    )(*operands)


def picker(shape, wanted):
    row = lax.broadcasted_iota(jnp.int32, shape, 0)
    column = lax.broadcasted_iota(jnp.int32, shape, 1)
    return jnp.where(column == wanted(row), 1.0, 0.0).astype(jnp.bfloat16)


def project_kernel(axes, x_hbm, w_hbm, *refs):
    out_refs, (x_ref, w_ref, x_sem, w_sem) = refs[:-4], refs[-4:]
    rows, depth = x_ref.shape
    share = out_refs[0].shape[0]
    x_copy = pltpu.make_async_copy(x_hbm.at[0], x_ref, x_sem)
    x_copy.start()
    copies = []
    for place, first in enumerate(range(0, depth, 2 * HD)):
        cut = slice(first, min(first + 2 * HD, depth))
        copies.append((cut, pltpu.make_async_copy(w_hbm.at[cut], w_ref.at[cut], w_sem.at[place])))
        copies[-1][1].start()
    total = jnp.zeros((rows, w_ref.shape[1]), jnp.float32)
    x_copy.wait()
    for cut, w_copy in copies:
        w_copy.wait()
        total = total + nn_dot(x_ref[:, cut], w_ref[cut])
    projected = total.astype(jnp.bfloat16)
    for offset, out_ref in enumerate(out_refs):
        first = target_of(axes, offset) * share
        chosen = picker((share, rows), lambda row: row + first)
        out_ref[...] = nn_dot(chosen, projected).astype(jnp.bfloat16)


def gather_kernel(*refs):
    hidden_ref, tail_ref = refs[-2:]
    total = refs[0][...].astype(jnp.float32)
    for ref in refs[1:-2]:
        total = total + ref[...].astype(jnp.float32)
    hidden = total.astype(jnp.bfloat16)
    hidden_ref[...] = hidden
    kept = KT - 1 + FADE
    shape = (tail_ref.shape[0], hidden.shape[0])
    chosen = picker(shape, lambda row: row // kept * FR + FR - kept + row % kept)
    tail_ref[...] = nn_dot(chosen, hidden).astype(jnp.bfloat16)


def decode_kernel(fade_ref, hidden_ref, tail_ref, conv_ref, out_ref):
    position = lax.axis_index("span")
    share = hidden_ref.shape[0]
    spatial = share // FR
    kept = KT - 1 + FADE
    wide = FADE + FR
    hidden, tail = hidden_ref[...], tail_ref[...]
    mixed = jnp.zeros((spatial * wide, out_ref.shape[2]), jnp.float32)
    for tap in range(KT):
        def from_tail(row):
            place = row % wide + KT - 1 - tap
            return jnp.where(place < kept, row // wide * kept + place, -1)

        def from_hidden(row):
            place = row % wide + KT - 1 - tap
            return jnp.where(place >= kept, row // wide * FR + place - kept, -1)

        window = nn_dot(picker((spatial * wide, tail.shape[0]), from_tail), tail)
        window = window + nn_dot(picker((spatial * wide, share), from_hidden), hidden)
        mixed = mixed + nn_dot(window.astype(jnp.bfloat16), conv_ref[tap])
    frames = (mixed * jax.nn.sigmoid(mixed)).astype(jnp.bfloat16)
    fade = fade_ref[0]
    shape = (share, spatial * wide)
    current = nn_dot(picker(shape, lambda row: row // FR * wide + FADE + row % FR), frames)

    def faded(row):
        return jnp.where(row % FR < fade, row // FR * wide + FADE - fade + row % FR, -1)

    previous = nn_dot(picker(shape, faded), frames)
    frame = lax.broadcasted_iota(jnp.int32, (share, out_ref.shape[2]), 0) % FR
    fade_float = jnp.full(frame.shape, fade, jnp.int32).astype(jnp.float32)
    weight = (frame.astype(jnp.float32) + 1.0) / (fade_float + 1.0)
    weight = jnp.where((frame < fade) & (position > 0), weight, 1.0)
    out_ref[0] = (weight * current + (1.0 - weight) * previous).astype(jnp.bfloat16)


def project(finished, w_in):
    axes = ("mp", "seq")
    parts = lax.axis_size(axes)
    _, rows, depth = finished.shape
    channels = w_in.shape[1]
    chunks = -(-depth // (2 * HD))
    return plain_call(
        functools.partial(project_kernel, axes),
        "project",
        [jax.ShapeDtypeStruct((rows // parts, channels), jnp.bfloat16)] * parts,
        2 * rows * depth * channels,
        (finished, w_in),
        [HBM_SPEC] * 2,
        scratch=[
            pltpu.VMEM((rows, depth), jnp.bfloat16),
            pltpu.VMEM((depth, channels), jnp.bfloat16),
            pltpu.SemaphoreType.DMA,
            pltpu.SemaphoreType.DMA((chunks,)),
        ],
    )


def gather(parts, rows):
    share, channels = parts[0].shape
    tail_rows = share // FR * (KT - 1 + FADE)
    return plain_call(
        gather_kernel,
        "gather",
        [jax.ShapeDtypeStruct((count, channels), jnp.bfloat16) for count in (share, tail_rows)],
        rows * channels,
        parts,
    )


def decode(hidden, tail, conv_w, fade_count):
    share, channels = hidden.shape
    return plain_call(
        decode_kernel,
        "decode",
        [jax.ShapeDtypeStruct((1, share, channels), jnp.bfloat16)],
        2 * share * KT * channels * channels,
        (fade_count, hidden, tail, conv_w),
        [SMEM_SPEC],
    )[0]


def per_device(
    query, noisy_kv, clean_kv, causal_mask, step_index, finished, w_in, conv_w, fade_count
):
    steps, _, rows, columns = query.shape
    heads = columns // HD
    middle = (heads - max(1, heads // 3)) * HD
    row_count = steps * rows
    span = lax.axis_size("span")
    axes = ("mp", "seq")
    acc_shape = jax.ShapeDtypeStruct((heads, HD, row_count), jnp.float32)
    stat_shape = jax.ShapeDtypeStruct((heads, row_count), jnp.float32)
    pair_flops = 4 * row_count * rows * columns

    first_pairs = [(0, 2), (2, 3)] if span == 4 else [(c, c + 1) for c in range(span - 1)]
    near = send(clean_kv, first_pairs)
    if span == 4:
        direct = send(clean_kv, [(1, 3)])
    carry = plain_call(
        own_kernel,
        "own",
        [acc_shape, stat_shape, stat_shape],
        pair_flops,
        (step_index, query, noisy_kv),
        [SMEM_SPEC],
    )
    pieces = project(after(finished, carry[1]), w_in)
    parts = [pieces[0]] + [swap(p, axes, offset + 1) for offset, p in enumerate(pieces[1:])]
    hidden, tail = gather(parts, rows)
    tail = hop(tail, "span", 1)
    if span == 4:
        near = after(near, carry[0], pieces[0])
        forwards = lax.axis_index("span") == 2
        passed = [jnp.where(forwards, near[which], clean_kv[which]) for which in range(2)]
        passed = [passed[0], passed[1][:, :, :middle], passed[1][:, :, middle:]]
        passed = [hop(block, "span", 1) for block in passed]
        early = [(near, {2: 0, 3: 2}), (direct, {3: 1})]
        keys, *values = passed
        last_plan = {1: 0, 2: 1, 3: 0}
    else:
        ring = [near]
        for _ in range(2, span):
            ring.append(hop(ring[-1], "span", 1))
        early = [(block, delivered(span, back + 1)) for back, block in enumerate(ring[:-1])]
        keys, values = ring[-1], ring[-1:] * 2
        last_plan = delivered(span, span - 1)
    for block, plan in early:
        carry = plain_call(
            functools.partial(mid_kernel, plan),
            "middle",
            [acc_shape, stat_shape, stat_shape],
            pair_flops,
            (step_index, causal_mask, query, block, *carry),
            [SMEM_SPEC] * 2,
        )
    acc, weights = plain_call(
        functools.partial(score_kernel, [last_plan]),
        "score",
        [acc_shape, jax.ShapeDtypeStruct((heads, rows, row_count), jnp.bfloat16)],
        pair_flops // 2,
        (step_index, causal_mask, query, keys, *carry),
        [SMEM_SPEC] * 2,
    )
    square_shape = jax.ShapeDtypeStruct((1, row_count), jnp.float32)
    front, squares = plain_call(
        functools.partial(average_kernel, 0, middle // HD),
        "average",
        [jax.ShapeDtypeStruct((steps, rows, middle), jnp.float32), square_shape],
        pair_flops // 4,
        (acc, weights, values[0]),
    )
    averaged, squares = plain_call(
        functools.partial(rest_kernel, middle // HD, heads),
        "rest",
        [jax.ShapeDtypeStruct((heads - middle // HD, HD, row_count), jnp.float32), square_shape],
        pair_flops // 4,
        (acc, weights, values[1], squares),
    )
    others = [swap(squares, axes, offset) for offset in range(2, lax.axis_size(axes))]
    back, squares = plain_call(
        turn_kernel,
        "turn",
        [jax.ShapeDtypeStruct((steps, rows, columns - middle), jnp.float32), square_shape],
        row_count * columns,
        (averaged, squares),
    )
    others.append(swap(squares, axes, 1))
    decoded = decode(after(hidden, back), tail, conv_w, fade_count)
    attended = plain_call(
        functools.partial(scale_kernel, columns * lax.axis_size(axes)),
        "scale",
        jax.ShapeDtypeStruct(query.shape, jnp.bfloat16),
        row_count * columns,
        (front, back, squares, *others),
        out_specs=HBM_SPEC,
        scratch=[
            pltpu.VMEM((steps, rows, columns), jnp.bfloat16),
            pltpu.SemaphoreType.DMA((steps,)),
        ],
    )
    return (attended, decoded)


def solution(mesh):
    placed = (
        P(None, ("groups", "span"), None, ("mp", "seq")),
        P(None, None, ("groups", "span"), None, ("mp", "seq")),
        P(None, ("groups", "span"), None, ("mp", "seq")),
        P("groups", None),
        P("groups", None),
        P(("groups", "span"), None, ("mp", "seq")),
        P(("mp", "seq"), None),
        P(),
        P(("groups", "span")),
    )
    return jax.shard_map(
        per_device,
        mesh=mesh,
        in_specs=placed,
        out_specs=(
            P(None, ("groups", "span"), None, ("mp", "seq")),
            P(("groups", "span"), ("mp", "seq"), None),
        ),
        check_vma=False,
    )
```

```python
import functools
import math

import jax
import jax.numpy as jnp
from jax import lax
from jax.experimental import pallas as pl
from jax.experimental.pallas import tpu as pltpu
from jax.sharding import PartitionSpec as P

FR = 6
HD = 128
KT = 3
FADE = 2
NSTEPS = 64
LOG2E = 1.4426950408889634
VMEM_LIMIT = 24 * 1024 * 1024
VMEM_ALL = 60 * 1024 * 1024

SMEM_SPEC = pl.BlockSpec(memory_space=pltpu.SMEM)
VMEM_SPEC = pl.BlockSpec(memory_space=pltpu.VMEM)
HBM_SPEC = pl.BlockSpec(memory_space=pltpu.HBM)


def cost(flops, nbytes):
    return pl.CostEstimate(flops=flops, bytes_accessed=nbytes, transcendentals=0)


def hop(value, axis, steps):
    count = lax.axis_size(axis)
    return lax.ppermute(value, axis, [(source, source + steps) for source in range(count - steps)])


def swap(value, axes, offset):
    count = lax.axis_size(axes)
    if count & (count - 1) == 0:
        pairs = [(source, source ^ offset) for source in range(count)]
    else:
        pairs = [(source, (source + offset) % count) for source in range(count)]
    return lax.ppermute(value, axes, pairs)


def target_of(axes, offset):
    count = lax.axis_size(axes)
    mine = lax.axis_index(axes)
    if count & (count - 1) == 0:
        return mine ^ offset
    return lax.rem(mine + offset, count)


def after(value, *earlier):
    return lax.optimization_barrier((value, *earlier))[0]


def nt_dot(left, right):
    return lax.dot_general(left, right, (((1,), (1,)), ((), ())), preferred_element_type=jnp.float32)


def tn_dot(left, right):
    return lax.dot_general(left, right, (((0,), (0,)), ((), ())), preferred_element_type=jnp.float32)


def nn_dot(left, right):
    return jnp.dot(left, right, preferred_element_type=jnp.float32)


def row_factors(step_ref, position, steps, rows):
    lane = lax.broadcasted_iota(jnp.int32, (1, steps * rows), 1)
    index = jnp.full(lane.shape, step_ref[position, 0], jnp.int32)
    for step in range(1, steps):
        index = jnp.where(lane >= step * rows, step_ref[position, step], index)
    fraction = 1.0 - index.astype(jnp.float32) / NSTEPS
    level = 3.0 * fraction / (1.0 + 2.0 * fraction)
    return (0.5 + level) * (LOG2E / math.sqrt(HD))


def lane_windows(steps, rows):
    total = steps * rows
    return [
        (step * rows // HD * HD, min(total, -(-(step + 1) * rows // HD) * HD))
        for step in range(steps)
    ]


def join_steps(pieces, windows, rows):
    total = windows[-1][1]
    tiles = []
    for first in range(0, total, HD):
        stop = min(first + HD, total)
        tile = None
        for step, (begin, end) in enumerate(windows):
            if begin <= first and stop <= end and step * rows < stop and first < (step + 1) * rows:
                part = pieces[step][:, first - begin : stop - begin]
                if tile is None:
                    tile = part
                else:
                    lane = lax.broadcasted_iota(jnp.int32, part.shape, 1) + first
                    tile = jnp.where(lane >= step * rows, part, tile)
        tiles.append(tile)
    return jnp.concatenate(tiles, 1)


def own_kernel(step_ref, q_ref, kv_ref, acc_ref, top_ref, total_ref):
    position = lax.axis_index("span")
    steps, _, rows, columns = q_ref.shape
    factors = row_factors(step_ref, position, steps, rows)
    windows = lane_windows(steps, rows)
    for head in range(columns // HD):
        cut = slice(head * HD, (head + 1) * HD)
        queries = q_ref[:, 0, :, cut].reshape(steps * rows, HD)
        scores = join_steps(
            [nt_dot(kv_ref[s, 0, 0, :, cut], queries[a:b]) for s, (a, b) in enumerate(windows)],
            windows,
            rows,
        )
        scores = scores * factors
        top = jnp.max(scores, axis=0, keepdims=True)
        weights = jnp.exp2(scores - top)
        rounded = weights.astype(jnp.bfloat16)
        acc_ref[head] = join_steps(
            [tn_dot(kv_ref[s, 1, 0, :, cut], rounded[:, a:b]) for s, (a, b) in enumerate(windows)],
            windows,
            rows,
        )
        top_ref[head : head + 1] = top
        total_ref[head : head + 1] = jnp.sum(weights, axis=0, keepdims=True)


def absorb(queries, keys, values, factors, acc, top, total):
    scores = nt_dot(keys, queries) * factors
    newest = jnp.maximum(top, jnp.max(scores, axis=0, keepdims=True))
    weights = jnp.exp2(scores - newest)
    shrink = jnp.exp2(top - newest)
    total = total * shrink + jnp.sum(weights, axis=0, keepdims=True)
    acc = acc * shrink + tn_dot(values, weights.astype(jnp.bfloat16))
    return acc, newest, total


def visible(mask_ref, position, blocks):
    seen = False
    for place, block in blocks.items():
        seen = seen | ((position == place) & (mask_ref[place, block] > 0))
    return seen


def half(ref, which, cut):
    return ref[which, 0, :, cut] if len(ref.shape) == 4 else ref[0, :, cut]


def mid_kernel(plan, step_ref, mask_ref, q_ref, *refs):
    block_refs, (acc_in, top_in, total_in, acc_ref, top_ref, total_ref) = refs[:-6], refs[-6:]
    position = lax.axis_index("span")
    steps, _, rows, columns = q_ref.shape
    seen = visible(mask_ref, position, plan)

    @pl.when(seen)
    def _():
        factors = row_factors(step_ref, position, steps, rows)
        for head in range(columns // HD):
            cut = slice(head * HD, (head + 1) * HD)
            queries = q_ref[:, 0, :, cut].reshape(steps * rows, HD)
            acc, top, total = absorb(
                queries,
                half(block_refs[0], 0, cut),
                half(block_refs[-1], 1, cut),
                factors,
                acc_in[head],
                top_in[head : head + 1],
                total_in[head : head + 1],
            )
            acc_ref[head] = acc
            top_ref[head : head + 1] = top
            total_ref[head : head + 1] = total

    @pl.when(jnp.logical_not(seen))
    def _():
        acc_ref[...] = acc_in[...]
        top_ref[...] = top_in[...]
        total_ref[...] = total_in[...]


def score_kernel(plans, step_ref, mask_ref, q_ref, *refs):
    key_refs, (acc_in, top_in, total_in, acc_ref, w_ref) = refs[:-5], refs[-5:]
    position = lax.axis_index("span")
    steps, _, rows, columns = q_ref.shape

    def finish(key_ref):
        factors = row_factors(step_ref, position, steps, rows)
        for head in range(columns // HD):
            cut = slice(head * HD, (head + 1) * HD)
            queries = q_ref[:, 0, :, cut].reshape(steps * rows, HD)
            scores = nt_dot(half(key_ref, 0, cut), queries) * factors
            top = top_in[head : head + 1]
            newest = jnp.maximum(top, jnp.max(scores, axis=0, keepdims=True))
            weights = jnp.exp2(scores - newest)
            shrink = jnp.exp2(top - newest)
            total = total_in[head : head + 1] * shrink + jnp.sum(weights, axis=0, keepdims=True)
            inverse = 1.0 / total
            w_ref[head] = (weights * inverse).astype(jnp.bfloat16)
            acc_ref[head] = acc_in[head] * (shrink * inverse)

    rest = True
    for plan, key_ref in zip(plans, key_refs):
        seen = visible(mask_ref, position, plan)
        rest = jnp.logical_and(rest, jnp.logical_not(seen))
        pl.when(seen)(functools.partial(finish, key_ref))

    @pl.when(rest)
    def _():
        w_ref[...] = jnp.zeros_like(w_ref)
        for head in range(columns // HD):
            acc_ref[head] = acc_in[head] * (1.0 / total_in[head : head + 1])


def average_head(head, acc_ref, w_ref, value_ref, first):
    if value_ref.shape[-1] == acc_ref.shape[0] * HD:
        first = 0
    cut = slice((head - first) * HD, (head - first + 1) * HD)
    return acc_ref[head] + tn_dot(half(value_ref, 1, cut), w_ref[head])


def average_kernel(begin, end, acc_ref, w_ref, value_ref, average_ref, square_ref):
    squares = jnp.zeros(square_ref.shape, jnp.float32)
    for head in range(begin, end):
        average = average_head(head, acc_ref, w_ref, value_ref, begin)
        squares = squares + jnp.sum(average * average, axis=0, keepdims=True)
        average_ref[:, :, (head - begin) * HD : (head - begin + 1) * HD] = average.T.reshape(
            average_ref.shape[:2] + (HD,)
        )
    square_ref[...] = squares


def rest_kernel(begin, end, acc_ref, w_ref, value_ref, before_ref, average_ref, square_ref):
    squares = before_ref[...]
    for head in range(begin, end):
        average = average_head(head, acc_ref, w_ref, value_ref, begin)
        squares = squares + jnp.sum(average * average, axis=0, keepdims=True)
        average_ref[head - begin] = average
    square_ref[...] = squares


def turn_kernel(in_ref, square_in, out_ref, square_ref):
    steps, rows, _ = out_ref.shape
    for head in range(in_ref.shape[0]):
        out_ref[:, :, head * HD : (head + 1) * HD] = in_ref[head].T.reshape(steps, rows, HD)
    square_ref[...] = square_in[...]


def scale_kernel(width, front_ref, back_ref, *refs):
    part_refs, (out_hbm, out_ref, sem) = refs[:-3], refs[-3:]
    total = part_refs[0][...]
    for ref in part_refs[1:]:
        total = total + ref[...]
    inverse = lax.rsqrt(total / width + 1e-06)
    steps, rows, columns = out_ref.shape
    copies = []
    for step in range(steps):
        own = inverse[:, step * rows : (step + 1) * rows]
        factor = jnp.broadcast_to(own, (HD, rows)).T
        place = 0
        for ref in (front_ref, back_ref):
            for first in range(0, ref.shape[2], HD):
                average = ref[step, :, first : first + HD]
                out_ref[step, :, place : place + HD] = (average * factor).astype(jnp.bfloat16)
                place += HD
        copies.append(pltpu.make_async_copy(out_ref.at[step], out_hbm.at[step, 0], sem.at[step]))
        copies[-1].start()
    for copy in copies:
        copy.wait()


def send(value, pairs):
    return lax.ppermute(value, "span", pairs)


def delivered(span, back):
    return {place: place - back for place in range(back, span)}


def plain_call(kernel, name, out_shape, flops, operands, in_specs=(), out_specs=None, scratch=(), limit=VMEM_LIMIT):
    nbytes = sum(math.prod(o.shape) * o.dtype.itemsize for o in operands)
    if out_specs is None:
        out_specs = [VMEM_SPEC] * len(out_shape)
    return pl.pallas_call(
        kernel,
        in_specs=list(in_specs) + [VMEM_SPEC] * (len(operands) - len(in_specs)),
        out_specs=out_specs,
        out_shape=out_shape,
        scratch_shapes=list(scratch),
        compiler_params=pltpu.CompilerParams(vmem_limit_bytes=limit),
        cost_estimate=cost(flops, nbytes),
        name=name,
    )(*operands)


def picker(shape, wanted):
    row = lax.broadcasted_iota(jnp.int32, shape, 0)
    column = lax.broadcasted_iota(jnp.int32, shape, 1)
    return jnp.where(column == wanted(row), 1.0, 0.0).astype(jnp.bfloat16)


def project_kernel(axes, x_hbm, w_hbm, *refs):
    out_refs, (x_ref, w_ref, x_sem, w_sem) = refs[:-4], refs[-4:]
    rows, depth = x_ref.shape
    share = out_refs[0].shape[0]
    x_copy = pltpu.make_async_copy(x_hbm.at[0], x_ref, x_sem)
    x_copy.start()
    copies = []
    for place, first in enumerate(range(0, depth, 2 * HD)):
        cut = slice(first, min(first + 2 * HD, depth))
        copies.append((cut, pltpu.make_async_copy(w_hbm.at[cut], w_ref.at[cut], w_sem.at[place])))
        copies[-1][1].start()
    total = jnp.zeros((rows, w_ref.shape[1]), jnp.float32)
    x_copy.wait()
    for cut, w_copy in copies:
        w_copy.wait()
        total = total + nn_dot(x_ref[:, cut], w_ref[cut])
    projected = total.astype(jnp.bfloat16)
    for offset, out_ref in enumerate(out_refs):
        first = target_of(axes, offset) * share
        chosen = picker((share, rows), lambda row: row + first)
        out_ref[...] = nn_dot(chosen, projected).astype(jnp.bfloat16)


def gather_kernel(*refs):
    hidden_ref, tail_ref = refs[-2:]
    total = refs[0][...].astype(jnp.float32)
    for ref in refs[1:-2]:
        total = total + ref[...].astype(jnp.float32)
    hidden = total.astype(jnp.bfloat16)
    hidden_ref[...] = hidden
    kept = KT - 1 + FADE
    shape = (tail_ref.shape[0], hidden.shape[0])
    chosen = picker(shape, lambda row: row // kept * FR + FR - kept + row % kept)
    tail_ref[...] = nn_dot(chosen, hidden).astype(jnp.bfloat16)


def decode_kernel(fade_ref, hidden_ref, tail_ref, conv_ref, out_ref):
    position = lax.axis_index("span")
    share = hidden_ref.shape[0]
    spatial = share // FR
    kept = KT - 1 + FADE
    wide = FADE + FR
    hidden, tail = hidden_ref[...], tail_ref[...]
    mixed = jnp.zeros((spatial * wide, out_ref.shape[2]), jnp.float32)
    for tap in range(KT):
        def from_tail(row):
            place = row % wide + KT - 1 - tap
            return jnp.where(place < kept, row // wide * kept + place, -1)

        def from_hidden(row):
            place = row % wide + KT - 1 - tap
            return jnp.where(place >= kept, row // wide * FR + place - kept, -1)

        window = nn_dot(picker((spatial * wide, tail.shape[0]), from_tail), tail)
        window = window + nn_dot(picker((spatial * wide, share), from_hidden), hidden)
        mixed = mixed + nn_dot(window.astype(jnp.bfloat16), conv_ref[tap])
    frames = (mixed * jax.nn.sigmoid(mixed)).astype(jnp.bfloat16)
    fade = fade_ref[0]
    shape = (share, spatial * wide)
    current = nn_dot(picker(shape, lambda row: row // FR * wide + FADE + row % FR), frames)

    def faded(row):
        return jnp.where(row % FR < fade, row // FR * wide + FADE - fade + row % FR, -1)

    previous = nn_dot(picker(shape, faded), frames)
    frame = lax.broadcasted_iota(jnp.int32, (share, out_ref.shape[2]), 0) % FR
    fade_float = jnp.full(frame.shape, fade, jnp.int32).astype(jnp.float32)
    weight = (frame.astype(jnp.float32) + 1.0) / (fade_float + 1.0)
    weight = jnp.where((frame < fade) & (position > 0), weight, 1.0)
    out_ref[0] = (weight * current + (1.0 - weight) * previous).astype(jnp.bfloat16)


def project(finished, w_in):
    axes = ("mp", "seq")
    parts = lax.axis_size(axes)
    _, rows, depth = finished.shape
    channels = w_in.shape[1]
    chunks = -(-depth // (2 * HD))
    return plain_call(
        functools.partial(project_kernel, axes),
        "project",
        [jax.ShapeDtypeStruct((rows // parts, channels), jnp.bfloat16)] * parts,
        2 * rows * depth * channels,
        (finished, w_in),
        [HBM_SPEC] * 2,
        scratch=[
            pltpu.VMEM((rows, depth), jnp.bfloat16),
            pltpu.VMEM((depth, channels), jnp.bfloat16),
            pltpu.SemaphoreType.DMA,
            pltpu.SemaphoreType.DMA((chunks,)),
        ],
        limit=VMEM_ALL,
    )


def gather(parts, rows):
    share, channels = parts[0].shape
    tail_rows = share // FR * (KT - 1 + FADE)
    return plain_call(
        gather_kernel,
        "gather",
        [jax.ShapeDtypeStruct((count, channels), jnp.bfloat16) for count in (share, tail_rows)],
        rows * channels,
        parts,
    )


def decode(hidden, tail, conv_w, fade_count):
    share, channels = hidden.shape
    return plain_call(
        decode_kernel,
        "decode",
        [jax.ShapeDtypeStruct((1, share, channels), jnp.bfloat16)],
        2 * share * KT * channels * channels,
        (fade_count, hidden, tail, conv_w),
        [SMEM_SPEC],
    )[0]


def per_device(
    query, noisy_kv, clean_kv, causal_mask, step_index, finished, w_in, conv_w, fade_count
):
    steps, _, rows, columns = query.shape
    heads = columns // HD
    middle = (heads - max(1, heads // 3)) * HD
    row_count = steps * rows
    span = lax.axis_size("span")
    axes = ("mp", "seq")
    acc_shape = jax.ShapeDtypeStruct((heads, HD, row_count), jnp.float32)
    stat_shape = jax.ShapeDtypeStruct((heads, row_count), jnp.float32)
    pair_flops = 4 * row_count * rows * columns

    first_pairs = [(0, 2), (2, 3)] if span == 4 else [(c, c + 1) for c in range(span - 1)]
    near = send(clean_kv, first_pairs)
    pieces = project(finished, w_in)
    parts = [pieces[0]] + [swap(p, axes, offset + 1) for offset, p in enumerate(pieces[1:])]
    if span == 4:
        direct = send(clean_kv, [(1, 3)])
    carry = plain_call(
        own_kernel,
        "own",
        [acc_shape, stat_shape, stat_shape],
        3 * pair_flops,
        (step_index, query, noisy_kv),
        [SMEM_SPEC],
    )
    hidden, tail = gather(parts, rows)
    tail = hop(tail, "span", 1)
    if span == 4:
        near = after(near, carry[0], hidden)
        forwards = lax.axis_index("span") == 2
        passed = [jnp.where(forwards, near[which], clean_kv[which]) for which in range(2)]
        passed = [passed[0], passed[1][:, :, :middle], passed[1][:, :, middle:]]
        passed = [hop(block, "span", 1) for block in passed]
        early = [(near, {2: 0, 3: 2}), (direct, {3: 1})]
        keys, *values = passed
        last_plan = {1: 0, 2: 1, 3: 0}
    else:
        ring = [near]
        for _ in range(2, span):
            ring.append(hop(ring[-1], "span", 1))
        early = [(block, delivered(span, back + 1)) for back, block in enumerate(ring[:-1])]
        keys, values = ring[-1], ring[-1:] * 2
        last_plan = delivered(span, span - 1)
    for block, plan in early:
        carry = plain_call(
            functools.partial(mid_kernel, plan),
            "middle",
            [acc_shape, stat_shape, stat_shape],
            pair_flops,
            (step_index, causal_mask, query, block, *carry),
            [SMEM_SPEC] * 2,
        )
    acc, weights = plain_call(
        functools.partial(score_kernel, [last_plan]),
        "score",
        [acc_shape, jax.ShapeDtypeStruct((heads, rows, row_count), jnp.bfloat16)],
        pair_flops // 2,
        (step_index, causal_mask, query, keys, *carry),
        [SMEM_SPEC] * 2,
    )
    square_shape = jax.ShapeDtypeStruct((1, row_count), jnp.float32)
    front, squares = plain_call(
        functools.partial(average_kernel, 0, middle // HD),
        "average",
        [jax.ShapeDtypeStruct((steps, rows, middle), jnp.float32), square_shape],
        pair_flops // 4,
        (acc, weights, values[0]),
    )
    averaged, squares = plain_call(
        functools.partial(rest_kernel, middle // HD, heads),
        "rest",
        [jax.ShapeDtypeStruct((heads - middle // HD, HD, row_count), jnp.float32), square_shape],
        pair_flops // 4,
        (acc, weights, values[1], squares),
    )
    others = [swap(squares, axes, offset) for offset in range(2, lax.axis_size(axes))]
    back, squares = plain_call(
        turn_kernel,
        "turn",
        [jax.ShapeDtypeStruct((steps, rows, columns - middle), jnp.float32), square_shape],
        row_count * columns,
        (averaged, squares),
    )
    others.append(swap(squares, axes, 1))
    decoded = decode(after(hidden, back), tail, conv_w, fade_count)
    attended = plain_call(
        functools.partial(scale_kernel, columns * lax.axis_size(axes)),
        "scale",
        jax.ShapeDtypeStruct(query.shape, jnp.bfloat16),
        row_count * columns,
        (front, back, squares, *others),
        out_specs=HBM_SPEC,
        scratch=[
            pltpu.VMEM((steps, rows, columns), jnp.bfloat16),
            pltpu.SemaphoreType.DMA((steps,)),
        ],
    )
    return (attended, decoded)


def solution(mesh):
    placed = (
        P(None, ("groups", "span"), None, ("mp", "seq")),
        P(None, None, ("groups", "span"), None, ("mp", "seq")),
        P(None, ("groups", "span"), None, ("mp", "seq")),
        P("groups", None),
        P("groups", None),
        P(("groups", "span"), None, ("mp", "seq")),
        P(("mp", "seq"), None),
        P(),
        P(("groups", "span")),
    )
    return jax.shard_map(
        per_device,
        mesh=mesh,
        in_specs=placed,
        out_specs=(
            P(None, ("groups", "span"), None, ("mp", "seq")),
            P(("groups", "span"), ("mp", "seq"), None),
        ),
        check_vma=False,
    )
```

```python
import functools
import math

import jax
import jax.numpy as jnp
from jax import lax
from jax.experimental import pallas as pl
from jax.experimental.pallas import tpu as pltpu
from jax.sharding import PartitionSpec as P

FR = 6
HD = 128
KT = 3
FADE = 2
NSTEPS = 64
LOG2E = 1.4426950408889634
VMEM_LIMIT = 24 * 1024 * 1024
VMEM_ALL = 60 * 1024 * 1024

SMEM_SPEC = pl.BlockSpec(memory_space=pltpu.SMEM)
VMEM_SPEC = pl.BlockSpec(memory_space=pltpu.VMEM)
HBM_SPEC = pl.BlockSpec(memory_space=pltpu.HBM)


def cost(flops, nbytes):
    return pl.CostEstimate(flops=flops, bytes_accessed=nbytes, transcendentals=0)


def hop(value, axis, steps):
    count = lax.axis_size(axis)
    return lax.ppermute(value, axis, [(source, source + steps) for source in range(count - steps)])


def swap(value, axes, offset):
    count = lax.axis_size(axes)
    if count & (count - 1) == 0:
        pairs = [(source, source ^ offset) for source in range(count)]
    else:
        pairs = [(source, (source + offset) % count) for source in range(count)]
    return lax.ppermute(value, axes, pairs)


def target_of(axes, offset):
    count = lax.axis_size(axes)
    mine = lax.axis_index(axes)
    if count & (count - 1) == 0:
        return mine ^ offset
    return lax.rem(mine + offset, count)


def after(value, *earlier):
    return lax.optimization_barrier((value, *earlier))[0]


def nt_dot(left, right):
    return lax.dot_general(left, right, (((1,), (1,)), ((), ())), preferred_element_type=jnp.float32)


def tn_dot(left, right):
    return lax.dot_general(left, right, (((0,), (0,)), ((), ())), preferred_element_type=jnp.float32)


def nn_dot(left, right):
    return jnp.dot(left, right, preferred_element_type=jnp.float32)


def row_factors(step_ref, position, steps, rows):
    lane = lax.broadcasted_iota(jnp.int32, (1, steps * rows), 1)
    index = jnp.full(lane.shape, step_ref[position, 0], jnp.int32)
    for step in range(1, steps):
        index = jnp.where(lane >= step * rows, step_ref[position, step], index)
    fraction = 1.0 - index.astype(jnp.float32) / NSTEPS
    level = 3.0 * fraction / (1.0 + 2.0 * fraction)
    return (0.5 + level) * (LOG2E / math.sqrt(HD))


def lane_windows(steps, rows):
    total = steps * rows
    return [
        (step * rows // HD * HD, min(total, -(-(step + 1) * rows // HD) * HD))
        for step in range(steps)
    ]


def join_steps(pieces, windows, rows):
    total = windows[-1][1]
    tiles = []
    for first in range(0, total, HD):
        stop = min(first + HD, total)
        tile = None
        for step, (begin, end) in enumerate(windows):
            if begin <= first and stop <= end and step * rows < stop and first < (step + 1) * rows:
                part = pieces[step][:, first - begin : stop - begin]
                if tile is None:
                    tile = part
                else:
                    lane = lax.broadcasted_iota(jnp.int32, part.shape, 1) + first
                    tile = jnp.where(lane >= step * rows, part, tile)
        tiles.append(tile)
    return jnp.concatenate(tiles, 1)


def own_kernel(step_ref, q_ref, kv_ref, acc_ref, top_ref, total_ref):
    position = lax.axis_index("span")
    steps, _, rows, columns = q_ref.shape
    factors = row_factors(step_ref, position, steps, rows)
    windows = lane_windows(steps, rows)
    for head in range(columns // HD):
        cut = slice(head * HD, (head + 1) * HD)
        queries = q_ref[:, 0, :, cut].reshape(steps * rows, HD)
        scores = join_steps(
            [nt_dot(kv_ref[s, 0, 0, :, cut], queries[a:b]) for s, (a, b) in enumerate(windows)],
            windows,
            rows,
        )
        scores = scores * factors
        top = jnp.max(scores, axis=0, keepdims=True)
        weights = jnp.exp2(scores - top)
        rounded = weights.astype(jnp.bfloat16)
        acc_ref[head] = join_steps(
            [tn_dot(kv_ref[s, 1, 0, :, cut], rounded[:, a:b]) for s, (a, b) in enumerate(windows)],
            windows,
            rows,
        )
        top_ref[head : head + 1] = top
        total_ref[head : head + 1] = jnp.sum(weights, axis=0, keepdims=True)


def absorb(queries, keys, values, factors, acc, top, total):
    scores = nt_dot(keys, queries) * factors
    newest = jnp.maximum(top, jnp.max(scores, axis=0, keepdims=True))
    weights = jnp.exp2(scores - newest)
    shrink = jnp.exp2(top - newest)
    total = total * shrink + jnp.sum(weights, axis=0, keepdims=True)
    acc = acc * shrink + tn_dot(values, weights.astype(jnp.bfloat16))
    return acc, newest, total


def visible(mask_ref, position, blocks):
    seen = False
    for place, block in blocks.items():
        seen = seen | ((position == place) & (mask_ref[place, block] > 0))
    return seen


def half(ref, which, cut):
    return ref[which, 0, :, cut] if len(ref.shape) == 4 else ref[0, :, cut]


def mid_kernel(plan, step_ref, mask_ref, q_ref, *refs):
    block_refs, (acc_in, top_in, total_in, acc_ref, top_ref, total_ref) = refs[:-6], refs[-6:]
    position = lax.axis_index("span")
    steps, _, rows, columns = q_ref.shape
    seen = visible(mask_ref, position, plan)

    @pl.when(seen)
    def _():
        factors = row_factors(step_ref, position, steps, rows)
        for head in range(columns // HD):
            cut = slice(head * HD, (head + 1) * HD)
            queries = q_ref[:, 0, :, cut].reshape(steps * rows, HD)
            acc, top, total = absorb(
                queries,
                half(block_refs[0], 0, cut),
                half(block_refs[-1], 1, cut),
                factors,
                acc_in[head],
                top_in[head : head + 1],
                total_in[head : head + 1],
            )
            acc_ref[head] = acc
            top_ref[head : head + 1] = top
            total_ref[head : head + 1] = total

    @pl.when(jnp.logical_not(seen))
    def _():
        acc_ref[...] = acc_in[...]
        top_ref[...] = top_in[...]
        total_ref[...] = total_in[...]


def score_kernel(plans, step_ref, mask_ref, q_ref, *refs):
    key_refs, (acc_in, top_in, total_in, acc_ref, w_ref) = refs[:-5], refs[-5:]
    position = lax.axis_index("span")
    steps, _, rows, columns = q_ref.shape

    def finish(key_ref):
        factors = row_factors(step_ref, position, steps, rows)
        for head in range(columns // HD):
            cut = slice(head * HD, (head + 1) * HD)
            queries = q_ref[:, 0, :, cut].reshape(steps * rows, HD)
            scores = nt_dot(half(key_ref, 0, cut), queries) * factors
            top = top_in[head : head + 1]
            newest = jnp.maximum(top, jnp.max(scores, axis=0, keepdims=True))
            weights = jnp.exp2(scores - newest)
            shrink = jnp.exp2(top - newest)
            total = total_in[head : head + 1] * shrink + jnp.sum(weights, axis=0, keepdims=True)
            inverse = 1.0 / total
            w_ref[head] = (weights * inverse).astype(jnp.bfloat16)
            acc_ref[head] = acc_in[head] * (shrink * inverse)

    rest = True
    for plan, key_ref in zip(plans, key_refs):
        seen = visible(mask_ref, position, plan)
        rest = jnp.logical_and(rest, jnp.logical_not(seen))
        pl.when(seen)(functools.partial(finish, key_ref))

    @pl.when(rest)
    def _():
        w_ref[...] = jnp.zeros_like(w_ref)
        for head in range(columns // HD):
            acc_ref[head] = acc_in[head] * (1.0 / total_in[head : head + 1])


def average_head(head, acc_ref, w_ref, value_ref, first):
    if value_ref.shape[-1] == acc_ref.shape[0] * HD:
        first = 0
    cut = slice((head - first) * HD, (head - first + 1) * HD)
    return acc_ref[head] + tn_dot(half(value_ref, 1, cut), w_ref[head])


def average_kernel(begin, end, acc_ref, w_ref, value_ref, average_ref, square_ref):
    squares = jnp.zeros(square_ref.shape, jnp.float32)
    for head in range(begin, end):
        average = average_head(head, acc_ref, w_ref, value_ref, begin)
        squares = squares + jnp.sum(average * average, axis=0, keepdims=True)
        average_ref[:, :, (head - begin) * HD : (head - begin + 1) * HD] = average.T.reshape(
            average_ref.shape[:2] + (HD,)
        )
    square_ref[...] = squares


def rest_kernel(begin, end, acc_ref, w_ref, value_ref, before_ref, average_ref, square_ref):
    squares = before_ref[...]
    for head in range(begin, end):
        average = average_head(head, acc_ref, w_ref, value_ref, begin)
        squares = squares + jnp.sum(average * average, axis=0, keepdims=True)
        average_ref[head - begin] = average
    square_ref[...] = squares


def turn_kernel(in_ref, out_ref):
    steps, rows, _ = out_ref.shape
    for head in range(in_ref.shape[0]):
        out_ref[:, :, head * HD : (head + 1) * HD] = in_ref[head].T.reshape(steps, rows, HD)


def scale_kernel(width, front_ref, back_ref, *refs):
    part_refs, (out_hbm, out_ref, sem) = refs[:-3], refs[-3:]
    total = part_refs[0][...]
    for ref in part_refs[1:]:
        total = total + ref[...]
    inverse = lax.rsqrt(total / width + 1e-06)
    steps, rows, columns = out_ref.shape
    copies = []
    for step in range(steps):
        own = inverse[:, step * rows : (step + 1) * rows]
        factor = jnp.broadcast_to(own, (HD, rows)).T
        place = 0
        for ref in (front_ref, back_ref):
            for first in range(0, ref.shape[2], HD):
                average = ref[step, :, first : first + HD]
                out_ref[step, :, place : place + HD] = (average * factor).astype(jnp.bfloat16)
                place += HD
        copies.append(pltpu.make_async_copy(out_ref.at[step], out_hbm.at[step, 0], sem.at[step]))
        copies[-1].start()
    for copy in copies:
        copy.wait()


def send(value, pairs):
    return lax.ppermute(value, "span", pairs)


def delivered(span, back):
    return {place: place - back for place in range(back, span)}


def plain_call(kernel, name, out_shape, flops, operands, in_specs=(), out_specs=None, scratch=(), limit=VMEM_LIMIT):
    nbytes = sum(math.prod(o.shape) * o.dtype.itemsize for o in operands)
    if out_specs is None:
        out_specs = [VMEM_SPEC] * len(out_shape)
    return pl.pallas_call(
        kernel,
        in_specs=list(in_specs) + [VMEM_SPEC] * (len(operands) - len(in_specs)),
        out_specs=out_specs,
        out_shape=out_shape,
        scratch_shapes=list(scratch),
        compiler_params=pltpu.CompilerParams(vmem_limit_bytes=limit),
        cost_estimate=cost(10 * flops, nbytes),
        name=name,
    )(*operands)


def picker(shape, wanted):
    row = lax.broadcasted_iota(jnp.int32, shape, 0)
    column = lax.broadcasted_iota(jnp.int32, shape, 1)
    return jnp.where(column == wanted(row), 1.0, 0.0).astype(jnp.bfloat16)


def project_kernel(axes, x_hbm, w_hbm, *refs):
    out_refs, (x_ref, w_ref, x_sem, w_sem) = refs[:-4], refs[-4:]
    rows, depth = x_ref.shape
    share = out_refs[0].shape[0]
    x_copy = pltpu.make_async_copy(x_hbm.at[0], x_ref, x_sem)
    x_copy.start()
    copies = []
    for place, first in enumerate(range(0, depth, 2 * HD)):
        cut = slice(first, min(first + 2 * HD, depth))
        copies.append((cut, pltpu.make_async_copy(w_hbm.at[cut], w_ref.at[cut], w_sem.at[place])))
        copies[-1][1].start()
    total = jnp.zeros((rows, w_ref.shape[1]), jnp.float32)
    x_copy.wait()
    for cut, w_copy in copies:
        w_copy.wait()
        total = total + nn_dot(x_ref[:, cut], w_ref[cut])
    projected = total.astype(jnp.bfloat16)
    for offset, out_ref in enumerate(out_refs):
        first = target_of(axes, offset) * share
        chosen = picker((share, rows), lambda row: row + first)
        out_ref[...] = nn_dot(chosen, projected).astype(jnp.bfloat16)


def gather_kernel(*refs):
    hidden_ref, tail_ref = refs[-2:]
    total = refs[0][...].astype(jnp.float32)
    for ref in refs[1:-2]:
        total = total + ref[...].astype(jnp.float32)
    hidden = total.astype(jnp.bfloat16)
    hidden_ref[...] = hidden
    kept = KT - 1 + FADE
    shape = (tail_ref.shape[0], hidden.shape[0])
    chosen = picker(shape, lambda row: row // kept * FR + FR - kept + row % kept)
    tail_ref[...] = nn_dot(chosen, hidden).astype(jnp.bfloat16)


def decode_kernel(fade_ref, hidden_ref, tail_ref, conv_ref, out_ref):
    position = lax.axis_index("span")
    share = hidden_ref.shape[0]
    spatial = share // FR
    kept = KT - 1 + FADE
    wide = FADE + FR
    hidden, tail = hidden_ref[...], tail_ref[...]
    mixed = jnp.zeros((spatial * wide, out_ref.shape[2]), jnp.float32)
    for tap in range(KT):
        def from_tail(row):
            place = row % wide + KT - 1 - tap
            return jnp.where(place < kept, row // wide * kept + place, -1)

        def from_hidden(row):
            place = row % wide + KT - 1 - tap
            return jnp.where(place >= kept, row // wide * FR + place - kept, -1)

        window = nn_dot(picker((spatial * wide, tail.shape[0]), from_tail), tail)
        window = window + nn_dot(picker((spatial * wide, share), from_hidden), hidden)
        mixed = mixed + nn_dot(window.astype(jnp.bfloat16), conv_ref[tap])
    frames = (mixed * jax.nn.sigmoid(mixed)).astype(jnp.bfloat16)
    fade = fade_ref[0]
    shape = (share, spatial * wide)
    current = nn_dot(picker(shape, lambda row: row // FR * wide + FADE + row % FR), frames)

    def faded(row):
        return jnp.where(row % FR < fade, row // FR * wide + FADE - fade + row % FR, -1)

    previous = nn_dot(picker(shape, faded), frames)
    frame = lax.broadcasted_iota(jnp.int32, (share, out_ref.shape[2]), 0) % FR
    fade_float = jnp.full(frame.shape, fade, jnp.int32).astype(jnp.float32)
    weight = (frame.astype(jnp.float32) + 1.0) / (fade_float + 1.0)
    weight = jnp.where((frame < fade) & (position > 0), weight, 1.0)
    out_ref[0] = (weight * current + (1.0 - weight) * previous).astype(jnp.bfloat16)


def project(finished, w_in):
    axes = ("mp", "seq")
    parts = lax.axis_size(axes)
    _, rows, depth = finished.shape
    channels = w_in.shape[1]
    chunks = -(-depth // (2 * HD))
    return plain_call(
        functools.partial(project_kernel, axes),
        "project",
        [jax.ShapeDtypeStruct((rows // parts, channels), jnp.bfloat16)] * parts,
        2 * rows * depth * channels,
        (finished, w_in),
        [HBM_SPEC] * 2,
        scratch=[
            pltpu.VMEM((rows, depth), jnp.bfloat16),
            pltpu.VMEM((depth, channels), jnp.bfloat16),
            pltpu.SemaphoreType.DMA,
            pltpu.SemaphoreType.DMA((chunks,)),
        ],
        limit=VMEM_ALL,
    )


def gather(parts, rows):
    share, channels = parts[0].shape
    tail_rows = share // FR * (KT - 1 + FADE)
    return plain_call(
        gather_kernel,
        "gather",
        [jax.ShapeDtypeStruct((count, channels), jnp.bfloat16) for count in (share, tail_rows)],
        rows * channels,
        parts,
    )


def decode(hidden, tail, conv_w, fade_count):
    share, channels = hidden.shape
    return plain_call(
        decode_kernel,
        "decode",
        [jax.ShapeDtypeStruct((1, share, channels), jnp.bfloat16)],
        2 * share * KT * channels * channels,
        (fade_count, hidden, tail, conv_w),
        [SMEM_SPEC],
    )[0]


def per_device(
    query, noisy_kv, clean_kv, causal_mask, step_index, finished, w_in, conv_w, fade_count
):
    steps, _, rows, columns = query.shape
    heads = columns // HD
    middle = (heads - max(1, heads // 3)) * HD
    row_count = steps * rows
    span = lax.axis_size("span")
    axes = ("mp", "seq")
    acc_shape = jax.ShapeDtypeStruct((heads, HD, row_count), jnp.float32)
    stat_shape = jax.ShapeDtypeStruct((heads, row_count), jnp.float32)
    pair_flops = 4 * row_count * rows * columns

    first_pairs = [(0, 2), (2, 3)] if span == 4 else [(c, c + 1) for c in range(span - 1)]
    near = send(clean_kv, first_pairs)
    pieces = project(finished, w_in)
    parts = [pieces[0]] + [swap(p, axes, offset + 1) for offset, p in enumerate(pieces[1:])]
    if span == 4:
        direct = send(clean_kv, [(1, 3)])
    carry = plain_call(
        own_kernel,
        "own",
        [acc_shape, stat_shape, stat_shape],
        pair_flops,
        (step_index, query, noisy_kv),
        [SMEM_SPEC],
    )
    hidden, tail = gather(parts, rows)
    tail = hop(tail, "span", 1)
    if span == 4:
        near = after(near, carry[0], hidden)
        forwards = lax.axis_index("span") == 2
        passed = [jnp.where(forwards, near[which], clean_kv[which]) for which in range(2)]
        passed = [passed[0], passed[1][:, :, :middle], passed[1][:, :, middle:]]
        passed = [hop(block, "span", 1) for block in passed]
        early = [(near, {2: 0, 3: 2}), (direct, {3: 1})]
        keys, *values = passed
        last_plan = {1: 0, 2: 1, 3: 0}
    else:
        ring = [near]
        for _ in range(2, span):
            ring.append(hop(ring[-1], "span", 1))
        early = [(block, delivered(span, back + 1)) for back, block in enumerate(ring[:-1])]
        keys, values = ring[-1], ring[-1:] * 2
        last_plan = delivered(span, span - 1)
    for block, plan in early:
        carry = plain_call(
            functools.partial(mid_kernel, plan),
            "middle",
            [acc_shape, stat_shape, stat_shape],
            pair_flops,
            (step_index, causal_mask, query, block, *carry),
            [SMEM_SPEC] * 2,
        )
    acc, weights = plain_call(
        functools.partial(score_kernel, [last_plan]),
        "score",
        [acc_shape, jax.ShapeDtypeStruct((heads, rows, row_count), jnp.bfloat16)],
        pair_flops // 2,
        (step_index, causal_mask, query, keys, *carry),
        [SMEM_SPEC] * 2,
    )
    square_shape = jax.ShapeDtypeStruct((1, row_count), jnp.float32)
    decoded = decode(after(hidden, weights), tail, conv_w, fade_count)
    front, squares = plain_call(
        functools.partial(average_kernel, 0, middle // HD),
        "average",
        [jax.ShapeDtypeStruct((steps, rows, middle), jnp.float32), square_shape],
        pair_flops // 4,
        (after(acc, decoded), weights, values[0]),
    )
    averaged, squares = plain_call(
        functools.partial(rest_kernel, middle // HD, heads),
        "rest",
        [jax.ShapeDtypeStruct((heads - middle // HD, HD, row_count), jnp.float32), square_shape],
        pair_flops // 4,
        (acc, weights, values[1], squares),
    )
    others = [swap(squares, axes, offset) for offset in range(1, lax.axis_size(axes))]
    back = plain_call(
        turn_kernel,
        "turn",
        [jax.ShapeDtypeStruct((steps, rows, columns - middle), jnp.float32)],
        row_count * columns,
        (averaged,),
    )[0]
    attended = plain_call(
        functools.partial(scale_kernel, columns * lax.axis_size(axes)),
        "scale",
        jax.ShapeDtypeStruct(query.shape, jnp.bfloat16),
        row_count * columns,
        (front, back, squares, *others),
        out_specs=HBM_SPEC,
        scratch=[
            pltpu.VMEM((steps, rows, columns), jnp.bfloat16),
            pltpu.SemaphoreType.DMA((steps,)),
        ],
    )
    return (attended, decoded)


def solution(mesh):
    placed = (
        P(None, ("groups", "span"), None, ("mp", "seq")),
        P(None, None, ("groups", "span"), None, ("mp", "seq")),
        P(None, ("groups", "span"), None, ("mp", "seq")),
        P("groups", None),
        P("groups", None),
        P(("groups", "span"), None, ("mp", "seq")),
        P(("mp", "seq"), None),
        P(),
        P(("groups", "span")),
    )
    return jax.shard_map(
        per_device,
        mesh=mesh,
        in_specs=placed,
        out_specs=(
            P(None, ("groups", "span"), None, ("mp", "seq")),
            P(("groups", "span"), ("mp", "seq"), None),
        ),
        check_vma=False,
    )
```

```python
import functools
import math

import jax
import jax.numpy as jnp
from jax import lax
from jax.experimental import pallas as pl
from jax.experimental.pallas import tpu as pltpu
from jax.sharding import PartitionSpec as P

FR = 6
HD = 128
KT = 3
FADE = 2
NSTEPS = 64
LOG2E = 1.4426950408889634
VMEM_LIMIT = 24 * 1024 * 1024
VMEM_ALL = 60 * 1024 * 1024

SMEM_SPEC = pl.BlockSpec(memory_space=pltpu.SMEM)
VMEM_SPEC = pl.BlockSpec(memory_space=pltpu.VMEM)
HBM_SPEC = pl.BlockSpec(memory_space=pltpu.HBM)


def cost(flops, nbytes):
    return pl.CostEstimate(flops=flops, bytes_accessed=nbytes, transcendentals=0)


def hop(value, axis, steps):
    count = lax.axis_size(axis)
    return lax.ppermute(value, axis, [(source, source + steps) for source in range(count - steps)])


def swap(value, axes, offset):
    count = lax.axis_size(axes)
    if count & (count - 1) == 0:
        pairs = [(source, source ^ offset) for source in range(count)]
    else:
        pairs = [(source, (source + offset) % count) for source in range(count)]
    return lax.ppermute(value, axes, pairs)


def cross(value, offset):
    chips, cores = lax.axis_size("mp"), lax.axis_size("seq")
    pairs = [
        (chip * cores + core, (chip + offset) % chips * cores + (core + 1) % cores)
        for chip in range(chips)
        for core in range(cores)
    ]
    return lax.ppermute(value, ("mp", "seq"), pairs)


def target_of(axes, offset):
    count = lax.axis_size(axes)
    mine = lax.axis_index(axes)
    if count & (count - 1) == 0:
        return mine ^ offset
    return lax.rem(mine + offset, count)


def after(value, *earlier):
    return lax.optimization_barrier((value, *earlier))[0]


def nt_dot(left, right):
    return lax.dot_general(left, right, (((1,), (1,)), ((), ())), preferred_element_type=jnp.float32)


def tn_dot(left, right):
    return lax.dot_general(left, right, (((0,), (0,)), ((), ())), preferred_element_type=jnp.float32)


def nn_dot(left, right):
    return jnp.dot(left, right, preferred_element_type=jnp.float32)


def row_factors(step_ref, position, steps, rows):
    lane = lax.broadcasted_iota(jnp.int32, (1, steps * rows), 1)
    index = jnp.full(lane.shape, step_ref[position, 0], jnp.int32)
    for step in range(1, steps):
        index = jnp.where(lane >= step * rows, step_ref[position, step], index)
    fraction = 1.0 - index.astype(jnp.float32) / NSTEPS
    level = 3.0 * fraction / (1.0 + 2.0 * fraction)
    return (0.5 + level) * (LOG2E / math.sqrt(HD))


def lane_windows(steps, rows):
    total = steps * rows
    return [
        (step * rows // HD * HD, min(total, -(-(step + 1) * rows // HD) * HD))
        for step in range(steps)
    ]


def join_steps(pieces, windows, rows):
    total = windows[-1][1]
    tiles = []
    for first in range(0, total, HD):
        stop = min(first + HD, total)
        tile = None
        for step, (begin, end) in enumerate(windows):
            if begin <= first and stop <= end and step * rows < stop and first < (step + 1) * rows:
                part = pieces[step][:, first - begin : stop - begin]
                if tile is None:
                    tile = part
                else:
                    lane = lax.broadcasted_iota(jnp.int32, part.shape, 1) + first
                    tile = jnp.where(lane >= step * rows, part, tile)
        tiles.append(tile)
    return jnp.concatenate(tiles, 1)


def own_kernel(step_ref, q_ref, kv_ref, acc_ref, top_ref, total_ref):
    position = lax.axis_index("span")
    steps, _, rows, columns = q_ref.shape
    factors = row_factors(step_ref, position, steps, rows)
    windows = lane_windows(steps, rows)
    for head in range(columns // HD):
        cut = slice(head * HD, (head + 1) * HD)
        queries = q_ref[:, 0, :, cut].reshape(steps * rows, HD)
        scores = join_steps(
            [nt_dot(kv_ref[s, 0, 0, :, cut], queries[a:b]) for s, (a, b) in enumerate(windows)],
            windows,
            rows,
        )
        scores = scores * factors
        top = jnp.max(scores, axis=0, keepdims=True)
        weights = jnp.exp2(scores - top)
        rounded = weights.astype(jnp.bfloat16)
        acc_ref[head] = join_steps(
            [tn_dot(kv_ref[s, 1, 0, :, cut], rounded[:, a:b]) for s, (a, b) in enumerate(windows)],
            windows,
            rows,
        )
        top_ref[head : head + 1] = top
        total_ref[head : head + 1] = jnp.sum(weights, axis=0, keepdims=True)


def absorb(queries, keys, values, factors, acc, top, total):
    scores = nt_dot(keys, queries) * factors
    newest = jnp.maximum(top, jnp.max(scores, axis=0, keepdims=True))
    weights = jnp.exp2(scores - newest)
    shrink = jnp.exp2(top - newest)
    total = total * shrink + jnp.sum(weights, axis=0, keepdims=True)
    acc = acc * shrink + tn_dot(values, weights.astype(jnp.bfloat16))
    return acc, newest, total


def visible(mask_ref, position, blocks):
    seen = False
    for place, block in blocks.items():
        seen = seen | ((position == place) & (mask_ref[place, block] > 0))
    return seen


def half(ref, which, cut):
    return ref[which, 0, :, cut] if len(ref.shape) == 4 else ref[0, :, cut]


def mid_kernel(plan, step_ref, mask_ref, q_ref, *refs):
    block_refs, (acc_in, top_in, total_in, acc_ref, top_ref, total_ref) = refs[:-6], refs[-6:]
    position = lax.axis_index("span")
    steps, _, rows, columns = q_ref.shape
    seen = visible(mask_ref, position, plan)

    @pl.when(seen)
    def _():
        factors = row_factors(step_ref, position, steps, rows)
        for head in range(columns // HD):
            cut = slice(head * HD, (head + 1) * HD)
            queries = q_ref[:, 0, :, cut].reshape(steps * rows, HD)
            acc, top, total = absorb(
                queries,
                half(block_refs[0], 0, cut),
                half(block_refs[-1], 1, cut),
                factors,
                acc_in[head],
                top_in[head : head + 1],
                total_in[head : head + 1],
            )
            acc_ref[head] = acc
            top_ref[head : head + 1] = top
            total_ref[head : head + 1] = total

    @pl.when(jnp.logical_not(seen))
    def _():
        acc_ref[...] = acc_in[...]
        top_ref[...] = top_in[...]
        total_ref[...] = total_in[...]


def score_kernel(plans, step_ref, mask_ref, q_ref, *refs):
    key_refs, (acc_in, top_in, total_in, acc_ref, w_ref) = refs[:-5], refs[-5:]
    position = lax.axis_index("span")
    steps, _, rows, columns = q_ref.shape

    def finish(key_ref):
        factors = row_factors(step_ref, position, steps, rows)
        for head in range(columns // HD):
            cut = slice(head * HD, (head + 1) * HD)
            queries = q_ref[:, 0, :, cut].reshape(steps * rows, HD)
            scores = nt_dot(half(key_ref, 0, cut), queries) * factors
            top = top_in[head : head + 1]
            newest = jnp.maximum(top, jnp.max(scores, axis=0, keepdims=True))
            weights = jnp.exp2(scores - newest)
            shrink = jnp.exp2(top - newest)
            total = total_in[head : head + 1] * shrink + jnp.sum(weights, axis=0, keepdims=True)
            inverse = 1.0 / total
            w_ref[head] = (weights * inverse).astype(jnp.bfloat16)
            acc_ref[head] = acc_in[head] * (shrink * inverse)

    rest = True
    for plan, key_ref in zip(plans, key_refs):
        seen = visible(mask_ref, position, plan)
        rest = jnp.logical_and(rest, jnp.logical_not(seen))
        pl.when(seen)(functools.partial(finish, key_ref))

    @pl.when(rest)
    def _():
        w_ref[...] = jnp.zeros_like(w_ref)
        for head in range(columns // HD):
            acc_ref[head] = acc_in[head] * (1.0 / total_in[head : head + 1])


def average_head(head, acc_ref, w_ref, value_ref, first):
    if value_ref.shape[-1] == acc_ref.shape[0] * HD:
        first = 0
    cut = slice((head - first) * HD, (head - first + 1) * HD)
    return acc_ref[head] + tn_dot(half(value_ref, 1, cut), w_ref[head])


def average_kernel(begin, end, acc_ref, w_ref, value_ref, average_ref, square_ref):
    squares = jnp.zeros(square_ref.shape, jnp.float32)
    for head in range(begin, end):
        average = average_head(head, acc_ref, w_ref, value_ref, begin)
        squares = squares + jnp.sum(average * average, axis=0, keepdims=True)
        average_ref[:, :, (head - begin) * HD : (head - begin + 1) * HD] = average.T.reshape(
            average_ref.shape[:2] + (HD,)
        )
    square_ref[...] = squares


def rest_kernel(begin, end, acc_ref, w_ref, value_ref, before_ref, average_ref, square_ref):
    squares = before_ref[...]
    for head in range(begin, end):
        average = average_head(head, acc_ref, w_ref, value_ref, begin)
        squares = squares + jnp.sum(average * average, axis=0, keepdims=True)
        average_ref[head - begin] = average
    square_ref[...] = squares


def turn_kernel(in_ref, *refs):
    square_refs, (out_ref, square_ref) = refs[:-2], refs[-2:]
    steps, rows, _ = out_ref.shape
    squares = square_refs[0][...]
    for ref in square_refs[1:]:
        squares = squares + ref[...]
    square_ref[...] = squares
    for head in range(in_ref.shape[0]):
        out_ref[:, :, head * HD : (head + 1) * HD] = in_ref[head].T.reshape(steps, rows, HD)


def scale_kernel(width, front_ref, back_ref, *refs):
    part_refs, (out_hbm, out_ref, sem) = refs[:-3], refs[-3:]
    total = part_refs[0][...]
    for ref in part_refs[1:]:
        total = total + ref[...]
    inverse = lax.rsqrt(total / width + 1e-06)
    steps, rows, columns = out_ref.shape
    copies = []
    for step in range(steps):
        own = inverse[:, step * rows : (step + 1) * rows]
        factor = jnp.broadcast_to(own, (HD, rows)).T
        place = 0
        for ref in (front_ref, back_ref):
            for first in range(0, ref.shape[2], HD):
                average = ref[step, :, first : first + HD]
                out_ref[step, :, place : place + HD] = (average * factor).astype(jnp.bfloat16)
                place += HD
        copies.append(pltpu.make_async_copy(out_ref.at[step], out_hbm.at[step, 0], sem.at[step]))
        copies[-1].start()
    for copy in copies:
        copy.wait()


def send(value, pairs):
    return lax.ppermute(value, "span", pairs)


def delivered(span, back):
    return {place: place - back for place in range(back, span)}


def plain_call(kernel, name, out_shape, flops, operands, in_specs=(), out_specs=None, scratch=(), limit=VMEM_LIMIT):
    nbytes = sum(math.prod(o.shape) * o.dtype.itemsize for o in operands)
    if out_specs is None:
        out_specs = [VMEM_SPEC] * len(out_shape)
    return pl.pallas_call(
        kernel,
        in_specs=list(in_specs) + [VMEM_SPEC] * (len(operands) - len(in_specs)),
        out_specs=out_specs,
        out_shape=out_shape,
        scratch_shapes=list(scratch),
        compiler_params=pltpu.CompilerParams(vmem_limit_bytes=limit),
        cost_estimate=cost(flops, nbytes),
        name=name,
    )(*operands)


def picker(shape, wanted):
    row = lax.broadcasted_iota(jnp.int32, shape, 0)
    column = lax.broadcasted_iota(jnp.int32, shape, 1)
    return jnp.where(column == wanted(row), 1.0, 0.0).astype(jnp.bfloat16)


def project_kernel(axes, x_hbm, w_hbm, *refs):
    out_refs, (x_ref, w_ref, x_sem, w_sem) = refs[:-4], refs[-4:]
    rows, depth = x_ref.shape
    share = out_refs[0].shape[0]
    x_copy = pltpu.make_async_copy(x_hbm.at[0], x_ref, x_sem)
    x_copy.start()
    copies = []
    for place, first in enumerate(range(0, depth, 2 * HD)):
        cut = slice(first, min(first + 2 * HD, depth))
        copies.append((cut, pltpu.make_async_copy(w_hbm.at[cut], w_ref.at[cut], w_sem.at[place])))
        copies[-1][1].start()
    total = jnp.zeros((rows, w_ref.shape[1]), jnp.float32)
    x_copy.wait()
    for cut, w_copy in copies:
        w_copy.wait()
        total = total + nn_dot(x_ref[:, cut], w_ref[cut])
    projected = total.astype(jnp.bfloat16)
    for offset, out_ref in enumerate(out_refs):
        first = target_of(axes, offset) * share
        chosen = picker((share, rows), lambda row: row + first)
        out_ref[...] = nn_dot(chosen, projected).astype(jnp.bfloat16)


def gather_kernel(*refs):
    hidden_ref, tail_ref = refs[-2:]
    total = refs[0][...].astype(jnp.float32)
    for ref in refs[1:-2]:
        total = total + ref[...].astype(jnp.float32)
    hidden = total.astype(jnp.bfloat16)
    hidden_ref[...] = hidden
    kept = KT - 1 + FADE
    shape = (tail_ref.shape[0], hidden.shape[0])
    chosen = picker(shape, lambda row: row // kept * FR + FR - kept + row % kept)
    tail_ref[...] = nn_dot(chosen, hidden).astype(jnp.bfloat16)


def decode_kernel(fade_ref, hidden_ref, tail_ref, conv_ref, out_ref):
    position = lax.axis_index("span")
    share = hidden_ref.shape[0]
    spatial = share // FR
    kept = KT - 1 + FADE
    wide = FADE + FR
    hidden, tail = hidden_ref[...], tail_ref[...]
    mixed = jnp.zeros((spatial * wide, out_ref.shape[2]), jnp.float32)
    for tap in range(KT):
        def from_tail(row):
            place = row % wide + KT - 1 - tap
            return jnp.where(place < kept, row // wide * kept + place, -1)

        def from_hidden(row):
            place = row % wide + KT - 1 - tap
            return jnp.where(place >= kept, row // wide * FR + place - kept, -1)

        window = nn_dot(picker((spatial * wide, tail.shape[0]), from_tail), tail)
        window = window + nn_dot(picker((spatial * wide, share), from_hidden), hidden)
        mixed = mixed + nn_dot(window.astype(jnp.bfloat16), conv_ref[tap])
    frames = (mixed * jax.nn.sigmoid(mixed)).astype(jnp.bfloat16)
    fade = fade_ref[0]
    shape = (share, spatial * wide)
    current = nn_dot(picker(shape, lambda row: row // FR * wide + FADE + row % FR), frames)

    def faded(row):
        return jnp.where(row % FR < fade, row // FR * wide + FADE - fade + row % FR, -1)

    previous = nn_dot(picker(shape, faded), frames)
    frame = lax.broadcasted_iota(jnp.int32, (share, out_ref.shape[2]), 0) % FR
    fade_float = jnp.full(frame.shape, fade, jnp.int32).astype(jnp.float32)
    weight = (frame.astype(jnp.float32) + 1.0) / (fade_float + 1.0)
    weight = jnp.where((frame < fade) & (position > 0), weight, 1.0)
    out_ref[0] = (weight * current + (1.0 - weight) * previous).astype(jnp.bfloat16)


def project(finished, w_in):
    axes = ("mp", "seq")
    parts = lax.axis_size(axes)
    _, rows, depth = finished.shape
    channels = w_in.shape[1]
    chunks = -(-depth // (2 * HD))
    return plain_call(
        functools.partial(project_kernel, axes),
        "project",
        [jax.ShapeDtypeStruct((rows // parts, channels), jnp.bfloat16)] * parts,
        2 * rows * depth * channels,
        (finished, w_in),
        [HBM_SPEC] * 2,
        scratch=[
            pltpu.VMEM((rows, depth), jnp.bfloat16),
            pltpu.VMEM((depth, channels), jnp.bfloat16),
            pltpu.SemaphoreType.DMA,
            pltpu.SemaphoreType.DMA((chunks,)),
        ],
        limit=VMEM_ALL,
    )


def gather(parts, rows):
    share, channels = parts[0].shape
    tail_rows = share // FR * (KT - 1 + FADE)
    return plain_call(
        gather_kernel,
        "gather",
        [jax.ShapeDtypeStruct((count, channels), jnp.bfloat16) for count in (share, tail_rows)],
        rows * channels,
        parts,
    )


def decode(hidden, tail, conv_w, fade_count):
    share, channels = hidden.shape
    return plain_call(
        decode_kernel,
        "decode",
        [jax.ShapeDtypeStruct((1, share, channels), jnp.bfloat16)],
        2 * share * KT * channels * channels,
        (fade_count, hidden, tail, conv_w),
        [SMEM_SPEC],
    )[0]


def per_device(
    query, noisy_kv, clean_kv, causal_mask, step_index, finished, w_in, conv_w, fade_count
):
    steps, _, rows, columns = query.shape
    heads = columns // HD
    middle = (heads - max(1, heads // 3)) * HD
    row_count = steps * rows
    span = lax.axis_size("span")
    axes = ("mp", "seq")
    acc_shape = jax.ShapeDtypeStruct((heads, HD, row_count), jnp.float32)
    stat_shape = jax.ShapeDtypeStruct((heads, row_count), jnp.float32)
    pair_flops = 4 * row_count * rows * columns

    first_pairs = [(0, 2), (2, 3)] if span == 4 else [(c, c + 1) for c in range(span - 1)]
    near = send(clean_kv, first_pairs)
    pieces = project(finished, w_in)
    parts = [pieces[0]] + [swap(p, axes, offset + 1) for offset, p in enumerate(pieces[1:])]
    if span == 4:
        direct = send(clean_kv, [(1, 3)])
    carry = plain_call(
        own_kernel,
        "own",
        [acc_shape, stat_shape, stat_shape],
        pair_flops,
        (step_index, query, noisy_kv),
        [SMEM_SPEC],
    )
    hidden, tail = gather(parts, rows)
    tail = hop(tail, "span", 1)
    if span == 4:
        near = after(near, carry[0], hidden)
        forwards = lax.axis_index("span") == 2
        passed = [jnp.where(forwards, near[which], clean_kv[which]) for which in range(2)]
        passed = [passed[0], passed[1][:, :, :middle], passed[1][:, :, middle:]]
        passed = [hop(block, "span", 1) for block in passed]
        early = [(near, {2: 0, 3: 2}), (direct, {3: 1})]
        keys, *values = passed
        last_plan = {1: 0, 2: 1, 3: 0}
    else:
        ring = [near]
        for _ in range(2, span):
            ring.append(hop(ring[-1], "span", 1))
        early = [(block, delivered(span, back + 1)) for back, block in enumerate(ring[:-1])]
        keys, values = ring[-1], ring[-1:] * 2
        last_plan = delivered(span, span - 1)
    for block, plan in early:
        carry = plain_call(
            functools.partial(mid_kernel, plan),
            "middle",
            [acc_shape, stat_shape, stat_shape],
            pair_flops,
            (step_index, causal_mask, query, block, *carry),
            [SMEM_SPEC] * 2,
        )
    acc, weights = plain_call(
        functools.partial(score_kernel, [last_plan]),
        "score",
        [acc_shape, jax.ShapeDtypeStruct((heads, rows, row_count), jnp.bfloat16)],
        pair_flops // 2,
        (step_index, causal_mask, query, keys, *carry),
        [SMEM_SPEC] * 2,
    )
    square_shape = jax.ShapeDtypeStruct((1, row_count), jnp.float32)
    front, squares = plain_call(
        functools.partial(average_kernel, 0, middle // HD),
        "average",
        [jax.ShapeDtypeStruct((steps, rows, middle), jnp.float32), square_shape],
        pair_flops // 4,
        (acc, weights, values[0]),
    )
    averaged, squares = plain_call(
        functools.partial(rest_kernel, middle // HD, heads),
        "rest",
        [jax.ShapeDtypeStruct((heads - middle // HD, HD, row_count), jnp.float32), square_shape],
        pair_flops // 4,
        (acc, weights, values[1], squares),
    )
    within = [swap(squares, "seq", offset) for offset in range(1, lax.axis_size("seq"))]
    back, squares = plain_call(
        turn_kernel,
        "turn",
        [jax.ShapeDtypeStruct((steps, rows, columns - middle), jnp.float32), square_shape],
        row_count * columns,
        (averaged, squares, *within),
    )
    others = [cross(squares, offset) for offset in range(1, lax.axis_size("mp"))]
    decoded = decode(after(hidden, back), tail, conv_w, fade_count)
    attended = plain_call(
        functools.partial(scale_kernel, columns * lax.axis_size(axes)),
        "scale",
        jax.ShapeDtypeStruct(query.shape, jnp.bfloat16),
        row_count * columns,
        (front, back, squares, *others),
        out_specs=HBM_SPEC,
        scratch=[
            pltpu.VMEM((steps, rows, columns), jnp.bfloat16),
            pltpu.SemaphoreType.DMA((steps,)),
        ],
    )
    return (attended, decoded)


def solution(mesh):
    placed = (
        P(None, ("groups", "span"), None, ("mp", "seq")),
        P(None, None, ("groups", "span"), None, ("mp", "seq")),
        P(None, ("groups", "span"), None, ("mp", "seq")),
        P("groups", None),
        P("groups", None),
        P(("groups", "span"), None, ("mp", "seq")),
        P(("mp", "seq"), None),
        P(),
        P(("groups", "span")),
    )
    return jax.shard_map(
        per_device,
        mesh=mesh,
        in_specs=placed,
        out_specs=(
            P(None, ("groups", "span"), None, ("mp", "seq")),
            P(("groups", "span"), ("mp", "seq"), None),
        ),
        check_vma=False,
    )
```

```python
import functools
import math

import jax
import jax.numpy as jnp
from jax import lax
from jax.experimental import pallas as pl
from jax.experimental.pallas import tpu as pltpu
from jax.sharding import PartitionSpec as P

FR = 6
HD = 128
KT = 3
FADE = 2
NSTEPS = 64
LOG2E = 1.4426950408889634
VMEM_LIMIT = 24 * 1024 * 1024
VMEM_ALL = 60 * 1024 * 1024

SMEM_SPEC = pl.BlockSpec(memory_space=pltpu.SMEM)
VMEM_SPEC = pl.BlockSpec(memory_space=pltpu.VMEM)
HBM_SPEC = pl.BlockSpec(memory_space=pltpu.HBM)


def cost(flops, nbytes):
    return pl.CostEstimate(flops=flops, bytes_accessed=nbytes, transcendentals=0)


def hop(value, axis, steps):
    count = lax.axis_size(axis)
    return lax.ppermute(value, axis, [(source, source + steps) for source in range(count - steps)])


def swap(value, axes, offset):
    count = lax.axis_size(axes)
    if count & (count - 1) == 0:
        pairs = [(source, source ^ offset) for source in range(count)]
    else:
        pairs = [(source, (source + offset) % count) for source in range(count)]
    return lax.ppermute(value, axes, pairs)


def target_of(axes, offset):
    count = lax.axis_size(axes)
    mine = lax.axis_index(axes)
    if count & (count - 1) == 0:
        return mine ^ offset
    return lax.rem(mine + offset, count)


def after(value, *earlier):
    return lax.optimization_barrier((value, *earlier))[0]


def nt_dot(left, right):
    return lax.dot_general(left, right, (((1,), (1,)), ((), ())), preferred_element_type=jnp.float32)


def tn_dot(left, right):
    return lax.dot_general(left, right, (((0,), (0,)), ((), ())), preferred_element_type=jnp.float32)


def nn_dot(left, right):
    return jnp.dot(left, right, preferred_element_type=jnp.float32)


def row_factors(step_ref, position, steps, rows):
    lane = lax.broadcasted_iota(jnp.int32, (1, steps * rows), 1)
    index = jnp.full(lane.shape, step_ref[position, 0], jnp.int32)
    for step in range(1, steps):
        index = jnp.where(lane >= step * rows, step_ref[position, step], index)
    fraction = 1.0 - index.astype(jnp.float32) / NSTEPS
    level = 3.0 * fraction / (1.0 + 2.0 * fraction)
    return (0.5 + level) * (LOG2E / math.sqrt(HD))


def lane_windows(steps, rows):
    total = steps * rows
    return [
        (step * rows // HD * HD, min(total, -(-(step + 1) * rows // HD) * HD))
        for step in range(steps)
    ]


def join_steps(pieces, windows, rows):
    total = windows[-1][1]
    tiles = []
    for first in range(0, total, HD):
        stop = min(first + HD, total)
        tile = None
        for step, (begin, end) in enumerate(windows):
            if begin <= first and stop <= end and step * rows < stop and first < (step + 1) * rows:
                part = pieces[step][:, first - begin : stop - begin]
                if tile is None:
                    tile = part
                else:
                    lane = lax.broadcasted_iota(jnp.int32, part.shape, 1) + first
                    tile = jnp.where(lane >= step * rows, part, tile)
        tiles.append(tile)
    return jnp.concatenate(tiles, 1)


def own_kernel(step_ref, q_ref, kv_ref, acc_ref, top_ref, total_ref):
    position = lax.axis_index("span")
    steps, _, rows, columns = q_ref.shape
    factors = row_factors(step_ref, position, steps, rows)
    windows = lane_windows(steps, rows)
    for head in range(columns // HD):
        cut = slice(head * HD, (head + 1) * HD)
        queries = q_ref[:, 0, :, cut].reshape(steps * rows, HD)
        scores = join_steps(
            [nt_dot(kv_ref[s, 0, 0, :, cut], queries[a:b]) for s, (a, b) in enumerate(windows)],
            windows,
            rows,
        )
        scores = scores * factors
        top = jnp.max(scores, axis=0, keepdims=True)
        weights = jnp.exp2(scores - top)
        rounded = weights.astype(jnp.bfloat16)
        acc_ref[head] = join_steps(
            [tn_dot(kv_ref[s, 1, 0, :, cut], rounded[:, a:b]) for s, (a, b) in enumerate(windows)],
            windows,
            rows,
        )
        top_ref[head : head + 1] = top
        total_ref[head : head + 1] = jnp.sum(weights, axis=0, keepdims=True)


def absorb(queries, keys, values, factors, acc, top, total):
    scores = nt_dot(keys, queries) * factors
    newest = jnp.maximum(top, jnp.max(scores, axis=0, keepdims=True))
    weights = jnp.exp2(scores - newest)
    shrink = jnp.exp2(top - newest)
    total = total * shrink + jnp.sum(weights, axis=0, keepdims=True)
    acc = acc * shrink + tn_dot(values, weights.astype(jnp.bfloat16))
    return acc, newest, total


def visible(mask_ref, position, blocks):
    seen = False
    for place, block in blocks.items():
        seen = seen | ((position == place) & (mask_ref[place, block] > 0))
    return seen


def half(ref, which, cut):
    return ref[which, 0, :, cut] if len(ref.shape) == 4 else ref[0, :, cut]


def mid_kernel(plan, step_ref, mask_ref, q_ref, *refs):
    block_refs, (acc_in, top_in, total_in, acc_ref, top_ref, total_ref) = refs[:-6], refs[-6:]
    position = lax.axis_index("span")
    steps, _, rows, columns = q_ref.shape
    seen = visible(mask_ref, position, plan)

    @pl.when(seen)
    def _():
        factors = row_factors(step_ref, position, steps, rows)
        for head in range(columns // HD):
            cut = slice(head * HD, (head + 1) * HD)
            queries = q_ref[:, 0, :, cut].reshape(steps * rows, HD)
            acc, top, total = absorb(
                queries,
                half(block_refs[0], 0, cut),
                half(block_refs[-1], 1, cut),
                factors,
                acc_in[head],
                top_in[head : head + 1],
                total_in[head : head + 1],
            )
            acc_ref[head] = acc
            top_ref[head : head + 1] = top
            total_ref[head : head + 1] = total

    @pl.when(jnp.logical_not(seen))
    def _():
        acc_ref[...] = acc_in[...]
        top_ref[...] = top_in[...]
        total_ref[...] = total_in[...]


def score_kernel(plans, step_ref, mask_ref, q_ref, *refs):
    key_refs, (acc_in, top_in, total_in, acc_ref, w_ref) = refs[:-5], refs[-5:]
    position = lax.axis_index("span")
    steps, _, rows, columns = q_ref.shape

    def finish(key_ref):
        factors = row_factors(step_ref, position, steps, rows)
        for head in range(columns // HD):
            cut = slice(head * HD, (head + 1) * HD)
            queries = q_ref[:, 0, :, cut].reshape(steps * rows, HD)
            scores = nt_dot(half(key_ref, 0, cut), queries) * factors
            top = top_in[head : head + 1]
            newest = jnp.maximum(top, jnp.max(scores, axis=0, keepdims=True))
            weights = jnp.exp2(scores - newest)
            shrink = jnp.exp2(top - newest)
            total = total_in[head : head + 1] * shrink + jnp.sum(weights, axis=0, keepdims=True)
            inverse = 1.0 / total
            w_ref[head] = (weights * inverse).astype(jnp.bfloat16)
            acc_ref[head] = acc_in[head] * (shrink * inverse)

    rest = True
    for plan, key_ref in zip(plans, key_refs):
        seen = visible(mask_ref, position, plan)
        rest = jnp.logical_and(rest, jnp.logical_not(seen))
        pl.when(seen)(functools.partial(finish, key_ref))

    @pl.when(rest)
    def _():
        w_ref[...] = jnp.zeros_like(w_ref)
        for head in range(columns // HD):
            acc_ref[head] = acc_in[head] * (1.0 / total_in[head : head + 1])


def average_head(head, acc_ref, w_ref, value_ref, first):
    if value_ref.shape[-1] == acc_ref.shape[0] * HD:
        first = 0
    cut = slice((head - first) * HD, (head - first + 1) * HD)
    return acc_ref[head] + tn_dot(half(value_ref, 1, cut), w_ref[head])


def average_kernel(begin, end, acc_ref, w_ref, value_ref, average_ref, square_ref):
    squares = jnp.zeros(square_ref.shape, jnp.float32)
    for head in range(begin, end):
        average = average_head(head, acc_ref, w_ref, value_ref, begin)
        squares = squares + jnp.sum(average * average, axis=0, keepdims=True)
        average_ref[:, :, (head - begin) * HD : (head - begin + 1) * HD] = average.T.reshape(
            average_ref.shape[:2] + (HD,)
        )
    square_ref[...] = squares


def rest_kernel(begin, end, acc_ref, w_ref, value_ref, before_ref, average_ref, square_ref):
    squares = before_ref[...]
    for head in range(begin, end):
        average = average_head(head, acc_ref, w_ref, value_ref, begin)
        squares = squares + jnp.sum(average * average, axis=0, keepdims=True)
        average_ref[head - begin] = average
    square_ref[...] = squares


def turn_kernel(in_ref, square_in, out_ref, square_ref):
    steps, rows, _ = out_ref.shape
    for head in range(in_ref.shape[0]):
        out_ref[:, :, head * HD : (head + 1) * HD] = in_ref[head].T.reshape(steps, rows, HD)
    square_ref[...] = square_in[...]


def scale_kernel(width, front_ref, back_ref, *refs):
    part_refs, (out_hbm, out_ref, sem) = refs[:-3], refs[-3:]
    total = part_refs[0][...]
    for ref in part_refs[1:]:
        total = total + ref[...]
    inverse = lax.rsqrt(total / width + 1e-06)
    steps, rows, columns = out_ref.shape
    copies = []
    for step in range(steps):
        own = inverse[:, step * rows : (step + 1) * rows]
        factor = jnp.broadcast_to(own, (HD, rows)).T
        place = 0
        for ref in (front_ref, back_ref):
            for first in range(0, ref.shape[2], HD):
                average = ref[step, :, first : first + HD]
                out_ref[step, :, place : place + HD] = (average * factor).astype(jnp.bfloat16)
                place += HD
        copies.append(pltpu.make_async_copy(out_ref.at[step], out_hbm.at[step, 0], sem.at[step]))
        copies[-1].start()
    for copy in copies:
        copy.wait()


def send(value, pairs):
    return lax.ppermute(value, "span", pairs)


def delivered(span, back):
    return {place: place - back for place in range(back, span)}


def plain_call(kernel, name, out_shape, flops, operands, in_specs=(), out_specs=None, scratch=(), limit=VMEM_LIMIT):
    nbytes = sum(math.prod(o.shape) * o.dtype.itemsize for o in operands)
    if out_specs is None:
        out_specs = [VMEM_SPEC] * len(out_shape)
    return pl.pallas_call(
        kernel,
        in_specs=list(in_specs) + [VMEM_SPEC] * (len(operands) - len(in_specs)),
        out_specs=out_specs,
        out_shape=out_shape,
        scratch_shapes=list(scratch),
        compiler_params=pltpu.CompilerParams(vmem_limit_bytes=limit),
        cost_estimate=cost(flops, nbytes),
        name=name,
    )(*operands)


def picker(shape, wanted):
    row = lax.broadcasted_iota(jnp.int32, shape, 0)
    column = lax.broadcasted_iota(jnp.int32, shape, 1)
    return jnp.where(column == wanted(row), 1.0, 0.0).astype(jnp.bfloat16)


def project_kernel(axes, x_hbm, w_hbm, *refs):
    out_refs, (x_ref, w_ref, x_sem, w_sem) = refs[:-4], refs[-4:]
    rows, depth = x_ref.shape
    share = out_refs[0].shape[0]
    x_copy = pltpu.make_async_copy(x_hbm.at[0], x_ref, x_sem)
    x_copy.start()
    copies = []
    for place, first in enumerate(range(0, depth, 2 * HD)):
        cut = slice(first, min(first + 2 * HD, depth))
        copies.append((cut, pltpu.make_async_copy(w_hbm.at[cut], w_ref.at[cut], w_sem.at[place])))
        copies[-1][1].start()
    total = jnp.zeros((rows, w_ref.shape[1]), jnp.float32)
    x_copy.wait()
    for cut, w_copy in copies:
        w_copy.wait()
        total = total + nn_dot(x_ref[:, cut], w_ref[cut])
    projected = total.astype(jnp.bfloat16)
    for offset, out_ref in enumerate(out_refs):
        first = target_of(axes, offset) * share
        chosen = picker((share, rows), lambda row: row + first)
        out_ref[...] = nn_dot(chosen, projected).astype(jnp.bfloat16)


def gather_kernel(*refs):
    hidden_ref, tail_ref = refs[-2:]
    total = refs[0][...].astype(jnp.float32)
    for ref in refs[1:-2]:
        total = total + ref[...].astype(jnp.float32)
    hidden = total.astype(jnp.bfloat16)
    hidden_ref[...] = hidden
    kept = KT - 1 + FADE
    shape = (tail_ref.shape[0], hidden.shape[0])
    chosen = picker(shape, lambda row: row // kept * FR + FR - kept + row % kept)
    tail_ref[...] = nn_dot(chosen, hidden).astype(jnp.bfloat16)


def decode_kernel(fade_ref, hidden_ref, tail_ref, conv_ref, out_ref):
    position = lax.axis_index("span")
    share = hidden_ref.shape[0]
    spatial = share // FR
    kept = KT - 1 + FADE
    wide = FADE + FR
    hidden, tail = hidden_ref[...], tail_ref[...]
    mixed = jnp.zeros((spatial * wide, out_ref.shape[2]), jnp.float32)
    for tap in range(KT):
        def from_tail(row):
            place = row % wide + KT - 1 - tap
            return jnp.where(place < kept, row // wide * kept + place, -1)

        def from_hidden(row):
            place = row % wide + KT - 1 - tap
            return jnp.where(place >= kept, row // wide * FR + place - kept, -1)

        window = nn_dot(picker((spatial * wide, tail.shape[0]), from_tail), tail)
        window = window + nn_dot(picker((spatial * wide, share), from_hidden), hidden)
        mixed = mixed + nn_dot(window.astype(jnp.bfloat16), conv_ref[tap])
    frames = (mixed * jax.nn.sigmoid(mixed)).astype(jnp.bfloat16)
    fade = fade_ref[0]
    shape = (share, spatial * wide)
    current = nn_dot(picker(shape, lambda row: row // FR * wide + FADE + row % FR), frames)

    def faded(row):
        return jnp.where(row % FR < fade, row // FR * wide + FADE - fade + row % FR, -1)

    previous = nn_dot(picker(shape, faded), frames)
    frame = lax.broadcasted_iota(jnp.int32, (share, out_ref.shape[2]), 0) % FR
    fade_float = jnp.full(frame.shape, fade, jnp.int32).astype(jnp.float32)
    weight = (frame.astype(jnp.float32) + 1.0) / (fade_float + 1.0)
    weight = jnp.where((frame < fade) & (position > 0), weight, 1.0)
    out_ref[0] = (weight * current + (1.0 - weight) * previous).astype(jnp.bfloat16)


def project(finished, w_in):
    axes = ("mp", "seq")
    parts = lax.axis_size(axes)
    _, rows, depth = finished.shape
    channels = w_in.shape[1]
    chunks = -(-depth // (2 * HD))
    return plain_call(
        functools.partial(project_kernel, axes),
        "project",
        [jax.ShapeDtypeStruct((rows // parts, channels), jnp.bfloat16)] * parts,
        2 * rows * depth * channels,
        (finished, w_in),
        [HBM_SPEC] * 2,
        scratch=[
            pltpu.VMEM((rows, depth), jnp.bfloat16),
            pltpu.VMEM((depth, channels), jnp.bfloat16),
            pltpu.SemaphoreType.DMA,
            pltpu.SemaphoreType.DMA((chunks,)),
        ],
        limit=VMEM_ALL,
    )


def gather(parts, rows):
    share, channels = parts[0].shape
    tail_rows = share // FR * (KT - 1 + FADE)
    return plain_call(
        gather_kernel,
        "gather",
        [jax.ShapeDtypeStruct((count, channels), jnp.bfloat16) for count in (share, tail_rows)],
        rows * channels,
        parts,
    )


def decode(hidden, tail, conv_w, fade_count):
    share, channels = hidden.shape
    return plain_call(
        decode_kernel,
        "decode",
        [jax.ShapeDtypeStruct((1, share, channels), jnp.bfloat16)],
        2 * share * KT * channels * channels,
        (fade_count, hidden, tail, conv_w),
        [SMEM_SPEC],
    )[0]


def per_device(
    query, noisy_kv, clean_kv, causal_mask, step_index, finished, w_in, conv_w, fade_count
):
    steps, _, rows, columns = query.shape
    heads = columns // HD
    middle = max(1, heads - 1) * HD
    row_count = steps * rows
    span = lax.axis_size("span")
    axes = ("mp", "seq")
    acc_shape = jax.ShapeDtypeStruct((heads, HD, row_count), jnp.float32)
    stat_shape = jax.ShapeDtypeStruct((heads, row_count), jnp.float32)
    pair_flops = 4 * row_count * rows * columns

    first_pairs = [(0, 2), (2, 3)] if span == 4 else [(c, c + 1) for c in range(span - 1)]
    near = send(clean_kv, first_pairs)
    pieces = project(finished, w_in)
    parts = [pieces[0]] + [swap(p, axes, offset + 1) for offset, p in enumerate(pieces[1:])]
    if span == 4:
        direct = send(clean_kv, [(1, 3)])
    carry = plain_call(
        own_kernel,
        "own",
        [acc_shape, stat_shape, stat_shape],
        pair_flops,
        (step_index, query, noisy_kv),
        [SMEM_SPEC],
    )
    hidden, tail = gather(parts, rows)
    tail = hop(tail, "span", 1)
    if span == 4:
        near = after(near, carry[0], hidden)
        forwards = lax.axis_index("span") == 2
        passed = [jnp.where(forwards, near[which], clean_kv[which]) for which in range(2)]
        passed = [passed[0], passed[1][:, :, :middle], passed[1][:, :, middle:]]
        passed = [hop(block, "span", 1) for block in passed]
        early = [(near, {2: 0, 3: 2}), (direct, {3: 1})]
        keys, *values = passed
        last_plan = {1: 0, 2: 1, 3: 0}
    else:
        ring = [near]
        for _ in range(2, span):
            ring.append(hop(ring[-1], "span", 1))
        early = [(block, delivered(span, back + 1)) for back, block in enumerate(ring[:-1])]
        keys, values = ring[-1], ring[-1:] * 2
        last_plan = delivered(span, span - 1)
    for block, plan in early:
        carry = plain_call(
            functools.partial(mid_kernel, plan),
            "middle",
            [acc_shape, stat_shape, stat_shape],
            pair_flops,
            (step_index, causal_mask, query, block, *carry),
            [SMEM_SPEC] * 2,
        )
    acc, weights = plain_call(
        functools.partial(score_kernel, [last_plan]),
        "score",
        [acc_shape, jax.ShapeDtypeStruct((heads, rows, row_count), jnp.bfloat16)],
        pair_flops // 2,
        (step_index, causal_mask, query, keys, *carry),
        [SMEM_SPEC] * 2,
    )
    square_shape = jax.ShapeDtypeStruct((1, row_count), jnp.float32)
    front, squares = plain_call(
        functools.partial(average_kernel, 0, middle // HD),
        "average",
        [jax.ShapeDtypeStruct((steps, rows, middle), jnp.float32), square_shape],
        pair_flops // 4,
        (acc, weights, values[0]),
    )
    averaged, squares = plain_call(
        functools.partial(rest_kernel, middle // HD, heads),
        "rest",
        [jax.ShapeDtypeStruct((heads - middle // HD, HD, row_count), jnp.float32), square_shape],
        pair_flops // 4,
        (acc, weights, values[1], squares),
    )
    others = [swap(squares, axes, offset) for offset in range(2, lax.axis_size(axes))]
    back, squares = plain_call(
        turn_kernel,
        "turn",
        [jax.ShapeDtypeStruct((steps, rows, columns - middle), jnp.float32), square_shape],
        row_count * columns,
        (averaged, squares),
    )
    others.append(swap(squares, axes, 1))
    decoded = decode(after(hidden, back), tail, conv_w, fade_count)
    attended = plain_call(
        functools.partial(scale_kernel, columns * lax.axis_size(axes)),
        "scale",
        jax.ShapeDtypeStruct(query.shape, jnp.bfloat16),
        row_count * columns,
        (front, back, squares, *others),
        out_specs=HBM_SPEC,
        scratch=[
            pltpu.VMEM((steps, rows, columns), jnp.bfloat16),
            pltpu.SemaphoreType.DMA((steps,)),
        ],
    )
    return (attended, decoded)


def solution(mesh):
    placed = (
        P(None, ("groups", "span"), None, ("mp", "seq")),
        P(None, None, ("groups", "span"), None, ("mp", "seq")),
        P(None, ("groups", "span"), None, ("mp", "seq")),
        P("groups", None),
        P("groups", None),
        P(("groups", "span"), None, ("mp", "seq")),
        P(("mp", "seq"), None),
        P(),
        P(("groups", "span")),
    )
    return jax.shard_map(
        per_device,
        mesh=mesh,
        in_specs=placed,
        out_specs=(
            P(None, ("groups", "span"), None, ("mp", "seq")),
            P(("groups", "span"), ("mp", "seq"), None),
        ),
        check_vma=False,
    )
```

```python
import functools
import math

import jax
import jax.numpy as jnp
from jax import lax
from jax.experimental import pallas as pl
from jax.experimental.pallas import tpu as pltpu
from jax.sharding import PartitionSpec as P

FR = 6
HD = 128
KT = 3
FADE = 2
NSTEPS = 64
LOG2E = 1.4426950408889634
VMEM_LIMIT = 24 * 1024 * 1024
VMEM_ALL = 60 * 1024 * 1024

SMEM_SPEC = pl.BlockSpec(memory_space=pltpu.SMEM)
VMEM_SPEC = pl.BlockSpec(memory_space=pltpu.VMEM)
HBM_SPEC = pl.BlockSpec(memory_space=pltpu.HBM)


def cost(flops, nbytes):
    return pl.CostEstimate(flops=flops, bytes_accessed=nbytes, transcendentals=0)


def hop(value, axis, steps):
    count = lax.axis_size(axis)
    return lax.ppermute(value, axis, [(source, source + steps) for source in range(count - steps)])


def swap(value, axes, offset):
    count = lax.axis_size(axes)
    if count & (count - 1) == 0:
        pairs = [(source, source ^ offset) for source in range(count)]
    else:
        pairs = [(source, (source + offset) % count) for source in range(count)]
    return lax.ppermute(value, axes, pairs)


def target_of(axes, offset):
    count = lax.axis_size(axes)
    mine = lax.axis_index(axes)
    if count & (count - 1) == 0:
        return mine ^ offset
    return lax.rem(mine + offset, count)


def after(value, *earlier):
    return lax.optimization_barrier((value, *earlier))[0]


def nt_dot(left, right):
    return lax.dot_general(left, right, (((1,), (1,)), ((), ())), preferred_element_type=jnp.float32)


def tn_dot(left, right):
    return lax.dot_general(left, right, (((0,), (0,)), ((), ())), preferred_element_type=jnp.float32)


def nn_dot(left, right):
    return jnp.dot(left, right, preferred_element_type=jnp.float32)


def row_factors(step_ref, position, steps, rows):
    lane = lax.broadcasted_iota(jnp.int32, (1, steps * rows), 1)
    index = jnp.full(lane.shape, step_ref[position, 0], jnp.int32)
    for step in range(1, steps):
        index = jnp.where(lane >= step * rows, step_ref[position, step], index)
    fraction = 1.0 - index.astype(jnp.float32) / NSTEPS
    level = 3.0 * fraction / (1.0 + 2.0 * fraction)
    return (0.5 + level) * (LOG2E / math.sqrt(HD))


def lane_windows(steps, rows):
    total = steps * rows
    return [
        (step * rows // HD * HD, min(total, -(-(step + 1) * rows // HD) * HD))
        for step in range(steps)
    ]


def join_steps(pieces, windows, rows):
    total = windows[-1][1]
    tiles = []
    for first in range(0, total, HD):
        stop = min(first + HD, total)
        tile = None
        for step, (begin, end) in enumerate(windows):
            if begin <= first and stop <= end and step * rows < stop and first < (step + 1) * rows:
                part = pieces[step][:, first - begin : stop - begin]
                if tile is None:
                    tile = part
                else:
                    lane = lax.broadcasted_iota(jnp.int32, part.shape, 1) + first
                    tile = jnp.where(lane >= step * rows, part, tile)
        tiles.append(tile)
    return jnp.concatenate(tiles, 1)


def own_kernel(step_ref, q_ref, kv_ref, acc_ref, top_ref, total_ref):
    position = lax.axis_index("span")
    steps, _, rows, columns = q_ref.shape
    factors = row_factors(step_ref, position, steps, rows)
    windows = lane_windows(steps, rows)
    for head in range(columns // HD):
        cut = slice(head * HD, (head + 1) * HD)
        queries = q_ref[:, 0, :, cut].reshape(steps * rows, HD)
        scores = join_steps(
            [nt_dot(kv_ref[s, 0, 0, :, cut], queries[a:b]) for s, (a, b) in enumerate(windows)],
            windows,
            rows,
        )
        scores = scores * factors
        top = jnp.max(scores, axis=0, keepdims=True)
        weights = jnp.exp2(scores - top)
        rounded = weights.astype(jnp.bfloat16)
        acc_ref[head] = join_steps(
            [tn_dot(kv_ref[s, 1, 0, :, cut], rounded[:, a:b]) for s, (a, b) in enumerate(windows)],
            windows,
            rows,
        )
        top_ref[head : head + 1] = top
        total_ref[head : head + 1] = jnp.sum(weights, axis=0, keepdims=True)


def absorb(queries, keys, values, factors, acc, top, total):
    scores = nt_dot(keys, queries) * factors
    newest = jnp.maximum(top, jnp.max(scores, axis=0, keepdims=True))
    weights = jnp.exp2(scores - newest)
    shrink = jnp.exp2(top - newest)
    total = total * shrink + jnp.sum(weights, axis=0, keepdims=True)
    acc = acc * shrink + tn_dot(values, weights.astype(jnp.bfloat16))
    return acc, newest, total


def visible(mask_ref, position, blocks):
    seen = False
    for place, block in blocks.items():
        seen = seen | ((position == place) & (mask_ref[place, block] > 0))
    return seen


def half(ref, which, cut):
    return ref[which, 0, :, cut] if len(ref.shape) == 4 else ref[0, :, cut]


def mid_kernel(plan, step_ref, mask_ref, q_ref, *refs):
    block_refs, (acc_in, top_in, total_in, acc_ref, top_ref, total_ref) = refs[:-6], refs[-6:]
    position = lax.axis_index("span")
    steps, _, rows, columns = q_ref.shape
    seen = visible(mask_ref, position, plan)

    @pl.when(seen)
    def _():
        factors = row_factors(step_ref, position, steps, rows)
        for head in range(columns // HD):
            cut = slice(head * HD, (head + 1) * HD)
            queries = q_ref[:, 0, :, cut].reshape(steps * rows, HD)
            acc, top, total = absorb(
                queries,
                half(block_refs[0], 0, cut),
                half(block_refs[-1], 1, cut),
                factors,
                acc_in[head],
                top_in[head : head + 1],
                total_in[head : head + 1],
            )
            acc_ref[head] = acc
            top_ref[head : head + 1] = top
            total_ref[head : head + 1] = total

    @pl.when(jnp.logical_not(seen))
    def _():
        acc_ref[...] = acc_in[...]
        top_ref[...] = top_in[...]
        total_ref[...] = total_in[...]


def score_kernel(plans, step_ref, mask_ref, q_ref, *refs):
    key_refs, (acc_in, top_in, total_in, acc_ref, w_ref) = refs[:-5], refs[-5:]
    position = lax.axis_index("span")
    steps, _, rows, columns = q_ref.shape

    def finish(key_ref):
        factors = row_factors(step_ref, position, steps, rows)
        for head in range(columns // HD):
            cut = slice(head * HD, (head + 1) * HD)
            queries = q_ref[:, 0, :, cut].reshape(steps * rows, HD)
            scores = nt_dot(half(key_ref, 0, cut), queries) * factors
            top = top_in[head : head + 1]
            newest = jnp.maximum(top, jnp.max(scores, axis=0, keepdims=True))
            weights = jnp.exp2(scores - newest)
            shrink = jnp.exp2(top - newest)
            total = total_in[head : head + 1] * shrink + jnp.sum(weights, axis=0, keepdims=True)
            inverse = 1.0 / total
            w_ref[head] = (weights * inverse).astype(jnp.bfloat16)
            acc_ref[head] = acc_in[head] * (shrink * inverse)

    rest = True
    for plan, key_ref in zip(plans, key_refs):
        seen = visible(mask_ref, position, plan)
        rest = jnp.logical_and(rest, jnp.logical_not(seen))
        pl.when(seen)(functools.partial(finish, key_ref))

    @pl.when(rest)
    def _():
        w_ref[...] = jnp.zeros_like(w_ref)
        for head in range(columns // HD):
            acc_ref[head] = acc_in[head] * (1.0 / total_in[head : head + 1])


def average_head(head, acc_ref, w_ref, value_ref, first):
    width = acc_ref.shape[0] * HD
    if value_ref.shape[-1] == width:
        first = 0
    if value_ref.shape[-1] > width:
        first = -acc_ref.shape[0]
    cut = slice((head - first) * HD, (head - first + 1) * HD)
    return acc_ref[head] + tn_dot(half(value_ref, 1, cut), w_ref[head])


def average_kernel(begin, end, acc_ref, w_ref, value_ref, average_ref, square_ref):
    squares = jnp.zeros(square_ref.shape, jnp.float32)
    for head in range(begin, end):
        average = average_head(head, acc_ref, w_ref, value_ref, begin)
        squares = squares + jnp.sum(average * average, axis=0, keepdims=True)
        average_ref[:, :, (head - begin) * HD : (head - begin + 1) * HD] = average.T.reshape(
            average_ref.shape[:2] + (HD,)
        )
    square_ref[...] = squares


def rest_kernel(begin, end, acc_ref, w_ref, value_ref, before_ref, average_ref, square_ref):
    squares = before_ref[...]
    for head in range(begin, end):
        average = average_head(head, acc_ref, w_ref, value_ref, begin)
        squares = squares + jnp.sum(average * average, axis=0, keepdims=True)
        average_ref[head - begin] = average
    square_ref[...] = squares


def turn_kernel(in_ref, square_in, out_ref, square_ref):
    steps, rows, _ = out_ref.shape
    for head in range(in_ref.shape[0]):
        out_ref[:, :, head * HD : (head + 1) * HD] = in_ref[head].T.reshape(steps, rows, HD)
    square_ref[...] = square_in[...]


def scale_kernel(width, front_ref, back_ref, *refs):
    part_refs, (out_hbm, out_ref, sem) = refs[:-3], refs[-3:]
    total = part_refs[0][...]
    for ref in part_refs[1:]:
        total = total + ref[...]
    inverse = lax.rsqrt(total / width + 1e-06)
    steps, rows, columns = out_ref.shape
    spread = jnp.broadcast_to(inverse, (HD, steps * rows)).T
    copies = []
    for step in range(steps):
        factor = spread[step * rows : (step + 1) * rows]
        place = 0
        for ref in (front_ref, back_ref):
            for first in range(0, ref.shape[2], HD):
                average = ref[step, :, first : first + HD]
                out_ref[step, :, place : place + HD] = (average * factor).astype(jnp.bfloat16)
                place += HD
        copies.append(pltpu.make_async_copy(out_ref.at[step], out_hbm.at[step, 0], sem.at[step]))
        copies[-1].start()
    for copy in copies:
        copy.wait()


def send(value, pairs):
    return lax.ppermute(value, "span", pairs)


def delivered(span, back):
    return {place: place - back for place in range(back, span)}


def plain_call(kernel, name, out_shape, flops, operands, in_specs=(), out_specs=None, scratch=(), limit=VMEM_LIMIT):
    nbytes = sum(math.prod(o.shape) * o.dtype.itemsize for o in operands)
    if out_specs is None:
        out_specs = [VMEM_SPEC] * len(out_shape)
    return pl.pallas_call(
        kernel,
        in_specs=list(in_specs) + [VMEM_SPEC] * (len(operands) - len(in_specs)),
        out_specs=out_specs,
        out_shape=out_shape,
        scratch_shapes=list(scratch),
        compiler_params=pltpu.CompilerParams(vmem_limit_bytes=limit),
        cost_estimate=cost(flops, nbytes),
        name=name,
    )(*operands)


def picker(shape, wanted):
    row = lax.broadcasted_iota(jnp.int32, shape, 0)
    column = lax.broadcasted_iota(jnp.int32, shape, 1)
    return jnp.where(column == wanted(row), 1.0, 0.0).astype(jnp.bfloat16)


def project_kernel(axes, x_hbm, w_hbm, *refs):
    out_refs, (x_ref, w_ref, x_sem, w_sem) = refs[:-4], refs[-4:]
    rows, depth = x_ref.shape
    share = out_refs[0].shape[0]
    x_copy = pltpu.make_async_copy(x_hbm.at[0], x_ref, x_sem)
    x_copy.start()
    copies = []
    for place, first in enumerate(range(0, depth, 2 * HD)):
        cut = slice(first, min(first + 2 * HD, depth))
        copies.append((cut, pltpu.make_async_copy(w_hbm.at[cut], w_ref.at[cut], w_sem.at[place])))
        copies[-1][1].start()
    total = jnp.zeros((rows, w_ref.shape[1]), jnp.float32)
    x_copy.wait()
    for cut, w_copy in copies:
        w_copy.wait()
        total = total + nn_dot(x_ref[:, cut], w_ref[cut])
    projected = total.astype(jnp.bfloat16)
    for offset, out_ref in enumerate(out_refs):
        first = target_of(axes, offset) * share
        chosen = picker((share, rows), lambda row: row + first)
        out_ref[...] = nn_dot(chosen, projected).astype(jnp.bfloat16)


def gather_kernel(*refs):
    hidden_ref, tail_ref = refs[-2:]
    total = refs[0][...].astype(jnp.float32)
    for ref in refs[1:-2]:
        total = total + ref[...].astype(jnp.float32)
    hidden = total.astype(jnp.bfloat16)
    hidden_ref[...] = hidden
    kept = KT - 1 + FADE
    shape = (tail_ref.shape[0], hidden.shape[0])
    chosen = picker(shape, lambda row: row // kept * FR + FR - kept + row % kept)
    tail_ref[...] = nn_dot(chosen, hidden).astype(jnp.bfloat16)


def decode_kernel(fade_ref, hidden_ref, tail_ref, conv_ref, out_ref):
    position = lax.axis_index("span")
    share = hidden_ref.shape[0]
    spatial = share // FR
    kept = KT - 1 + FADE
    wide = FADE + FR
    hidden, tail = hidden_ref[...], tail_ref[...]
    mixed = jnp.zeros((spatial * wide, out_ref.shape[2]), jnp.float32)
    for tap in range(KT):
        def from_tail(row):
            place = row % wide + KT - 1 - tap
            return jnp.where(place < kept, row // wide * kept + place, -1)

        def from_hidden(row):
            place = row % wide + KT - 1 - tap
            return jnp.where(place >= kept, row // wide * FR + place - kept, -1)

        window = nn_dot(picker((spatial * wide, tail.shape[0]), from_tail), tail)
        window = window + nn_dot(picker((spatial * wide, share), from_hidden), hidden)
        mixed = mixed + nn_dot(window.astype(jnp.bfloat16), conv_ref[tap])
    frames = (mixed * jax.nn.sigmoid(mixed)).astype(jnp.bfloat16)
    fade = fade_ref[0]
    shape = (share, spatial * wide)
    current = nn_dot(picker(shape, lambda row: row // FR * wide + FADE + row % FR), frames)

    def faded(row):
        return jnp.where(row % FR < fade, row // FR * wide + FADE - fade + row % FR, -1)

    previous = nn_dot(picker(shape, faded), frames)
    frame = lax.broadcasted_iota(jnp.int32, (share, out_ref.shape[2]), 0) % FR
    fade_float = jnp.full(frame.shape, fade, jnp.int32).astype(jnp.float32)
    weight = (frame.astype(jnp.float32) + 1.0) / (fade_float + 1.0)
    weight = jnp.where((frame < fade) & (position > 0), weight, 1.0)
    out_ref[0] = (weight * current + (1.0 - weight) * previous).astype(jnp.bfloat16)


def project(finished, w_in):
    axes = ("mp", "seq")
    parts = lax.axis_size(axes)
    _, rows, depth = finished.shape
    channels = w_in.shape[1]
    chunks = -(-depth // (2 * HD))
    return plain_call(
        functools.partial(project_kernel, axes),
        "project",
        [jax.ShapeDtypeStruct((rows // parts, channels), jnp.bfloat16)] * parts,
        2 * rows * depth * channels,
        (finished, w_in),
        [HBM_SPEC] * 2,
        scratch=[
            pltpu.VMEM((rows, depth), jnp.bfloat16),
            pltpu.VMEM((depth, channels), jnp.bfloat16),
            pltpu.SemaphoreType.DMA,
            pltpu.SemaphoreType.DMA((chunks,)),
        ],
        limit=VMEM_ALL,
    )


def gather(parts, rows):
    share, channels = parts[0].shape
    tail_rows = share // FR * (KT - 1 + FADE)
    return plain_call(
        gather_kernel,
        "gather",
        [jax.ShapeDtypeStruct((count, channels), jnp.bfloat16) for count in (share, tail_rows)],
        rows * channels,
        parts,
    )


def decode(hidden, tail, conv_w, fade_count):
    share, channels = hidden.shape
    return plain_call(
        decode_kernel,
        "decode",
        [jax.ShapeDtypeStruct((1, share, channels), jnp.bfloat16)],
        2 * share * KT * channels * channels,
        (fade_count, hidden, tail, conv_w),
        [SMEM_SPEC],
    )[0]


def per_device(
    query, noisy_kv, clean_kv, causal_mask, step_index, finished, w_in, conv_w, fade_count
):
    steps, _, rows, columns = query.shape
    heads = columns // HD
    middle = (heads + 1) // 2 * HD
    row_count = steps * rows
    span = lax.axis_size("span")
    axes = ("mp", "seq")
    acc_shape = jax.ShapeDtypeStruct((heads, HD, row_count), jnp.float32)
    stat_shape = jax.ShapeDtypeStruct((heads, row_count), jnp.float32)
    pair_flops = 4 * row_count * rows * columns

    first_pairs = [(0, 2), (2, 3)] if span == 4 else [(c, c + 1) for c in range(span - 1)]
    near = send(clean_kv, first_pairs)
    pieces = project(finished, w_in)
    parts = [pieces[0]] + [swap(p, axes, offset + 1) for offset, p in enumerate(pieces[1:])]
    if span == 4:
        direct = send(clean_kv, [(1, 3)])
    carry = plain_call(
        own_kernel,
        "own",
        [acc_shape, stat_shape, stat_shape],
        pair_flops,
        (step_index, query, noisy_kv),
        [SMEM_SPEC],
    )
    hidden, tail = gather(parts, rows)
    tail = hop(tail, "span", 1)
    if span == 4:
        near = after(near, carry[0], hidden)
        forwards = lax.axis_index("span") == 2
        passed = [jnp.where(forwards, near[which], clean_kv[which]) for which in range(2)]
        front = jnp.concatenate([passed[0], passed[1][:, :, :middle]], 2)
        passed = [front, passed[1][:, :, middle:]]
        passed = [hop(block, "span", 1) for block in passed]
        early = [(near, {2: 0, 3: 2}), (direct, {3: 1})]
        keys, values = passed[0], passed
        last_plan = {1: 0, 2: 1, 3: 0}
    else:
        ring = [near]
        for _ in range(2, span):
            ring.append(hop(ring[-1], "span", 1))
        early = [(block, delivered(span, back + 1)) for back, block in enumerate(ring[:-1])]
        keys, values = ring[-1], ring[-1:] * 2
        last_plan = delivered(span, span - 1)
    for block, plan in early:
        carry = plain_call(
            functools.partial(mid_kernel, plan),
            "middle",
            [acc_shape, stat_shape, stat_shape],
            pair_flops,
            (step_index, causal_mask, query, block, *carry),
            [SMEM_SPEC] * 2,
        )
    acc, weights = plain_call(
        functools.partial(score_kernel, [last_plan]),
        "score",
        [acc_shape, jax.ShapeDtypeStruct((heads, rows, row_count), jnp.bfloat16)],
        pair_flops // 2,
        (step_index, causal_mask, query, keys, *carry),
        [SMEM_SPEC] * 2,
    )
    square_shape = jax.ShapeDtypeStruct((1, row_count), jnp.float32)
    front, squares = plain_call(
        functools.partial(average_kernel, 0, middle // HD),
        "average",
        [jax.ShapeDtypeStruct((steps, rows, middle), jnp.float32), square_shape],
        pair_flops // 4,
        (acc, weights, values[0]),
    )
    averaged, squares = plain_call(
        functools.partial(rest_kernel, middle // HD, heads),
        "rest",
        [jax.ShapeDtypeStruct((heads - middle // HD, HD, row_count), jnp.float32), square_shape],
        pair_flops // 4,
        (acc, weights, values[1], squares),
    )
    others = [swap(squares, axes, offset) for offset in range(2, lax.axis_size(axes))]
    back, squares = plain_call(
        turn_kernel,
        "turn",
        [jax.ShapeDtypeStruct((steps, rows, columns - middle), jnp.float32), square_shape],
        row_count * columns,
        (averaged, squares),
    )
    others.append(swap(squares, axes, 1))
    decoded = decode(after(hidden, back), tail, conv_w, fade_count)
    attended = plain_call(
        functools.partial(scale_kernel, columns * lax.axis_size(axes)),
        "scale",
        jax.ShapeDtypeStruct(query.shape, jnp.bfloat16),
        row_count * columns,
        (front, back, squares, *others),
        out_specs=HBM_SPEC,
        scratch=[
            pltpu.VMEM((steps, rows, columns), jnp.bfloat16),
            pltpu.SemaphoreType.DMA((steps,)),
        ],
    )
    return (attended, decoded)


def solution(mesh):
    placed = (
        P(None, ("groups", "span"), None, ("mp", "seq")),
        P(None, None, ("groups", "span"), None, ("mp", "seq")),
        P(None, ("groups", "span"), None, ("mp", "seq")),
        P("groups", None),
        P("groups", None),
        P(("groups", "span"), None, ("mp", "seq")),
        P(("mp", "seq"), None),
        P(),
        P(("groups", "span")),
    )
    return jax.shard_map(
        per_device,
        mesh=mesh,
        in_specs=placed,
        out_specs=(
            P(None, ("groups", "span"), None, ("mp", "seq")),
            P(("groups", "span"), ("mp", "seq"), None),
        ),
        check_vma=False,
    )
```

```python
import functools
import math

import jax
import jax.numpy as jnp
from jax import lax
from jax.experimental import pallas as pl
from jax.experimental.pallas import tpu as pltpu
from jax.sharding import PartitionSpec as P

FR = 6
HD = 128
KT = 3
FADE = 2
NSTEPS = 64
LOG2E = 1.4426950408889634
VMEM_LIMIT = 24 * 1024 * 1024
VMEM_ALL = 60 * 1024 * 1024

SMEM_SPEC = pl.BlockSpec(memory_space=pltpu.SMEM)
VMEM_SPEC = pl.BlockSpec(memory_space=pltpu.VMEM)
HBM_SPEC = pl.BlockSpec(memory_space=pltpu.HBM)


def cost(flops, nbytes):
    return pl.CostEstimate(flops=flops, bytes_accessed=nbytes, transcendentals=0)


def hop(value, axis, steps):
    count = lax.axis_size(axis)
    return lax.ppermute(value, axis, [(source, source + steps) for source in range(count - steps)])


def swap(value, axes, offset):
    count = lax.axis_size(axes)
    if count & (count - 1) == 0:
        pairs = [(source, source ^ offset) for source in range(count)]
    else:
        pairs = [(source, (source + offset) % count) for source in range(count)]
    return lax.ppermute(value, axes, pairs)


def target_of(axes, offset):
    count = lax.axis_size(axes)
    mine = lax.axis_index(axes)
    if count & (count - 1) == 0:
        return mine ^ offset
    return lax.rem(mine + offset, count)


def after(value, *earlier):
    return lax.optimization_barrier((value, *earlier))[0]


def nt_dot(left, right):
    return lax.dot_general(left, right, (((1,), (1,)), ((), ())), preferred_element_type=jnp.float32)


def tn_dot(left, right):
    return lax.dot_general(left, right, (((0,), (0,)), ((), ())), preferred_element_type=jnp.float32)


def nn_dot(left, right):
    return jnp.dot(left, right, preferred_element_type=jnp.float32)


def row_factors(step_ref, position, steps, rows):
    lane = lax.broadcasted_iota(jnp.int32, (1, steps * rows), 1)
    index = jnp.full(lane.shape, step_ref[position, 0], jnp.int32)
    for step in range(1, steps):
        index = jnp.where(lane >= step * rows, step_ref[position, step], index)
    fraction = 1.0 - index.astype(jnp.float32) / NSTEPS
    level = 3.0 * fraction / (1.0 + 2.0 * fraction)
    return (0.5 + level) * (LOG2E / math.sqrt(HD))


def lane_windows(steps, rows):
    total = steps * rows
    return [
        (step * rows // HD * HD, min(total, -(-(step + 1) * rows // HD) * HD))
        for step in range(steps)
    ]


def join_steps(pieces, windows, rows):
    total = windows[-1][1]
    tiles = []
    for first in range(0, total, HD):
        stop = min(first + HD, total)
        tile = None
        for step, (begin, end) in enumerate(windows):
            if begin <= first and stop <= end and step * rows < stop and first < (step + 1) * rows:
                part = pieces[step][:, first - begin : stop - begin]
                if tile is None:
                    tile = part
                else:
                    lane = lax.broadcasted_iota(jnp.int32, part.shape, 1) + first
                    tile = jnp.where(lane >= step * rows, part, tile)
        tiles.append(tile)
    return jnp.concatenate(tiles, 1)


def own_kernel(step_ref, q_ref, kv_ref, acc_ref, top_ref, total_ref):
    position = lax.axis_index("span")
    steps, _, rows, columns = q_ref.shape
    factors = row_factors(step_ref, position, steps, rows)
    windows = lane_windows(steps, rows)
    for head in range(columns // HD):
        cut = slice(head * HD, (head + 1) * HD)
        queries = q_ref[:, 0, :, cut].reshape(steps * rows, HD)
        scores = join_steps(
            [nt_dot(kv_ref[s, 0, 0, :, cut], queries[a:b]) for s, (a, b) in enumerate(windows)],
            windows,
            rows,
        )
        scores = scores * factors
        top = jnp.max(scores, axis=0, keepdims=True)
        weights = jnp.exp2(scores - top)
        rounded = weights.astype(jnp.bfloat16)
        acc_ref[head] = join_steps(
            [tn_dot(kv_ref[s, 1, 0, :, cut], rounded[:, a:b]) for s, (a, b) in enumerate(windows)],
            windows,
            rows,
        )
        top_ref[head : head + 1] = top
        total_ref[head : head + 1] = jnp.sum(weights, axis=0, keepdims=True)


def absorb(queries, keys, values, factors, acc, top, total):
    scores = nt_dot(keys, queries) * factors
    newest = jnp.maximum(top, jnp.max(scores, axis=0, keepdims=True))
    weights = jnp.exp2(scores - newest)
    shrink = jnp.exp2(top - newest)
    total = total * shrink + jnp.sum(weights, axis=0, keepdims=True)
    acc = acc * shrink + tn_dot(values, weights.astype(jnp.bfloat16))
    return acc, newest, total


def visible(mask_ref, position, blocks):
    seen = False
    for place, block in blocks.items():
        seen = seen | ((position == place) & (mask_ref[place, block] > 0))
    return seen


def half(ref, which, cut):
    return ref[which, 0, :, cut] if len(ref.shape) == 4 else ref[0, :, cut]


def mid_kernel(plan, step_ref, mask_ref, q_ref, *refs):
    block_refs, (acc_in, top_in, total_in, acc_ref, top_ref, total_ref) = refs[:-6], refs[-6:]
    position = lax.axis_index("span")
    steps, _, rows, columns = q_ref.shape
    seen = visible(mask_ref, position, plan)

    @pl.when(seen)
    def _():
        factors = row_factors(step_ref, position, steps, rows)
        for head in range(columns // HD):
            cut = slice(head * HD, (head + 1) * HD)
            queries = q_ref[:, 0, :, cut].reshape(steps * rows, HD)
            acc, top, total = absorb(
                queries,
                half(block_refs[0], 0, cut),
                half(block_refs[-1], 1, cut),
                factors,
                acc_in[head],
                top_in[head : head + 1],
                total_in[head : head + 1],
            )
            acc_ref[head] = acc
            top_ref[head : head + 1] = top
            total_ref[head : head + 1] = total

    @pl.when(jnp.logical_not(seen))
    def _():
        acc_ref[...] = acc_in[...]
        top_ref[...] = top_in[...]
        total_ref[...] = total_in[...]


def score_kernel(plans, step_ref, mask_ref, q_ref, *refs):
    key_refs, (acc_in, top_in, total_in, acc_ref, w_ref) = refs[:-5], refs[-5:]
    position = lax.axis_index("span")
    steps, _, rows, columns = q_ref.shape

    def finish(key_ref):
        factors = row_factors(step_ref, position, steps, rows)
        for head in range(columns // HD):
            cut = slice(head * HD, (head + 1) * HD)
            queries = q_ref[:, 0, :, cut].reshape(steps * rows, HD)
            scores = nt_dot(half(key_ref, 0, cut), queries) * factors
            top = top_in[head : head + 1]
            newest = jnp.maximum(top, jnp.max(scores, axis=0, keepdims=True))
            weights = jnp.exp2(scores - newest)
            shrink = jnp.exp2(top - newest)
            total = total_in[head : head + 1] * shrink + jnp.sum(weights, axis=0, keepdims=True)
            inverse = 1.0 / total
            w_ref[head] = (weights * inverse).astype(jnp.bfloat16)
            acc_ref[head] = acc_in[head] * (shrink * inverse)

    rest = True
    for plan, key_ref in zip(plans, key_refs):
        seen = visible(mask_ref, position, plan)
        rest = jnp.logical_and(rest, jnp.logical_not(seen))
        pl.when(seen)(functools.partial(finish, key_ref))

    @pl.when(rest)
    def _():
        w_ref[...] = jnp.zeros_like(w_ref)
        for head in range(columns // HD):
            acc_ref[head] = acc_in[head] * (1.0 / total_in[head : head + 1])


def average_head(head, acc_ref, w_ref, value_ref, first):
    width = acc_ref.shape[0] * HD
    if value_ref.shape[-1] == width:
        first = 0
    if value_ref.shape[-1] > width:
        first = -acc_ref.shape[0]
    cut = slice((head - first) * HD, (head - first + 1) * HD)
    return acc_ref[head] + tn_dot(half(value_ref, 1, cut), w_ref[head])


def average_kernel(begin, end, acc_ref, w_ref, value_ref, average_ref, square_ref):
    squares = jnp.zeros(square_ref.shape, jnp.float32)
    for head in range(begin, end):
        average = average_head(head, acc_ref, w_ref, value_ref, begin)
        squares = squares + jnp.sum(average * average, axis=0, keepdims=True)
        average_ref[:, :, (head - begin) * HD : (head - begin + 1) * HD] = average.T.reshape(
            average_ref.shape[:2] + (HD,)
        )
    square_ref[...] = squares


def rest_kernel(begin, end, acc_ref, w_ref, value_ref, before_ref, average_ref, square_ref):
    squares = before_ref[...]
    for head in range(begin, end):
        average = average_head(head, acc_ref, w_ref, value_ref, begin)
        squares = squares + jnp.sum(average * average, axis=0, keepdims=True)
        average_ref[head - begin] = average
    square_ref[...] = squares


def turn_kernel(in_ref, square_in, out_ref, square_ref):
    steps, rows, _ = out_ref.shape
    for head in range(in_ref.shape[0]):
        out_ref[:, :, head * HD : (head + 1) * HD] = in_ref[head].T.reshape(steps, rows, HD)
    square_ref[...] = square_in[...]


def scale_kernel(width, front_ref, back_ref, *refs):
    part_refs, (out_hbm, out_ref, sem) = refs[:-3], refs[-3:]
    total = part_refs[0][...]
    for ref in part_refs[1:]:
        total = total + ref[...]
    inverse = lax.rsqrt(total / width + 1e-06)
    steps, rows, columns = out_ref.shape
    copies = []
    for step in range(steps):
        own = inverse[:, step * rows : (step + 1) * rows]
        factor = jnp.broadcast_to(own, (HD, rows)).T
        place = 0
        for ref in (front_ref, back_ref):
            for first in range(0, ref.shape[2], HD):
                average = ref[step, :, first : first + HD]
                out_ref[step, :, place : place + HD] = (average * factor).astype(jnp.bfloat16)
                place += HD
        copies.append(pltpu.make_async_copy(out_ref.at[step], out_hbm.at[step, 0], sem.at[step]))
        copies[-1].start()
    for copy in copies:
        copy.wait()


def send(value, pairs):
    return lax.ppermute(value, "span", pairs)


def delivered(span, back):
    return {place: place - back for place in range(back, span)}


def plain_call(kernel, name, out_shape, flops, operands, in_specs=(), out_specs=None, scratch=(), limit=VMEM_LIMIT):
    nbytes = sum(math.prod(o.shape) * o.dtype.itemsize for o in operands)
    if out_specs is None:
        out_specs = [VMEM_SPEC] * len(out_shape)
    return pl.pallas_call(
        kernel,
        in_specs=list(in_specs) + [VMEM_SPEC] * (len(operands) - len(in_specs)),
        out_specs=out_specs,
        out_shape=out_shape,
        scratch_shapes=list(scratch),
        compiler_params=pltpu.CompilerParams(vmem_limit_bytes=limit),
        cost_estimate=cost(flops, nbytes),
        name=name,
    )(*operands)


def picker(shape, wanted):
    row = lax.broadcasted_iota(jnp.int32, shape, 0)
    column = lax.broadcasted_iota(jnp.int32, shape, 1)
    return jnp.where(column == wanted(row), 1.0, 0.0).astype(jnp.bfloat16)


def project_kernel(axes, x_hbm, w_hbm, *refs):
    out_refs, (x_ref, w_ref, x_sem, w_sem) = refs[:-4], refs[-4:]
    rows, depth = x_ref.shape
    share = out_refs[0].shape[0]
    x_copy = pltpu.make_async_copy(x_hbm.at[0], x_ref, x_sem)
    x_copy.start()
    copies = []
    for place, first in enumerate(range(0, depth, 2 * HD)):
        cut = slice(first, min(first + 2 * HD, depth))
        copies.append((cut, pltpu.make_async_copy(w_hbm.at[cut], w_ref.at[cut], w_sem.at[place])))
        copies[-1][1].start()
    total = jnp.zeros((rows, w_ref.shape[1]), jnp.float32)
    x_copy.wait()
    for cut, w_copy in copies:
        w_copy.wait()
        total = total + nn_dot(x_ref[:, cut], w_ref[cut])
    projected = total.astype(jnp.bfloat16)
    for offset, out_ref in enumerate(out_refs):
        first = target_of(axes, offset) * share
        chosen = picker((share, rows), lambda row: row + first)
        out_ref[...] = nn_dot(chosen, projected).astype(jnp.bfloat16)


def gather_kernel(*refs):
    hidden_ref, tail_ref = refs[-2:]
    total = refs[0][...].astype(jnp.float32)
    for ref in refs[1:-2]:
        total = total + ref[...].astype(jnp.float32)
    hidden = total.astype(jnp.bfloat16)
    hidden_ref[...] = hidden
    kept = KT - 1 + FADE
    shape = (tail_ref.shape[0], hidden.shape[0])
    chosen = picker(shape, lambda row: row // kept * FR + FR - kept + row % kept)
    tail_ref[...] = nn_dot(chosen, hidden).astype(jnp.bfloat16)


def decode_kernel(fade_ref, hidden_ref, tail_ref, conv_ref, out_ref):
    position = lax.axis_index("span")
    share = hidden_ref.shape[0]
    spatial = share // FR
    kept = KT - 1 + FADE
    wide = FADE + FR
    hidden, tail = hidden_ref[...], tail_ref[...]
    mixed = jnp.zeros((spatial * wide, out_ref.shape[2]), jnp.float32)
    for tap in range(KT):
        def from_tail(row):
            place = row % wide + KT - 1 - tap
            return jnp.where(place < kept, row // wide * kept + place, -1)

        def from_hidden(row):
            place = row % wide + KT - 1 - tap
            return jnp.where(place >= kept, row // wide * FR + place - kept, -1)

        window = nn_dot(picker((spatial * wide, tail.shape[0]), from_tail), tail)
        window = window + nn_dot(picker((spatial * wide, share), from_hidden), hidden)
        mixed = mixed + nn_dot(window.astype(jnp.bfloat16), conv_ref[tap])
    frames = (mixed * jax.nn.sigmoid(mixed)).astype(jnp.bfloat16)
    fade = fade_ref[0]
    shape = (share, spatial * wide)
    current = nn_dot(picker(shape, lambda row: row // FR * wide + FADE + row % FR), frames)

    def faded(row):
        return jnp.where(row % FR < fade, row // FR * wide + FADE - fade + row % FR, -1)

    previous = nn_dot(picker(shape, faded), frames)
    frame = lax.broadcasted_iota(jnp.int32, (share, out_ref.shape[2]), 0) % FR
    fade_float = jnp.full(frame.shape, fade, jnp.int32).astype(jnp.float32)
    weight = (frame.astype(jnp.float32) + 1.0) / (fade_float + 1.0)
    weight = jnp.where((frame < fade) & (position > 0), weight, 1.0)
    out_ref[0] = (weight * current + (1.0 - weight) * previous).astype(jnp.bfloat16)


def project(finished, w_in):
    axes = ("mp", "seq")
    parts = lax.axis_size(axes)
    _, rows, depth = finished.shape
    channels = w_in.shape[1]
    chunks = -(-depth // (2 * HD))
    return plain_call(
        functools.partial(project_kernel, axes),
        "project",
        [jax.ShapeDtypeStruct((rows // parts, channels), jnp.bfloat16)] * parts,
        2 * rows * depth * channels,
        (finished, w_in),
        [HBM_SPEC] * 2,
        scratch=[
            pltpu.VMEM((rows, depth), jnp.bfloat16),
            pltpu.VMEM((depth, channels), jnp.bfloat16),
            pltpu.SemaphoreType.DMA,
            pltpu.SemaphoreType.DMA((chunks,)),
        ],
        limit=VMEM_ALL,
    )


def gather(parts, rows):
    share, channels = parts[0].shape
    tail_rows = share // FR * (KT - 1 + FADE)
    return plain_call(
        gather_kernel,
        "gather",
        [jax.ShapeDtypeStruct((count, channels), jnp.bfloat16) for count in (share, tail_rows)],
        rows * channels,
        parts,
    )


def decode(hidden, tail, conv_w, fade_count):
    share, channels = hidden.shape
    return plain_call(
        decode_kernel,
        "decode",
        [jax.ShapeDtypeStruct((1, share, channels), jnp.bfloat16)],
        2 * share * KT * channels * channels,
        (fade_count, hidden, tail, conv_w),
        [SMEM_SPEC],
    )[0]


def per_device(
    query, noisy_kv, clean_kv, causal_mask, step_index, finished, w_in, conv_w, fade_count
):
    steps, _, rows, columns = query.shape
    heads = columns // HD
    middle = (heads + 1) // 2 * HD
    row_count = steps * rows
    span = lax.axis_size("span")
    axes = ("mp", "seq")
    acc_shape = jax.ShapeDtypeStruct((heads, HD, row_count), jnp.float32)
    stat_shape = jax.ShapeDtypeStruct((heads, row_count), jnp.float32)
    pair_flops = 4 * row_count * rows * columns

    first_pairs = [(0, 2), (2, 3)] if span == 4 else [(c, c + 1) for c in range(span - 1)]
    near = send(clean_kv, first_pairs)
    pieces = project(finished, w_in)
    parts = [pieces[0]] + [swap(p, axes, offset + 1) for offset, p in enumerate(pieces[1:])]
    if span == 4:
        direct = send(clean_kv, [(1, 3)])
    carry = plain_call(
        own_kernel,
        "own",
        [acc_shape, stat_shape, stat_shape],
        pair_flops,
        (step_index, query, noisy_kv),
        [SMEM_SPEC],
    )
    hidden, tail = gather(parts, rows)
    tail = hop(tail, "span", 1)
    if span == 4:
        near = after(near, carry[0], hidden)
        forwards = lax.axis_index("span") == 2
        passed = [jnp.where(forwards, near[which], clean_kv[which]) for which in range(2)]
        front = jnp.concatenate([passed[0], passed[1][:, :, :middle]], 2)
        passed = [front, passed[1][:, :, middle:]]
        passed = [hop(block, "span", 1) for block in passed]
        early = [(near, {2: 0, 3: 2}), (direct, {3: 1})]
        keys, values = passed[0], passed
        last_plan = {1: 0, 2: 1, 3: 0}
    else:
        ring = [near]
        for _ in range(2, span):
            ring.append(hop(ring[-1], "span", 1))
        early = [(block, delivered(span, back + 1)) for back, block in enumerate(ring[:-1])]
        keys, values = ring[-1], ring[-1:] * 2
        last_plan = delivered(span, span - 1)
    for block, plan in early:
        carry = plain_call(
            functools.partial(mid_kernel, plan),
            "middle",
            [acc_shape, stat_shape, stat_shape],
            pair_flops,
            (step_index, causal_mask, query, block, *carry),
            [SMEM_SPEC] * 2,
        )
    acc, weights = plain_call(
        functools.partial(score_kernel, [last_plan]),
        "score",
        [acc_shape, jax.ShapeDtypeStruct((heads, rows, row_count), jnp.bfloat16)],
        pair_flops // 2,
        (step_index, causal_mask, query, keys, *carry),
        [SMEM_SPEC] * 2,
    )
    square_shape = jax.ShapeDtypeStruct((1, row_count), jnp.float32)
    front, squares = plain_call(
        functools.partial(average_kernel, 0, middle // HD),
        "average",
        [jax.ShapeDtypeStruct((steps, rows, middle), jnp.float32), square_shape],
        pair_flops // 4,
        (acc, weights, values[0]),
    )
    averaged, squares = plain_call(
        functools.partial(rest_kernel, middle // HD, heads),
        "rest",
        [jax.ShapeDtypeStruct((heads - middle // HD, HD, row_count), jnp.float32), square_shape],
        pair_flops // 4,
        (acc, weights, values[1], squares),
    )
    others = [swap(squares, axes, offset) for offset in range(2, lax.axis_size(axes))]
    back, squares = plain_call(
        turn_kernel,
        "turn",
        [jax.ShapeDtypeStruct((steps, rows, columns - middle), jnp.float32), square_shape],
        row_count * columns,
        (averaged, squares),
    )
    others.append(swap(squares, axes, 1))
    decoded = decode(after(hidden, back), tail, conv_w, fade_count)
    attended = plain_call(
        functools.partial(scale_kernel, columns * lax.axis_size(axes)),
        "scale",
        jax.ShapeDtypeStruct(query.shape, jnp.bfloat16),
        row_count * columns,
        (front, back, squares, *others),
        out_specs=HBM_SPEC,
        scratch=[
            pltpu.VMEM((steps, rows, columns), jnp.bfloat16),
            pltpu.SemaphoreType.DMA((steps,)),
        ],
    )
    return (attended, decoded)


def solution(mesh):
    placed = (
        P(None, ("groups", "span"), None, ("mp", "seq")),
        P(None, None, ("groups", "span"), None, ("mp", "seq")),
        P(None, ("groups", "span"), None, ("mp", "seq")),
        P("groups", None),
        P("groups", None),
        P(("groups", "span"), None, ("mp", "seq")),
        P(("mp", "seq"), None),
        P(),
        P(("groups", "span")),
    )
    return jax.shard_map(
        per_device,
        mesh=mesh,
        in_specs=placed,
        out_specs=(
            P(None, ("groups", "span"), None, ("mp", "seq")),
            P(("groups", "span"), ("mp", "seq"), None),
        ),
        check_vma=False,
    )
```

```python
import functools
import math

import jax
import jax.numpy as jnp
from jax import lax
from jax.experimental import pallas as pl
from jax.experimental.pallas import tpu as pltpu
from jax.sharding import PartitionSpec as P

FR = 6
HD = 128
KT = 3
FADE = 2
NSTEPS = 64
LOG2E = 1.4426950408889634
VMEM_LIMIT = 24 * 1024 * 1024
VMEM_ALL = 60 * 1024 * 1024

SMEM_SPEC = pl.BlockSpec(memory_space=pltpu.SMEM)
VMEM_SPEC = pl.BlockSpec(memory_space=pltpu.VMEM)
HBM_SPEC = pl.BlockSpec(memory_space=pltpu.HBM)


def cost(flops, nbytes):
    return pl.CostEstimate(flops=flops, bytes_accessed=nbytes, transcendentals=0)


def hop(value, axis, steps):
    count = lax.axis_size(axis)
    return lax.ppermute(value, axis, [(source, source + steps) for source in range(count - steps)])


def swap(value, axes, offset):
    count = lax.axis_size(axes)
    if count & (count - 1) == 0:
        pairs = [(source, source ^ offset) for source in range(count)]
    else:
        pairs = [(source, (source + offset) % count) for source in range(count)]
    return lax.ppermute(value, axes, pairs)


def target_of(axes, offset):
    count = lax.axis_size(axes)
    mine = lax.axis_index(axes)
    if count & (count - 1) == 0:
        return mine ^ offset
    return lax.rem(mine + offset, count)


def after(value, *earlier):
    return lax.optimization_barrier((value, *earlier))[0]


def nt_dot(left, right):
    return lax.dot_general(left, right, (((1,), (1,)), ((), ())), preferred_element_type=jnp.float32)


def tn_dot(left, right):
    return lax.dot_general(left, right, (((0,), (0,)), ((), ())), preferred_element_type=jnp.float32)


def nn_dot(left, right):
    return jnp.dot(left, right, preferred_element_type=jnp.float32)


def row_factors(step_ref, position, steps, rows):
    lane = lax.broadcasted_iota(jnp.int32, (1, steps * rows), 1)
    index = jnp.full(lane.shape, step_ref[position, 0], jnp.int32)
    for step in range(1, steps):
        index = jnp.where(lane >= step * rows, step_ref[position, step], index)
    fraction = 1.0 - index.astype(jnp.float32) / NSTEPS
    level = 3.0 * fraction / (1.0 + 2.0 * fraction)
    return (0.5 + level) * (LOG2E / math.sqrt(HD))


def lane_windows(steps, rows):
    total = steps * rows
    return [
        (step * rows // HD * HD, min(total, -(-(step + 1) * rows // HD) * HD))
        for step in range(steps)
    ]


def join_steps(pieces, windows, rows):
    total = windows[-1][1]
    tiles = []
    for first in range(0, total, HD):
        stop = min(first + HD, total)
        tile = None
        for step, (begin, end) in enumerate(windows):
            if begin <= first and stop <= end and step * rows < stop and first < (step + 1) * rows:
                part = pieces[step][:, first - begin : stop - begin]
                if tile is None:
                    tile = part
                else:
                    lane = lax.broadcasted_iota(jnp.int32, part.shape, 1) + first
                    tile = jnp.where(lane >= step * rows, part, tile)
        tiles.append(tile)
    return jnp.concatenate(tiles, 1)


def own_kernel(step_ref, q_ref, kv_ref, acc_ref, top_ref, total_ref):
    position = lax.axis_index("span")
    steps, _, rows, columns = q_ref.shape
    factors = row_factors(step_ref, position, steps, rows)
    windows = lane_windows(steps, rows)
    for head in range(columns // HD):
        cut = slice(head * HD, (head + 1) * HD)
        queries = q_ref[:, 0, :, cut].reshape(steps * rows, HD)
        scores = join_steps(
            [nt_dot(kv_ref[s, 0, 0, :, cut], queries[a:b]) for s, (a, b) in enumerate(windows)],
            windows,
            rows,
        )
        scores = scores * factors
        top = jnp.max(scores, axis=0, keepdims=True)
        weights = jnp.exp2(scores - top)
        rounded = weights.astype(jnp.bfloat16)
        acc_ref[head] = join_steps(
            [tn_dot(kv_ref[s, 1, 0, :, cut], rounded[:, a:b]) for s, (a, b) in enumerate(windows)],
            windows,
            rows,
        )
        top_ref[head : head + 1] = top
        total_ref[head : head + 1] = jnp.sum(weights, axis=0, keepdims=True)


def absorb(queries, keys, values, factors, acc, top, total):
    scores = nt_dot(keys, queries) * factors
    newest = jnp.maximum(top, jnp.max(scores, axis=0, keepdims=True))
    weights = jnp.exp2(scores - newest)
    shrink = jnp.exp2(top - newest)
    total = total * shrink + jnp.sum(weights, axis=0, keepdims=True)
    acc = acc * shrink + tn_dot(values, weights.astype(jnp.bfloat16))
    return acc, newest, total


def visible(mask_ref, position, blocks):
    seen = False
    for place, block in blocks.items():
        seen = seen | ((position == place) & (mask_ref[place, block] > 0))
    return seen


def half(ref, which, cut):
    return ref[which, 0, :, cut] if len(ref.shape) == 4 else ref[0, :, cut]


def mid_kernel(plan, step_ref, mask_ref, q_ref, *refs):
    block_refs, (acc_in, top_in, total_in, acc_ref, top_ref, total_ref) = refs[:-6], refs[-6:]
    position = lax.axis_index("span")
    steps, _, rows, columns = q_ref.shape
    seen = visible(mask_ref, position, plan)

    @pl.when(seen)
    def _():
        factors = row_factors(step_ref, position, steps, rows)
        for head in range(columns // HD):
            cut = slice(head * HD, (head + 1) * HD)
            queries = q_ref[:, 0, :, cut].reshape(steps * rows, HD)
            acc, top, total = absorb(
                queries,
                half(block_refs[0], 0, cut),
                half(block_refs[-1], 1, cut),
                factors,
                acc_in[head],
                top_in[head : head + 1],
                total_in[head : head + 1],
            )
            acc_ref[head] = acc
            top_ref[head : head + 1] = top
            total_ref[head : head + 1] = total

    @pl.when(jnp.logical_not(seen))
    def _():
        acc_ref[...] = acc_in[...]
        top_ref[...] = top_in[...]
        total_ref[...] = total_in[...]


def score_kernel(plans, step_ref, mask_ref, q_ref, *refs):
    key_refs, (acc_in, top_in, total_in, acc_ref, w_ref) = refs[:-5], refs[-5:]
    position = lax.axis_index("span")
    steps, _, rows, columns = q_ref.shape

    def finish(key_ref):
        factors = row_factors(step_ref, position, steps, rows)
        for head in range(columns // HD):
            cut = slice(head * HD, (head + 1) * HD)
            queries = q_ref[:, 0, :, cut].reshape(steps * rows, HD)
            scores = nt_dot(half(key_ref, 0, cut), queries) * factors
            top = top_in[head : head + 1]
            newest = jnp.maximum(top, jnp.max(scores, axis=0, keepdims=True))
            weights = jnp.exp2(scores - newest)
            shrink = jnp.exp2(top - newest)
            total = total_in[head : head + 1] * shrink + jnp.sum(weights, axis=0, keepdims=True)
            inverse = 1.0 / total
            w_ref[head] = (weights * inverse).astype(jnp.bfloat16)
            acc_ref[head] = acc_in[head] * (shrink * inverse)

    rest = True
    for plan, key_ref in zip(plans, key_refs):
        seen = visible(mask_ref, position, plan)
        rest = jnp.logical_and(rest, jnp.logical_not(seen))
        pl.when(seen)(functools.partial(finish, key_ref))

    @pl.when(rest)
    def _():
        w_ref[...] = jnp.zeros_like(w_ref)
        for head in range(columns // HD):
            acc_ref[head] = acc_in[head] * (1.0 / total_in[head : head + 1])


def average_head(head, acc_ref, w_ref, value_ref, first):
    width = acc_ref.shape[0] * HD
    if value_ref.shape[-1] == width:
        first = 0
    if value_ref.shape[-1] > width:
        first = -acc_ref.shape[0]
    cut = slice((head - first) * HD, (head - first + 1) * HD)
    return acc_ref[head] + tn_dot(half(value_ref, 1, cut), w_ref[head])


def average_kernel(begin, end, acc_ref, w_ref, value_ref, average_ref, square_ref):
    squares = jnp.zeros(square_ref.shape, jnp.float32)
    for head in range(begin, end):
        average = average_head(head, acc_ref, w_ref, value_ref, begin)
        squares = squares + jnp.sum(average * average, axis=0, keepdims=True)
        average_ref[:, :, (head - begin) * HD : (head - begin + 1) * HD] = average.T.reshape(
            average_ref.shape[:2] + (HD,)
        )
    square_ref[...] = squares


def rest_kernel(begin, end, acc_ref, w_ref, value_ref, before_ref, average_ref, square_ref):
    squares = before_ref[...]
    for head in range(begin, end):
        average = average_head(head, acc_ref, w_ref, value_ref, begin)
        squares = squares + jnp.sum(average * average, axis=0, keepdims=True)
        average_ref[head - begin] = average
    square_ref[...] = squares


def turn_kernel(in_ref, square_in, out_ref, square_ref):
    steps, rows, _ = out_ref.shape
    for head in range(in_ref.shape[0]):
        out_ref[:, :, head * HD : (head + 1) * HD] = in_ref[head].T.reshape(steps, rows, HD)
    square_ref[...] = square_in[...]


def scale_kernel(width, front_ref, back_ref, *refs):
    part_refs, (out_hbm, out_ref, sem) = refs[:-3], refs[-3:]
    total = part_refs[0][...]
    for ref in part_refs[1:]:
        total = total + ref[...]
    inverse = lax.rsqrt(total / width + 1e-06)
    steps, rows, columns = out_ref.shape
    spread = jnp.broadcast_to(inverse, (HD, steps * rows)).T
    copies = []
    for step in range(steps):
        factor = spread[step * rows : (step + 1) * rows]
        place = 0
        for ref in (front_ref, back_ref):
            for first in range(0, ref.shape[2], HD):
                average = ref[step, :, first : first + HD]
                out_ref[step, :, place : place + HD] = (average * factor).astype(jnp.bfloat16)
                place += HD
        copies.append(pltpu.make_async_copy(out_ref.at[step], out_hbm.at[step, 0], sem.at[step]))
        copies[-1].start()
    for copy in copies:
        copy.wait()


def send(value, pairs):
    return lax.ppermute(value, "span", pairs)


def delivered(span, back):
    return {place: place - back for place in range(back, span)}


def plain_call(kernel, name, out_shape, flops, operands, in_specs=(), out_specs=None, scratch=(), limit=VMEM_LIMIT):
    nbytes = sum(math.prod(o.shape) * o.dtype.itemsize for o in operands)
    if out_specs is None:
        out_specs = [VMEM_SPEC] * len(out_shape)
    return pl.pallas_call(
        kernel,
        in_specs=list(in_specs) + [VMEM_SPEC] * (len(operands) - len(in_specs)),
        out_specs=out_specs,
        out_shape=out_shape,
        scratch_shapes=list(scratch),
        compiler_params=pltpu.CompilerParams(vmem_limit_bytes=limit),
        cost_estimate=cost(flops, nbytes),
        name=name,
    )(*operands)


def picker(shape, wanted):
    row = lax.broadcasted_iota(jnp.int32, shape, 0)
    column = lax.broadcasted_iota(jnp.int32, shape, 1)
    return jnp.where(column == wanted(row), 1.0, 0.0).astype(jnp.bfloat16)


def project_kernel(axes, x_hbm, w_hbm, *refs):
    out_refs, (x_ref, w_ref, x_sem, w_sem) = refs[:-4], refs[-4:]
    rows, depth = x_ref.shape
    share = out_refs[0].shape[0]
    x_copy = pltpu.make_async_copy(x_hbm.at[0], x_ref, x_sem)
    x_copy.start()
    copies = []
    for place, first in enumerate(range(0, depth, 2 * HD)):
        cut = slice(first, min(first + 2 * HD, depth))
        copies.append((cut, pltpu.make_async_copy(w_hbm.at[cut], w_ref.at[cut], w_sem.at[place])))
        copies[-1][1].start()
    total = jnp.zeros((rows, w_ref.shape[1]), jnp.float32)
    x_copy.wait()
    for cut, w_copy in copies:
        w_copy.wait()
        total = total + nn_dot(x_ref[:, cut], w_ref[cut])
    projected = total.astype(jnp.bfloat16)
    for offset, out_ref in enumerate(out_refs):
        first = target_of(axes, offset) * share
        chosen = picker((share, rows), lambda row: row + first)
        out_ref[...] = nn_dot(chosen, projected).astype(jnp.bfloat16)


def gather_kernel(*refs):
    hidden_ref, tail_ref = refs[-2:]
    total = refs[0][...].astype(jnp.float32)
    for ref in refs[1:-2]:
        total = total + ref[...].astype(jnp.float32)
    hidden = total.astype(jnp.bfloat16)
    hidden_ref[...] = hidden
    kept = KT - 1 + FADE
    shape = (tail_ref.shape[0], hidden.shape[0])
    chosen = picker(shape, lambda row: row // kept * FR + FR - kept + row % kept)
    tail_ref[...] = nn_dot(chosen, hidden).astype(jnp.bfloat16)


def decode_kernel(fade_ref, hidden_ref, tail_ref, conv_ref, out_ref):
    position = lax.axis_index("span")
    share = hidden_ref.shape[0]
    spatial = share // FR
    kept = KT - 1 + FADE
    wide = FADE + FR
    hidden, tail = hidden_ref[...], tail_ref[...]
    mixed = jnp.zeros((spatial * wide, out_ref.shape[2]), jnp.float32)
    for tap in range(KT):
        def from_tail(row):
            place = row % wide + KT - 1 - tap
            return jnp.where(place < kept, row // wide * kept + place, -1)

        def from_hidden(row):
            place = row % wide + KT - 1 - tap
            return jnp.where(place >= kept, row // wide * FR + place - kept, -1)

        window = nn_dot(picker((spatial * wide, tail.shape[0]), from_tail), tail)
        window = window + nn_dot(picker((spatial * wide, share), from_hidden), hidden)
        mixed = mixed + nn_dot(window.astype(jnp.bfloat16), conv_ref[tap])
    frames = (mixed * jax.nn.sigmoid(mixed)).astype(jnp.bfloat16)
    fade = fade_ref[0]
    shape = (share, spatial * wide)
    current = nn_dot(picker(shape, lambda row: row // FR * wide + FADE + row % FR), frames)

    def faded(row):
        return jnp.where(row % FR < fade, row // FR * wide + FADE - fade + row % FR, -1)

    previous = nn_dot(picker(shape, faded), frames)
    frame = lax.broadcasted_iota(jnp.int32, (share, out_ref.shape[2]), 0) % FR
    fade_float = jnp.full(frame.shape, fade, jnp.int32).astype(jnp.float32)
    weight = (frame.astype(jnp.float32) + 1.0) / (fade_float + 1.0)
    weight = jnp.where((frame < fade) & (position > 0), weight, 1.0)
    out_ref[0] = (weight * current + (1.0 - weight) * previous).astype(jnp.bfloat16)


def project(finished, w_in):
    axes = ("mp", "seq")
    parts = lax.axis_size(axes)
    _, rows, depth = finished.shape
    channels = w_in.shape[1]
    chunks = -(-depth // (2 * HD))
    return plain_call(
        functools.partial(project_kernel, axes),
        "project",
        [jax.ShapeDtypeStruct((rows // parts, channels), jnp.bfloat16)] * parts,
        2 * rows * depth * channels,
        (finished, w_in),
        [HBM_SPEC] * 2,
        scratch=[
            pltpu.VMEM((rows, depth), jnp.bfloat16),
            pltpu.VMEM((depth, channels), jnp.bfloat16),
            pltpu.SemaphoreType.DMA,
            pltpu.SemaphoreType.DMA((chunks,)),
        ],
        limit=VMEM_ALL,
    )


def gather(parts, rows):
    share, channels = parts[0].shape
    tail_rows = share // FR * (KT - 1 + FADE)
    return plain_call(
        gather_kernel,
        "gather",
        [jax.ShapeDtypeStruct((count, channels), jnp.bfloat16) for count in (share, tail_rows)],
        rows * channels,
        parts,
    )


def decode(hidden, tail, conv_w, fade_count):
    share, channels = hidden.shape
    return plain_call(
        decode_kernel,
        "decode",
        [jax.ShapeDtypeStruct((1, share, channels), jnp.bfloat16)],
        2 * share * KT * channels * channels,
        (fade_count, hidden, tail, conv_w),
        [SMEM_SPEC],
    )[0]


def per_device(
    query, noisy_kv, clean_kv, causal_mask, step_index, finished, w_in, conv_w, fade_count
):
    steps, _, rows, columns = query.shape
    heads = columns // HD
    middle = (heads + 1) // 2 * HD
    row_count = steps * rows
    span = lax.axis_size("span")
    axes = ("mp", "seq")
    acc_shape = jax.ShapeDtypeStruct((heads, HD, row_count), jnp.float32)
    stat_shape = jax.ShapeDtypeStruct((heads, row_count), jnp.float32)
    pair_flops = 4 * row_count * rows * columns

    first_pairs = [(0, 2), (2, 3)] if span == 4 else [(c, c + 1) for c in range(span - 1)]
    near = send(clean_kv, first_pairs)
    pieces = project(finished, w_in)
    parts = [pieces[0]] + [swap(p, axes, offset + 1) for offset, p in enumerate(pieces[1:])]
    if span == 4:
        direct = send(clean_kv, [(1, 3)])
    carry = plain_call(
        own_kernel,
        "own",
        [acc_shape, stat_shape, stat_shape],
        3 * pair_flops,
        (step_index, query, noisy_kv),
        [SMEM_SPEC],
    )
    hidden, tail = gather(parts, rows)
    tail = hop(tail, "span", 1)
    if span == 4:
        near = after(near, carry[0], hidden)
        forwards = lax.axis_index("span") == 2
        passed = [jnp.where(forwards, near[which], clean_kv[which]) for which in range(2)]
        front = jnp.concatenate([passed[0], passed[1][:, :, :middle]], 2)
        passed = [front, passed[1][:, :, middle:]]
        passed = [hop(block, "span", 1) for block in passed]
        early = [(near, {2: 0, 3: 2}), (direct, {3: 1})]
        keys, values = passed[0], passed
        last_plan = {1: 0, 2: 1, 3: 0}
    else:
        ring = [near]
        for _ in range(2, span):
            ring.append(hop(ring[-1], "span", 1))
        early = [(block, delivered(span, back + 1)) for back, block in enumerate(ring[:-1])]
        keys, values = ring[-1], ring[-1:] * 2
        last_plan = delivered(span, span - 1)
    for block, plan in early:
        carry = plain_call(
            functools.partial(mid_kernel, plan),
            "middle",
            [acc_shape, stat_shape, stat_shape],
            pair_flops,
            (step_index, causal_mask, query, block, *carry),
            [SMEM_SPEC] * 2,
        )
    acc, weights = plain_call(
        functools.partial(score_kernel, [last_plan]),
        "score",
        [acc_shape, jax.ShapeDtypeStruct((heads, rows, row_count), jnp.bfloat16)],
        pair_flops // 2,
        (step_index, causal_mask, query, keys, *carry),
        [SMEM_SPEC] * 2,
    )
    square_shape = jax.ShapeDtypeStruct((1, row_count), jnp.float32)
    front, squares = plain_call(
        functools.partial(average_kernel, 0, middle // HD),
        "average",
        [jax.ShapeDtypeStruct((steps, rows, middle), jnp.float32), square_shape],
        pair_flops // 4,
        (acc, weights, values[0]),
    )
    averaged, squares = plain_call(
        functools.partial(rest_kernel, middle // HD, heads),
        "rest",
        [jax.ShapeDtypeStruct((heads - middle // HD, HD, row_count), jnp.float32), square_shape],
        pair_flops // 4,
        (acc, weights, values[1], squares),
    )
    others = [swap(squares, axes, offset) for offset in range(2, lax.axis_size(axes))]
    back, squares = plain_call(
        turn_kernel,
        "turn",
        [jax.ShapeDtypeStruct((steps, rows, columns - middle), jnp.float32), square_shape],
        row_count * columns,
        (averaged, squares),
    )
    others.append(swap(squares, axes, 1))
    decoded = decode(after(hidden, back), tail, conv_w, fade_count)
    attended = plain_call(
        functools.partial(scale_kernel, columns * lax.axis_size(axes)),
        "scale",
        jax.ShapeDtypeStruct(query.shape, jnp.bfloat16),
        row_count * columns,
        (front, back, squares, *others),
        out_specs=HBM_SPEC,
        scratch=[
            pltpu.VMEM((steps, rows, columns), jnp.bfloat16),
            pltpu.SemaphoreType.DMA((steps,)),
        ],
    )
    return (attended, decoded)


def solution(mesh):
    placed = (
        P(None, ("groups", "span"), None, ("mp", "seq")),
        P(None, None, ("groups", "span"), None, ("mp", "seq")),
        P(None, ("groups", "span"), None, ("mp", "seq")),
        P("groups", None),
        P("groups", None),
        P(("groups", "span"), None, ("mp", "seq")),
        P(("mp", "seq"), None),
        P(),
        P(("groups", "span")),
    )
    return jax.shard_map(
        per_device,
        mesh=mesh,
        in_specs=placed,
        out_specs=(
            P(None, ("groups", "span"), None, ("mp", "seq")),
            P(("groups", "span"), ("mp", "seq"), None),
        ),
        check_vma=False,
    )
```
